128 devices in a mesh: dp: 4 (over y), expert: 8 (over z, core), tensor: 4 (over x).
Axes of the slice: x: 4, y: 4, z: 4, core: 2. Of those that a mesh axis runs over, the one named last changes fastest.
Arguments:
- tokens: bfloat16 [16384, 1536], P(('dp', 'expert', 'tensor')), may hold values from -6 to 6
- documents: int32 [16384], P(('dp', 'expert')), may hold values from 0 to 2, as said below
- expert_routes: int32 [16384, 8], P(('dp', 'expert', 'tensor')), may hold values from 0 to 39, all different within a row; in each aligned block of 128 rows (0 to 127, 128 to 255, ...) at most 36 rows name the same one
- attention_gain: bfloat16 [1536], replicated, may hold values from 0.5 to 1.5
- query_weight: bfloat16 [1536, 1536], P(None, 'tensor'), may hold values from -0.15625 to 0.15625
- key_matrix: bfloat16 [1536, 512], P(None, 'tensor'), may hold values from -0.15625 to 0.15625
- value_matrix: bfloat16 [1536, 512], P(None, 'tensor'), may hold values from -0.15625 to 0.15625
- output_weight: bfloat16 [1536, 1536], P('tensor'), may hold values from -1.25 to 1.25
- expert_gain: bfloat16 [1536], replicated, may hold values from 0.5 to 1.5
- router_weight: bfloat16 [1536, 40], replicated, may hold values from -0.078125 to 0.078125
- gate_weight: bfloat16 [40, 1536, 512], P('expert', None, 'tensor'), may hold values from -0.15625 to 0.15625
- up_weight: bfloat16 [40, 1536, 512], P('expert', None, 'tensor'), may hold values from -0.15625 to 0.15625
- down_weight: bfloat16 [40, 512, 1536], P('expert', 'tensor'), may hold values from -1 to 1
- out_cotangent: bfloat16 [16384, 1536], P(('dp', 'expert', 'tensor')), may hold values from -6 to 6
Outputs:
- layer_output: bfloat16 [16384, 1536], P(('dp', 'expert', 'tensor'))
- input_gradient: float32 [16384, 1536], P(('dp', 'expert', 'tensor'))
- attention_gain_gradient: float32 [1536], replicated
- query_gradient: float32 [1536, 1536], P(None, 'tensor')
- key_gradient: float32 [1536, 512], P(None, 'tensor')
- value_gradient: float32 [1536, 512], P(None, 'tensor')
- output_gradient: float32 [1536, 1536], P('tensor')
- expert_gain_gradient: float32 [1536], replicated
- router_gradient: float32 [1536, 40], replicated
- gate_gradient: float32 [40, 1536, 512], P('expert', None, 'tensor')
- up_gradient: float32 [40, 1536, 512], P('expert', None, 'tensor')
- down_gradient: float32 [40, 512, 1536], P('expert', 'tensor')
The draws below stay inside these ranges and needn't reach their ends.
Inputs may be any that keep to these rules, and one draw needn't show every extreme that they name: `documents`: in each group of 512 consecutive tokens the ids never fall and begin at 0. `expert_routes`: each token names 8 different experts; among the pairs of the 128 tokens of one device no expert is named more than 36 times.
All inputs are finite; a program needn't handle non-finite values.
Results may differ from the reference program's by a relative error of at most 0.025.
Values may be sent and summed in bfloat16 or wider, within the bound.
A program may use at most 384 MiB of HBM per device.

```python
import math
import jax
import jax.numpy as jnp
import numpy as np
from jax import lax

MODEL_WIDTH = 1536
QUERY_HEADS = 24
KEY_VALUE_HEADS = 8
HEAD_SIZE = 64
FF = 512
EXPERTS = 40
TOP = 8
TOK_DEV = 128
GROUP_TOK = 512
GROUPS = 32
TOKENS = 16384
CAP = 36
DEVICES = 128


def draw_documents(key, part):
    key = jax.random.fold_in(key, 7)
    first_key, second_key = jax.random.split(key)
    first_cut = jax.random.randint(first_key, (GROUPS, 1), 1, TOK_DEV, dtype=jnp.int32)
    second_cut = jax.random.randint(second_key, (GROUPS, 1), 3 * TOK_DEV, GROUP_TOK, dtype=jnp.int32)
    positions = jnp.arange(GROUP_TOK, dtype=jnp.int32)[None, :]
    labels = (positions >= first_cut).astype(jnp.int32) + (positions >= second_cut).astype(jnp.int32)
    return labels.reshape(GROUPS * GROUP_TOK)


def shard_levels(stream_key, dims, cuts, low, top_value):
    level = 1.0
    for axis_at, shards_of in cuts:
        heights = jax.random.uniform(jax.random.fold_in(jax.random.fold_in(stream_key, 6), axis_at), (shards_of,), jnp.float32, low / len(cuts), top_value / len(cuts))
        level = level * jnp.repeat(jnp.exp(heights), dims[axis_at] // shards_of).reshape((-1,) + (1,) * (len(dims) - 1 - axis_at))
    return level


def deal_out(key, own, number, rows, number_of, top, bound, skew):
    sequence = jax.random.permutation(key, number_of)
    crowded, ordinary = shares(number_of, rows * top, bound, skew, True), shares(number_of, rows * top, bound, skew, False)
    places = jnp.arange(number_of)

    def named(sizes, turn):
        used = int((sizes > 0).sum())
        fixed = max(1, used // 4)
        passed = fixed + (places - fixed + turn * (used - fixed)) % max(1, number_of - fixed)
        return jnp.zeros((number_of,), jnp.int32).at[sequence[jnp.where(places < fixed, places, passed)]].set(jnp.asarray(sizes, jnp.int32))

    sizes = jnp.where(number % 4 == 0, named(crowded, number // 4), named(ordinary, number - number // 4 - 1))
    mixed = jax.random.permutation(jax.random.fold_in(own, 3), number_of)
    giver, taker = mixed[0:number_of // 2 * 2:2], mixed[1:number_of // 2 * 2:2]
    slack = jnp.minimum(sizes[giver] - 1, bound - sizes[taker]) // 2
    slack = jnp.where((giver == sequence[0]) | (taker == sequence[0]) | (sizes[taker] == 0), 0, jnp.maximum(slack, 0))
    passed = jax.random.randint(jax.random.fold_in(own, 4), (number_of // 2,), 0, 1 << 20) % (slack + 1)
    sizes = sizes.at[giver].add(-passed).at[taker].add(passed)
    items = jnp.searchsorted(jnp.cumsum(sizes), jnp.arange(rows * top), side="right").astype(jnp.int32)
    table = items.reshape(top, rows).T
    table = table[jax.random.permutation(jax.random.fold_in(own, 1), rows)]
    turn = jax.random.randint(jax.random.fold_in(own, 2), (rows, 1), 0, top)
    return jnp.take_along_axis(table, (jnp.arange(top)[None, :] + turn) % top, axis=1)


def shares(amount, total, reach, skew, full):
    weights = [(1 << 20) // math.isqrt(standing ** skew) + 1 for standing in range(1, amount + 1)]
    largest = reach if full else min(reach, max(-(-total // amount), total * weights[0] // sum(weights)))
    least = 1 if total - largest >= amount - 1 else 0
    holding, surplus = [largest] + [least] * (amount - 1), total - largest - least * (amount - 1)
    while surplus > 0:
        movable = [i for i in range(1, amount) if holding[i] < largest] or [i for i in range(1, amount) if holding[i] < reach]
        pool, left = sum([weights[i] for i in movable]), surplus
        for i in movable:
            more = min(reach - holding[i], max(1, left * weights[i] // pool), surplus)
            holding[i] = holding[i] + more
            surplus = surplus - more
    return np.array(holding)


def noise(rng, dims, scale, most, cuts=(), kind=jnp.bfloat16):
    level = shard_levels(rng, dims, cuts, -0.22, 0.18) if cuts else 1.0
    array = jax.random.normal(rng, dims, jnp.float32) * scale * level
    return jnp.minimum(jnp.maximum(array, -most), most).astype(kind)


def setup_inputs(seed: int = 0) -> dict:
    key_list = jax.random.split(jax.random.key(seed), 15)
    tokens = noise(key_list[0], (TOKENS, MODEL_WIDTH), 1.0, 6.0, ((0, 128),))
    documents = draw_documents(jax.random.fold_in(key_list[14], 71), 0)
    expert_routes_keys = jax.random.split(jax.random.fold_in(key_list[2], 1), TOKENS // TOK_DEV)
    expert_routes_turns = jax.random.permutation(jax.random.fold_in(key_list[2], 3), TOKENS // TOK_DEV)
    expert_routes = jax.vmap(lambda own, number: deal_out(jax.random.fold_in(key_list[2], 2), own, number, TOK_DEV, EXPERTS, TOP, CAP, 2))(expert_routes_keys, expert_routes_turns).reshape((TOKENS, TOP))
    attention_gain = jnp.clip(1.0 + 0.1 * jax.random.normal(key_list[3], (MODEL_WIDTH,), jnp.float32), 0.5, 1.5).astype(jnp.bfloat16)
    query_weight = noise(key_list[4], (MODEL_WIDTH, QUERY_HEADS * HEAD_SIZE), MODEL_WIDTH ** -0.5, 0.15625, ((1, 4),))
    key_matrix = noise(key_list[5], (MODEL_WIDTH, KEY_VALUE_HEADS * HEAD_SIZE), MODEL_WIDTH ** -0.5, 0.15625, ((1, 4),))
    value_matrix = noise(key_list[6], (MODEL_WIDTH, KEY_VALUE_HEADS * HEAD_SIZE), MODEL_WIDTH ** -0.5, 0.15625, ((1, 4),))
    output_weight = noise(key_list[7], (QUERY_HEADS * HEAD_SIZE, MODEL_WIDTH), (QUERY_HEADS * HEAD_SIZE // 64) ** -0.5, 1.25, ((0, 4),))
    expert_gain = jnp.clip(1.0 + 0.1 * jax.random.normal(key_list[8], (MODEL_WIDTH,), jnp.float32), 0.5, 1.5).astype(jnp.bfloat16)
    router_weight = noise(key_list[9], (MODEL_WIDTH, EXPERTS), (4 * MODEL_WIDTH) ** -0.5, 0.078125)
    gate_weight = noise(key_list[10], (EXPERTS, MODEL_WIDTH, FF), MODEL_WIDTH ** -0.5, 0.15625, ((0, 8), (2, 4)))
    up_weight = noise(key_list[11], (EXPERTS, MODEL_WIDTH, FF), MODEL_WIDTH ** -0.5, 0.15625, ((0, 8), (2, 4)))
    down_weight = noise(key_list[12], (EXPERTS, FF, MODEL_WIDTH), (FF // 16) ** -0.5, 1.0, ((0, 8), (1, 4)))
    out_cotangent = noise(key_list[13], (TOKENS, MODEL_WIDTH), 1.0, 6.0, ((0, 128),))
    return {"tokens": tokens, "documents": documents, "expert_routes": expert_routes, "attention_gain": attention_gain, "query_weight": query_weight, "key_matrix": key_matrix, "value_matrix": value_matrix, "output_weight": output_weight, "expert_gain": expert_gain, "router_weight": router_weight, "gate_weight": gate_weight, "up_weight": up_weight, "down_weight": down_weight, "out_cotangent": out_cotangent}


@jax.custom_vjp
def lowered_input(v):
    return lax.optimization_barrier(v.astype(jnp.bfloat16)).astype(jnp.float32)

@jax.custom_vjp
def lowered_gradient(v):
    return v

def low_keep(v):
    return (lowered_input(v), None)

def low_pass(kept, grad):
    return (grad,)

def back_keep(v):
    return (v, None)

def back_low(kept, grad):
    return (lowered_input(grad),)
lowered_input.defvjp(low_keep, low_pass)
lowered_gradient.defvjp(back_keep, back_low)
epsilon = 1e-06
theta = 10000.0
highest = lax.Precision.HIGHEST

def multiplier(left, right):
    return jnp.dot(left, right, precision=highest, preferred_element_type=jnp.float32)

def rms_scale(value_rows, gain):
    return value_rows * lax.rsqrt(lax.optimization_barrier(jnp.mean(value_rows * value_rows, -1, keepdims=True)) + epsilon) * gain

def rope_tables(positions, width):
    half = width // 2
    freq = theta ** (-(jnp.arange(half, dtype=jnp.float32) * 2.0 / width))
    angle = positions.astype(jnp.float32)[:, None] * freq[None, :]
    return (jnp.cos(angle), jnp.sin(angle))

def apply_rotation(value_rows, cosine_table, sine_table):
    half = value_rows.shape[-1] // 2
    first = value_rows[..., :half]
    second = value_rows[..., half:]
    cosine_table = cosine_table[:, None, :]
    sine_table = sine_table[:, None, :]
    return jnp.concatenate([first * cosine_table - second * sine_table, second * cosine_table + first * sine_table], -1)

def attend_group(normalized_rows, documents, query_weight, key_matrix, value_matrix, output_weight):
    sequence_length = normalized_rows.shape[0]
    frequency_ratio = QUERY_HEADS // KEY_VALUE_HEADS
    index = jnp.arange(sequence_length, dtype=jnp.int32)
    earlier = lax.optimization_barrier(jnp.sum((documents[None, :] < documents[:, None]).astype(jnp.int32), 1)).astype(jnp.int32)
    positions = index - earlier
    cosine_table, sine_table = rope_tables(positions, HEAD_SIZE)
    query_linear = lowered_gradient(multiplier(normalized_rows, query_weight)).reshape(sequence_length, QUERY_HEADS, HEAD_SIZE)
    key_linear = lowered_gradient(multiplier(normalized_rows, key_matrix)).reshape(sequence_length, KEY_VALUE_HEADS, HEAD_SIZE)
    value_rows = lowered_gradient(lowered_input(multiplier(normalized_rows, value_matrix))).reshape(sequence_length, KEY_VALUE_HEADS, HEAD_SIZE)
    query_rows = lowered_input(apply_rotation(query_linear, cosine_table, sine_table)).reshape(sequence_length, KEY_VALUE_HEADS, frequency_ratio, HEAD_SIZE)
    keys = lowered_input(apply_rotation(key_linear, cosine_table, sine_table))
    scores = jnp.einsum('qhgd,khd->hgqk', query_rows, keys, precision=highest, preferred_element_type=jnp.float32) * (1.0 / math.sqrt(HEAD_SIZE))
    scores = lowered_gradient(scores)
    allowed = (documents[:, None] == documents[None, :]) & (index[None, :] <= index[:, None])
    scores = jnp.where(allowed, scores, -1e+30)
    top = lax.optimization_barrier(jnp.max(scores, -1, keepdims=True))
    weights = jnp.exp(scores - top)
    probs = lowered_input(weights / lax.optimization_barrier(jnp.sum(weights, -1, keepdims=True)))
    mixed = jnp.einsum('hgqk,khd->qhgd', probs, value_rows, precision=highest, preferred_element_type=jnp.float32)
    attended = lowered_gradient(lowered_input(mixed.reshape(sequence_length, QUERY_HEADS * HEAD_SIZE)))
    return lowered_gradient(multiplier(attended, output_weight))

def expert_term(second_low, gates_flat, gate_piece, up_piece, down_piece, token_piece, route_piece, valid_piece):
    rows = lowered_gradient(second_low[token_piece] * valid_piece[:, None])
    gate_pre = lowered_gradient(multiplier(rows, gate_piece))
    up_pre = lowered_gradient(multiplier(rows, up_piece))
    activated = lowered_input(gate_pre * jax.nn.sigmoid(gate_pre) * up_pre)
    expert_out = lowered_gradient(lowered_input(multiplier(activated, down_piece)))
    return expert_out * (gates_flat[route_piece] * valid_piece)[:, None]

def slot_sources(expert_routes):
    route_total = TOK_DEV * TOP
    routes_dev = expert_routes.reshape(DEVICES, route_total)

    def one_block(block_routes):
        flat_hot = (block_routes[:, None] == jnp.arange(EXPERTS, dtype=jnp.int32)[None, :]).astype(jnp.int32)
        running = jnp.cumsum(flat_hot, 0).astype(jnp.int32)
        rank = lax.optimization_barrier(jnp.sum((running - 1) * flat_hot, 1)).astype(jnp.int32)
        slots = (block_routes * CAP + rank).astype(jnp.int32)
        empty = jnp.full((EXPERTS * CAP,), route_total, jnp.int32)
        return empty.at[slots].set(jnp.arange(route_total, dtype=jnp.int32))
    sources = jax.vmap(one_block)(routes_dev)
    filled = sources < route_total
    offsets = (jnp.arange(DEVICES, dtype=jnp.int32) * route_total)[:, None]
    global_route = (jnp.minimum(sources, route_total - 1) + offsets).astype(jnp.int32)
    per_expert = global_route.reshape(DEVICES, EXPERTS, CAP).transpose(1, 0, 2).reshape(EXPERTS, DEVICES * CAP)
    valid = filled.reshape(DEVICES, EXPERTS, CAP).transpose(1, 0, 2).reshape(EXPERTS, DEVICES * CAP).astype(jnp.float32)
    return (per_expert, valid)

def reference(tokens, documents, expert_routes, attention_gain, query_weight, key_matrix, value_matrix, output_weight, expert_gain, router_weight, gate_weight, up_weight, down_weight, out_cotangent):
    per_expert, valid = slot_sources(expert_routes)
    tokens_of = (per_expert // TOP).astype(jnp.int32)
    onehot = (expert_routes[:, :, None] == jnp.arange(EXPERTS, dtype=jnp.int32)[None, None, :]).astype(jnp.float32)

    def forward(inputs, first_gain, query_w, key_w, value_w, output_w, second_gain, router_w, gate_w, up_w, down_w):
        first_low = lowered_input(rms_scale(inputs, first_gain))

        def group_step(pieces):
            return attend_group(pieces[0], pieces[1], query_w, key_w, value_w, output_w)
        branch = lax.map(jax.checkpoint(group_step), (first_low.reshape(GROUPS, GROUP_TOK, MODEL_WIDTH), documents.reshape(GROUPS, GROUP_TOK)))
        residual = inputs + branch.reshape(TOKENS, MODEL_WIDTH)
        second_low = lowered_input(rms_scale(residual, second_gain))
        logits = multiplier(second_low, router_w)
        chosen = lax.optimization_barrier(jnp.sum(onehot * logits[:, None, :], -1))
        chosen_exp = jnp.exp(chosen - lax.optimization_barrier(jnp.max(chosen, -1, keepdims=True)))
        gates = chosen_exp / lax.optimization_barrier(jnp.sum(chosen_exp, -1, keepdims=True))
        gates_flat = gates.reshape(-1)
        term = jax.checkpoint(expert_term)

        def expert_step(mixture, pieces):
            contribution = term(second_low, gates_flat, pieces[0], pieces[1], pieces[2], pieces[3], pieces[4], pieces[5])
            return (mixture.at[pieces[3]].add(contribution), None)
        start = jnp.zeros((TOKENS, MODEL_WIDTH), jnp.float32)
        mixture, unused = lax.scan(expert_step, start, (gate_w, up_w, down_w, tokens_of, per_expert, valid))
        return lowered_input(residual + mixture)
    floats = (tokens.astype(jnp.float32), attention_gain.astype(jnp.float32), query_weight.astype(jnp.float32), key_matrix.astype(jnp.float32), value_matrix.astype(jnp.float32), output_weight.astype(jnp.float32), expert_gain.astype(jnp.float32), router_weight.astype(jnp.float32), gate_weight.astype(jnp.float32), up_weight.astype(jnp.float32), down_weight.astype(jnp.float32))
    result, pullback = jax.vjp(forward, *floats)
    grads = pullback(out_cotangent.astype(jnp.float32))
    return (result.astype(jnp.bfloat16), grads[0], grads[1], grads[2], grads[3], grads[4], grads[5], grads[6], grads[7], grads[8], grads[9], grads[10])
```

```python
import math

import jax
import jax.numpy as jnp
from jax import lax
from jax.sharding import PartitionSpec as P

HEAD_SIZE = 64


epsilon = 1e-06
theta = 10000.0
highest = lax.Precision.HIGHEST


def normalize(value_rows, gain):
    scale = lax.rsqrt(jnp.mean(value_rows * value_rows, -1, keepdims=True) + epsilon)
    return (value_rows * scale * gain, scale)


def norm_back(value_rows, scale, gain, upstream):
    weighted = upstream * gain
    inner = jnp.mean(weighted * value_rows, -1, keepdims=True)
    result = scale * weighted - value_rows * scale**3 * inner
    gain_part = jnp.sum(upstream * value_rows * scale, 0)
    return (result, gain_part)


def rope_tables(positions, width):
    half = width // 2
    freq = theta ** (-(jnp.arange(half, dtype=jnp.float32) * 2.0 / width))
    angle = positions.astype(jnp.float32)[:, None] * freq[None, :]
    return (jnp.cos(angle), jnp.sin(angle))


def apply_rotation(value_rows, cosine_table, sine_table):
    half = value_rows.shape[-1] // 2
    first = value_rows[..., :half]
    second = value_rows[..., half:]
    cosine_table = cosine_table[:, None, :]
    sine_table = sine_table[:, None, :]
    return jnp.concatenate(
        [first * cosine_table - second * sine_table, second * cosine_table + first * sine_table], -1
    )


def rotate_back(value_rows, cosine_table, sine_table):
    half = value_rows.shape[-1] // 2
    first = value_rows[..., :half]
    second = value_rows[..., half:]
    cosine_table = cosine_table[:, None, :]
    sine_table = sine_table[:, None, :]
    return jnp.concatenate(
        [first * cosine_table + second * sine_table, second * cosine_table - first * sine_table], -1
    )


def shards(
    tokens,
    documents,
    expert_routes,
    attention_gain,
    query_weight,
    key_matrix,
    value_matrix,
    output_weight,
    expert_gain,
    router_weight,
    gate_weight,
    up_weight,
    down_weight,
    out_cotangent,
):
    n_tensor = lax.axis_size("tensor")
    n_expert = lax.axis_size("expert")
    tok_local = tokens.shape[0]
    width = tokens.shape[1]
    group_len = documents.shape[0]
    query_heads = query_weight.shape[1] // HEAD_SIZE
    pair_heads = key_matrix.shape[1] // HEAD_SIZE
    frequency_ratio = query_heads // pair_heads
    local_experts = gate_weight.shape[0]
    experts_all = router_weight.shape[1]
    scale = 1.0 / math.sqrt(HEAD_SIZE)
    inputs = tokens.astype(jnp.float32)
    first_gain = attention_gain.astype(jnp.float32)
    first_normed, first_scale = normalize(inputs, first_gain)
    group_rows = lax.all_gather(first_normed.astype(jnp.bfloat16), "tensor", axis=0, tiled=True)
    index = jnp.arange(group_len, dtype=jnp.int32)
    positions = index - jnp.sum((documents[None, :] < documents[:, None]).astype(jnp.int32), 1)
    cosine_table, sine_table = rope_tables(positions, HEAD_SIZE)
    query_linear = jnp.dot(group_rows, query_weight, preferred_element_type=jnp.float32).reshape(
        group_len, query_heads, HEAD_SIZE
    )
    key_linear = jnp.dot(group_rows, key_matrix, preferred_element_type=jnp.float32).reshape(
        group_len, pair_heads, HEAD_SIZE
    )
    value_low = (
        jnp.dot(group_rows, value_matrix, preferred_element_type=jnp.float32)
        .astype(jnp.bfloat16)
        .reshape(group_len, pair_heads, HEAD_SIZE)
    )
    query_low = (
        apply_rotation(query_linear, cosine_table, sine_table)
        .astype(jnp.bfloat16)
        .reshape(group_len, pair_heads, frequency_ratio, HEAD_SIZE)
    )
    key_low = apply_rotation(key_linear, cosine_table, sine_table).astype(jnp.bfloat16)
    block_rows = min(512, group_len)
    count = group_len // block_rows
    starts = jnp.arange(count, dtype=jnp.int32) * block_rows

    def block_scores(start):
        rows_index = start + jnp.arange(block_rows, dtype=jnp.int32)
        scores = (
            jnp.einsum("qhgd,khd->hgqk", query_low, key_low, preferred_element_type=jnp.float32)
            * scale
        )
        allowed = (documents[:, None] == documents[None, :]) & (
            index[None, :] <= rows_index[:, None]
        )
        return (jnp.where(allowed, scores, -1e30), query_low)

    def forward_block(start):
        scores, block_query = block_scores(start)
        top = jnp.max(scores, -1, keepdims=True)
        weights = jnp.exp(scores - top)
        total = jnp.sum(weights, -1, keepdims=True)
        probs = (weights / total).astype(jnp.bfloat16)
        mixed = jnp.einsum("hgqk,khd->qhgd", probs, value_low, preferred_element_type=jnp.float32)
        return (
            mixed.astype(jnp.bfloat16).reshape(block_rows, query_heads * HEAD_SIZE),
            (top + jnp.log(total))[..., 0],
        )

    mixed_blocks, logsum_blocks = lax.map(forward_block, starts)
    attended = mixed_blocks.reshape(group_len, query_heads * HEAD_SIZE)
    head_part = jnp.dot(attended, output_weight, preferred_element_type=jnp.float32)
    branch = lax.psum_scatter(
        head_part.astype(jnp.bfloat16), "tensor", scatter_dimension=0, tiled=True
    ).astype(jnp.float32)
    residual = inputs + branch
    second_gain = expert_gain.astype(jnp.float32)
    second_normed, second_scale = normalize(residual, second_gain)
    second_low = second_normed.astype(jnp.bfloat16)
    plane = ("expert", "tensor")
    experts_index = jnp.arange(experts_all, dtype=jnp.int32)
    plane_routes = lax.all_gather(expert_routes, plane, axis=0, tiled=True)
    plane_upstream = lax.all_gather(out_cotangent, plane, axis=0, tiled=True)
    plane_rows = lax.all_gather(second_low, plane, axis=0, tiled=True)

    def dense_gates(rows, routes):
        named = jnp.any(routes[:, :, None] == experts_index[None, None, :], 1)
        logits = jnp.dot(rows, router_weight, preferred_element_type=jnp.float32)
        logits = jnp.where(named, logits, -1e30)
        raised = jnp.exp(logits - jnp.max(logits, -1, keepdims=True))
        return raised / jnp.sum(raised, -1, keepdims=True)

    first_expert = lax.axis_index("expert") * local_experts
    plane_gates = lax.dynamic_slice_in_dim(
        dense_gates(plane_rows, plane_routes), first_expert, local_experts, 1
    )
    plane_len = plane_rows.shape[0]
    hidden = gate_weight.shape[2]
    wide = local_experts * hidden
    gate_flat = gate_weight.transpose(1, 0, 2).reshape(width, wide)
    up_flat = up_weight.transpose(1, 0, 2).reshape(width, wide)
    down_flat = down_weight.reshape(wide, width)
    gate_pre = jnp.dot(plane_rows, gate_flat, preferred_element_type=jnp.float32)
    up_pre = jnp.dot(plane_rows, up_flat, preferred_element_type=jnp.float32)
    raw_grad = jnp.einsum(
        "td,fd->tf", plane_upstream, down_flat, preferred_element_type=jnp.float32
    )
    gates_wide = jnp.repeat(plane_gates, hidden, axis=1)
    sigmoid_gate = jax.nn.sigmoid(gate_pre)
    silu_gate = gate_pre * sigmoid_gate
    activated = silu_gate * up_pre
    gate_grad_part = jnp.sum(
        (activated * raw_grad).reshape(plane_len, local_experts, hidden), -1
    )
    gated = (gates_wide * activated).astype(jnp.bfloat16)
    act_grad = gates_wide * raw_grad
    gate_pre_grad = (
        act_grad * up_pre * sigmoid_gate * (1.0 + gate_pre * (1.0 - sigmoid_gate))
    ).astype(jnp.bfloat16)
    up_pre_grad = (act_grad * silu_gate).astype(jnp.bfloat16)
    mixture_part = jnp.dot(gated, down_flat, preferred_element_type=jnp.float32)
    mixture = lax.psum_scatter(
        mixture_part.astype(jnp.bfloat16), plane, scatter_dimension=0, tiled=True
    ).astype(jnp.float32)
    layer_output = (residual + mixture).astype(jnp.bfloat16)
    rows_part = jnp.einsum(
        "tf,df->td", gate_pre_grad, gate_flat, preferred_element_type=jnp.float32
    ) + jnp.einsum("tf,df->td", up_pre_grad, up_flat, preferred_element_type=jnp.float32)
    route_rows = lax.psum_scatter(
        rows_part.astype(jnp.bfloat16), plane, scatter_dimension=0, tiled=True
    ).astype(jnp.float32)
    down_local = jnp.einsum(
        "tf,td->fd", gated, plane_upstream, preferred_element_type=jnp.float32
    ).reshape(local_experts, hidden, width)
    gate_local = (
        jnp.einsum("td,tf->df", plane_rows, gate_pre_grad, preferred_element_type=jnp.float32)
        .reshape(width, local_experts, hidden)
        .transpose(1, 0, 2)
    )
    up_local = (
        jnp.einsum("td,tf->df", plane_rows, up_pre_grad, preferred_element_type=jnp.float32)
        .reshape(width, local_experts, hidden)
        .transpose(1, 0, 2)
    )
    sent_grads = gate_grad_part.reshape(n_expert * n_tensor, tok_local, local_experts)
    come_grads = lax.all_to_all(sent_grads, plane, split_axis=0, concat_axis=0, tiled=True)
    gate_grad = (
        jnp.sum(come_grads.reshape(n_expert, n_tensor, tok_local, local_experts), 1)
        .transpose(1, 0, 2)
        .reshape(tok_local, experts_all)
    )
    gates = dense_gates(second_low, expert_routes)
    upstream = out_cotangent.astype(jnp.float32)
    gate_mean = jnp.sum(gates * gate_grad, -1, keepdims=True)
    logit_grad = gates * (gate_grad - gate_mean)
    router_local = jnp.einsum(
        "td,te->de",
        second_low.astype(jnp.float32),
        logit_grad,
        precision=highest,
        preferred_element_type=jnp.float32,
    )
    normed_back = route_rows + jnp.einsum(
        "te,de->td",
        logit_grad,
        router_weight.astype(jnp.float32),
        precision=highest,
        preferred_element_type=jnp.float32,
    )
    residual_back, expert_gain_local = norm_back(residual, second_scale, second_gain, normed_back)
    residual_grad = upstream + residual_back
    group_grad = lax.all_gather(residual_grad.astype(jnp.bfloat16), "tensor", axis=0, tiled=True)
    attended_grad = jnp.einsum(
        "td,hd->th", group_grad, output_weight, preferred_element_type=jnp.float32
    ).astype(jnp.bfloat16)
    attended_grad = attended_grad.reshape(group_len, pair_heads, frequency_ratio, HEAD_SIZE)
    output_local = jnp.einsum("th,td->hd", attended, group_grad, preferred_element_type=jnp.float32)

    def backward_block(carry, pieces):
        key_acc, value_acc = carry
        start, logsum = pieces
        scores, block_query = block_scores(start)
        probs = jnp.exp(scores - logsum[..., None])
        prob_grad = jnp.einsum(
            "qhgd,khd->hgqk", attended_grad, value_low, preferred_element_type=jnp.float32
        )
        value_acc = value_acc + jnp.einsum(
            "hgqk,qhgd->khd",
            probs.astype(jnp.bfloat16),
            attended_grad,
            preferred_element_type=jnp.float32,
        )
        inner = jnp.sum(probs * prob_grad, -1, keepdims=True)
        score_grad = (probs * (prob_grad - inner)).astype(jnp.bfloat16)
        query_turned = (
            jnp.einsum("hgqk,khd->qhgd", score_grad, key_low, preferred_element_type=jnp.float32)
            * scale
        )
        key_acc = (
            key_acc
            + jnp.einsum(
                "hgqk,qhgd->khd", score_grad, block_query, preferred_element_type=jnp.float32
            )
            * scale
        )
        return ((key_acc, value_acc), query_turned)

    zero_keys = jnp.zeros((group_len, pair_heads, HEAD_SIZE), jnp.float32)
    (key_turned, value_acc), query_blocks = lax.scan(
        backward_block, (zero_keys, zero_keys), (starts, logsum_blocks)
    )
    query_turned = query_blocks.reshape(group_len, query_heads, HEAD_SIZE)
    query_back = (
        rotate_back(query_turned, cosine_table, sine_table)
        .astype(jnp.bfloat16)
        .reshape(group_len, query_heads * HEAD_SIZE)
    )
    key_back = (
        rotate_back(key_turned, cosine_table, sine_table)
        .astype(jnp.bfloat16)
        .reshape(group_len, pair_heads * HEAD_SIZE)
    )
    value_back = value_acc.astype(jnp.bfloat16).reshape(group_len, pair_heads * HEAD_SIZE)
    query_local = jnp.einsum(
        "td,th->dh", group_rows, query_back, preferred_element_type=jnp.float32
    )
    key_local = jnp.einsum("td,th->dh", group_rows, key_back, preferred_element_type=jnp.float32)
    value_local = jnp.einsum(
        "td,th->dh", group_rows, value_back, preferred_element_type=jnp.float32
    )
    normed_part = jnp.einsum(
        "th,dh->td", query_back, query_weight, preferred_element_type=jnp.float32
    )
    normed_part = normed_part + jnp.einsum(
        "th,dh->td", key_back, key_matrix, preferred_element_type=jnp.float32
    )
    normed_part = normed_part + jnp.einsum(
        "th,dh->td", value_back, value_matrix, preferred_element_type=jnp.float32
    )
    normed_grad = lax.psum_scatter(
        normed_part.astype(jnp.bfloat16), "tensor", scatter_dimension=0, tiled=True
    ).astype(jnp.float32)
    input_back, attention_gain_local = norm_back(inputs, first_scale, first_gain, normed_grad)
    input_gradient = residual_grad + input_back
    query_gradient, key_gradient, value_gradient, output_gradient = (
        lax.psum(query_local.astype(jnp.bfloat16), ("dp", "expert")).astype(jnp.float32),
        lax.psum(key_local.astype(jnp.bfloat16), ("dp", "expert")).astype(jnp.float32),
        lax.psum(value_local.astype(jnp.bfloat16), ("dp", "expert")).astype(jnp.float32),
        lax.psum(output_local.astype(jnp.bfloat16), ("dp", "expert")).astype(jnp.float32),
    )
    router_gradient, attention_gain_gradient, expert_gain_gradient = lax.psum(
        (router_local, attention_gain_local, expert_gain_local), ("dp", "expert", "tensor")
    )
    gate_gradient, up_gradient, down_gradient = (
        lax.psum(gate_local.astype(jnp.bfloat16), "dp").astype(jnp.float32),
        lax.psum(up_local.astype(jnp.bfloat16), "dp").astype(jnp.float32),
        lax.psum(down_local.astype(jnp.bfloat16), "dp").astype(jnp.float32),
    )
    return (
        layer_output,
        input_gradient,
        attention_gain_gradient,
        query_gradient,
        key_gradient,
        value_gradient,
        output_gradient,
        expert_gain_gradient,
        router_gradient,
        gate_gradient,
        up_gradient,
        down_gradient,
    )


def solution(mesh):
    placed = (
        P(("dp", "expert", "tensor"), None),
        P(("dp", "expert")),
        P(("dp", "expert", "tensor"), None),
        P(),
        P(None, "tensor"),
        P(None, "tensor"),
        P(None, "tensor"),
        P("tensor", None),
        P(),
        P(),
        P("expert", None, "tensor"),
        P("expert", None, "tensor"),
        P("expert", "tensor", None),
        P(("dp", "expert", "tensor"), None),
    )
    return jax.shard_map(
        shards,
        mesh=mesh,
        in_specs=placed,
        out_specs=(
            P(("dp", "expert", "tensor"), None),
            P(("dp", "expert", "tensor"), None),
            P(),
            P(None, "tensor"),
            P(None, "tensor"),
            P(None, "tensor"),
            P("tensor", None),
            P(),
            P(),
            P("expert", None, "tensor"),
            P("expert", None, "tensor"),
            P("expert", "tensor", None),
        ),
        check_vma=False,
    )
```

```python
import functools
import math

import jax
import jax.numpy as jnp
from jax import lax
from jax.experimental import pallas as pl
from jax.experimental.pallas import tpu as pltpu
from jax.sharding import PartitionSpec as P

HEAD_SIZE = 64


epsilon = 1e-06
theta = 10000.0
highest = lax.Precision.HIGHEST


def normalize(value_rows, gain):
    scale = lax.rsqrt(jnp.mean(value_rows * value_rows, -1, keepdims=True) + epsilon)
    return (value_rows * scale * gain, scale)


def norm_back(value_rows, scale, gain, upstream):
    weighted = upstream * gain
    inner = jnp.mean(weighted * value_rows, -1, keepdims=True)
    result = scale * weighted - value_rows * scale**3 * inner
    gain_part = jnp.sum(upstream * value_rows * scale, 0)
    return (result, gain_part)


def rope_tables(positions, width):
    half = width // 2
    freq = theta ** (-(jnp.arange(half, dtype=jnp.float32) * 2.0 / width))
    angle = positions.astype(jnp.float32)[:, None] * freq[None, :]
    return (jnp.cos(angle), jnp.sin(angle))


def apply_rotation(value_rows, cosine_table, sine_table):
    half = value_rows.shape[-1] // 2
    first = value_rows[..., :half]
    second = value_rows[..., half:]
    cosine_table = cosine_table[:, None, :]
    sine_table = sine_table[:, None, :]
    return jnp.concatenate(
        [first * cosine_table - second * sine_table, second * cosine_table + first * sine_table], -1
    )


def rotate_back(value_rows, cosine_table, sine_table):
    half = value_rows.shape[-1] // 2
    first = value_rows[..., :half]
    second = value_rows[..., half:]
    cosine_table = cosine_table[:, None, :]
    sine_table = sine_table[:, None, :]
    return jnp.concatenate(
        [first * cosine_table + second * sine_table, second * cosine_table - first * sine_table], -1
    )


MESH = pl.DeviceIdType.MESH

def ag_plane_kernel(src, out, own_sem, send_sem, recv_sem, sib_send, sib_recv):
    x = lax.axis_index("tensor"); e = lax.axis_index("expert")
    z = e // 2; c = e % 2
    def peer(ox, oz):
        return {"expert": ((z + oz) % 4) * 2 + c, "tensor": (x + ox) % 4}
    sib = {"expert": z * 2 + 1 - c}
    def blk(dx, dz):
        return (((z + dz) % 4) * 2 + c) * 4 + (x + dx) % 4
    def sblk(dx, dz):
        return (((z + dz) % 4) * 2 + 1 - c) * 4 + (x + dx) % 4
    barrier = pltpu.get_barrier_semaphore()
    near = [peer(1, 0), peer(-1, 0), peer(0, 1), peer(0, -1), sib]
    for p in near:
        pl.semaphore_signal(barrier, inc=1, device_id=p, device_id_type=MESH)
    pl.semaphore_wait(barrier, len(near))
    n = [0]
    pend = []
    def desc(dx, dz, ox, oz, q, nq, sidx, own=False):
        rows = pl.ds(q * 32, nq * 32)
        s = src.at[rows] if own else out.at[blk(dx, dz), rows]
        return pltpu.make_async_remote_copy(
            src_ref=s, dst_ref=out.at[blk(dx, dz), rows],
            send_sem=send_sem.at[sidx],
            recv_sem=recv_sem.at[(dx - ox) % 4, (dz - oz) % 4, q],
            device_id=peer(ox, oz), device_id_type=MESH)
    def send(dx, dz, ox, oz, q, nq, own=False):
        cp = desc(dx, dz, ox, oz, q, nq, n[0], own)
        n[0] += 1
        cp.start(); pend.append(cp)
    def recv(dx, dz, q, nq):
        rows = pl.ds(q * 32, nq * 32)
        pltpu.make_async_remote_copy(
            src_ref=out.at[blk(dx, dz), rows], dst_ref=out.at[blk(dx, dz), rows],
            send_sem=send_sem.at[0], recv_sem=recv_sem.at[dx % 4, dz % 4, q],
            device_id=peer(1, 0), device_id_type=MESH).wait_recv()
    sn = [0]
    def sibsend(dx, dz, own=False):
        cp = pltpu.make_async_remote_copy(
            src_ref=src if own else out.at[blk(dx, dz)], dst_ref=out.at[blk(dx, dz)],
            send_sem=sib_send.at[dx % 4, dz % 4], recv_sem=sib_recv.at[dx % 4, dz % 4],
            device_id=sib, device_id_type=MESH)
        cp.start(); pend.append(cp)
    for ox, oz in ((1, 0), (-1, 0), (0, 1), (0, -1)):
        send(0, 0, ox, oz, 0, 4, own=True)
    mine = pltpu.make_async_copy(src, out.at[blk(0, 0)], own_sem)
    mine.start()
    sibsend(0, 0, own=True)
    for s in (1, -1):
        recv(s, 0, 0, 4)
        if s == -1:
            send(s, 0, 1, 0, 1, 2)
        else:
            send(s, 0, -1, 0, 0, 1); send(s, 0, -1, 0, 3, 1)
        for oz in (1, -1):
            send(s, 0, 0, oz, 0, 2)
        recv(0, s, 0, 4)
        if s == -1:
            send(0, s, 0, 1, 1, 2)
        else:
            send(0, s, 0, -1, 0, 1); send(0, s, 0, -1, 3, 1)
        for ox in (1, -1):
            send(0, s, ox, 0, 2, 2)
        sibsend(s, 0); sibsend(0, s)
    recv(2, 0, 1, 2); recv(2, 0, 0, 1); recv(2, 0, 3, 1)
    for oz in (1, -1):
        send(2, 0, 0, oz, 0, 2)
    recv(0, 2, 1, 2); recv(0, 2, 0, 1); recv(0, 2, 3, 1)
    for ox in (1, -1):
        send(0, 2, ox, 0, 2, 2)
    sibsend(2, 0); sibsend(0, 2)
    for dx in (1, -1, 2):
        for s in (1, -1):
            recv(dx, s, 0, 2)
            send(dx, s, 0, -s, 0 if s == 1 else 1, 1)
            recv(s, dx, 2, 2)
            send(s, dx, -s, 0, 2 if s == 1 else 3, 1)
    for dx in (1, -1):
        for dz in (1, -1):
            sibsend(dx, dz)
    for dx in (1, -1, 2):
        recv(dx, 2, 0, 1); recv(dx, 2, 1, 1)
        recv(2, dx, 2, 1); recv(2, dx, 3, 1)
    for dx in (1, -1, 2):
        sibsend(dx, 2)
        if dx != 2: sibsend(2, dx)
    for dx in range(4):
        for dz in range(4):
            pltpu.make_async_remote_copy(
                src_ref=src, dst_ref=out.at[sblk(dx, dz)],
                send_sem=sib_send.at[dx, dz], recv_sem=sib_recv.at[dx, dz],
                device_id=sib, device_id_type=MESH).wait_recv()
    mine.wait()
    for cp in pend:
        cp.wait_send()

def ag_plane(shard, cid):
    rows, width = shard.shape
    return pl.pallas_call(
        ag_plane_kernel,
        out_shape=jax.ShapeDtypeStruct((32, rows, width), shard.dtype),
        in_specs=[pl.BlockSpec(memory_space=pl.ANY)],
        out_specs=pl.BlockSpec(memory_space=pl.ANY),
        scratch_shapes=[pltpu.SemaphoreType.DMA(()), pltpu.SemaphoreType.DMA((40,)),
                        pltpu.SemaphoreType.DMA((4, 4, 4)), pltpu.SemaphoreType.DMA((4, 4)), pltpu.SemaphoreType.DMA((4, 4))],
        compiler_params=pltpu.CompilerParams(collective_id=cid, has_side_effects=True),
        name="ag_plane",
    )(shard)


def rs_plane_kernel(nk, p0, p1, out, q, sib, a3, b3, a4, b4, a5, b5, a6, b6,
                    load_sem, sib_send, sib_recv, ssem, rsem):
    x = lax.axis_index("tensor"); e = lax.axis_index("expert")
    z = e // 2; c = e % 2
    def zi(d): return (z + d) % 4
    def xi(d): return (x + d) % 4
    def peer(oz, ox):
        return {"expert": zi(oz) * 2 + c, "tensor": xi(ox)}
    partner = {"expert": z * 2 + 1 - c}
    barrier = pltpu.get_barrier_semaphore()
    near = [peer(1, 0), peer(-1, 0), peer(0, 1), peer(0, -1), partner]
    for p in near:
        pl.semaphore_signal(barrier, inc=1, device_id=p, device_id_type=MESH)
    pl.semaphore_wait(barrier, len(near))
    H = slice(0, 32)
    f32 = jnp.float32

    def cols(k): return pl.ds(pl.multiple_of(k * 128, 128), 128)
    def loads(k):
        return [pltpu.make_async_copy(p.at[:, c, :, :, cols(k)], q.at[k, :, :, :, pl.ds(128 * i, 128)], load_sem.at[k, i])
                for i, p in enumerate((p0, p1))]
    def sibs(k):
        return [pltpu.make_async_remote_copy(
            src_ref=p.at[:, 1 - c, :, :, cols(k)], dst_ref=sib.at[k, :, :, :, pl.ds(128 * i, 128)],
            send_sem=sib_send.at[k, i], recv_sem=sib_recv.at[k, i], device_id=partner, device_id_type=MESH)
            for i, p in enumerate((p0, p1))]
    def rc(k, n, src, dst, to):
        return pltpu.make_async_remote_copy(src_ref=src, dst_ref=dst, send_sem=ssem.at[k, n], recv_sem=rsem.at[k, n],
                                            device_id=to, device_id_type=MESH)
    def copies3(k):
        return [rc(k, 0, q.at[k, zi(2), :, pl.ds(0, 32)], a3.at[k, 0], peer(1, 0)),
                rc(k, 1, q.at[k, zi(2), :, pl.ds(32, 32)], a3.at[k, 1], peer(-1, 0)),
                rc(k, 2, q.at[k, :, xi(2), pl.ds(64, 32)], b3.at[k, 0], peer(0, 1)),
                rc(k, 3, q.at[k, :, xi(2), pl.ds(96, 32)], b3.at[k, 1], peer(0, -1))]
    def copies4(k):
        return [rc(k, 4, q.at[k, zi(1), :, pl.ds(0, 64)], a4.at[k, 0], peer(1, 0)),
                rc(k, 5, q.at[k, zi(-1), :, pl.ds(0, 64)], a4.at[k, 1], peer(-1, 0)),
                rc(k, 6, q.at[k, :, xi(1), pl.ds(64, 64)], b4.at[k, 0], peer(0, 1)),
                rc(k, 7, q.at[k, :, xi(-1), pl.ds(64, 64)], b4.at[k, 1], peer(0, -1))]
    def copies5(k):
        return [rc(k, 8, q.at[k, z, xi(2), pl.ds(0, 32)], a5.at[k, 0], peer(0, 1)),
                rc(k, 9, q.at[k, z, xi(2), pl.ds(32, 32)], a5.at[k, 1], peer(0, -1)),
                rc(k, 10, q.at[k, zi(2), x, pl.ds(64, 32)], b5.at[k, 0], peer(1, 0)),
                rc(k, 11, q.at[k, zi(2), x, pl.ds(96, 32)], b5.at[k, 1], peer(-1, 0))]
    def copies6(k):
        return [rc(k, 12, q.at[k, z, xi(1), pl.ds(0, 64)], a6.at[k, 0], peer(0, 1)),
                rc(k, 13, q.at[k, z, xi(-1), pl.ds(0, 64)], a6.at[k, 1], peer(0, -1)),
                rc(k, 14, q.at[k, zi(1), x, pl.ds(64, 64)], b6.at[k, 0], peer(1, 0)),
                rc(k, 15, q.at[k, zi(-1), x, pl.ds(64, 64)], b6.at[k, 1], peer(-1, 0))]
    def add(k, i, j, rows, *terms):
        t = q[k, i, j, rows].astype(f32)
        for s in terms:
            t = t + s.astype(f32)
        q[k, i, j, rows] = t.astype(jnp.bfloat16)

    def stage1(k):
        for cp in sibs(k): cp.start()
        for cp in loads(k): cp.start()
    def stage2(k):
        for cp in loads(k): cp.wait()
        for cp in sibs(k): cp.wait_recv()
        def body(n, _):
            add(k, n // 4, n % 4, pl.ds(0, 128), sib[k, n // 4, n % 4])
            return 0
        lax.fori_loop(0, 16, body, 0)
        for cp in copies3(k): cp.start()
    def stage4(k):
        for cp in copies3(k): cp.wait_recv()
        def body(n, _):
            add(k, zi(1), n, pl.ds(0, 32), a3[k, 0, n])
            add(k, zi(-1), n, pl.ds(32, 32), a3[k, 1, n])
            add(k, n, xi(1), pl.ds(64, 32), b3[k, 0, n])
            add(k, n, xi(-1), pl.ds(96, 32), b3[k, 1, n])
            return 0
        lax.fori_loop(0, 4, body, 0)
        for cp in copies4(k): cp.start()
    def stage5(k):
        for cp in copies4(k): cp.wait_recv()
        def body(n, _):
            add(k, z, n, pl.ds(0, 64), a4[k, 0, n], a4[k, 1, n])
            add(k, n, x, pl.ds(64, 64), b4[k, 0, n], b4[k, 1, n])
            return 0
        lax.fori_loop(0, 4, body, 0)
        for cp in copies5(k): cp.start()
    def stage6(k):
        for cp in copies5(k): cp.wait_recv()
        add(k, z, xi(1), pl.ds(0, 32), a5[k, 0])
        add(k, z, xi(-1), pl.ds(32, 32), a5[k, 1])
        add(k, zi(1), x, pl.ds(64, 32), b5[k, 0])
        add(k, zi(-1), x, pl.ds(96, 32), b5[k, 1])
        for cp in copies6(k): cp.start()
    def stage7(k):
        for cp in copies6(k): cp.wait_recv()
        for h, m in ((0, a6), (64, b6)):
            t = q[k, z, x, pl.ds(h, 64)].astype(f32) + m[k, 0].astype(f32) + m[k, 1].astype(f32)
            out[0, pl.ds(h, 64), cols(k)] = t[:, :128]
            out[1, pl.ds(h, 64), cols(k)] = t[:, 128:]
        for cp in sibs(k) + copies3(k) + copies4(k) + copies5(k) + copies6(k): cp.wait_send()
    def step(i, _):
        for lag, st in ((8, stage7), (7, stage6), (5, stage5), (3, stage4), (1, stage2), (0, stage1)):
            k = i - lag
            @pl.when((k >= 0) & (k < nk))
            def _():
                st(k)
        return 0
    lax.fori_loop(0, nk + 8, step, 0)

def rs_plane(p0, p1, cid, nk=12):
    bf = jnp.bfloat16
    width = p0.shape[-1]
    p0 = p0.reshape(4, 2, 4, 128, width); p1 = p1.reshape(4, 2, 4, 128, width)
    V = pltpu.VMEM
    return pl.pallas_call(
        functools.partial(rs_plane_kernel, nk),
        out_shape=jax.ShapeDtypeStruct((2, 128, width), jnp.float32),
        in_specs=[pl.BlockSpec(memory_space=pl.ANY)] * 2,
        out_specs=pl.BlockSpec(memory_space=pltpu.VMEM),
        scratch_shapes=[V((nk, 4, 4, 128, 256), bf), V((nk, 4, 4, 128, 256), bf),
                        V((nk, 2, 4, 32, 256), bf), V((nk, 2, 4, 32, 256), bf),
                        V((nk, 2, 4, 64, 256), bf), V((nk, 2, 4, 64, 256), bf),
                        V((nk, 2, 32, 256), bf), V((nk, 2, 32, 256), bf),
                        V((nk, 2, 64, 256), bf), V((nk, 2, 64, 256), bf),
                        pltpu.SemaphoreType.DMA((nk, 2)), pltpu.SemaphoreType.DMA((nk, 2)), pltpu.SemaphoreType.DMA((nk, 2)),
                        pltpu.SemaphoreType.DMA((nk, 16)), pltpu.SemaphoreType.DMA((nk, 16))],
        compiler_params=pltpu.CompilerParams(collective_id=cid, has_side_effects=True, vmem_limit_bytes=56 << 20),
        name="rs_plane",
    )(p0, p1)


def shards(
    tokens,
    documents,
    expert_routes,
    attention_gain,
    query_weight,
    key_matrix,
    value_matrix,
    output_weight,
    expert_gain,
    router_weight,
    gate_weight,
    up_weight,
    down_weight,
    out_cotangent,
):
    n_tensor = lax.axis_size("tensor")
    n_expert = lax.axis_size("expert")
    tok_local = tokens.shape[0]
    width = tokens.shape[1]
    group_len = documents.shape[0]
    query_heads = query_weight.shape[1] // HEAD_SIZE
    pair_heads = key_matrix.shape[1] // HEAD_SIZE
    frequency_ratio = query_heads // pair_heads
    local_experts = gate_weight.shape[0]
    experts_all = router_weight.shape[1]
    scale = 1.0 / math.sqrt(HEAD_SIZE)
    inputs = tokens.astype(jnp.float32)
    first_gain = attention_gain.astype(jnp.float32)
    first_normed, first_scale = normalize(inputs, first_gain)
    group_rows = lax.all_gather(first_normed.astype(jnp.bfloat16), "tensor", axis=0, tiled=True)
    index = jnp.arange(group_len, dtype=jnp.int32)
    positions = index - jnp.sum((documents[None, :] < documents[:, None]).astype(jnp.int32), 1)
    cosine_table, sine_table = rope_tables(positions, HEAD_SIZE)
    query_linear = jnp.dot(group_rows, query_weight, preferred_element_type=jnp.float32).reshape(
        group_len, query_heads, HEAD_SIZE
    )
    key_linear = jnp.dot(group_rows, key_matrix, preferred_element_type=jnp.float32).reshape(
        group_len, pair_heads, HEAD_SIZE
    )
    value_low = (
        jnp.dot(group_rows, value_matrix, preferred_element_type=jnp.float32)
        .astype(jnp.bfloat16)
        .reshape(group_len, pair_heads, HEAD_SIZE)
    )
    query_low = (
        apply_rotation(query_linear, cosine_table, sine_table)
        .astype(jnp.bfloat16)
        .reshape(group_len, pair_heads, frequency_ratio, HEAD_SIZE)
    )
    key_low = apply_rotation(key_linear, cosine_table, sine_table).astype(jnp.bfloat16)
    block_rows = min(512, group_len)
    count = group_len // block_rows
    starts = jnp.arange(count, dtype=jnp.int32) * block_rows

    def block_scores(start):
        rows_index = start + jnp.arange(block_rows, dtype=jnp.int32)
        scores = (
            jnp.einsum("qhgd,khd->hgqk", query_low, key_low, preferred_element_type=jnp.float32)
            * scale
        )
        allowed = (documents[:, None] == documents[None, :]) & (
            index[None, :] <= rows_index[:, None]
        )
        return (jnp.where(allowed, scores, -1e30), query_low)

    def forward_block(start):
        scores, block_query = block_scores(start)
        top = jnp.max(scores, -1, keepdims=True)
        weights = jnp.exp(scores - top)
        total = jnp.sum(weights, -1, keepdims=True)
        probs = (weights / total).astype(jnp.bfloat16)
        mixed = jnp.einsum("hgqk,khd->qhgd", probs, value_low, preferred_element_type=jnp.float32)
        return (
            mixed.astype(jnp.bfloat16).reshape(block_rows, query_heads * HEAD_SIZE),
            (top + jnp.log(total))[..., 0],
        )

    mixed_blocks, logsum_blocks = lax.map(forward_block, starts)
    attended = mixed_blocks.reshape(group_len, query_heads * HEAD_SIZE)
    head_part = jnp.dot(attended, output_weight, preferred_element_type=jnp.float32)
    branch = lax.psum_scatter(
        head_part.astype(jnp.bfloat16), "tensor", scatter_dimension=0, tiled=True
    ).astype(jnp.float32)
    residual = inputs + branch
    second_gain = expert_gain.astype(jnp.float32)
    second_normed, second_scale = normalize(residual, second_gain)
    second_low = second_normed.astype(jnp.bfloat16)
    plane = ("expert", "tensor")
    experts_index = jnp.arange(experts_all, dtype=jnp.int32)
    plane_routes = lax.all_gather(expert_routes, plane, axis=0, tiled=True)
    plane_upstream = lax.all_gather(out_cotangent, plane, axis=0, tiled=True)
    plane_rows = ag_plane(second_low, 1).reshape(-1, width)

    def dense_gates(rows, routes):
        named = jnp.any(routes[:, :, None] == experts_index[None, None, :], 1)
        logits = jnp.dot(rows, router_weight, preferred_element_type=jnp.float32)
        logits = jnp.where(named, logits, -1e30)
        raised = jnp.exp(logits - jnp.max(logits, -1, keepdims=True))
        return raised / jnp.sum(raised, -1, keepdims=True)

    first_expert = lax.axis_index("expert") * local_experts
    plane_gates = lax.dynamic_slice_in_dim(
        dense_gates(plane_rows, plane_routes), first_expert, local_experts, 1
    )
    plane_len = plane_rows.shape[0]
    hidden = gate_weight.shape[2]
    wide = local_experts * hidden
    gate_flat = gate_weight.transpose(1, 0, 2).reshape(width, wide)
    up_flat = up_weight.transpose(1, 0, 2).reshape(width, wide)
    down_flat = down_weight.reshape(wide, width)
    gate_pre = jnp.dot(plane_rows, gate_flat, preferred_element_type=jnp.float32)
    up_pre = jnp.dot(plane_rows, up_flat, preferred_element_type=jnp.float32)
    raw_grad = jnp.einsum(
        "td,fd->tf", plane_upstream, down_flat, preferred_element_type=jnp.float32
    )
    gates_wide = jnp.repeat(plane_gates, hidden, axis=1)
    sigmoid_gate = jax.nn.sigmoid(gate_pre)
    silu_gate = gate_pre * sigmoid_gate
    activated = silu_gate * up_pre
    gate_grad_part = jnp.sum(
        (activated * raw_grad).reshape(plane_len, local_experts, hidden), -1
    )
    gated = (gates_wide * activated).astype(jnp.bfloat16)
    act_grad = gates_wide * raw_grad
    gate_pre_grad = (
        act_grad * up_pre * sigmoid_gate * (1.0 + gate_pre * (1.0 - sigmoid_gate))
    ).astype(jnp.bfloat16)
    up_pre_grad = (act_grad * silu_gate).astype(jnp.bfloat16)
    mixture_part = jnp.dot(gated, down_flat, preferred_element_type=jnp.float32)
    rows_part = jnp.einsum(
        "tf,df->td", gate_pre_grad, gate_flat, preferred_element_type=jnp.float32
    ) + jnp.einsum("tf,df->td", up_pre_grad, up_flat, preferred_element_type=jnp.float32)
    weighted = plane_gates * gate_grad_part
    weighted_high = weighted.astype(jnp.bfloat16)
    weighted_low = (weighted - weighted_high.astype(jnp.float32)).astype(jnp.bfloat16)
    own_router = lax.dynamic_slice_in_dim(router_weight, first_expert, local_experts, 1)
    rows_part = rows_part + jnp.einsum(
        "te,de->td", weighted_high, own_router, preferred_element_type=jnp.float32
    )
    mixture, route_rows = rs_plane(
        mixture_part.astype(jnp.bfloat16), rows_part.astype(jnp.bfloat16), 2
    )
    layer_output = (residual + mixture).astype(jnp.bfloat16)
    router_pairs = jnp.einsum(
        "td,te->de",
        plane_rows,
        jnp.concatenate([weighted_high, weighted_low], 1),
        preferred_element_type=jnp.float32,
    )
    router_pairs = router_pairs[:, :local_experts] + router_pairs[:, local_experts:]
    down_local = jnp.einsum(
        "tf,td->fd", gated, plane_upstream, preferred_element_type=jnp.float32
    ).reshape(local_experts, hidden, width)
    gate_local = (
        jnp.einsum("td,tf->df", plane_rows, gate_pre_grad, preferred_element_type=jnp.float32)
        .reshape(width, local_experts, hidden)
        .transpose(1, 0, 2)
    )
    up_local = (
        jnp.einsum("td,tf->df", plane_rows, up_pre_grad, preferred_element_type=jnp.float32)
        .reshape(width, local_experts, hidden)
        .transpose(1, 0, 2)
    )
    gates = dense_gates(second_low, expert_routes)
    upstream = out_cotangent.astype(jnp.float32)
    shared = gates * jnp.sum(mixture * upstream, -1, keepdims=True)
    router_local = -jnp.einsum(
        "td,te->de",
        second_low.astype(jnp.float32),
        shared,
        precision=highest,
        preferred_element_type=jnp.float32,
    ) + lax.dynamic_update_slice_in_dim(
        jnp.zeros((width, experts_all), jnp.float32), router_pairs, first_expert, 1
    )
    normed_back = route_rows - jnp.einsum(
        "te,de->td",
        shared,
        router_weight.astype(jnp.float32),
        precision=highest,
        preferred_element_type=jnp.float32,
    )
    residual_back, expert_gain_local = norm_back(residual, second_scale, second_gain, normed_back)
    residual_grad = upstream + residual_back
    group_grad = lax.all_gather(residual_grad.astype(jnp.bfloat16), "tensor", axis=0, tiled=True)
    attended_grad = jnp.einsum(
        "td,hd->th", group_grad, output_weight, preferred_element_type=jnp.float32
    ).astype(jnp.bfloat16)
    attended_grad = attended_grad.reshape(group_len, pair_heads, frequency_ratio, HEAD_SIZE)
    output_local = jnp.einsum("th,td->hd", attended, group_grad, preferred_element_type=jnp.float32)

    def backward_block(carry, pieces):
        key_acc, value_acc = carry
        start, logsum = pieces
        scores, block_query = block_scores(start)
        probs = jnp.exp(scores - logsum[..., None])
        prob_grad = jnp.einsum(
            "qhgd,khd->hgqk", attended_grad, value_low, preferred_element_type=jnp.float32
        )
        value_acc = value_acc + jnp.einsum(
            "hgqk,qhgd->khd",
            probs.astype(jnp.bfloat16),
            attended_grad,
            preferred_element_type=jnp.float32,
        )
        inner = jnp.sum(probs * prob_grad, -1, keepdims=True)
        score_grad = (probs * (prob_grad - inner)).astype(jnp.bfloat16)
        query_turned = (
            jnp.einsum("hgqk,khd->qhgd", score_grad, key_low, preferred_element_type=jnp.float32)
            * scale
        )
        key_acc = (
            key_acc
            + jnp.einsum(
                "hgqk,qhgd->khd", score_grad, block_query, preferred_element_type=jnp.float32
            )
            * scale
        )
        return ((key_acc, value_acc), query_turned)

    zero_keys = jnp.zeros((group_len, pair_heads, HEAD_SIZE), jnp.float32)
    (key_turned, value_acc), query_blocks = lax.scan(
        backward_block, (zero_keys, zero_keys), (starts, logsum_blocks)
    )
    query_turned = query_blocks.reshape(group_len, query_heads, HEAD_SIZE)
    query_back = (
        rotate_back(query_turned, cosine_table, sine_table)
        .astype(jnp.bfloat16)
        .reshape(group_len, query_heads * HEAD_SIZE)
    )
    key_back = (
        rotate_back(key_turned, cosine_table, sine_table)
        .astype(jnp.bfloat16)
        .reshape(group_len, pair_heads * HEAD_SIZE)
    )
    value_back = value_acc.astype(jnp.bfloat16).reshape(group_len, pair_heads * HEAD_SIZE)
    query_local = jnp.einsum(
        "td,th->dh", group_rows, query_back, preferred_element_type=jnp.float32
    )
    key_local = jnp.einsum("td,th->dh", group_rows, key_back, preferred_element_type=jnp.float32)
    value_local = jnp.einsum(
        "td,th->dh", group_rows, value_back, preferred_element_type=jnp.float32
    )
    normed_part = jnp.einsum(
        "th,dh->td", query_back, query_weight, preferred_element_type=jnp.float32
    )
    normed_part = normed_part + jnp.einsum(
        "th,dh->td", key_back, key_matrix, preferred_element_type=jnp.float32
    )
    normed_part = normed_part + jnp.einsum(
        "th,dh->td", value_back, value_matrix, preferred_element_type=jnp.float32
    )
    normed_grad = lax.psum_scatter(
        normed_part.astype(jnp.bfloat16), "tensor", scatter_dimension=0, tiled=True
    ).astype(jnp.float32)
    input_back, attention_gain_local = norm_back(inputs, first_scale, first_gain, normed_grad)
    input_gradient = residual_grad + input_back
    query_gradient, key_gradient, value_gradient, output_gradient = (
        lax.psum(query_local.astype(jnp.bfloat16), ("dp", "expert")).astype(jnp.float32),
        lax.psum(key_local.astype(jnp.bfloat16), ("dp", "expert")).astype(jnp.float32),
        lax.psum(value_local.astype(jnp.bfloat16), ("dp", "expert")).astype(jnp.float32),
        lax.psum(output_local.astype(jnp.bfloat16), ("dp", "expert")).astype(jnp.float32),
    )
    router_gradient, attention_gain_gradient, expert_gain_gradient = lax.psum(
        (router_local, attention_gain_local, expert_gain_local), ("dp", "expert", "tensor")
    )
    gate_gradient, up_gradient, down_gradient = (
        lax.psum(gate_local.astype(jnp.bfloat16), "dp").astype(jnp.float32),
        lax.psum(up_local.astype(jnp.bfloat16), "dp").astype(jnp.float32),
        lax.psum(down_local.astype(jnp.bfloat16), "dp").astype(jnp.float32),
    )
    return (
        layer_output,
        input_gradient,
        attention_gain_gradient,
        query_gradient,
        key_gradient,
        value_gradient,
        output_gradient,
        expert_gain_gradient,
        router_gradient,
        gate_gradient,
        up_gradient,
        down_gradient,
    )


def solution(mesh):
    placed = (
        P(("dp", "expert", "tensor"), None),
        P(("dp", "expert")),
        P(("dp", "expert", "tensor"), None),
        P(),
        P(None, "tensor"),
        P(None, "tensor"),
        P(None, "tensor"),
        P("tensor", None),
        P(),
        P(),
        P("expert", None, "tensor"),
        P("expert", None, "tensor"),
        P("expert", "tensor", None),
        P(("dp", "expert", "tensor"), None),
    )
    return jax.shard_map(
        shards,
        mesh=mesh,
        in_specs=placed,
        out_specs=(
            P(("dp", "expert", "tensor"), None),
            P(("dp", "expert", "tensor"), None),
            P(),
            P(None, "tensor"),
            P(None, "tensor"),
            P(None, "tensor"),
            P("tensor", None),
            P(),
            P(),
            P("expert", None, "tensor"),
            P("expert", None, "tensor"),
            P("expert", "tensor", None),
        ),
        check_vma=False,
    )
```

```python
import functools
import math

import jax
import jax.numpy as jnp
from jax import lax
from jax.experimental import pallas as pl
from jax.experimental.pallas import tpu as pltpu
from jax.sharding import PartitionSpec as P

HEAD_SIZE = 64


epsilon = 1e-06
theta = 10000.0
highest = lax.Precision.HIGHEST


def normalize(value_rows, gain):
    scale = lax.rsqrt(jnp.mean(value_rows * value_rows, -1, keepdims=True) + epsilon)
    return (value_rows * scale * gain, scale)


def norm_back(value_rows, scale, gain, upstream):
    weighted = upstream * gain
    inner = jnp.mean(weighted * value_rows, -1, keepdims=True)
    result = scale * weighted - value_rows * scale**3 * inner
    gain_part = jnp.sum(upstream * value_rows * scale, 0)
    return (result, gain_part)


def rope_tables(positions, width):
    half = width // 2
    freq = theta ** (-(jnp.arange(half, dtype=jnp.float32) * 2.0 / width))
    angle = positions.astype(jnp.float32)[:, None] * freq[None, :]
    return (jnp.cos(angle), jnp.sin(angle))


def apply_rotation(value_rows, cosine_table, sine_table):
    half = value_rows.shape[-1] // 2
    first = value_rows[..., :half]
    second = value_rows[..., half:]
    cosine_table = cosine_table[:, None, :]
    sine_table = sine_table[:, None, :]
    return jnp.concatenate(
        [first * cosine_table - second * sine_table, second * cosine_table + first * sine_table], -1
    )


def rotate_back(value_rows, cosine_table, sine_table):
    half = value_rows.shape[-1] // 2
    first = value_rows[..., :half]
    second = value_rows[..., half:]
    cosine_table = cosine_table[:, None, :]
    sine_table = sine_table[:, None, :]
    return jnp.concatenate(
        [first * cosine_table + second * sine_table, second * cosine_table - first * sine_table], -1
    )


MESH = pl.DeviceIdType.MESH

def ag_plane_kernel(src, out, own_sem, send_sem, recv_sem, sib_send, sib_recv):
    x = lax.axis_index("tensor"); e = lax.axis_index("expert")
    z = e // 2; c = e % 2
    def peer(ox, oz):
        return {"expert": ((z + oz) % 4) * 2 + c, "tensor": (x + ox) % 4}
    sib = {"expert": z * 2 + 1 - c}
    def blk(dx, dz):
        return (c * 4 + (z + dz) % 4) * 4 + (x + dx) % 4
    def sblk(dx, dz):
        return ((1 - c) * 4 + (z + dz) % 4) * 4 + (x + dx) % 4
    barrier = pltpu.get_barrier_semaphore()
    near = [peer(1, 0), peer(-1, 0), peer(0, 1), peer(0, -1), sib]
    for p in near:
        pl.semaphore_signal(barrier, inc=1, device_id=p, device_id_type=MESH)
    pl.semaphore_wait(barrier, len(near))
    n = [0]
    pend = []
    def desc(dx, dz, ox, oz, q, nq, sidx, own=False):
        rows = pl.ds(q * 32, nq * 32)
        s = src.at[rows] if own else out.at[blk(dx, dz), rows]
        return pltpu.make_async_remote_copy(
            src_ref=s, dst_ref=out.at[blk(dx, dz), rows],
            send_sem=send_sem.at[sidx],
            recv_sem=recv_sem.at[(dx - ox) % 4, (dz - oz) % 4, q],
            device_id=peer(ox, oz), device_id_type=MESH)
    def send(dx, dz, ox, oz, q, nq, own=False):
        cp = desc(dx, dz, ox, oz, q, nq, n[0], own)
        n[0] += 1
        cp.start(); pend.append(cp)
    def recv(dx, dz, q, nq):
        rows = pl.ds(q * 32, nq * 32)
        pltpu.make_async_remote_copy(
            src_ref=out.at[blk(dx, dz), rows], dst_ref=out.at[blk(dx, dz), rows],
            send_sem=send_sem.at[0], recv_sem=recv_sem.at[dx % 4, dz % 4, q],
            device_id=peer(1, 0), device_id_type=MESH).wait_recv()
    sn = [0]
    def sibsend(dx, dz, own=False):
        cp = pltpu.make_async_remote_copy(
            src_ref=src if own else out.at[blk(dx, dz)], dst_ref=out.at[blk(dx, dz)],
            send_sem=sib_send.at[dx % 4, dz % 4], recv_sem=sib_recv.at[dx % 4, dz % 4],
            device_id=sib, device_id_type=MESH)
        cp.start(); pend.append(cp)
    for ox, oz in ((1, 0), (-1, 0), (0, 1), (0, -1)):
        send(0, 0, ox, oz, 0, 4, own=True)
    mine = pltpu.make_async_copy(src, out.at[blk(0, 0)], own_sem)
    mine.start()
    sibsend(0, 0, own=True)
    for s in (1, -1):
        recv(s, 0, 0, 4)
        if s == -1:
            send(s, 0, 1, 0, 1, 2)
        else:
            send(s, 0, -1, 0, 0, 1); send(s, 0, -1, 0, 3, 1)
        for oz in (1, -1):
            send(s, 0, 0, oz, 0, 2)
        recv(0, s, 0, 4)
        if s == -1:
            send(0, s, 0, 1, 1, 2)
        else:
            send(0, s, 0, -1, 0, 1); send(0, s, 0, -1, 3, 1)
        for ox in (1, -1):
            send(0, s, ox, 0, 2, 2)
        sibsend(s, 0); sibsend(0, s)
    recv(2, 0, 1, 2); recv(2, 0, 0, 1); recv(2, 0, 3, 1)
    for oz in (1, -1):
        send(2, 0, 0, oz, 0, 2)
    recv(0, 2, 1, 2); recv(0, 2, 0, 1); recv(0, 2, 3, 1)
    for ox in (1, -1):
        send(0, 2, ox, 0, 2, 2)
    sibsend(2, 0); sibsend(0, 2)
    for dx in (1, -1, 2):
        for s in (1, -1):
            recv(dx, s, 0, 2)
            send(dx, s, 0, -s, 0 if s == 1 else 1, 1)
            recv(s, dx, 2, 2)
            send(s, dx, -s, 0, 2 if s == 1 else 3, 1)
    for dx in (1, -1):
        for dz in (1, -1):
            sibsend(dx, dz)
    for dx in (1, -1, 2):
        recv(dx, 2, 0, 1); recv(dx, 2, 1, 1)
        recv(2, dx, 2, 1); recv(2, dx, 3, 1)
    for dx in (1, -1, 2):
        sibsend(dx, 2)
        if dx != 2: sibsend(2, dx)
    for dx in range(4):
        for dz in range(4):
            pltpu.make_async_remote_copy(
                src_ref=src, dst_ref=out.at[sblk(dx, dz)],
                send_sem=sib_send.at[dx, dz], recv_sem=sib_recv.at[dx, dz],
                device_id=sib, device_id_type=MESH).wait_recv()
    mine.wait()
    for cp in pend:
        cp.wait_send()

def ag_plane(shard, cid):
    rows, width = shard.shape
    return pl.pallas_call(
        ag_plane_kernel,
        out_shape=jax.ShapeDtypeStruct((32, rows, width), shard.dtype),
        in_specs=[pl.BlockSpec(memory_space=pl.ANY)],
        out_specs=pl.BlockSpec(memory_space=pl.ANY),
        scratch_shapes=[pltpu.SemaphoreType.DMA(()), pltpu.SemaphoreType.DMA((40,)),
                        pltpu.SemaphoreType.DMA((4, 4, 4)), pltpu.SemaphoreType.DMA((4, 4)), pltpu.SemaphoreType.DMA((4, 4))],
        compiler_params=pltpu.CompilerParams(collective_id=cid, has_side_effects=True),
        name="ag_plane",
    )(shard)


def expert_forward_kernel(x_ref, u_ref, routes_ref, w_ref, down_ref, acts_ref):
    f32, low = jnp.float32, jnp.bfloat16
    rows = x_ref.shape[0]
    wide = down_ref.shape[0]
    count = wide // 128
    first = lax.axis_index("expert") * count
    pre = jnp.dot(x_ref[...], w_ref[...], preferred_element_type=f32)
    raw = lax.dot_general(u_ref[...], down_ref[...], (((1,), (1,)), ((), ())), preferred_element_type=f32)
    lane = lax.broadcasted_iota(jnp.int32, (rows, 128), 1)
    named = lane == routes_ref[:, 0:1]
    for n in range(1, routes_ref.shape[1]):
        named = named | (lane == routes_ref[:, n : n + 1])
    logits = jnp.where(named, pre[:, 2 * wide :], -1e30)
    raised = jnp.exp(logits - jnp.max(logits, -1, keepdims=True))
    gates = raised / jnp.sum(raised, -1, keepdims=True)
    weighted = jnp.zeros((rows, 128), f32)
    for n in range(count):
        here = slice(128 * n, 128 * (n + 1))
        gate = jnp.sum(jnp.where(lane == first + n, gates, 0.0), -1, keepdims=True)
        gate_pre = pre[:, here]
        up_pre = pre[:, wide + 128 * n : wide + 128 * (n + 1)]
        sig = jax.nn.sigmoid(gate_pre)
        silu = gate_pre * sig
        active = silu * up_pre
        back = raw[:, here]
        share = gate * jnp.sum(active * back, -1, keepdims=True)
        high = share.astype(low).astype(f32)
        weighted = weighted + jnp.where(lane == first + n, high, 0.0)
        weighted = weighted + jnp.where(lane == first + n + 64, share - high, 0.0)
        back = gate * back
        acts_ref[:, here] = (gate * active).astype(low)
        acts_ref[:, wide + 128 * n : wide + 128 * (n + 1)] = (
            back * up_pre * (sig * (1.0 + gate_pre * (1.0 - sig)))
        ).astype(low)
        acts_ref[:, 2 * wide + 128 * n : 2 * wide + 128 * (n + 1)] = (back * silu).astype(low)
    acts_ref[:, 3 * wide :] = weighted.astype(low)


def expert_forward(x, u, routes, w_all, down, block=256):
    rows, width = x.shape
    wide = down.shape[0]
    total = w_all.shape[1]
    half = 512 // block

    def place(i):
        core, z = i // (4 * half), i // half % 4
        return (z * 2 + core) * half + i % half

    return pl.pallas_call(
        expert_forward_kernel,
        grid=(rows // block,),
        out_shape=jax.ShapeDtypeStruct((rows, 3 * wide + 128), jnp.bfloat16),
        in_specs=[
            pl.BlockSpec((block, width), lambda i: (i, 0)),
            pl.BlockSpec((block, width), lambda i: (place(i), 0)),
            pl.BlockSpec((block, routes.shape[1]), lambda i: (place(i), 0)),
            pl.BlockSpec((width, total), lambda i: (0, 0)),
            pl.BlockSpec((wide, width), lambda i: (0, 0)),
        ],
        out_specs=pl.BlockSpec((block, 3 * wide + 128), lambda i: (i, 0)),
        compiler_params=pltpu.CompilerParams(vmem_limit_bytes=48 << 20),
        name="expert_forward",
    )(x, u, routes, w_all, down)


def expert_back_kernel(acts_hbm, x_hbm, u_hbm, w_ref, down_ref, out, dw_out, router_out,
                       acts, stage, q, sib, a3, b3, a4, b4, a5, b5, a6, b6, xu, acc, dwb, ya, yb,
                       act_sem, load_sem, sib_send, sib_recv, ssem, rsem, ysend, yrecv):
    f32, low = jnp.float32, jnp.bfloat16
    nk = 12
    wide = 640
    x = lax.axis_index("tensor"); e = lax.axis_index("expert"); y = lax.axis_index("dp")
    z = e // 2; c = e % 2
    def zi(d): return (z + d) % 4
    def xi(d): return (x + d) % 4
    def yi(d): return (y + d) % 4
    def peer(oz, ox):
        return {"expert": zi(oz) * 2 + c, "tensor": xi(ox)}
    def ypeer(o):
        return {"dp": yi(o)}
    partner = {"expert": z * 2 + 1 - c}

    def act_load(n):
        rows = pl.ds(pl.multiple_of(n * 2048, 2048), 2048)
        return pltpu.make_async_copy(acts_hbm.at[rows], acts.at[rows], act_sem.at[n])
    def x_load(j, k):
        cols = pl.ds(pl.multiple_of(j * 256, 256), 256)
        return [pltpu.make_async_copy(x_hbm.at[:, cols], xu.at[k % 2], load_sem.at[k % 2, 0])]
    def u_load(j, k):
        cols = pl.ds(pl.multiple_of(j * 256, 256), 256)
        return [pltpu.make_async_copy(u_hbm.at[:, n, :, cols], xu.at[k % 2, pl.ds(2048 * n, 2048)].reshape(4, 512, 256),
                                      load_sem.at[k % 2, n]) for n in range(2)]
    act_load(1 - c).start()
    act_load(c).start()
    for cp in x_load(0, 0): cp.start()
    barrier = pltpu.get_barrier_semaphore()
    near = [peer(1, 0), peer(-1, 0), peer(0, 1), peer(0, -1), partner, ypeer(1), ypeer(-1)]
    for p in near:
        pl.semaphore_signal(barrier, inc=1, device_id=p, device_id_type=MESH)
    pl.semaphore_wait(barrier, len(near))

    def sibs(k):
        return [pltpu.make_async_remote_copy(
            src_ref=stage.at[k % 2], dst_ref=sib.at[k % 2],
            send_sem=sib_send.at[k], recv_sem=sib_recv.at[k], device_id=partner, device_id_type=MESH)]
    def rc(k, n, src, dst, to):
        return pltpu.make_async_remote_copy(src_ref=src, dst_ref=dst, send_sem=ssem.at[k, n], recv_sem=rsem.at[k, n],
                                            device_id=to, device_id_type=MESH)
    def copies3(k):
        s = k % 4
        return [rc(k, 0, q.at[k % 9, zi(2), :, pl.ds(0, 32)], a3.at[s, 0], peer(1, 0)),
                rc(k, 1, q.at[k % 9, zi(2), :, pl.ds(32, 32)], a3.at[s, 1], peer(-1, 0)),
                rc(k, 2, q.at[k % 9, :, xi(2), pl.ds(64, 32)], b3.at[s, 0], peer(0, 1)),
                rc(k, 3, q.at[k % 9, :, xi(2), pl.ds(96, 32)], b3.at[s, 1], peer(0, -1))]
    def copies4(k):
        s = k % 4
        return [rc(k, 4, q.at[k % 9, zi(1), :, pl.ds(0, 64)], a4.at[s, 0], peer(1, 0)),
                rc(k, 5, q.at[k % 9, zi(-1), :, pl.ds(0, 64)], a4.at[s, 1], peer(-1, 0)),
                rc(k, 6, q.at[k % 9, :, xi(1), pl.ds(64, 64)], b4.at[s, 0], peer(0, 1)),
                rc(k, 7, q.at[k % 9, :, xi(-1), pl.ds(64, 64)], b4.at[s, 1], peer(0, -1))]
    def copies5(k):
        s = k % 4
        return [rc(k, 8, q.at[k % 9, z, xi(2), pl.ds(0, 32)], a5.at[s, 0], peer(0, 1)),
                rc(k, 9, q.at[k % 9, z, xi(2), pl.ds(32, 32)], a5.at[s, 1], peer(0, -1)),
                rc(k, 10, q.at[k % 9, zi(2), x, pl.ds(64, 32)], b5.at[s, 0], peer(1, 0)),
                rc(k, 11, q.at[k % 9, zi(2), x, pl.ds(96, 32)], b5.at[s, 1], peer(-1, 0))]
    def copies6(k):
        s = k % 4
        return [rc(k, 12, q.at[k % 9, z, xi(1), pl.ds(0, 64)], a6.at[s, 0], peer(0, 1)),
                rc(k, 13, q.at[k % 9, z, xi(-1), pl.ds(0, 64)], a6.at[s, 1], peer(0, -1)),
                rc(k, 14, q.at[k % 9, zi(1), x, pl.ds(64, 64)], b6.at[s, 0], peer(1, 0)),
                rc(k, 15, q.at[k % 9, zi(-1), x, pl.ds(64, 64)], b6.at[s, 1], peer(-1, 0))]
    def add(k, i, j, rows, *terms):
        t = q[k % 9, i, j, rows].astype(f32)
        for s in terms:
            t = t + s.astype(f32)
        q[k % 9, i, j, rows] = t.astype(low)

    def compute(k):
        cols = pl.ds(pl.multiple_of((k // 2) * 256, 256), 256)
        def piece(cc, put):
            rows = pl.ds(pl.multiple_of(cc * 2048, 2048), 2048)
            @pl.when(k == 0)
            def _(): act_load(cc).wait()
            @pl.when(k % 2 == 0)
            def _():
                put(jnp.dot(acts[rows, 0:wide], down_ref[:, cols], preferred_element_type=f32))
            @pl.when(k % 2 == 1)
            def _():
                put(lax.dot_general(acts[rows, wide:], w_ref[cols, :], (((1,), (1,)), ((), ())),
                                    preferred_element_type=f32))
        def put_stage(r):
            stage[k % 2] = r.astype(low).reshape(4, 4, 128, 256)
        def put_own(r):
            q[k % 9] = r.astype(low).reshape(4, 4, 128, 256)
        piece(1 - c, put_stage)
        for cp in sibs(k): cp.start()
        piece(c, put_own)

    def weight_part(k):
        @pl.when(k % 2 == 0)
        def _():
            for cp in x_load(0, k): cp.wait()
            for cp in u_load(k // 2, k + 1): cp.start()
        @pl.when(k % 2 == 1)
        def _():
            for cp in u_load(0, k): cp.wait()
        @pl.when((k + 1 < nk) & (k % 2 == 1))
        def _():
            for cp in x_load(k // 2 + 1, k + 1): cp.start()
        slot = (k // 2) % 3
        def make(lanes):
            return lax.dot_general(xu[k % 2], acts[:, lanes], (((0,), (0,)), ((), ())), preferred_element_type=f32)
        @pl.when(k % 2 == 0)
        def _():
            acc[...] = make(slice(wide, None))
            dwb[slot, :, :, 0 : 2 * wide] = acc[:, 0 : 2 * wide].astype(low).reshape(4, 64, 2 * wide)
            router_out[pl.ds(pl.multiple_of((k // 2) * 256, 256), 256), :] = acc[:, 2 * wide :]
        @pl.when(k % 2 == 1)
        def _():
            acc[:, 0:wide] = make(slice(0, wide))
            dwb[slot, :, :, 2 * wide :] = acc[:, 0:wide].astype(low).reshape(4, 64, wide)

    def yrc(j, n, src, dst, to):
        return pltpu.make_async_remote_copy(src_ref=src, dst_ref=dst, send_sem=ysend.at[j, n], recv_sem=yrecv.at[j, n],
                                            device_id=to, device_id_type=MESH)
    def ycopies1(j):
        s = j % 3
        return [yrc(j, 0, dwb.at[s, yi(2), pl.ds(0, 32)], ya.at[j % 4, 0], ypeer(1)),
                yrc(j, 1, dwb.at[s, yi(2), pl.ds(32, 32)], ya.at[j % 4, 1], ypeer(-1))]
    def ycopies2(j):
        s = j % 3
        return [yrc(j, 2, dwb.at[s, yi(1)], yb.at[j % 4, 0], ypeer(1)),
                yrc(j, 3, dwb.at[s, yi(-1)], yb.at[j % 4, 1], ypeer(-1))]
    def ystage1(j):
        for cp in ycopies1(j): cp.start()
    def ystage2(j):
        for cp in ycopies1(j): cp.wait_recv()
        s = j % 3
        for d, r, m in ((1, 0, 0), (-1, 32, 1)):
            dwb[s, yi(d), pl.ds(r, 32)] = (dwb[s, yi(d), pl.ds(r, 32)].astype(f32) + ya[j % 4, m].astype(f32)).astype(low)
        for cp in ycopies2(j): cp.start()
    def ystage3(j):
        for cp in ycopies2(j): cp.wait_recv()
        dw_out[j] = (dwb[j % 3, y].astype(f32) + yb[j % 4, 0].astype(f32) + yb[j % 4, 1].astype(f32)).astype(low)
        for cp in ycopies1(j) + ycopies2(j): cp.wait_send()

    def stage2(k):
        for cp in sibs(k): cp.wait()
        def body(n, _):
            add(k, n // 4, n % 4, pl.ds(0, 128), sib[k % 2, n // 4, n % 4])
            return 0
        lax.fori_loop(0, 16, body, 0)
        for cp in copies3(k): cp.start()
    def stage4(k):
        for cp in copies3(k): cp.wait_recv()
        s = k % 4
        def body(n, _):
            add(k, zi(1), n, pl.ds(0, 32), a3[s, 0, n])
            add(k, zi(-1), n, pl.ds(32, 32), a3[s, 1, n])
            add(k, n, xi(1), pl.ds(64, 32), b3[s, 0, n])
            add(k, n, xi(-1), pl.ds(96, 32), b3[s, 1, n])
            return 0
        lax.fori_loop(0, 4, body, 0)
        for cp in copies4(k): cp.start()
    def stage5(k):
        for cp in copies4(k): cp.wait_recv()
        s = k % 4
        def body(n, _):
            add(k, z, n, pl.ds(0, 64), a4[s, 0, n], a4[s, 1, n])
            add(k, n, x, pl.ds(64, 64), b4[s, 0, n], b4[s, 1, n])
            return 0
        lax.fori_loop(0, 4, body, 0)
        for cp in copies5(k): cp.start()
    def stage6(k):
        for cp in copies5(k): cp.wait_recv()
        s = k % 4
        add(k, z, xi(1), pl.ds(0, 32), a5[s, 0])
        add(k, z, xi(-1), pl.ds(32, 32), a5[s, 1])
        add(k, zi(1), x, pl.ds(64, 32), b5[s, 0])
        add(k, zi(-1), x, pl.ds(96, 32), b5[s, 1])
        for cp in copies6(k): cp.start()
    def stage7(k):
        for cp in copies6(k): cp.wait_recv()
        s = k % 4
        for h, m in ((0, a6), (64, b6)):
            t = q[k % 9, z, x, pl.ds(h, 64)].astype(f32) + m[s, 0].astype(f32) + m[s, 1].astype(f32)
            out[k % 2, pl.ds(h, 64), pl.ds(pl.multiple_of((k // 2) * 256, 256), 256)] = t
        for cp in copies3(k) + copies4(k) + copies5(k) + copies6(k): cp.wait_send()

    def step(i, _):
        for lag, st in ((8, stage7), (7, stage6), (5, stage5), (3, stage4), (1, stage2)):
            k = i - lag
            @pl.when((k >= 0) & (k < nk))
            def _():
                st(k)
        for lag, st in ((5, ystage3), (3, ystage2)):
            k = i - lag
            @pl.when((k >= 0) & (k < nk) & (k % 2 == 0))
            def _():
                st(k // 2)
        @pl.when(i < nk)
        def _():
            compute(i)
            weight_part(i)
            @pl.when(i % 2 == 1)
            def _():
                ystage1(i // 2)
        return 0
    lax.fori_loop(0, nk + 8, step, 0)


def expert_back(acts, x, u, w_all, down, cid):
    bf = jnp.bfloat16
    V = pltpu.VMEM
    nk = 12
    u = u.reshape(4, 2, 512, 1536)
    D = pltpu.SemaphoreType.DMA
    vm = pl.BlockSpec(memory_space=pltpu.VMEM)
    anym = pl.BlockSpec(memory_space=pl.ANY)
    return pl.pallas_call(
        expert_back_kernel,
        out_shape=(jax.ShapeDtypeStruct((2, 128, 1536), jnp.float32),
                   jax.ShapeDtypeStruct((6, 64, 1920), bf),
                   jax.ShapeDtypeStruct((1536, 128), jnp.float32)),
        in_specs=[anym, anym, anym, vm, vm],
        out_specs=(vm, vm, vm),
        scratch_shapes=[V((4096, 2048), bf), V((2, 4, 4, 128, 256), bf), V((9, 4, 4, 128, 256), bf), V((2, 4, 4, 128, 256), bf),
                        V((4, 2, 4, 32, 256), bf), V((4, 2, 4, 32, 256), bf),
                        V((4, 2, 4, 64, 256), bf), V((4, 2, 4, 64, 256), bf),
                        V((4, 2, 32, 256), bf), V((4, 2, 32, 256), bf),
                        V((4, 2, 64, 256), bf), V((4, 2, 64, 256), bf),
                        V((2, 4096, 256), bf), V((256, 1408), jnp.float32), V((3, 4, 64, 1920), bf),
                        V((4, 2, 32, 1920), bf), V((4, 2, 64, 1920), bf),
                        D((2,)), D((2, 2)), D((nk,)), D((nk,)), D((nk, 16)), D((nk, 16)), D((6, 4)), D((6, 4))],
        compiler_params=pltpu.CompilerParams(collective_id=cid, has_side_effects=True, vmem_limit_bytes=63 << 20),
        name="expert_back",
    )(acts, x, u, w_all, down)


def shards(
    tokens,
    documents,
    expert_routes,
    attention_gain,
    query_weight,
    key_matrix,
    value_matrix,
    output_weight,
    expert_gain,
    router_weight,
    gate_weight,
    up_weight,
    down_weight,
    out_cotangent,
):
    n_tensor = lax.axis_size("tensor")
    n_expert = lax.axis_size("expert")
    tok_local = tokens.shape[0]
    width = tokens.shape[1]
    group_len = documents.shape[0]
    query_heads = query_weight.shape[1] // HEAD_SIZE
    pair_heads = key_matrix.shape[1] // HEAD_SIZE
    frequency_ratio = query_heads // pair_heads
    local_experts = gate_weight.shape[0]
    experts_all = router_weight.shape[1]
    scale = 1.0 / math.sqrt(HEAD_SIZE)
    inputs = tokens.astype(jnp.float32)
    first_gain = attention_gain.astype(jnp.float32)
    first_normed, first_scale = normalize(inputs, first_gain)
    group_rows = lax.all_gather(first_normed.astype(jnp.bfloat16), "tensor", axis=0, tiled=True)
    index = jnp.arange(group_len, dtype=jnp.int32)
    positions = index - jnp.sum((documents[None, :] < documents[:, None]).astype(jnp.int32), 1)
    cosine_table, sine_table = rope_tables(positions, HEAD_SIZE)
    query_linear = jnp.dot(group_rows, query_weight, preferred_element_type=jnp.float32).reshape(
        group_len, query_heads, HEAD_SIZE
    )
    key_linear = jnp.dot(group_rows, key_matrix, preferred_element_type=jnp.float32).reshape(
        group_len, pair_heads, HEAD_SIZE
    )
    value_low = (
        jnp.dot(group_rows, value_matrix, preferred_element_type=jnp.float32)
        .astype(jnp.bfloat16)
        .reshape(group_len, pair_heads, HEAD_SIZE)
    )
    query_low = (
        apply_rotation(query_linear, cosine_table, sine_table)
        .astype(jnp.bfloat16)
        .reshape(group_len, pair_heads, frequency_ratio, HEAD_SIZE)
    )
    key_low = apply_rotation(key_linear, cosine_table, sine_table).astype(jnp.bfloat16)
    block_rows = min(512, group_len)
    count = group_len // block_rows
    starts = jnp.arange(count, dtype=jnp.int32) * block_rows

    def block_scores(start):
        rows_index = start + jnp.arange(block_rows, dtype=jnp.int32)
        scores = (
            jnp.einsum("qhgd,khd->hgqk", query_low, key_low, preferred_element_type=jnp.float32)
            * scale
        )
        allowed = (documents[:, None] == documents[None, :]) & (
            index[None, :] <= rows_index[:, None]
        )
        return (jnp.where(allowed, scores, -1e30), query_low)

    def forward_block(start):
        scores, block_query = block_scores(start)
        top = jnp.max(scores, -1, keepdims=True)
        weights = jnp.exp(scores - top)
        total = jnp.sum(weights, -1, keepdims=True)
        probs = (weights / total).astype(jnp.bfloat16)
        mixed = jnp.einsum("hgqk,khd->qhgd", probs, value_low, preferred_element_type=jnp.float32)
        return (
            mixed.astype(jnp.bfloat16).reshape(block_rows, query_heads * HEAD_SIZE),
            (top + jnp.log(total))[..., 0],
        )

    mixed_blocks, logsum_blocks = lax.map(forward_block, starts)
    attended = mixed_blocks.reshape(group_len, query_heads * HEAD_SIZE)
    head_part = jnp.dot(attended, output_weight, preferred_element_type=jnp.float32)
    branch = lax.psum_scatter(
        head_part.astype(jnp.bfloat16), "tensor", scatter_dimension=0, tiled=True
    ).astype(jnp.float32)
    residual = inputs + branch
    second_gain = expert_gain.astype(jnp.float32)
    second_normed, second_scale = normalize(residual, second_gain)
    second_low = second_normed.astype(jnp.bfloat16)
    plane = ("expert", "tensor")
    experts_index = jnp.arange(experts_all, dtype=jnp.int32)
    plane_routes = lax.all_gather(expert_routes, plane, axis=0, tiled=True)
    plane_upstream = lax.all_gather(out_cotangent, plane, axis=0, tiled=True)
    plane_rows = ag_plane(second_low, 1).reshape(-1, width)

    def dense_gates(rows, routes):
        named = jnp.any(routes[:, :, None] == experts_index[None, None, :], 1)
        logits = jnp.dot(rows, router_weight, preferred_element_type=jnp.float32)
        logits = jnp.where(named, logits, -1e30)
        raised = jnp.exp(logits - jnp.max(logits, -1, keepdims=True))
        return raised / jnp.sum(raised, -1, keepdims=True)

    hidden = gate_weight.shape[2]
    wide = local_experts * hidden
    router_pad = jnp.pad(router_weight, ((0, 0), (0, 64 - experts_all)))
    in_weights = jnp.concatenate(
        [
            gate_weight.transpose(1, 0, 2).reshape(width, wide),
            up_weight.transpose(1, 0, 2).reshape(width, wide),
            router_pad,
            router_pad,
        ],
        1,
    )
    down_flat = down_weight.reshape(wide, width)
    acts = expert_forward(plane_rows, plane_upstream, plane_routes, in_weights, down_flat)
    sums, weight_grads, router_pairs = expert_back(
        acts, plane_rows, plane_upstream, in_weights, down_flat, 2
    )
    mixture, route_rows = sums[0], sums[1]
    layer_output = (residual + mixture).astype(jnp.bfloat16)
    router_pairs = router_pairs[:, :experts_all] + router_pairs[:, 64 : 64 + experts_all]
    weight_grads = lax.all_gather(weight_grads, "dp", axis=0)
    gates = dense_gates(second_low, expert_routes)
    upstream = out_cotangent.astype(jnp.float32)
    shared = gates * jnp.sum(mixture * upstream, -1, keepdims=True)
    router_local = -jnp.einsum(
        "td,te->de",
        second_low.astype(jnp.float32),
        shared,
        precision=highest,
        preferred_element_type=jnp.float32,
    ) + router_pairs
    normed_back = route_rows - jnp.einsum(
        "te,de->td",
        shared,
        router_weight.astype(jnp.float32),
        precision=highest,
        preferred_element_type=jnp.float32,
    )
    residual_back, expert_gain_local = norm_back(residual, second_scale, second_gain, normed_back)
    residual_grad = upstream + residual_back
    group_grad = lax.all_gather(residual_grad.astype(jnp.bfloat16), "tensor", axis=0, tiled=True)
    attended_grad = jnp.einsum(
        "td,hd->th", group_grad, output_weight, preferred_element_type=jnp.float32
    ).astype(jnp.bfloat16)
    attended_grad = attended_grad.reshape(group_len, pair_heads, frequency_ratio, HEAD_SIZE)
    output_local = jnp.einsum("th,td->hd", attended, group_grad, preferred_element_type=jnp.float32)

    def backward_block(carry, pieces):
        key_acc, value_acc = carry
        start, logsum = pieces
        scores, block_query = block_scores(start)
        probs = jnp.exp(scores - logsum[..., None])
        prob_grad = jnp.einsum(
            "qhgd,khd->hgqk", attended_grad, value_low, preferred_element_type=jnp.float32
        )
        value_acc = value_acc + jnp.einsum(
            "hgqk,qhgd->khd",
            probs.astype(jnp.bfloat16),
            attended_grad,
            preferred_element_type=jnp.float32,
        )
        inner = jnp.sum(probs * prob_grad, -1, keepdims=True)
        score_grad = (probs * (prob_grad - inner)).astype(jnp.bfloat16)
        query_turned = (
            jnp.einsum("hgqk,khd->qhgd", score_grad, key_low, preferred_element_type=jnp.float32)
            * scale
        )
        key_acc = (
            key_acc
            + jnp.einsum(
                "hgqk,qhgd->khd", score_grad, block_query, preferred_element_type=jnp.float32
            )
            * scale
        )
        return ((key_acc, value_acc), query_turned)

    zero_keys = jnp.zeros((group_len, pair_heads, HEAD_SIZE), jnp.float32)
    (key_turned, value_acc), query_blocks = lax.scan(
        backward_block, (zero_keys, zero_keys), (starts, logsum_blocks)
    )
    query_turned = query_blocks.reshape(group_len, query_heads, HEAD_SIZE)
    query_back = (
        rotate_back(query_turned, cosine_table, sine_table)
        .astype(jnp.bfloat16)
        .reshape(group_len, query_heads * HEAD_SIZE)
    )
    key_back = (
        rotate_back(key_turned, cosine_table, sine_table)
        .astype(jnp.bfloat16)
        .reshape(group_len, pair_heads * HEAD_SIZE)
    )
    value_back = value_acc.astype(jnp.bfloat16).reshape(group_len, pair_heads * HEAD_SIZE)
    query_local = jnp.einsum(
        "td,th->dh", group_rows, query_back, preferred_element_type=jnp.float32
    )
    key_local = jnp.einsum("td,th->dh", group_rows, key_back, preferred_element_type=jnp.float32)
    value_local = jnp.einsum(
        "td,th->dh", group_rows, value_back, preferred_element_type=jnp.float32
    )
    normed_part = jnp.einsum(
        "th,dh->td", query_back, query_weight, preferred_element_type=jnp.float32
    )
    normed_part = normed_part + jnp.einsum(
        "th,dh->td", key_back, key_matrix, preferred_element_type=jnp.float32
    )
    normed_part = normed_part + jnp.einsum(
        "th,dh->td", value_back, value_matrix, preferred_element_type=jnp.float32
    )
    normed_grad = lax.psum_scatter(
        normed_part.astype(jnp.bfloat16), "tensor", scatter_dimension=0, tiled=True
    ).astype(jnp.float32)
    input_back, attention_gain_local = norm_back(inputs, first_scale, first_gain, normed_grad)
    input_gradient = residual_grad + input_back
    query_gradient, key_gradient, value_gradient, output_gradient = (
        lax.psum(query_local.astype(jnp.bfloat16), ("dp", "expert")).astype(jnp.float32),
        lax.psum(key_local.astype(jnp.bfloat16), ("dp", "expert")).astype(jnp.float32),
        lax.psum(value_local.astype(jnp.bfloat16), ("dp", "expert")).astype(jnp.float32),
        lax.psum(output_local.astype(jnp.bfloat16), ("dp", "expert")).astype(jnp.float32),
    )
    router_gradient, attention_gain_gradient, expert_gain_gradient = lax.psum(
        (router_local, attention_gain_local, expert_gain_local), ("dp", "expert", "tensor")
    )
    weight_grads = weight_grads.transpose(1, 0, 2, 3).reshape(width, 3 * wide).astype(jnp.float32)
    gate_gradient, up_gradient = (
        weight_grads[:, part : part + wide]
        .reshape(width, local_experts, hidden)
        .transpose(1, 0, 2)
        for part in (0, wide)
    )
    down_gradient = weight_grads[:, 2 * wide :].T.reshape(local_experts, hidden, width)
    return (
        layer_output,
        input_gradient,
        attention_gain_gradient,
        query_gradient,
        key_gradient,
        value_gradient,
        output_gradient,
        expert_gain_gradient,
        router_gradient,
        gate_gradient,
        up_gradient,
        down_gradient,
    )


def solution(mesh):
    placed = (
        P(("dp", "expert", "tensor"), None),
        P(("dp", "expert")),
        P(("dp", "expert", "tensor"), None),
        P(),
        P(None, "tensor"),
        P(None, "tensor"),
        P(None, "tensor"),
        P("tensor", None),
        P(),
        P(),
        P("expert", None, "tensor"),
        P("expert", None, "tensor"),
        P("expert", "tensor", None),
        P(("dp", "expert", "tensor"), None),
    )
    return jax.shard_map(
        shards,
        mesh=mesh,
        in_specs=placed,
        out_specs=(
            P(("dp", "expert", "tensor"), None),
            P(("dp", "expert", "tensor"), None),
            P(),
            P(None, "tensor"),
            P(None, "tensor"),
            P(None, "tensor"),
            P("tensor", None),
            P(),
            P(),
            P("expert", None, "tensor"),
            P("expert", None, "tensor"),
            P("expert", "tensor", None),
        ),
        check_vma=False,
    )
```

```python
import functools
import math

import jax
import jax.numpy as jnp
from jax import lax
from jax.experimental import pallas as pl
from jax.experimental.pallas import tpu as pltpu
from jax.sharding import PartitionSpec as P

HEAD_SIZE = 64


epsilon = 1e-06
theta = 10000.0
highest = lax.Precision.HIGHEST


def normalize(value_rows, gain):
    scale = lax.rsqrt(jnp.mean(value_rows * value_rows, -1, keepdims=True) + epsilon)
    return (value_rows * scale * gain, scale)


def norm_back(value_rows, scale, gain, upstream):
    weighted = upstream * gain
    inner = jnp.mean(weighted * value_rows, -1, keepdims=True)
    result = scale * weighted - value_rows * scale**3 * inner
    gain_part = jnp.sum(upstream * value_rows * scale, 0)
    return (result, gain_part)


def rope_tables(positions, width):
    half = width // 2
    freq = theta ** (-(jnp.arange(half, dtype=jnp.float32) * 2.0 / width))
    angle = positions.astype(jnp.float32)[:, None] * freq[None, :]
    return (jnp.cos(angle), jnp.sin(angle))


def apply_rotation(value_rows, cosine_table, sine_table):
    half = value_rows.shape[-1] // 2
    first = value_rows[..., :half]
    second = value_rows[..., half:]
    cosine_table = cosine_table[:, None, :]
    sine_table = sine_table[:, None, :]
    return jnp.concatenate(
        [first * cosine_table - second * sine_table, second * cosine_table + first * sine_table], -1
    )


def rotate_back(value_rows, cosine_table, sine_table):
    half = value_rows.shape[-1] // 2
    first = value_rows[..., :half]
    second = value_rows[..., half:]
    cosine_table = cosine_table[:, None, :]
    sine_table = sine_table[:, None, :]
    return jnp.concatenate(
        [first * cosine_table + second * sine_table, second * cosine_table - first * sine_table], -1
    )


MESH = pl.DeviceIdType.MESH

def ring_gather_kernel(src, out, own_sem, ssem, rsem):
    x = lax.axis_index("tensor")
    def xi(d): return (x + d) % 4
    def peer(o): return {"tensor": xi(o)}
    barrier = pltpu.get_barrier_semaphore()
    for o in (1, -1):
        pl.semaphore_signal(barrier, inc=1, device_id=peer(o), device_id_type=MESH)
    pl.semaphore_wait(barrier, 2)
    def copy(n, block, half, to, own):
        rows = pl.ds(64 * half, 64)
        return pltpu.make_async_remote_copy(
            src_ref=src.at[rows] if own else out.at[block, rows], dst_ref=out.at[block, rows],
            send_sem=ssem.at[n], recv_sem=rsem.at[n], device_id=peer(to), device_id_type=MESH)
    right = [copy(0, x, 0, 1, True), copy(1, x, 1, 1, True)]
    left = [copy(2, x, 1, -1, True), copy(3, x, 0, -1, True)]
    for a, b in zip(right, left):
        a.start(); b.start()
    mine = pltpu.make_async_copy(src, out.at[x], own_sem)
    mine.start()
    copy(0, xi(-1), 0, 1, False).wait_recv()
    on_right = copy(4, xi(-1), 0, 1, False)
    on_right.start()
    copy(2, xi(1), 1, -1, False).wait_recv()
    on_left = copy(5, xi(1), 1, -1, False)
    on_left.start()
    copy(1, xi(-1), 1, 1, False).wait_recv()
    copy(3, xi(1), 0, -1, False).wait_recv()
    copy(4, xi(2), 0, 1, False).wait_recv()
    copy(5, xi(2), 1, -1, False).wait_recv()
    mine.wait()
    for cp in right + left + [on_right, on_left]:
        cp.wait_send()


def ring_gather(shard, cid):
    rows, width = shard.shape
    D = pltpu.SemaphoreType.DMA
    return pl.pallas_call(
        ring_gather_kernel,
        out_shape=jax.ShapeDtypeStruct((4, rows, width), shard.dtype),
        in_specs=[pl.BlockSpec(memory_space=pltpu.VMEM)],
        out_specs=pl.BlockSpec(memory_space=pltpu.VMEM),
        scratch_shapes=[D(()), D((6,)), D((6,))],
        compiler_params=pltpu.CompilerParams(collective_id=cid, has_side_effects=True),
        name="ring_gather",
    )(shard).reshape(4 * rows, width)


def branch_gather_kernel(part, tokens, gain, residual, out, nr1, nb, nr2, low_rows, nsend, nrecv,
                         own_sem, send_sem, recv_sem, sib_send, sib_recv):
    f32, low = jnp.float32, jnp.bfloat16
    x = lax.axis_index("tensor"); e = lax.axis_index("expert")
    z = e // 2; c = e % 2
    def xi(d): return (x + d) % 4
    def peer(ox, oz):
        return {"expert": ((z + oz) % 4) * 2 + c, "tensor": xi(ox)}
    sib = {"expert": z * 2 + 1 - c}
    def blk(dx, dz): return (c * 4 + (z + dz) % 4) * 4 + xi(dx)
    def sblk(dx, dz): return ((1 - c) * 4 + (z + dz) % 4) * 4 + xi(dx)
    barrier = pltpu.get_barrier_semaphore()
    near = [peer(1, 0), peer(-1, 0), peer(0, 1), peer(0, -1), sib]
    for p in near:
        pl.semaphore_signal(barrier, inc=1, device_id=p, device_id_type=MESH)
    pl.semaphore_wait(barrier, len(near))
    pend = []
    def go(cps):
        for cp in cps: cp.start()
        pend.extend(cps)
        return cps
    def nrc(n, src, dst, to):
        return pltpu.make_async_remote_copy(src_ref=src, dst_ref=dst, send_sem=nsend.at[n], recv_sem=nrecv.at[n],
                                            device_id=peer(to, 0), device_id_type=MESH)
    n1 = go([nrc(0, part.at[xi(2), pl.ds(0, 64)], nr1.at[0], 1), nrc(1, part.at[xi(2), pl.ds(64, 64)], nr1.at[1], -1)])
    n2 = go([nrc(2, part.at[xi(1), pl.ds(64, 64)], nr2.at[0, pl.ds(64, 64)], 1),
             nrc(3, part.at[xi(-1), pl.ds(0, 64)], nr2.at[1, pl.ds(0, 64)], -1)])
    n1[0].wait_recv()
    nb[0] = (part[xi(1), 0:64].astype(f32) + nr1[0].astype(f32)).astype(low)
    n3 = go([nrc(4, nb.at[0], nr2.at[0, pl.ds(0, 64)], 1)])
    n1[1].wait_recv()
    nb[1] = (part[xi(-1), 64:128].astype(f32) + nr1[1].astype(f32)).astype(low)
    n3 += go([nrc(5, nb.at[1], nr2.at[1, pl.ds(64, 64)], -1)])
    for cp in n2 + n3: cp.wait_recv()
    total = tokens[...].astype(f32) + part[x].astype(f32) + nr2[0].astype(f32) + nr2[1].astype(f32)
    residual[...] = total
    scale = lax.rsqrt(jnp.mean(total * total, -1, keepdims=True) + epsilon)
    low_rows[...] = (total * scale * gain[...]).astype(low)
    src = low_rows

    count = [0]
    def desc(dx, dz, ox, oz, q, nq, n, own=False):
        rows = pl.ds(q * 32, nq * 32)
        return pltpu.make_async_remote_copy(
            src_ref=src.at[rows] if own else out.at[blk(dx, dz), rows], dst_ref=out.at[blk(dx, dz), rows],
            send_sem=send_sem.at[n], recv_sem=recv_sem.at[(dx - ox) % 4, (dz - oz) % 4, q],
            device_id=peer(ox, oz), device_id_type=MESH)
    def send(dx, dz, ox, oz, q, nq, own=False):
        go([desc(dx, dz, ox, oz, q, nq, count[0], own)])
        count[0] += 1
    def recv(dx, dz, q, nq):
        desc(dx, dz, 0, 0, q, nq, 0).wait_recv()
    def sibcopy(block, dx, dz, own=False):
        return pltpu.make_async_remote_copy(
            src_ref=src if own else out.at[block], dst_ref=out.at[block],
            send_sem=sib_send.at[dx % 4, dz % 4], recv_sem=sib_recv.at[dx % 4, dz % 4],
            device_id=sib, device_id_type=MESH)
    def sibsend(dx, dz, own=False): go([sibcopy(blk(dx, dz), dx, dz, own)])
    for ox, oz in ((1, 0), (-1, 0), (0, 1), (0, -1)):
        send(0, 0, ox, oz, 0, 4, own=True)
    mine = pltpu.make_async_copy(src, out.at[blk(0, 0)], own_sem)
    mine.start()
    sibsend(0, 0, own=True)
    for s in (1, -1):
        recv(s, 0, 0, 4)
        if s == -1:
            send(s, 0, 1, 0, 1, 2)
        else:
            send(s, 0, -1, 0, 0, 1); send(s, 0, -1, 0, 3, 1)
        for oz in (1, -1):
            send(s, 0, 0, oz, 0, 2)
        recv(0, s, 0, 4)
        if s == -1:
            send(0, s, 0, 1, 1, 2)
        else:
            send(0, s, 0, -1, 0, 1); send(0, s, 0, -1, 3, 1)
        for ox in (1, -1):
            send(0, s, ox, 0, 2, 2)
        sibsend(s, 0); sibsend(0, s)
    recv(2, 0, 1, 2); recv(2, 0, 0, 1); recv(2, 0, 3, 1)
    for oz in (1, -1):
        send(2, 0, 0, oz, 0, 2)
    recv(0, 2, 1, 2); recv(0, 2, 0, 1); recv(0, 2, 3, 1)
    for ox in (1, -1):
        send(0, 2, ox, 0, 2, 2)
    sibsend(2, 0); sibsend(0, 2)
    for dx in (1, -1, 2):
        for s in (1, -1):
            recv(dx, s, 0, 2)
            send(dx, s, 0, -s, 0 if s == 1 else 1, 1)
            recv(s, dx, 2, 2)
            send(s, dx, -s, 0, 2 if s == 1 else 3, 1)
    for dx in (1, -1):
        for dz in (1, -1):
            sibsend(dx, dz)
    for d in (1, -1, 2):
        recv(d, 2, 0, 1); recv(d, 2, 1, 1)
        recv(2, d, 2, 1); recv(2, d, 3, 1)
    for d in (1, -1, 2):
        sibsend(d, 2)
        if d != 2: sibsend(2, d)
    for dx in range(4):
        for dz in range(4):
            sibcopy(sblk(dx, dz), dx, dz).wait_recv()
    mine.wait()
    for cp in pend: cp.wait_send()


def branch_gather(part, tokens, gain, cid):
    bf = jnp.bfloat16
    V = pltpu.VMEM
    D = pltpu.SemaphoreType.DMA
    vm = pl.BlockSpec(memory_space=pltpu.VMEM)
    rows, width = tokens.shape
    return pl.pallas_call(
        branch_gather_kernel,
        out_shape=(jax.ShapeDtypeStruct((rows, width), jnp.float32), jax.ShapeDtypeStruct((32, rows, width), bf)),
        in_specs=[vm, vm, vm],
        out_specs=(vm, pl.BlockSpec(memory_space=pl.ANY)),
        scratch_shapes=[V((2, 64, width), bf), V((2, 64, width), bf), V((2, 128, width), bf), V((rows, width), bf),
                        D((6,)), D((6,)), D(()), D((40,)), D((4, 4, 4)), D((4, 4)), D((4, 4))],
        compiler_params=pltpu.CompilerParams(collective_id=cid, has_side_effects=True, vmem_limit_bytes=32 << 20),
        name="branch_gather",
    )(part.reshape(4, rows, width), tokens, gain)


def grad_layout_kernel(src, gate, up, down):
    f32 = jnp.float32
    for n in range(5):
        for i, ref in enumerate((gate, up)):
            ref[n] = src[:, 0, :, pl.ds(640 * i + 128 * n, 128)].astype(f32).reshape(256, 128)
        down[n] = src[:, 0, :, pl.ds(1280 + 128 * n, 128)].astype(f32).reshape(256, 128).T


def grad_layout(sums):
    return pl.pallas_call(
        grad_layout_kernel,
        grid=(6,),
        out_shape=(jax.ShapeDtypeStruct((5, 1536, 128), jnp.float32),) * 2 + (jax.ShapeDtypeStruct((5, 128, 1536), jnp.float32),),
        in_specs=[pl.BlockSpec((4, 1, 64, 1920), lambda j: (0, j, 0, 0))],
        out_specs=(pl.BlockSpec((5, 256, 128), lambda j: (0, j, 0)),) * 2 + (pl.BlockSpec((5, 128, 256), lambda j: (0, 0, j)),),
        compiler_params=pltpu.CompilerParams(vmem_limit_bytes=32 << 20),
        name="grad_layout",
    )(sums)


def grad_sum_kernel(g, n_part, g_out, n_out, q, sib, a3a, a3b, b3, a4, b4, a5a, a5b, b5, a6, b6, extra,
                    nr1, nb, nr2, sib_sems, ssem, rsem, gsend, grecv, gsib_send, gsib_recv, esend, erecv, nsend, nrecv):
    f32, low = jnp.float32, jnp.bfloat16
    x = lax.axis_index("tensor"); e = lax.axis_index("expert"); y = lax.axis_index("dp")
    z = e // 2; c = e % 2
    def zi(d): return (z + d) % 4
    def yi(d): return (y + d) % 4
    def xi(d): return (x + d) % 4
    def peer(oz, oy):
        return {"expert": zi(oz) * 2 + c, "dp": yi(oy)}
    def xpeer(o):
        return {"tensor": xi(o)}
    partner = {"expert": z * 2 + 1 - c}
    barrier = pltpu.get_barrier_semaphore()
    near = [peer(1, 0), peer(-1, 0), peer(0, 1), peer(0, -1), partner, xpeer(1), xpeer(2), xpeer(3)]
    for p in near:
        pl.semaphore_signal(barrier, inc=1, device_id=p, device_id_type=MESH)
    pl.semaphore_wait(barrier, len(near))
    A0, A1, B0, B1 = pl.ds(0, 384), pl.ds(384, 256), pl.ds(640, 256), pl.ds(896, 256)
    A, B = pl.ds(0, 640), pl.ds(640, 512)
    sent = []
    def rc(n, src, dst, to):
        cp = pltpu.make_async_remote_copy(src_ref=src, dst_ref=dst, send_sem=ssem.at[n], recv_sem=rsem.at[n],
                                          device_id=to, device_id_type=MESH)
        return cp
    def go(cps):
        for cp in cps: cp.start()
        sent.extend(cps)
        return cps
    def nrc(n, src, dst, to):
        return pltpu.make_async_remote_copy(src_ref=src, dst_ref=dst, send_sem=nsend.at[n], recv_sem=nrecv.at[n],
                                            device_id=to, device_id_type=MESH)
    sibling = go([pltpu.make_async_remote_copy(src_ref=g.at[1 - c], dst_ref=sib, send_sem=sib_sems.at[0], recv_sem=sib_sems.at[1],
                                               device_id=partner, device_id_type=MESH)])
    n1 = go([nrc(0, n_part.at[xi(2), pl.ds(0, 64)], nr1.at[0], xpeer(1)),
             nrc(1, n_part.at[xi(2), pl.ds(64, 64)], nr1.at[1], xpeer(-1))])
    sibling[0].wait_recv()
    def body(n, _):
        i, j = n // 4, n % 4
        q[i, j] = (g[c, i, j].astype(f32) + sib[i, j].astype(f32)).astype(low)
        return 0
    lax.fori_loop(0, 16, body, 0)
    def add(i, j, cols, *terms):
        t = q[i, j, :, cols].astype(f32)
        for s in terms:
            t = t + s.astype(f32)
        q[i, j, :, cols] = t.astype(low)
    c3 = go([rc(0, q.at[zi(2), :, :, A0], a3a, peer(1, 0)),
             rc(1, q.at[zi(2), :, :, A1], a3b, peer(-1, 0)),
             rc(2, q.at[:, yi(2), :, B0], b3.at[0], peer(0, 1)),
             rc(3, q.at[:, yi(2), :, B1], b3.at[1], peer(0, -1))])
    for cp in n1: cp.wait_recv()
    nb[0, 0:64] = (n_part[xi(1), 0:64].astype(f32) + nr1[0].astype(f32)).astype(low)
    nb[0, 64:128] = n_part[xi(1), 64:128]
    nb[1, 0:64] = n_part[xi(-1), 0:64]
    nb[1, 64:128] = (n_part[xi(-1), 64:128].astype(f32) + nr1[1].astype(f32)).astype(low)
    n2 = go([nrc(2, nb.at[0], nr2.at[0], xpeer(1)), nrc(3, nb.at[1], nr2.at[1], xpeer(-1))])
    for cp in c3: cp.wait_recv()
    def body4(n, _):
        add(zi(1), n, A0, a3a[n])
        add(zi(-1), n, A1, a3b[n])
        add(n, yi(1), B0, b3[0, n])
        add(n, yi(-1), B1, b3[1, n])
        return 0
    lax.fori_loop(0, 4, body4, 0)
    c4 = go([rc(4, q.at[zi(1), :, :, A], a4.at[0], peer(1, 0)),
             rc(5, q.at[zi(-1), :, :, A], a4.at[1], peer(-1, 0)),
             rc(6, q.at[:, yi(1), :, B], b4.at[0], peer(0, 1)),
             rc(7, q.at[:, yi(-1), :, B], b4.at[1], peer(0, -1))])
    for cp in c4: cp.wait_recv()
    def body5(n, _):
        add(z, n, A, a4[0, n], a4[1, n])
        add(n, y, B, b4[0, n], b4[1, n])
        return 0
    lax.fori_loop(0, 4, body5, 0)
    c5 = go([rc(8, q.at[z, yi(2), :, A0], a5a, peer(0, 1)),
             rc(9, q.at[z, yi(2), :, A1], a5b, peer(0, -1)),
             rc(10, q.at[zi(2), y, :, B0], b5.at[0], peer(1, 0)),
             rc(11, q.at[zi(2), y, :, B1], b5.at[1], peer(-1, 0))])
    for cp in n2: cp.wait_recv()
    n_out[...] = n_part[x].astype(f32) + nr2[0].astype(f32) + nr2[1].astype(f32)
    for cp in c5: cp.wait_recv()
    add(z, yi(1), A0, a5a[...])
    add(z, yi(-1), A1, a5b[...])
    add(zi(1), y, B0, b5[0])
    add(zi(-1), y, B1, b5[1])
    c6 = go([rc(12, q.at[z, yi(1), :, A], a6.at[0], peer(0, 1)),
             rc(13, q.at[z, yi(-1), :, A], a6.at[1], peer(0, -1)),
             rc(14, q.at[zi(1), y, :, B], b6.at[0], peer(1, 0)),
             rc(15, q.at[zi(-1), y, :, B], b6.at[1], peer(-1, 0))])
    for cp in c6: cp.wait_recv()
    own = g_out.at[c, z, y]
    own[:, A] = (q[z, y, :, A].astype(f32) + a6[0].astype(f32) + a6[1].astype(f32)).astype(low)
    last = q[z, y, :, B].astype(f32) + b6[0].astype(f32) + b6[1].astype(f32)
    own[:, pl.ds(640, 384)] = last[:, 0:384].astype(low)
    extra[0] = last[:, 384:512].astype(low)
    es = go([pltpu.make_async_remote_copy(src_ref=extra.at[0], dst_ref=extra.at[o], send_sem=esend.at[o], recv_sem=erecv.at[o],
                                          device_id=xpeer(o), device_id_type=MESH) for o in (1, 2, 3)])
    for cp in es: cp.wait_recv()
    own[:, pl.ds(1024, 128)] = (extra[0].astype(f32) + extra[1].astype(f32) + extra[2].astype(f32) + extra[3].astype(f32)).astype(low)

    starts = (0, 384, 640, 896, 1152)
    def part(qq, nq): return pl.ds(starts[qq], starts[qq + nq] - starts[qq])
    count = [0]
    def send(dy, dz, oy, oz, qq, nq):
        cp = pltpu.make_async_remote_copy(
            src_ref=g_out.at[c, zi(dz), yi(dy), :, part(qq, nq)], dst_ref=g_out.at[c, zi(dz), yi(dy), :, part(qq, nq)],
            send_sem=gsend.at[count[0]], recv_sem=grecv.at[(dy - oy) % 4, (dz - oz) % 4, qq],
            device_id=peer(oz, oy), device_id_type=MESH)
        count[0] += 1
        go([cp])
    def recv(dy, dz, qq, nq):
        ref = g_out.at[c, zi(dz), yi(dy), :, part(qq, nq)]
        pltpu.make_async_remote_copy(src_ref=ref, dst_ref=ref, send_sem=gsend.at[0], recv_sem=grecv.at[dy % 4, dz % 4, qq],
                                     device_id=peer(1, 0), device_id_type=MESH).wait_recv()
    def sibcopy(cc, dy, dz):
        ref = g_out.at[cc, zi(dz), yi(dy)]
        return pltpu.make_async_remote_copy(src_ref=ref, dst_ref=ref, send_sem=gsib_send.at[dy % 4, dz % 4],
                                            recv_sem=gsib_recv.at[dy % 4, dz % 4], device_id=partner, device_id_type=MESH)
    def sibsend(dy, dz): go([sibcopy(c, dy, dz)])
    for oy, oz in ((1, 0), (-1, 0), (0, 1), (0, -1)):
        send(0, 0, oy, oz, 0, 4)
    sibsend(0, 0)
    for s in (1, -1):
        recv(s, 0, 0, 4)
        if s == -1:
            send(s, 0, 1, 0, 1, 2)
        else:
            send(s, 0, -1, 0, 0, 1); send(s, 0, -1, 0, 3, 1)
        for oz in (1, -1):
            send(s, 0, 0, oz, 0, 2)
        recv(0, s, 0, 4)
        if s == -1:
            send(0, s, 0, 1, 1, 2)
        else:
            send(0, s, 0, -1, 0, 1); send(0, s, 0, -1, 3, 1)
        for oy in (1, -1):
            send(0, s, oy, 0, 2, 2)
        sibsend(s, 0); sibsend(0, s)
    recv(2, 0, 1, 2); recv(2, 0, 0, 1); recv(2, 0, 3, 1)
    for oz in (1, -1):
        send(2, 0, 0, oz, 0, 2)
    recv(0, 2, 1, 2); recv(0, 2, 0, 1); recv(0, 2, 3, 1)
    for oy in (1, -1):
        send(0, 2, oy, 0, 2, 2)
    sibsend(2, 0); sibsend(0, 2)
    for dy in (1, -1, 2):
        for s in (1, -1):
            recv(dy, s, 0, 2)
            send(dy, s, 0, -s, 0 if s == 1 else 1, 1)
            recv(s, dy, 2, 2)
            send(s, dy, -s, 0, 2 if s == 1 else 3, 1)
    for dy in (1, -1):
        for dz in (1, -1):
            sibsend(dy, dz)
    for d in (1, -1, 2):
        recv(d, 2, 0, 1); recv(d, 2, 1, 1)
        recv(2, d, 2, 1); recv(2, d, 3, 1)
    for d in (1, -1, 2):
        sibsend(d, 2)
        if d != 2: sibsend(2, d)
    for dy in range(4):
        for dz in range(4):
            sibcopy(1 - c, dy, dz).wait_recv()
    for cp in sent: cp.wait_send()


def grad_sum(g, n_part, cid):
    bf = jnp.bfloat16
    V = pltpu.VMEM
    D = pltpu.SemaphoreType.DMA
    vm = pl.BlockSpec(memory_space=pltpu.VMEM)
    g = g.reshape(2, 4, 4, 48, 1152)
    n_part = n_part.reshape(4, 128, 1536)
    total, rows = pl.pallas_call(
        grad_sum_kernel,
        out_shape=(jax.ShapeDtypeStruct((2, 4, 4, 48, 1152), bf), jax.ShapeDtypeStruct((128, 1536), jnp.float32)),
        in_specs=[vm, vm], out_specs=(vm, vm),
        scratch_shapes=[V((4, 4, 48, 1152), bf), V((4, 4, 48, 1152), bf),
                        V((4, 48, 384), bf), V((4, 48, 256), bf), V((2, 4, 48, 256), bf),
                        V((2, 4, 48, 640), bf), V((2, 4, 48, 512), bf),
                        V((48, 384), bf), V((48, 256), bf), V((2, 48, 256), bf),
                        V((2, 48, 640), bf), V((2, 48, 512), bf), V((4, 48, 128), bf),
                        V((2, 64, 1536), bf), V((2, 128, 1536), bf), V((2, 128, 1536), bf),
                        D((2,)), D((16,)), D((16,)), D((40,)), D((4, 4, 4)), D((4, 4)), D((4, 4)), D((4,)), D((4,)), D((4,)), D((4,))],
        compiler_params=pltpu.CompilerParams(collective_id=cid, has_side_effects=True, vmem_limit_bytes=40 << 20),
        name="grad_sum",
    )(g, n_part)
    return total.reshape(1536, 1152), rows


def expert_forward_kernel(x_ref, u_ref, w_ref, down_ref, acts_ref):
    f32, low = jnp.float32, jnp.bfloat16
    rows = x_ref.shape[0]
    wide = down_ref.shape[0]
    count = wide // 128
    first = lax.axis_index("expert") * count
    pre = jnp.dot(x_ref[...], w_ref[...], preferred_element_type=f32)
    width = x_ref.shape[1]
    raw = lax.dot_general(u_ref[:, 0:width], down_ref[...], (((1,), (1,)), ((), ())), preferred_element_type=f32)
    lane = lax.broadcasted_iota(jnp.int32, (rows, 128), 1)
    routes = u_ref[:, width : width + 128].astype(f32).astype(jnp.int32)
    named = lane == routes[:, 0:1]
    for n in range(1, 8):
        named = named | (lane == routes[:, n : n + 1])
    logits = jnp.where(named, pre[:, 2 * wide :], -1e30)
    raised = jnp.exp(logits - jnp.max(logits, -1, keepdims=True))
    gates = raised / jnp.sum(raised, -1, keepdims=True)
    weighted = jnp.zeros((rows, 128), f32)
    for n in range(count):
        here = slice(128 * n, 128 * (n + 1))
        gate = jnp.sum(jnp.where(lane == first + n, gates, 0.0), -1, keepdims=True)
        gate_pre = pre[:, here]
        up_pre = pre[:, wide + 128 * n : wide + 128 * (n + 1)]
        sig = jax.nn.sigmoid(gate_pre)
        silu = gate_pre * sig
        active = silu * up_pre
        back = raw[:, here]
        share = gate * jnp.sum(active * back, -1, keepdims=True)
        high = share.astype(low).astype(f32)
        weighted = weighted + jnp.where(lane == first + n, high, 0.0)
        weighted = weighted + jnp.where(lane == first + n + 64, share - high, 0.0)
        back = gate * back
        acts_ref[:, here] = (gate * active).astype(low)
        acts_ref[:, wide + 128 * n : wide + 128 * (n + 1)] = (
            back * up_pre * (sig * (1.0 + gate_pre * (1.0 - sig)))
        ).astype(low)
        acts_ref[:, 2 * wide + 128 * n : 2 * wide + 128 * (n + 1)] = (back * silu).astype(low)
    acts_ref[:, 3 * wide :] = weighted.astype(low)


def expert_forward(x, u, w_all, down, block=256):
    rows, width = x.shape
    wide = down.shape[0]
    total = w_all.shape[1]
    half = 512 // block

    def place(i):
        core, z = i // (4 * half), i // half % 4
        return (z * 2 + core) * half + i % half

    return pl.pallas_call(
        expert_forward_kernel,
        grid=(rows // block,),
        out_shape=jax.ShapeDtypeStruct((rows, 3 * wide + 128), jnp.bfloat16),
        in_specs=[
            pl.BlockSpec((block, width), lambda i: (i, 0)),
            pl.BlockSpec((block, u.shape[1]), lambda i: (place(i), 0)),
            pl.BlockSpec((width, total), lambda i: (0, 0)),
            pl.BlockSpec((wide, width), lambda i: (0, 0)),
        ],
        out_specs=pl.BlockSpec((block, 3 * wide + 128), lambda i: (i, 0)),
        compiler_params=pltpu.CompilerParams(vmem_limit_bytes=48 << 20),
        name="expert_forward",
    )(x, u, w_all, down)


def expert_back_kernel(acts_hbm, x_hbm, u_hbm, w_ref, down_ref, out, dw_out, router_out,
                       acts, stage, q, sib, a3, b3, a4, b4, a5, b5, a6, b6, xu, acc, dwb, ya, yb,
                       act_sem, load_sem, sib_send, sib_recv, ssem, rsem, ysend, yrecv):
    f32, low = jnp.float32, jnp.bfloat16
    nk = 12
    wide = 640
    x = lax.axis_index("tensor"); e = lax.axis_index("expert"); y = lax.axis_index("dp")
    z = e // 2; c = e % 2
    def zi(d): return (z + d) % 4
    def xi(d): return (x + d) % 4
    def yi(d): return (y + d) % 4
    def peer(oz, ox):
        return {"expert": zi(oz) * 2 + c, "tensor": xi(ox)}
    def ypeer(o):
        return {"dp": yi(o)}
    partner = {"expert": z * 2 + 1 - c}

    def act_load(n):
        rows = pl.ds(pl.multiple_of(n * 2048, 2048), 2048)
        return pltpu.make_async_copy(acts_hbm.at[rows], acts.at[rows], act_sem.at[n])
    def x_load(j, k):
        cols = pl.ds(pl.multiple_of(j * 256, 256), 256)
        return [pltpu.make_async_copy(x_hbm.at[:, cols], xu.at[k % 2], load_sem.at[k % 2, 0])]
    def u_load(j, k):
        cols = pl.ds(pl.multiple_of(j * 256, 256), 256)
        return [pltpu.make_async_copy(u_hbm.at[:, n, :, cols], xu.at[k % 2, pl.ds(2048 * n, 2048)].reshape(4, 512, 256),
                                      load_sem.at[k % 2, n]) for n in range(2)]
    act_load(1 - c).start()
    act_load(c).start()
    for cp in x_load(0, 0): cp.start()
    barrier = pltpu.get_barrier_semaphore()
    near = [peer(1, 0), peer(-1, 0), peer(0, 1), peer(0, -1), partner, ypeer(1), ypeer(-1)]
    for p in near:
        pl.semaphore_signal(barrier, inc=1, device_id=p, device_id_type=MESH)
    pl.semaphore_wait(barrier, len(near))

    def sibs(k):
        return [pltpu.make_async_remote_copy(
            src_ref=stage.at[k % 2], dst_ref=sib.at[k % 2],
            send_sem=sib_send.at[k], recv_sem=sib_recv.at[k], device_id=partner, device_id_type=MESH)]
    def rc(k, n, src, dst, to):
        return pltpu.make_async_remote_copy(src_ref=src, dst_ref=dst, send_sem=ssem.at[k, n], recv_sem=rsem.at[k, n],
                                            device_id=to, device_id_type=MESH)
    def copies3(k):
        s = k % 4
        return [rc(k, 0, q.at[k % 9, zi(2), :, pl.ds(0, 32)], a3.at[s, 0], peer(1, 0)),
                rc(k, 1, q.at[k % 9, zi(2), :, pl.ds(32, 32)], a3.at[s, 1], peer(-1, 0)),
                rc(k, 2, q.at[k % 9, :, xi(2), pl.ds(64, 32)], b3.at[s, 0], peer(0, 1)),
                rc(k, 3, q.at[k % 9, :, xi(2), pl.ds(96, 32)], b3.at[s, 1], peer(0, -1))]
    def copies4(k):
        s = k % 4
        return [rc(k, 4, q.at[k % 9, zi(1), :, pl.ds(0, 64)], a4.at[s, 0], peer(1, 0)),
                rc(k, 5, q.at[k % 9, zi(-1), :, pl.ds(0, 64)], a4.at[s, 1], peer(-1, 0)),
                rc(k, 6, q.at[k % 9, :, xi(1), pl.ds(64, 64)], b4.at[s, 0], peer(0, 1)),
                rc(k, 7, q.at[k % 9, :, xi(-1), pl.ds(64, 64)], b4.at[s, 1], peer(0, -1))]
    def copies5(k):
        s = k % 4
        return [rc(k, 8, q.at[k % 9, z, xi(2), pl.ds(0, 32)], a5.at[s, 0], peer(0, 1)),
                rc(k, 9, q.at[k % 9, z, xi(2), pl.ds(32, 32)], a5.at[s, 1], peer(0, -1)),
                rc(k, 10, q.at[k % 9, zi(2), x, pl.ds(64, 32)], b5.at[s, 0], peer(1, 0)),
                rc(k, 11, q.at[k % 9, zi(2), x, pl.ds(96, 32)], b5.at[s, 1], peer(-1, 0))]
    def copies6(k):
        s = k % 4
        return [rc(k, 12, q.at[k % 9, z, xi(1), pl.ds(0, 64)], a6.at[s, 0], peer(0, 1)),
                rc(k, 13, q.at[k % 9, z, xi(-1), pl.ds(0, 64)], a6.at[s, 1], peer(0, -1)),
                rc(k, 14, q.at[k % 9, zi(1), x, pl.ds(64, 64)], b6.at[s, 0], peer(1, 0)),
                rc(k, 15, q.at[k % 9, zi(-1), x, pl.ds(64, 64)], b6.at[s, 1], peer(-1, 0))]
    def add(k, i, j, rows, *terms):
        t = q[k % 9, i, j, rows].astype(f32)
        for s in terms:
            t = t + s.astype(f32)
        q[k % 9, i, j, rows] = t.astype(low)

    def compute(k):
        cols = pl.ds(pl.multiple_of((k // 2) * 256, 256), 256)
        def piece(cc, put):
            rows = pl.ds(pl.multiple_of(cc * 2048, 2048), 2048)
            @pl.when(k == 0)
            def _(): act_load(cc).wait()
            @pl.when(k % 2 == 0)
            def _():
                put(jnp.dot(acts[rows, 0:wide], down_ref[:, cols], preferred_element_type=f32))
            @pl.when(k % 2 == 1)
            def _():
                put(lax.dot_general(acts[rows, wide:], w_ref[cols, :], (((1,), (1,)), ((), ())),
                                    preferred_element_type=f32))
        def put_stage(r):
            stage[k % 2] = r.astype(low).reshape(4, 4, 128, 256)
        def put_own(r):
            q[k % 9] = r.astype(low).reshape(4, 4, 128, 256)
        piece(1 - c, put_stage)
        for cp in sibs(k): cp.start()
        piece(c, put_own)

    def weight_part(k):
        @pl.when(k % 2 == 0)
        def _():
            for cp in x_load(0, k): cp.wait()
            for cp in u_load(k // 2, k + 1): cp.start()
        @pl.when(k % 2 == 1)
        def _():
            for cp in u_load(0, k): cp.wait()
        @pl.when((k + 1 < nk) & (k % 2 == 1))
        def _():
            for cp in x_load(k // 2 + 1, k + 1): cp.start()
        slot = (k // 2) % 3
        def make(lanes):
            return lax.dot_general(xu[k % 2], acts[:, lanes], (((0,), (0,)), ((), ())), preferred_element_type=f32)
        @pl.when(k % 2 == 0)
        def _():
            acc[...] = make(slice(wide, None))
            dwb[slot, :, :, 0 : 2 * wide] = acc[:, 0 : 2 * wide].astype(low).reshape(4, 64, 2 * wide)
            router_out[pl.ds(pl.multiple_of((k // 2) * 256, 256), 256), :] = acc[:, 2 * wide :]
        @pl.when(k % 2 == 1)
        def _():
            acc[:, 0:wide] = make(slice(0, wide))
            dwb[slot, :, :, 2 * wide :] = acc[:, 0:wide].astype(low).reshape(4, 64, wide)

    def yrc(j, n, src, dst, to):
        return pltpu.make_async_remote_copy(src_ref=src, dst_ref=dst, send_sem=ysend.at[j, n], recv_sem=yrecv.at[j, n],
                                            device_id=to, device_id_type=MESH)
    def ycopies1(j):
        s = j % 3
        return [yrc(j, 0, dwb.at[s, yi(2), pl.ds(0, 32)], ya.at[j % 4, 0], ypeer(1)),
                yrc(j, 1, dwb.at[s, yi(2), pl.ds(32, 32)], ya.at[j % 4, 1], ypeer(-1))]
    def ycopies2(j):
        s = j % 3
        return [yrc(j, 2, dwb.at[s, yi(1)], yb.at[j % 4, 0], ypeer(1)),
                yrc(j, 3, dwb.at[s, yi(-1)], yb.at[j % 4, 1], ypeer(-1))]
    def ystage1(j):
        for cp in ycopies1(j): cp.start()
    def ystage2(j):
        for cp in ycopies1(j): cp.wait_recv()
        s = j % 3
        for d, r, m in ((1, 0, 0), (-1, 32, 1)):
            dwb[s, yi(d), pl.ds(r, 32)] = (dwb[s, yi(d), pl.ds(r, 32)].astype(f32) + ya[j % 4, m].astype(f32)).astype(low)
        for cp in ycopies2(j): cp.start()
    def ystage3(j):
        for cp in ycopies2(j): cp.wait_recv()
        dw_out[j] = (dwb[j % 3, y].astype(f32) + yb[j % 4, 0].astype(f32) + yb[j % 4, 1].astype(f32)).astype(low)
        for cp in ycopies1(j) + ycopies2(j): cp.wait_send()

    def stage2(k):
        for cp in sibs(k): cp.wait()
        def body(n, _):
            add(k, n // 4, n % 4, pl.ds(0, 128), sib[k % 2, n // 4, n % 4])
            return 0
        lax.fori_loop(0, 16, body, 0)
        for cp in copies3(k): cp.start()
    def stage4(k):
        for cp in copies3(k): cp.wait_recv()
        s = k % 4
        def body(n, _):
            add(k, zi(1), n, pl.ds(0, 32), a3[s, 0, n])
            add(k, zi(-1), n, pl.ds(32, 32), a3[s, 1, n])
            add(k, n, xi(1), pl.ds(64, 32), b3[s, 0, n])
            add(k, n, xi(-1), pl.ds(96, 32), b3[s, 1, n])
            return 0
        lax.fori_loop(0, 4, body, 0)
        for cp in copies4(k): cp.start()
    def stage5(k):
        for cp in copies4(k): cp.wait_recv()
        s = k % 4
        def body(n, _):
            add(k, z, n, pl.ds(0, 64), a4[s, 0, n], a4[s, 1, n])
            add(k, n, x, pl.ds(64, 64), b4[s, 0, n], b4[s, 1, n])
            return 0
        lax.fori_loop(0, 4, body, 0)
        for cp in copies5(k): cp.start()
    def stage6(k):
        for cp in copies5(k): cp.wait_recv()
        s = k % 4
        add(k, z, xi(1), pl.ds(0, 32), a5[s, 0])
        add(k, z, xi(-1), pl.ds(32, 32), a5[s, 1])
        add(k, zi(1), x, pl.ds(64, 32), b5[s, 0])
        add(k, zi(-1), x, pl.ds(96, 32), b5[s, 1])
        for cp in copies6(k): cp.start()
    def stage7(k):
        for cp in copies6(k): cp.wait_recv()
        s = k % 4
        for h, m in ((0, a6), (64, b6)):
            t = q[k % 9, z, x, pl.ds(h, 64)].astype(f32) + m[s, 0].astype(f32) + m[s, 1].astype(f32)
            out[k % 2, pl.ds(h, 64), pl.ds(pl.multiple_of((k // 2) * 256, 256), 256)] = t
        for cp in copies3(k) + copies4(k) + copies5(k) + copies6(k): cp.wait_send()

    def step(i, _):
        for lag, st in ((8, stage7), (7, stage6), (5, stage5), (3, stage4), (1, stage2)):
            k = i - lag
            @pl.when((k >= 0) & (k < nk))
            def _():
                st(k)
        for lag, st in ((5, ystage3), (3, ystage2)):
            k = i - lag
            @pl.when((k >= 0) & (k < nk) & (k % 2 == 0))
            def _():
                st(k // 2)
        @pl.when(i < nk)
        def _():
            compute(i)
            weight_part(i)
            @pl.when(i % 2 == 1)
            def _():
                ystage1(i // 2)
        return 0
    lax.fori_loop(0, nk + 8, step, 0)


def expert_back(acts, x, u, w_all, down, cid):
    bf = jnp.bfloat16
    V = pltpu.VMEM
    nk = 12
    u = u.reshape(4, 2, 512, u.shape[1])
    D = pltpu.SemaphoreType.DMA
    vm = pl.BlockSpec(memory_space=pltpu.VMEM)
    anym = pl.BlockSpec(memory_space=pl.ANY)
    return pl.pallas_call(
        expert_back_kernel,
        out_shape=(jax.ShapeDtypeStruct((2, 128, 1536), jnp.float32),
                   jax.ShapeDtypeStruct((6, 64, 1920), bf),
                   jax.ShapeDtypeStruct((1536, 128), jnp.float32)),
        in_specs=[anym, anym, anym, vm, vm],
        out_specs=(vm, vm, vm),
        scratch_shapes=[V((4096, 2048), bf), V((2, 4, 4, 128, 256), bf), V((9, 4, 4, 128, 256), bf), V((2, 4, 4, 128, 256), bf),
                        V((4, 2, 4, 32, 256), bf), V((4, 2, 4, 32, 256), bf),
                        V((4, 2, 4, 64, 256), bf), V((4, 2, 4, 64, 256), bf),
                        V((4, 2, 32, 256), bf), V((4, 2, 32, 256), bf),
                        V((4, 2, 64, 256), bf), V((4, 2, 64, 256), bf),
                        V((2, 4096, 256), bf), V((256, 1408), jnp.float32), V((3, 4, 64, 1920), bf),
                        V((4, 2, 32, 1920), bf), V((4, 2, 64, 1920), bf),
                        D((2,)), D((2, 2)), D((nk,)), D((nk,)), D((nk, 16)), D((nk, 16)), D((6, 4)), D((6, 4))],
        compiler_params=pltpu.CompilerParams(collective_id=cid, has_side_effects=True, vmem_limit_bytes=63 << 20),
        name="expert_back",
    )(acts, x, u, w_all, down)


def shards(
    tokens,
    documents,
    expert_routes,
    attention_gain,
    query_weight,
    key_matrix,
    value_matrix,
    output_weight,
    expert_gain,
    router_weight,
    gate_weight,
    up_weight,
    down_weight,
    out_cotangent,
):
    n_tensor = lax.axis_size("tensor")
    n_expert = lax.axis_size("expert")
    tok_local = tokens.shape[0]
    width = tokens.shape[1]
    group_len = documents.shape[0]
    query_heads = query_weight.shape[1] // HEAD_SIZE
    pair_heads = key_matrix.shape[1] // HEAD_SIZE
    frequency_ratio = query_heads // pair_heads
    local_experts = gate_weight.shape[0]
    experts_all = router_weight.shape[1]
    scale = 1.0 / math.sqrt(HEAD_SIZE)
    inputs = tokens.astype(jnp.float32)
    first_gain = attention_gain.astype(jnp.float32)
    group_tokens = ring_gather(tokens, 5).astype(jnp.float32)
    group_normed, group_scale = normalize(group_tokens, first_gain)
    group_rows = group_normed.astype(jnp.bfloat16)
    first_scale = lax.rsqrt(jnp.mean(inputs * inputs, -1, keepdims=True) + epsilon)
    index = jnp.arange(group_len, dtype=jnp.int32)
    positions = index - jnp.sum((documents[None, :] < documents[:, None]).astype(jnp.int32), 1)
    cosine_table, sine_table = rope_tables(positions, HEAD_SIZE)
    query_linear = jnp.dot(group_rows, query_weight, preferred_element_type=jnp.float32).reshape(
        group_len, query_heads, HEAD_SIZE
    )
    key_linear = jnp.dot(group_rows, key_matrix, preferred_element_type=jnp.float32).reshape(
        group_len, pair_heads, HEAD_SIZE
    )
    value_low = (
        jnp.dot(group_rows, value_matrix, preferred_element_type=jnp.float32)
        .astype(jnp.bfloat16)
        .reshape(group_len, pair_heads, HEAD_SIZE)
    )
    query_low = (
        apply_rotation(query_linear, cosine_table, sine_table)
        .astype(jnp.bfloat16)
        .reshape(group_len, pair_heads, frequency_ratio, HEAD_SIZE)
    )
    key_low = apply_rotation(key_linear, cosine_table, sine_table).astype(jnp.bfloat16)
    block_rows = min(512, group_len)
    count = group_len // block_rows
    starts = jnp.arange(count, dtype=jnp.int32) * block_rows

    def block_scores(start):
        rows_index = start + jnp.arange(block_rows, dtype=jnp.int32)
        scores = (
            jnp.einsum("qhgd,khd->hgqk", query_low, key_low, preferred_element_type=jnp.float32)
            * scale
        )
        allowed = (documents[:, None] == documents[None, :]) & (
            index[None, :] <= rows_index[:, None]
        )
        return (jnp.where(allowed, scores, -1e30), query_low)

    def forward_block(start):
        scores, block_query = block_scores(start)
        top = jnp.max(scores, -1, keepdims=True)
        weights = jnp.exp(scores - top)
        total = jnp.sum(weights, -1, keepdims=True)
        probs = (weights / total).astype(jnp.bfloat16)
        mixed = jnp.einsum("hgqk,khd->qhgd", probs, value_low, preferred_element_type=jnp.float32)
        return (
            mixed.astype(jnp.bfloat16).reshape(block_rows, query_heads * HEAD_SIZE),
            (top + jnp.log(total))[..., 0],
        )

    mixed_blocks, logsum_blocks = lax.map(forward_block, starts)
    attended = mixed_blocks.reshape(group_len, query_heads * HEAD_SIZE)
    head_part = jnp.dot(attended, output_weight, preferred_element_type=jnp.float32)
    second_gain = expert_gain.astype(jnp.float32)
    residual, plane_rows = branch_gather(
        head_part.astype(jnp.bfloat16), tokens, second_gain.reshape(1, width), 6
    )
    plane_rows = plane_rows.reshape(-1, width)
    second_normed, second_scale = normalize(residual, second_gain)
    second_low = second_normed.astype(jnp.bfloat16)
    plane = ("expert", "tensor")
    experts_index = jnp.arange(experts_all, dtype=jnp.int32)
    lined_routes = jnp.pad(expert_routes, ((0, 0), (0, 128 - expert_routes.shape[1])))
    plane_upstream = lax.all_gather(
        jnp.concatenate([out_cotangent, lined_routes.astype(jnp.bfloat16)], 1),
        plane,
        axis=0,
        tiled=True,
    )

    def dense_gates(rows, routes):
        named = jnp.any(routes[:, :, None] == experts_index[None, None, :], 1)
        logits = jnp.dot(rows, router_weight, preferred_element_type=jnp.float32)
        logits = jnp.where(named, logits, -1e30)
        raised = jnp.exp(logits - jnp.max(logits, -1, keepdims=True))
        return raised / jnp.sum(raised, -1, keepdims=True)

    hidden = gate_weight.shape[2]
    wide = local_experts * hidden
    router_pad = jnp.pad(router_weight, ((0, 0), (0, 64 - experts_all)))
    in_weights = jnp.concatenate(
        [
            gate_weight.transpose(1, 0, 2).reshape(width, wide),
            up_weight.transpose(1, 0, 2).reshape(width, wide),
            router_pad,
            router_pad,
        ],
        1,
    )
    down_flat = down_weight.reshape(wide, width)
    acts = expert_forward(plane_rows, plane_upstream, in_weights, down_flat)
    sums, weight_grads, router_pairs = expert_back(
        acts, plane_rows, plane_upstream, in_weights, down_flat, 2
    )
    mixture, route_rows = sums[0], sums[1]
    layer_output = (residual + mixture).astype(jnp.bfloat16)
    router_pairs = router_pairs[:, :experts_all] + router_pairs[:, 64 : 64 + experts_all]
    weight_grads = lax.all_gather(weight_grads, "dp", axis=0)
    gates = dense_gates(second_low, expert_routes)
    upstream = out_cotangent.astype(jnp.float32)
    shared = gates * jnp.sum(mixture * upstream, -1, keepdims=True)
    router_local = -jnp.einsum(
        "td,te->de",
        second_low.astype(jnp.float32),
        shared,
        precision=highest,
        preferred_element_type=jnp.float32,
    ) + router_pairs
    normed_back = route_rows - jnp.einsum(
        "te,de->td",
        shared,
        router_weight.astype(jnp.float32),
        precision=highest,
        preferred_element_type=jnp.float32,
    )
    residual_back, expert_gain_local = norm_back(residual, second_scale, second_gain, normed_back)
    residual_grad = upstream + residual_back
    group_grad = ring_gather(residual_grad.astype(jnp.bfloat16), 7)
    attended_grad = jnp.einsum(
        "td,hd->th", group_grad, output_weight, preferred_element_type=jnp.float32
    ).astype(jnp.bfloat16)
    attended_grad = attended_grad.reshape(group_len, pair_heads, frequency_ratio, HEAD_SIZE)
    output_local = jnp.einsum("td,th->dh", group_grad, attended, preferred_element_type=jnp.float32)

    def backward_block(carry, pieces):
        key_acc, value_acc = carry
        start, logsum = pieces
        scores, block_query = block_scores(start)
        probs = jnp.exp(scores - logsum[..., None])
        prob_grad = jnp.einsum(
            "qhgd,khd->hgqk", attended_grad, value_low, preferred_element_type=jnp.float32
        )
        value_acc = value_acc + jnp.einsum(
            "hgqk,qhgd->khd",
            probs.astype(jnp.bfloat16),
            attended_grad,
            preferred_element_type=jnp.float32,
        )
        inner = jnp.sum(probs * prob_grad, -1, keepdims=True)
        score_grad = (probs * (prob_grad - inner)).astype(jnp.bfloat16)
        query_turned = (
            jnp.einsum("hgqk,khd->qhgd", score_grad, key_low, preferred_element_type=jnp.float32)
            * scale
        )
        key_acc = (
            key_acc
            + jnp.einsum(
                "hgqk,qhgd->khd", score_grad, block_query, preferred_element_type=jnp.float32
            )
            * scale
        )
        return ((key_acc, value_acc), query_turned)

    zero_keys = jnp.zeros((group_len, pair_heads, HEAD_SIZE), jnp.float32)
    (key_turned, value_acc), query_blocks = lax.scan(
        backward_block, (zero_keys, zero_keys), (starts, logsum_blocks)
    )
    query_turned = query_blocks.reshape(group_len, query_heads, HEAD_SIZE)
    query_back = (
        rotate_back(query_turned, cosine_table, sine_table)
        .astype(jnp.bfloat16)
        .reshape(group_len, query_heads * HEAD_SIZE)
    )
    key_back = (
        rotate_back(key_turned, cosine_table, sine_table)
        .astype(jnp.bfloat16)
        .reshape(group_len, pair_heads * HEAD_SIZE)
    )
    value_back = value_acc.astype(jnp.bfloat16).reshape(group_len, pair_heads * HEAD_SIZE)
    query_local = jnp.einsum(
        "td,th->dh", group_rows, query_back, preferred_element_type=jnp.float32
    )
    key_local = jnp.einsum("td,th->dh", group_rows, key_back, preferred_element_type=jnp.float32)
    value_local = jnp.einsum(
        "td,th->dh", group_rows, value_back, preferred_element_type=jnp.float32
    )
    normed_part = jnp.einsum(
        "th,dh->td", query_back, query_weight, preferred_element_type=jnp.float32
    )
    normed_part = normed_part + jnp.einsum(
        "th,dh->td", key_back, key_matrix, preferred_element_type=jnp.float32
    )
    normed_part = normed_part + jnp.einsum(
        "th,dh->td", value_back, value_matrix, preferred_element_type=jnp.float32
    )
    attention_gain_local = jnp.sum(normed_part * group_tokens * group_scale, 0)
    small = jnp.concatenate(
        [
            router_local,
            attention_gain_local[:, None],
            expert_gain_local[:, None],
            jnp.zeros((width, 126 - experts_all), jnp.float32),
        ],
        1,
    )
    grads = jnp.concatenate([query_local, key_local, value_local, output_local, small], 1)
    grads, normed_grad = grad_sum(grads.astype(jnp.bfloat16), normed_part.astype(jnp.bfloat16), 4)
    input_back, _ = norm_back(inputs, first_scale, first_gain, normed_grad)
    input_gradient = residual_grad + input_back
    grads = grads.astype(jnp.float32)
    query_wide = query_weight.shape[1]
    key_wide = query_wide + key_matrix.shape[1]
    value_wide = key_wide + value_matrix.shape[1]
    output_wide = value_wide + query_wide
    query_gradient = grads[:, :query_wide]
    key_gradient = grads[:, query_wide:key_wide]
    value_gradient = grads[:, key_wide:value_wide]
    output_gradient = grads[:, value_wide:output_wide].T
    router_gradient = grads[:, output_wide : output_wide + experts_all]
    attention_gain_gradient = grads[:, output_wide + experts_all]
    expert_gain_gradient = grads[:, output_wide + experts_all + 1]
    gate_gradient, up_gradient, down_gradient = grad_layout(weight_grads)
    return (
        layer_output,
        input_gradient,
        attention_gain_gradient,
        query_gradient,
        key_gradient,
        value_gradient,
        output_gradient,
        expert_gain_gradient,
        router_gradient,
        gate_gradient,
        up_gradient,
        down_gradient,
    )


def solution(mesh):
    placed = (
        P(("dp", "expert", "tensor"), None),
        P(("dp", "expert")),
        P(("dp", "expert", "tensor"), None),
        P(),
        P(None, "tensor"),
        P(None, "tensor"),
        P(None, "tensor"),
        P("tensor", None),
        P(),
        P(),
        P("expert", None, "tensor"),
        P("expert", None, "tensor"),
        P("expert", "tensor", None),
        P(("dp", "expert", "tensor"), None),
    )
    return jax.shard_map(
        shards,
        mesh=mesh,
        in_specs=placed,
        out_specs=(
            P(("dp", "expert", "tensor"), None),
            P(("dp", "expert", "tensor"), None),
            P(),
            P(None, "tensor"),
            P(None, "tensor"),
            P(None, "tensor"),
            P("tensor", None),
            P(),
            P(),
            P("expert", None, "tensor"),
            P("expert", None, "tensor"),
            P("expert", "tensor", None),
        ),
        check_vma=False,
    )
```

```python
import functools
import math

import jax
import jax.numpy as jnp
from jax import lax
from jax.experimental import pallas as pl
from jax.experimental.pallas import tpu as pltpu
from jax.sharding import PartitionSpec as P

HEAD_SIZE = 64


epsilon = 1e-06
theta = 10000.0
highest = lax.Precision.HIGHEST


def normalize(value_rows, gain):
    scale = lax.rsqrt(jnp.mean(value_rows * value_rows, -1, keepdims=True) + epsilon)
    return (value_rows * scale * gain, scale)


def norm_back(value_rows, scale, gain, upstream):
    weighted = upstream * gain
    inner = jnp.mean(weighted * value_rows, -1, keepdims=True)
    result = scale * weighted - value_rows * scale**3 * inner
    gain_part = jnp.sum(upstream * value_rows * scale, 0)
    return (result, gain_part)


def rope_tables(positions, width):
    half = width // 2
    freq = theta ** (-(jnp.arange(half, dtype=jnp.float32) * 2.0 / width))
    angle = positions.astype(jnp.float32)[:, None] * freq[None, :]
    return (jnp.cos(angle), jnp.sin(angle))


def apply_rotation(value_rows, cosine_table, sine_table):
    half = value_rows.shape[-1] // 2
    first = value_rows[..., :half]
    second = value_rows[..., half:]
    cosine_table = cosine_table[:, None, :]
    sine_table = sine_table[:, None, :]
    return jnp.concatenate(
        [first * cosine_table - second * sine_table, second * cosine_table + first * sine_table], -1
    )


def rotate_back(value_rows, cosine_table, sine_table):
    half = value_rows.shape[-1] // 2
    first = value_rows[..., :half]
    second = value_rows[..., half:]
    cosine_table = cosine_table[:, None, :]
    sine_table = sine_table[:, None, :]
    return jnp.concatenate(
        [first * cosine_table + second * sine_table, second * cosine_table - first * sine_table], -1
    )


MESH = pl.DeviceIdType.MESH

def ring_gather_kernel(src, out, own_sem, ssem, rsem):
    x = lax.axis_index("tensor")
    def xi(d): return (x + d) % 4
    def peer(o): return {"tensor": xi(o)}
    barrier = pltpu.get_barrier_semaphore()
    for o in (1, -1):
        pl.semaphore_signal(barrier, inc=1, device_id=peer(o), device_id_type=MESH)
    pl.semaphore_wait(barrier, 2)
    def copy(n, block, half, to, own):
        rows = pl.ds(64 * half, 64)
        return pltpu.make_async_remote_copy(
            src_ref=src.at[rows] if own else out.at[block, rows], dst_ref=out.at[block, rows],
            send_sem=ssem.at[n], recv_sem=rsem.at[n], device_id=peer(to), device_id_type=MESH)
    right = [copy(0, x, 0, 1, True), copy(1, x, 1, 1, True)]
    left = [copy(2, x, 1, -1, True), copy(3, x, 0, -1, True)]
    for a, b in zip(right, left):
        a.start(); b.start()
    mine = pltpu.make_async_copy(src, out.at[x], own_sem)
    mine.start()
    copy(0, xi(-1), 0, 1, False).wait_recv()
    on_right = copy(4, xi(-1), 0, 1, False)
    on_right.start()
    copy(2, xi(1), 1, -1, False).wait_recv()
    on_left = copy(5, xi(1), 1, -1, False)
    on_left.start()
    copy(1, xi(-1), 1, 1, False).wait_recv()
    copy(3, xi(1), 0, -1, False).wait_recv()
    copy(4, xi(2), 0, 1, False).wait_recv()
    copy(5, xi(2), 1, -1, False).wait_recv()
    mine.wait()
    for cp in right + left + [on_right, on_left]:
        cp.wait_send()


def ring_gather(shard, cid):
    rows, width = shard.shape
    D = pltpu.SemaphoreType.DMA
    return pl.pallas_call(
        ring_gather_kernel,
        out_shape=jax.ShapeDtypeStruct((4, rows, width), shard.dtype),
        in_specs=[pl.BlockSpec(memory_space=pltpu.VMEM)],
        out_specs=pl.BlockSpec(memory_space=pltpu.VMEM),
        scratch_shapes=[D(()), D((6,)), D((6,))],
        compiler_params=pltpu.CompilerParams(collective_id=cid, has_side_effects=True),
        name="ring_gather",
    )(shard).reshape(4 * rows, width)


def weight_loads(gate, up, router, w, sem):
    return (
        [pltpu.make_async_copy(gate.at[n], w.at[:, pl.ds(128 * n, 128)], sem.at[n]) for n in range(5)]
        + [pltpu.make_async_copy(up.at[n], w.at[:, pl.ds(640 + 128 * n, 128)], sem.at[5 + n]) for n in range(5)]
        + [pltpu.make_async_copy(router, w.at[:, pl.ds(1280, 128)], sem.at[10])]
    )


PAIRS = ((0, 0), (1, 0), (3, 0), (0, 1), (0, 3), (2, 0), (0, 2), (1, 1), (1, 3), (3, 1), (3, 3), (2, 1), (2, 3), (1, 2), (3, 2), (2, 2))


def branch_forward_kernel(part, tokens, gain, u_hbm, gate_hbm, up_hbm, router_hbm, down_hbm, residual, rows_out, acts_out,
                          nr1, nb, nr2, low_rows, rows, w, down, u_buf, act_buf,
                          nsend, nrecv, own_sem, send_sem, recv_sem, sib_send, sib_recv, w_sem, down_sem, u_sem, act_sem, out_sem):
    f32, low = jnp.float32, jnp.bfloat16
    wide = 640
    width = 1536
    x = lax.axis_index("tensor"); e = lax.axis_index("expert")
    z = e // 2; c = e % 2
    first = e * 5
    def xi(d): return (x + d) % 4
    def zi(d): return (z + d) % 4
    def peer(ox, oz):
        return {"expert": zi(oz) * 2 + c, "tensor": xi(ox)}
    sib = {"expert": z * 2 + 1 - c}
    def pair(step):
        if isinstance(step, int):
            return PAIRS[step]
        dx = dz = 0
        for n in range(4):
            here = lax.convert_element_type(step // 4 == n, jnp.int32)
            dx = dx + here * sum(PAIRS[4 * n + m][0] * 4**m for m in range(4))
            dz = dz + here * sum(PAIRS[4 * n + m][1] * 4**m for m in range(4))
        for n in range(3):
            more = lax.convert_element_type(step % 4 > n, jnp.int32)
            dx = dx // (1 + 3 * more)
            dz = dz // (1 + 3 * more)
        dx, dz = dx % 4, dz % 4
        return dx, dz
    def u_loads(step):
        dx, dz = pair(step)
        return [pltpu.make_async_copy(u_hbm.at[zi(dz), cc, xi(dx)], u_buf.at[step % 2, cc], u_sem.at[step % 2, cc]) for cc in range(2)]
    loads = weight_loads(gate_hbm, up_hbm, router_hbm, w, w_sem) + [pltpu.make_async_copy(down_hbm, down, down_sem)]
    for cp in loads: cp.start()
    barrier = pltpu.get_barrier_semaphore()
    near = [peer(1, 0), peer(-1, 0), peer(0, 1), peer(0, -1), sib]
    for p in near:
        pl.semaphore_signal(barrier, inc=1, device_id=p, device_id_type=MESH)
    pl.semaphore_wait(barrier, len(near))
    pend, later = [], []
    def go(cps):
        for cp in cps: cp.start()
        pend.extend(cps)
        return cps
    def nrc(n, src, dst, to):
        return pltpu.make_async_remote_copy(src_ref=src, dst_ref=dst, send_sem=nsend.at[n], recv_sem=nrecv.at[n],
                                            device_id=peer(to, 0), device_id_type=MESH)
    n1 = go([nrc(0, part.at[xi(2), pl.ds(0, 64)], nr1.at[0], 1), nrc(1, part.at[xi(2), pl.ds(64, 64)], nr1.at[1], -1)])
    n2 = go([nrc(2, part.at[xi(1), pl.ds(64, 64)], nr2.at[0, pl.ds(64, 64)], 1),
             nrc(3, part.at[xi(-1), pl.ds(0, 64)], nr2.at[1, pl.ds(0, 64)], -1)])
    for cp in u_loads(0): cp.start()
    n1[0].wait_recv()
    nb[0] = (part[xi(1), 0:64].astype(f32) + nr1[0].astype(f32)).astype(low)
    n3 = go([nrc(4, nb.at[0], nr2.at[0, pl.ds(0, 64)], 1)])
    n1[1].wait_recv()
    nb[1] = (part[xi(-1), 64:128].astype(f32) + nr1[1].astype(f32)).astype(low)
    n3 += go([nrc(5, nb.at[1], nr2.at[1, pl.ds(64, 64)], -1)])
    for cp in n2 + n3: cp.wait_recv()
    total = tokens[...].astype(f32) + part[x].astype(f32) + nr2[0].astype(f32) + nr2[1].astype(f32)
    residual[...] = total
    scale = lax.rsqrt(jnp.mean(total * total, -1, keepdims=True) + epsilon)
    low_rows[...] = (total * scale * gain[...]).astype(low)
    rows[z, x, c] = low_rows[...]

    count = [0]
    def desc(dx, dz, ox, oz, q, nq, n, own=False):
        quarter = pl.ds(q * 32, nq * 32)
        there = rows.at[zi(dz), xi(dx), c, quarter]
        return pltpu.make_async_remote_copy(
            src_ref=low_rows.at[quarter] if own else there, dst_ref=there,
            send_sem=send_sem.at[n], recv_sem=recv_sem.at[(dx - ox) % 4, (dz - oz) % 4, q],
            device_id=peer(ox, oz), device_id_type=MESH)
    def send(dx, dz, ox, oz, q, nq, own=False):
        make = functools.partial(desc, dx, dz, ox, oz, q, nq, count[0], own)
        make().start()
        later.append(make)
        count[0] += 1
    def recv(dx, dz, q, nq):
        desc(dx, dz, 0, 0, q, nq, 0).wait_recv()
    def sibcopy(cc, dx, dz, own=False):
        there = rows.at[zi(dz), xi(dx), cc]
        return pltpu.make_async_remote_copy(
            src_ref=low_rows if own else there, dst_ref=there,
            send_sem=sib_send.at[dx % 4, dz % 4], recv_sem=sib_recv.at[dx % 4, dz % 4],
            device_id=sib, device_id_type=MESH)
    def sibsend(dx, dz, own=False):
        make = functools.partial(sibcopy, c, dx, dz, own)
        make().start()
        later.append(make)
    for ox, oz in ((1, 0), (-1, 0), (0, 1), (0, -1)):
        send(0, 0, ox, oz, 0, 4, own=True)
    sibsend(0, 0, own=True)
    for cp in loads: cp.wait()

    def wave1():
        for s in (1, -1):
            recv(s, 0, 0, 4)
            if s == -1:
                send(s, 0, 1, 0, 1, 2)
            else:
                send(s, 0, -1, 0, 0, 1); send(s, 0, -1, 0, 3, 1)
            for oz in (1, -1):
                send(s, 0, 0, oz, 0, 2)
            recv(0, s, 0, 4)
            if s == -1:
                send(0, s, 0, 1, 1, 2)
            else:
                send(0, s, 0, -1, 0, 1); send(0, s, 0, -1, 3, 1)
            for ox in (1, -1):
                send(0, s, ox, 0, 2, 2)
            sibsend(s, 0); sibsend(0, s)
    def wave2():
        recv(2, 0, 1, 2); recv(2, 0, 0, 1); recv(2, 0, 3, 1)
        for oz in (1, -1):
            send(2, 0, 0, oz, 0, 2)
        recv(0, 2, 1, 2); recv(0, 2, 0, 1); recv(0, 2, 3, 1)
        for ox in (1, -1):
            send(0, 2, ox, 0, 2, 2)
        sibsend(2, 0); sibsend(0, 2)
        for dx in (1, -1):
            for s in (1, -1):
                recv(dx, s, 0, 2)
                send(dx, s, 0, -s, 0 if s == 1 else 1, 1)
                recv(s, dx, 2, 2)
                send(s, dx, -s, 0, 2 if s == 1 else 3, 1)
        for dx in (1, -1):
            for dz in (1, -1):
                sibsend(dx, dz)
    def wave3():
        for s in (1, -1):
            recv(2, s, 0, 2)
            send(2, s, 0, -s, 0 if s == 1 else 1, 1)
            recv(s, 2, 2, 2)
            send(s, 2, -s, 0, 2 if s == 1 else 3, 1)
        for d in (1, -1):
            recv(d, 2, 0, 1); recv(d, 2, 1, 1)
            recv(2, d, 2, 1); recv(2, d, 3, 1)
        for d in (1, -1):
            sibsend(d, 2); sibsend(2, d)
    def wave4():
        for q in range(4): recv(2, 2, q, 1)
        sibsend(2, 2)

    def act_store(step):
        dx, dz = pair(step)
        return pltpu.make_async_copy(act_buf.at[step % 2], acts_out.at[zi(dz), xi(dx)].reshape(256, 2048), act_sem.at[step % 2])
    def row_store(step):
        dx, dz = pair(step)
        there = (zi(dz), xi(dx))
        return pltpu.make_async_copy(rows.at[there], rows_out.at[there], out_sem.at[step])
    def compute(step):
        dx, dz = pair(step)
        sibcopy(1 - c, dx, dz).wait_recv()
        for cp in u_loads(step): cp.wait()
        @pl.when(step < 15)
        def _():
            for cp in u_loads(step + 1): cp.start()
        row_store(step).start()
        @pl.when(step >= 2)
        def _(): act_store(step - 2).wait()
        slot = step % 2
        here = act_buf.at[slot]
        pre = jnp.dot(rows[zi(dz), xi(dx)].reshape(256, width), w[...], preferred_element_type=f32)
        raw = lax.dot_general(u_buf[slot, :, :, 0:width].reshape(256, width), down[...], (((1,), (1,)), ((), ())), preferred_element_type=f32)
        lane = lax.broadcasted_iota(jnp.int32, (256, 128), 1)
        routes = u_buf[slot, :, :, width:].reshape(256, 128).astype(f32).astype(jnp.int32)
        named = lane == routes[:, 0:1]
        for n in range(1, 8):
            named = named | (lane == routes[:, n : n + 1])
        logits = jnp.where(named, pre[:, 2 * wide :], -1e30)
        raised = jnp.exp(logits - jnp.max(logits, -1, keepdims=True))
        gates = raised / jnp.sum(raised, -1, keepdims=True)
        weighted = jnp.zeros((256, 128), f32)
        for n in range(5):
            cols = slice(128 * n, 128 * (n + 1))
            gate = jnp.sum(jnp.where(lane == first + n, gates, 0.0), -1, keepdims=True)
            gate_pre = pre[:, cols]
            up_pre = pre[:, wide + 128 * n : wide + 128 * (n + 1)]
            sig = jax.nn.sigmoid(gate_pre)
            silu = gate_pre * sig
            active = silu * up_pre
            back = raw[:, cols]
            share = gate * jnp.sum(active * back, -1, keepdims=True)
            high = share.astype(low).astype(f32)
            weighted = weighted + jnp.where(lane == first + n, high, 0.0)
            weighted = weighted + jnp.where(lane == first + n + 64, share - high, 0.0)
            back = gate * back
            here[:, cols] = (gate * active).astype(low)
            here[:, wide + 128 * n : wide + 128 * (n + 1)] = (
                back * up_pre * (sig * (1.0 + gate_pre * (1.0 - sig)))
            ).astype(low)
            here[:, 2 * wide + 128 * n : 2 * wide + 128 * (n + 1)] = (back * silu).astype(low)
        here[:, 3 * wide :] = weighted.astype(low)
        act_store(step).start()

    def body(step, _):
        for at, wave in ((1, wave1), (5, wave2), (9, wave3), (13, wave4)):
            @pl.when(step == at)
            def _():
                wave()
        compute(step)
        return 0
    lax.fori_loop(0, 16, body, 0)
    act_store(14).wait()
    act_store(15).wait()
    for n in range(16): row_store(n).wait()
    for cp in pend: cp.wait_send()
    for make in later: make().wait_send()


def branch_forward(part, tokens, gain, u, gate, up, router, down, cid):
    bf = jnp.bfloat16
    V = pltpu.VMEM
    D = pltpu.SemaphoreType.DMA
    vm = pl.BlockSpec(memory_space=pltpu.VMEM)
    anym = pl.BlockSpec(memory_space=pl.ANY)
    n, width = tokens.shape
    return pl.pallas_call(
        branch_forward_kernel,
        out_shape=(jax.ShapeDtypeStruct((n, width), jnp.float32),
                   jax.ShapeDtypeStruct((4, 4, 2, n, width), bf),
                   jax.ShapeDtypeStruct((4, 4, 2, n, 2048), bf)),
        in_specs=[vm, vm, vm] + [anym] * 5,
        out_specs=(vm, anym, anym),
        scratch_shapes=[V((2, 64, width), bf), V((2, 64, width), bf), V((2, 128, width), bf), V((n, width), bf),
                        V((4, 4, 2, n, width), bf), V((width, 1408), bf), V((640, width), bf),
                        V((2, 2, n, 1664), bf), V((2, 256, 2048), bf),
                        D((6,)), D((6,)), D(()), D((40,)), D((4, 4, 4)), D((4, 4)), D((4, 4)),
                        D((11,)), D(()), D((2, 2)), D((2,)), D((16,))],
        compiler_params=pltpu.CompilerParams(collective_id=cid, has_side_effects=True, vmem_limit_bytes=50 << 20),
        name="branch_forward",
    )(part.reshape(4, n, width), tokens, gain, u.reshape(4, 2, 4, n, 1664), gate, up, router, down)


def grad_layout_kernel(src, gate, up, down):
    f32 = jnp.float32
    for n in range(5):
        for i, ref in enumerate((gate, up)):
            ref[n] = src[:, 0, :, pl.ds(640 * i + 128 * n, 128)].astype(f32).reshape(256, 128)
        down[n] = src[:, 0, :, pl.ds(1280 + 128 * n, 128)].astype(f32).reshape(256, 128).T


def grad_layout(sums):
    return pl.pallas_call(
        grad_layout_kernel,
        grid=(6,),
        out_shape=(jax.ShapeDtypeStruct((5, 1536, 128), jnp.float32),) * 2 + (jax.ShapeDtypeStruct((5, 128, 1536), jnp.float32),),
        in_specs=[pl.BlockSpec((4, 1, 64, 1920), lambda j: (0, j, 0, 0))],
        out_specs=(pl.BlockSpec((5, 256, 128), lambda j: (0, j, 0)),) * 2 + (pl.BlockSpec((5, 128, 256), lambda j: (0, 0, j)),),
        compiler_params=pltpu.CompilerParams(vmem_limit_bytes=32 << 20),
        name="grad_layout",
    )(sums)


def grad_sum_kernel(g, n_part, g_out, n_out, q, sib, a3a, a3b, b3, a4, b4, a5a, a5b, b5, a6, b6, extra,
                    nr1, nb, nr2, sib_sems, ssem, rsem, gsend, grecv, gsib_send, gsib_recv, esend, erecv, nsend, nrecv):
    f32, low = jnp.float32, jnp.bfloat16
    x = lax.axis_index("tensor"); e = lax.axis_index("expert"); y = lax.axis_index("dp")
    z = e // 2; c = e % 2
    def zi(d): return (z + d) % 4
    def yi(d): return (y + d) % 4
    def xi(d): return (x + d) % 4
    def peer(oz, oy):
        return {"expert": zi(oz) * 2 + c, "dp": yi(oy)}
    def xpeer(o):
        return {"tensor": xi(o)}
    partner = {"expert": z * 2 + 1 - c}
    barrier = pltpu.get_barrier_semaphore()
    near = [peer(1, 0), peer(-1, 0), peer(0, 1), peer(0, -1), partner, xpeer(1), xpeer(2), xpeer(3)]
    for p in near:
        pl.semaphore_signal(barrier, inc=1, device_id=p, device_id_type=MESH)
    pl.semaphore_wait(barrier, len(near))
    A0, A1, B0, B1 = pl.ds(0, 384), pl.ds(384, 256), pl.ds(640, 256), pl.ds(896, 256)
    A, B = pl.ds(0, 640), pl.ds(640, 512)
    sent = []
    def rc(n, src, dst, to):
        cp = pltpu.make_async_remote_copy(src_ref=src, dst_ref=dst, send_sem=ssem.at[n], recv_sem=rsem.at[n],
                                          device_id=to, device_id_type=MESH)
        return cp
    def go(cps):
        for cp in cps: cp.start()
        sent.extend(cps)
        return cps
    def nrc(n, src, dst, to):
        return pltpu.make_async_remote_copy(src_ref=src, dst_ref=dst, send_sem=nsend.at[n], recv_sem=nrecv.at[n],
                                            device_id=to, device_id_type=MESH)
    sibling = go([pltpu.make_async_remote_copy(src_ref=g.at[1 - c], dst_ref=sib, send_sem=sib_sems.at[0], recv_sem=sib_sems.at[1],
                                               device_id=partner, device_id_type=MESH)])
    n1 = go([nrc(0, n_part.at[xi(2), pl.ds(0, 64)], nr1.at[0], xpeer(1)),
             nrc(1, n_part.at[xi(2), pl.ds(64, 64)], nr1.at[1], xpeer(-1))])
    sibling[0].wait_recv()
    def body(n, _):
        i, j = n // 4, n % 4
        q[i, j] = (g[c, i, j].astype(f32) + sib[i, j].astype(f32)).astype(low)
        return 0
    lax.fori_loop(0, 16, body, 0)
    def add(i, j, cols, *terms):
        t = q[i, j, :, cols].astype(f32)
        for s in terms:
            t = t + s.astype(f32)
        q[i, j, :, cols] = t.astype(low)
    c3 = go([rc(0, q.at[zi(2), :, :, A0], a3a, peer(1, 0)),
             rc(1, q.at[zi(2), :, :, A1], a3b, peer(-1, 0)),
             rc(2, q.at[:, yi(2), :, B0], b3.at[0], peer(0, 1)),
             rc(3, q.at[:, yi(2), :, B1], b3.at[1], peer(0, -1))])
    for cp in n1: cp.wait_recv()
    nb[0, 0:64] = (n_part[xi(1), 0:64].astype(f32) + nr1[0].astype(f32)).astype(low)
    nb[0, 64:128] = n_part[xi(1), 64:128]
    nb[1, 0:64] = n_part[xi(-1), 0:64]
    nb[1, 64:128] = (n_part[xi(-1), 64:128].astype(f32) + nr1[1].astype(f32)).astype(low)
    n2 = go([nrc(2, nb.at[0], nr2.at[0], xpeer(1)), nrc(3, nb.at[1], nr2.at[1], xpeer(-1))])
    for cp in c3: cp.wait_recv()
    def body4(n, _):
        add(zi(1), n, A0, a3a[n])
        add(zi(-1), n, A1, a3b[n])
        add(n, yi(1), B0, b3[0, n])
        add(n, yi(-1), B1, b3[1, n])
        return 0
    lax.fori_loop(0, 4, body4, 0)
    c4 = go([rc(4, q.at[zi(1), :, :, A], a4.at[0], peer(1, 0)),
             rc(5, q.at[zi(-1), :, :, A], a4.at[1], peer(-1, 0)),
             rc(6, q.at[:, yi(1), :, B], b4.at[0], peer(0, 1)),
             rc(7, q.at[:, yi(-1), :, B], b4.at[1], peer(0, -1))])
    for cp in c4: cp.wait_recv()
    def body5(n, _):
        add(z, n, A, a4[0, n], a4[1, n])
        add(n, y, B, b4[0, n], b4[1, n])
        return 0
    lax.fori_loop(0, 4, body5, 0)
    c5 = go([rc(8, q.at[z, yi(2), :, A0], a5a, peer(0, 1)),
             rc(9, q.at[z, yi(2), :, A1], a5b, peer(0, -1)),
             rc(10, q.at[zi(2), y, :, B0], b5.at[0], peer(1, 0)),
             rc(11, q.at[zi(2), y, :, B1], b5.at[1], peer(-1, 0))])
    for cp in n2: cp.wait_recv()
    n_out[...] = n_part[x].astype(f32) + nr2[0].astype(f32) + nr2[1].astype(f32)
    for cp in c5: cp.wait_recv()
    add(z, yi(1), A0, a5a[...])
    add(z, yi(-1), A1, a5b[...])
    add(zi(1), y, B0, b5[0])
    add(zi(-1), y, B1, b5[1])
    c6 = go([rc(12, q.at[z, yi(1), :, A], a6.at[0], peer(0, 1)),
             rc(13, q.at[z, yi(-1), :, A], a6.at[1], peer(0, -1)),
             rc(14, q.at[zi(1), y, :, B], b6.at[0], peer(1, 0)),
             rc(15, q.at[zi(-1), y, :, B], b6.at[1], peer(-1, 0))])
    for cp in c6: cp.wait_recv()
    own = g_out.at[c, z, y]
    own[:, A] = (q[z, y, :, A].astype(f32) + a6[0].astype(f32) + a6[1].astype(f32)).astype(low)
    last = q[z, y, :, B].astype(f32) + b6[0].astype(f32) + b6[1].astype(f32)
    own[:, pl.ds(640, 384)] = last[:, 0:384].astype(low)
    extra[0] = last[:, 384:512].astype(low)
    es = go([pltpu.make_async_remote_copy(src_ref=extra.at[0], dst_ref=extra.at[o], send_sem=esend.at[o], recv_sem=erecv.at[o],
                                          device_id=xpeer(o), device_id_type=MESH) for o in (1, 2, 3)])
    for cp in es: cp.wait_recv()
    own[:, pl.ds(1024, 128)] = (extra[0].astype(f32) + extra[1].astype(f32) + extra[2].astype(f32) + extra[3].astype(f32)).astype(low)

    starts = (0, 384, 640, 896, 1152)
    def part(qq, nq): return pl.ds(starts[qq], starts[qq + nq] - starts[qq])
    count = [0]
    def send(dy, dz, oy, oz, qq, nq):
        cp = pltpu.make_async_remote_copy(
            src_ref=g_out.at[c, zi(dz), yi(dy), :, part(qq, nq)], dst_ref=g_out.at[c, zi(dz), yi(dy), :, part(qq, nq)],
            send_sem=gsend.at[count[0]], recv_sem=grecv.at[(dy - oy) % 4, (dz - oz) % 4, qq],
            device_id=peer(oz, oy), device_id_type=MESH)
        count[0] += 1
        go([cp])
    def recv(dy, dz, qq, nq):
        ref = g_out.at[c, zi(dz), yi(dy), :, part(qq, nq)]
        pltpu.make_async_remote_copy(src_ref=ref, dst_ref=ref, send_sem=gsend.at[0], recv_sem=grecv.at[dy % 4, dz % 4, qq],
                                     device_id=peer(1, 0), device_id_type=MESH).wait_recv()
    def sibcopy(cc, dy, dz):
        ref = g_out.at[cc, zi(dz), yi(dy)]
        return pltpu.make_async_remote_copy(src_ref=ref, dst_ref=ref, send_sem=gsib_send.at[dy % 4, dz % 4],
                                            recv_sem=gsib_recv.at[dy % 4, dz % 4], device_id=partner, device_id_type=MESH)
    def sibsend(dy, dz): go([sibcopy(c, dy, dz)])
    for oy, oz in ((1, 0), (-1, 0), (0, 1), (0, -1)):
        send(0, 0, oy, oz, 0, 4)
    sibsend(0, 0)
    for s in (1, -1):
        recv(s, 0, 0, 4)
        if s == -1:
            send(s, 0, 1, 0, 1, 2)
        else:
            send(s, 0, -1, 0, 0, 1); send(s, 0, -1, 0, 3, 1)
        for oz in (1, -1):
            send(s, 0, 0, oz, 0, 2)
        recv(0, s, 0, 4)
        if s == -1:
            send(0, s, 0, 1, 1, 2)
        else:
            send(0, s, 0, -1, 0, 1); send(0, s, 0, -1, 3, 1)
        for oy in (1, -1):
            send(0, s, oy, 0, 2, 2)
        sibsend(s, 0); sibsend(0, s)
    recv(2, 0, 1, 2); recv(2, 0, 0, 1); recv(2, 0, 3, 1)
    for oz in (1, -1):
        send(2, 0, 0, oz, 0, 2)
    recv(0, 2, 1, 2); recv(0, 2, 0, 1); recv(0, 2, 3, 1)
    for oy in (1, -1):
        send(0, 2, oy, 0, 2, 2)
    sibsend(2, 0); sibsend(0, 2)
    for dy in (1, -1, 2):
        for s in (1, -1):
            recv(dy, s, 0, 2)
            send(dy, s, 0, -s, 0 if s == 1 else 1, 1)
            recv(s, dy, 2, 2)
            send(s, dy, -s, 0, 2 if s == 1 else 3, 1)
    for dy in (1, -1):
        for dz in (1, -1):
            sibsend(dy, dz)
    for d in (1, -1, 2):
        recv(d, 2, 0, 1); recv(d, 2, 1, 1)
        recv(2, d, 2, 1); recv(2, d, 3, 1)
    for d in (1, -1, 2):
        sibsend(d, 2)
        if d != 2: sibsend(2, d)
    for dy in range(4):
        for dz in range(4):
            sibcopy(1 - c, dy, dz).wait_recv()
    for cp in sent: cp.wait_send()


def grad_sum(g, n_part, cid):
    bf = jnp.bfloat16
    V = pltpu.VMEM
    D = pltpu.SemaphoreType.DMA
    vm = pl.BlockSpec(memory_space=pltpu.VMEM)
    g = g.reshape(2, 4, 4, 48, 1152)
    n_part = n_part.reshape(4, 128, 1536)
    total, rows = pl.pallas_call(
        grad_sum_kernel,
        out_shape=(jax.ShapeDtypeStruct((2, 4, 4, 48, 1152), bf), jax.ShapeDtypeStruct((128, 1536), jnp.float32)),
        in_specs=[vm, vm], out_specs=(vm, vm),
        scratch_shapes=[V((4, 4, 48, 1152), bf), V((4, 4, 48, 1152), bf),
                        V((4, 48, 384), bf), V((4, 48, 256), bf), V((2, 4, 48, 256), bf),
                        V((2, 4, 48, 640), bf), V((2, 4, 48, 512), bf),
                        V((48, 384), bf), V((48, 256), bf), V((2, 48, 256), bf),
                        V((2, 48, 640), bf), V((2, 48, 512), bf), V((4, 48, 128), bf),
                        V((2, 64, 1536), bf), V((2, 128, 1536), bf), V((2, 128, 1536), bf),
                        D((2,)), D((16,)), D((16,)), D((40,)), D((4, 4, 4)), D((4, 4)), D((4, 4)), D((4,)), D((4,)), D((4,)), D((4,))],
        compiler_params=pltpu.CompilerParams(collective_id=cid, has_side_effects=True, vmem_limit_bytes=40 << 20),
        name="grad_sum",
    )(g, n_part)
    return total.reshape(1536, 1152), rows


def expert_back_kernel(acts_hbm, x_hbm, u_hbm, gate_hbm, up_hbm, router_hbm, down_hbm, out, dw_out, router_out,
                       w_ref, down_ref, acts, stage, q, sib, a3, b3, a4, b4, a5, b5, a6, b6, xu, acc, dwb, ya, yb,
                       w_sem, down_sem, act_sem, load_sem, sib_send, sib_recv, ssem, rsem, ysend, yrecv):
    f32, low = jnp.float32, jnp.bfloat16
    nk = 12
    wide = 640
    x = lax.axis_index("tensor"); e = lax.axis_index("expert"); y = lax.axis_index("dp")
    z = e // 2; c = e % 2
    def zi(d): return (z + d) % 4
    def xi(d): return (x + d) % 4
    def yi(d): return (y + d) % 4
    def peer(oz, ox):
        return {"expert": zi(oz) * 2 + c, "tensor": xi(ox)}
    def ypeer(o):
        return {"dp": yi(o)}
    partner = {"expert": z * 2 + 1 - c}

    def act_load(n):
        return pltpu.make_async_copy(acts_hbm.at[:, :, n], acts.at[:, :, n], act_sem.at[n])
    def x_load(j, k):
        cols = pl.ds(pl.multiple_of(j * 256, 256), 256)
        return [pltpu.make_async_copy(x_hbm.at[:, :, :, :, cols], xu.at[k % 2], load_sem.at[k % 2, 0])]
    def u_load(j, k):
        cols = pl.ds(pl.multiple_of(j * 256, 256), 256)
        return [pltpu.make_async_copy(u_hbm.at[:, n, :, :, cols], xu.at[k % 2, :, :, n], load_sem.at[k % 2, n]) for n in range(2)]
    w_loads = weight_loads(gate_hbm, up_hbm, router_hbm, w_ref, w_sem)
    down_load = pltpu.make_async_copy(down_hbm, down_ref, down_sem)
    down_load.start()
    act_load(1 - c).start()
    act_load(c).start()
    for cp in x_load(0, 0): cp.start()
    for cp in w_loads: cp.start()
    barrier = pltpu.get_barrier_semaphore()
    near = [peer(1, 0), peer(-1, 0), peer(0, 1), peer(0, -1), partner, ypeer(1), ypeer(-1)]
    for p in near:
        pl.semaphore_signal(barrier, inc=1, device_id=p, device_id_type=MESH)
    pl.semaphore_wait(barrier, len(near))

    def sibs(k):
        return [pltpu.make_async_remote_copy(
            src_ref=stage.at[k % 2], dst_ref=sib.at[k % 2],
            send_sem=sib_send.at[k], recv_sem=sib_recv.at[k], device_id=partner, device_id_type=MESH)]
    def rc(k, n, src, dst, to):
        return pltpu.make_async_remote_copy(src_ref=src, dst_ref=dst, send_sem=ssem.at[k, n], recv_sem=rsem.at[k, n],
                                            device_id=to, device_id_type=MESH)
    def copies3(k):
        s = k % 4
        return [rc(k, 0, q.at[k % 9, zi(2), :, pl.ds(0, 32)], a3.at[s, 0], peer(1, 0)),
                rc(k, 1, q.at[k % 9, zi(2), :, pl.ds(32, 32)], a3.at[s, 1], peer(-1, 0)),
                rc(k, 2, q.at[k % 9, :, xi(2), pl.ds(64, 32)], b3.at[s, 0], peer(0, 1)),
                rc(k, 3, q.at[k % 9, :, xi(2), pl.ds(96, 32)], b3.at[s, 1], peer(0, -1))]
    def copies4(k):
        s = k % 4
        return [rc(k, 4, q.at[k % 9, zi(1), :, pl.ds(0, 64)], a4.at[s, 0], peer(1, 0)),
                rc(k, 5, q.at[k % 9, zi(-1), :, pl.ds(0, 64)], a4.at[s, 1], peer(-1, 0)),
                rc(k, 6, q.at[k % 9, :, xi(1), pl.ds(64, 64)], b4.at[s, 0], peer(0, 1)),
                rc(k, 7, q.at[k % 9, :, xi(-1), pl.ds(64, 64)], b4.at[s, 1], peer(0, -1))]
    def copies5(k):
        s = k % 4
        return [rc(k, 8, q.at[k % 9, z, xi(2), pl.ds(0, 32)], a5.at[s, 0], peer(0, 1)),
                rc(k, 9, q.at[k % 9, z, xi(2), pl.ds(32, 32)], a5.at[s, 1], peer(0, -1)),
                rc(k, 10, q.at[k % 9, zi(2), x, pl.ds(64, 32)], b5.at[s, 0], peer(1, 0)),
                rc(k, 11, q.at[k % 9, zi(2), x, pl.ds(96, 32)], b5.at[s, 1], peer(-1, 0))]
    def copies6(k):
        s = k % 4
        return [rc(k, 12, q.at[k % 9, z, xi(1), pl.ds(0, 64)], a6.at[s, 0], peer(0, 1)),
                rc(k, 13, q.at[k % 9, z, xi(-1), pl.ds(0, 64)], a6.at[s, 1], peer(0, -1)),
                rc(k, 14, q.at[k % 9, zi(1), x, pl.ds(64, 64)], b6.at[s, 0], peer(1, 0)),
                rc(k, 15, q.at[k % 9, zi(-1), x, pl.ds(64, 64)], b6.at[s, 1], peer(-1, 0))]
    def add(k, i, j, rows, *terms):
        t = q[k % 9, i, j, rows].astype(f32)
        for s in terms:
            t = t + s.astype(f32)
        q[k % 9, i, j, rows] = t.astype(low)

    def compute(k):
        cols = pl.ds(pl.multiple_of((k // 2) * 256, 256), 256)
        def piece(cc, put):
            def rows(lanes): return acts[:, :, cc, :, lanes].reshape(2048, -1)
            @pl.when(k == 0)
            def _(): act_load(cc).wait()
            @pl.when(k % 2 == 0)
            def _():
                put(jnp.dot(rows(slice(0, wide)), down_ref[:, cols], preferred_element_type=f32))
            @pl.when(k % 2 == 1)
            def _():
                put(lax.dot_general(rows(slice(wide, 2048)), w_ref[cols, :], (((1,), (1,)), ((), ())),
                                    preferred_element_type=f32))
        def put_stage(r):
            stage[k % 2] = r.astype(low).reshape(4, 4, 128, 256)
        def put_own(r):
            q[k % 9] = r.astype(low).reshape(4, 4, 128, 256)
        @pl.when(k == 0)
        def _(): down_load.wait()
        @pl.when(k == 1)
        def _():
            for cp in w_loads: cp.wait()
        piece(1 - c, put_stage)
        for cp in sibs(k): cp.start()
        piece(c, put_own)

    def weight_part(k):
        @pl.when(k % 2 == 0)
        def _():
            for cp in x_load(0, k): cp.wait()
            for cp in u_load(k // 2, k + 1): cp.start()
        @pl.when(k % 2 == 1)
        def _():
            for cp in u_load(0, k): cp.wait()
        @pl.when((k + 1 < nk) & (k % 2 == 1))
        def _():
            for cp in x_load(k // 2 + 1, k + 1): cp.start()
        slot = (k // 2) % 3
        def make(lanes):
            return lax.dot_general(xu[k % 2].reshape(4096, 256), acts[:, :, :, :, lanes].reshape(4096, -1),
                                   (((0,), (0,)), ((), ())), preferred_element_type=f32)
        @pl.when(k % 2 == 0)
        def _():
            acc[...] = make(slice(wide, 2048))
            dwb[slot, :, :, 0 : 2 * wide] = acc[:, 0 : 2 * wide].astype(low).reshape(4, 64, 2 * wide)
            router_out[pl.ds(pl.multiple_of((k // 2) * 256, 256), 256), :] = acc[:, 2 * wide :]
        @pl.when(k % 2 == 1)
        def _():
            acc[:, 0:wide] = make(slice(0, wide))
            dwb[slot, :, :, 2 * wide :] = acc[:, 0:wide].astype(low).reshape(4, 64, wide)

    def yrc(j, n, src, dst, to):
        return pltpu.make_async_remote_copy(src_ref=src, dst_ref=dst, send_sem=ysend.at[j, n], recv_sem=yrecv.at[j, n],
                                            device_id=to, device_id_type=MESH)
    def ycopies1(j):
        s = j % 3
        return [yrc(j, 0, dwb.at[s, yi(2), pl.ds(0, 32)], ya.at[j % 4, 0], ypeer(1)),
                yrc(j, 1, dwb.at[s, yi(2), pl.ds(32, 32)], ya.at[j % 4, 1], ypeer(-1))]
    def ycopies2(j):
        s = j % 3
        return [yrc(j, 2, dwb.at[s, yi(1)], yb.at[j % 4, 0], ypeer(1)),
                yrc(j, 3, dwb.at[s, yi(-1)], yb.at[j % 4, 1], ypeer(-1))]
    def ystage1(j):
        for cp in ycopies1(j): cp.start()
    def ystage2(j):
        for cp in ycopies1(j): cp.wait_recv()
        s = j % 3
        for d, r, m in ((1, 0, 0), (-1, 32, 1)):
            dwb[s, yi(d), pl.ds(r, 32)] = (dwb[s, yi(d), pl.ds(r, 32)].astype(f32) + ya[j % 4, m].astype(f32)).astype(low)
        for cp in ycopies2(j): cp.start()
    def ystage3(j):
        for cp in ycopies2(j): cp.wait_recv()
        dw_out[j] = (dwb[j % 3, y].astype(f32) + yb[j % 4, 0].astype(f32) + yb[j % 4, 1].astype(f32)).astype(low)
        for cp in ycopies1(j) + ycopies2(j): cp.wait_send()

    def stage2(k):
        for cp in sibs(k): cp.wait()
        def body(n, _):
            add(k, n // 4, n % 4, pl.ds(0, 128), sib[k % 2, n // 4, n % 4])
            return 0
        lax.fori_loop(0, 16, body, 0)
        for cp in copies3(k): cp.start()
    def stage4(k):
        for cp in copies3(k): cp.wait_recv()
        s = k % 4
        def body(n, _):
            add(k, zi(1), n, pl.ds(0, 32), a3[s, 0, n])
            add(k, zi(-1), n, pl.ds(32, 32), a3[s, 1, n])
            add(k, n, xi(1), pl.ds(64, 32), b3[s, 0, n])
            add(k, n, xi(-1), pl.ds(96, 32), b3[s, 1, n])
            return 0
        lax.fori_loop(0, 4, body, 0)
        for cp in copies4(k): cp.start()
    def stage5(k):
        for cp in copies4(k): cp.wait_recv()
        s = k % 4
        def body(n, _):
            add(k, z, n, pl.ds(0, 64), a4[s, 0, n], a4[s, 1, n])
            add(k, n, x, pl.ds(64, 64), b4[s, 0, n], b4[s, 1, n])
            return 0
        lax.fori_loop(0, 4, body, 0)
        for cp in copies5(k): cp.start()
    def stage6(k):
        for cp in copies5(k): cp.wait_recv()
        s = k % 4
        add(k, z, xi(1), pl.ds(0, 32), a5[s, 0])
        add(k, z, xi(-1), pl.ds(32, 32), a5[s, 1])
        add(k, zi(1), x, pl.ds(64, 32), b5[s, 0])
        add(k, zi(-1), x, pl.ds(96, 32), b5[s, 1])
        for cp in copies6(k): cp.start()
    def stage7(k):
        for cp in copies6(k): cp.wait_recv()
        s = k % 4
        for h, m in ((0, a6), (64, b6)):
            t = q[k % 9, z, x, pl.ds(h, 64)].astype(f32) + m[s, 0].astype(f32) + m[s, 1].astype(f32)
            out[k % 2, pl.ds(h, 64), pl.ds(pl.multiple_of((k // 2) * 256, 256), 256)] = t
        for cp in copies3(k) + copies4(k) + copies5(k) + copies6(k): cp.wait_send()

    def step(i, _):
        for lag, st in ((8, stage7), (7, stage6), (5, stage5), (3, stage4), (1, stage2)):
            k = i - lag
            @pl.when((k >= 0) & (k < nk))
            def _():
                st(k)
        for lag, st in ((5, ystage3), (3, ystage2)):
            k = i - lag
            @pl.when((k >= 0) & (k < nk) & (k % 2 == 0))
            def _():
                st(k // 2)
        @pl.when(i < nk)
        def _():
            compute(i)
            weight_part(i)
            @pl.when(i % 2 == 1)
            def _():
                ystage1(i // 2)
        return 0
    lax.fori_loop(0, nk + 8, step, 0)


def expert_back(acts, x, u, gate, up, router, down, cid):
    bf = jnp.bfloat16
    V = pltpu.VMEM
    nk = 12
    u = u.reshape(4, 2, 4, 128, u.shape[-1])
    D = pltpu.SemaphoreType.DMA
    vm = pl.BlockSpec(memory_space=pltpu.VMEM)
    anym = pl.BlockSpec(memory_space=pl.ANY)
    return pl.pallas_call(
        expert_back_kernel,
        out_shape=(jax.ShapeDtypeStruct((2, 128, 1536), jnp.float32),
                   jax.ShapeDtypeStruct((6, 64, 1920), bf),
                   jax.ShapeDtypeStruct((1536, 128), jnp.float32)),
        in_specs=[anym] * 7,
        out_specs=(vm, vm, vm),
        scratch_shapes=[V((1536, 1408), bf), V((640, 1536), bf), V((4, 4, 2, 128, 2048), bf), V((2, 4, 4, 128, 256), bf), V((9, 4, 4, 128, 256), bf), V((2, 4, 4, 128, 256), bf),
                        V((4, 2, 4, 32, 256), bf), V((4, 2, 4, 32, 256), bf),
                        V((4, 2, 4, 64, 256), bf), V((4, 2, 4, 64, 256), bf),
                        V((4, 2, 32, 256), bf), V((4, 2, 32, 256), bf),
                        V((4, 2, 64, 256), bf), V((4, 2, 64, 256), bf),
                        V((2, 4, 4, 2, 128, 256), bf), V((256, 1408), jnp.float32), V((3, 4, 64, 1920), bf),
                        V((4, 2, 32, 1920), bf), V((4, 2, 64, 1920), bf),
                        D((11,)), D(()), D((2,)), D((2, 2)), D((nk,)), D((nk,)), D((nk, 16)), D((nk, 16)), D((6, 4)), D((6, 4))],
        compiler_params=pltpu.CompilerParams(collective_id=cid, has_side_effects=True, vmem_limit_bytes=63 << 20),
        name="expert_back",
    )(acts, x, u, gate, up, router, down)


def shards(
    tokens,
    documents,
    expert_routes,
    attention_gain,
    query_weight,
    key_matrix,
    value_matrix,
    output_weight,
    expert_gain,
    router_weight,
    gate_weight,
    up_weight,
    down_weight,
    out_cotangent,
):
    n_tensor = lax.axis_size("tensor")
    n_expert = lax.axis_size("expert")
    tok_local = tokens.shape[0]
    width = tokens.shape[1]
    group_len = documents.shape[0]
    query_heads = query_weight.shape[1] // HEAD_SIZE
    pair_heads = key_matrix.shape[1] // HEAD_SIZE
    frequency_ratio = query_heads // pair_heads
    local_experts = gate_weight.shape[0]
    experts_all = router_weight.shape[1]
    scale = 1.0 / math.sqrt(HEAD_SIZE)
    inputs = tokens.astype(jnp.float32)
    first_gain = attention_gain.astype(jnp.float32)
    group_tokens = ring_gather(tokens, 5).astype(jnp.float32)
    group_normed, group_scale = normalize(group_tokens, first_gain)
    group_rows = group_normed.astype(jnp.bfloat16)
    first_scale = lax.rsqrt(jnp.mean(inputs * inputs, -1, keepdims=True) + epsilon)
    index = jnp.arange(group_len, dtype=jnp.int32)
    positions = index - jnp.sum((documents[None, :] < documents[:, None]).astype(jnp.int32), 1)
    cosine_table, sine_table = rope_tables(positions, HEAD_SIZE)
    query_linear = jnp.dot(group_rows, query_weight, preferred_element_type=jnp.float32).reshape(
        group_len, query_heads, HEAD_SIZE
    )
    key_linear = jnp.dot(group_rows, key_matrix, preferred_element_type=jnp.float32).reshape(
        group_len, pair_heads, HEAD_SIZE
    )
    value_low = (
        jnp.dot(group_rows, value_matrix, preferred_element_type=jnp.float32)
        .astype(jnp.bfloat16)
        .reshape(group_len, pair_heads, HEAD_SIZE)
    )
    query_low = (
        apply_rotation(query_linear, cosine_table, sine_table)
        .astype(jnp.bfloat16)
        .reshape(group_len, pair_heads, frequency_ratio, HEAD_SIZE)
    )
    key_low = apply_rotation(key_linear, cosine_table, sine_table).astype(jnp.bfloat16)
    block_rows = min(512, group_len)
    count = group_len // block_rows
    starts = jnp.arange(count, dtype=jnp.int32) * block_rows

    def block_scores(start):
        rows_index = start + jnp.arange(block_rows, dtype=jnp.int32)
        scores = (
            jnp.einsum("qhgd,khd->hgqk", query_low, key_low, preferred_element_type=jnp.float32)
            * scale
        )
        allowed = (documents[:, None] == documents[None, :]) & (
            index[None, :] <= rows_index[:, None]
        )
        return (jnp.where(allowed, scores, -1e30), query_low)

    def forward_block(start):
        scores, block_query = block_scores(start)
        top = jnp.max(scores, -1, keepdims=True)
        weights = jnp.exp(scores - top)
        total = jnp.sum(weights, -1, keepdims=True)
        probs = (weights / total).astype(jnp.bfloat16)
        mixed = jnp.einsum("hgqk,khd->qhgd", probs, value_low, preferred_element_type=jnp.float32)
        return (
            mixed.astype(jnp.bfloat16).reshape(block_rows, query_heads * HEAD_SIZE),
            (top + jnp.log(total))[..., 0],
        )

    mixed_blocks, logsum_blocks = lax.map(forward_block, starts)
    attended = mixed_blocks.reshape(group_len, query_heads * HEAD_SIZE)
    head_part = jnp.dot(attended, output_weight, preferred_element_type=jnp.float32)
    second_gain = expert_gain.astype(jnp.float32)
    plane = ("expert", "tensor")
    experts_index = jnp.arange(experts_all, dtype=jnp.int32)
    lined_routes = jnp.pad(expert_routes, ((0, 0), (0, 128 - expert_routes.shape[1])))
    plane_upstream = lax.all_gather(
        jnp.concatenate([out_cotangent, lined_routes.astype(jnp.bfloat16)], 1),
        plane,
        axis=0,
        tiled=True,
    )
    wide = local_experts * gate_weight.shape[2]
    router_pad = jnp.pad(router_weight, ((0, 0), (0, 64 - experts_all)))
    expert_weights = (
        gate_weight,
        up_weight,
        jnp.concatenate([router_pad, router_pad], 1),
        down_weight.reshape(wide, width),
    )
    residual, plane_rows, acts = branch_forward(
        head_part.astype(jnp.bfloat16),
        tokens,
        second_gain.reshape(1, width),
        plane_upstream,
        *expert_weights,
        6,
    )
    second_normed, second_scale = normalize(residual, second_gain)
    second_low = second_normed.astype(jnp.bfloat16)
    def dense_gates(rows, routes):
        named = jnp.any(routes[:, :, None] == experts_index[None, None, :], 1)
        logits = jnp.dot(rows, router_weight, preferred_element_type=jnp.float32)
        logits = jnp.where(named, logits, -1e30)
        raised = jnp.exp(logits - jnp.max(logits, -1, keepdims=True))
        return raised / jnp.sum(raised, -1, keepdims=True)

    sums, weight_grads, router_pairs = expert_back(
        acts, plane_rows, plane_upstream, *expert_weights, 2
    )
    mixture, route_rows = sums[0], sums[1]
    layer_output = (residual + mixture).astype(jnp.bfloat16)
    router_pairs = router_pairs[:, :experts_all] + router_pairs[:, 64 : 64 + experts_all]
    weight_grads = lax.all_gather(weight_grads, "dp", axis=0)
    gates = dense_gates(second_low, expert_routes)
    upstream = out_cotangent.astype(jnp.float32)
    shared = gates * jnp.sum(mixture * upstream, -1, keepdims=True)
    router_local = -jnp.einsum(
        "td,te->de",
        second_low.astype(jnp.float32),
        shared,
        precision=highest,
        preferred_element_type=jnp.float32,
    ) + router_pairs
    normed_back = route_rows - jnp.einsum(
        "te,de->td",
        shared,
        router_weight.astype(jnp.float32),
        precision=highest,
        preferred_element_type=jnp.float32,
    )
    residual_back, expert_gain_local = norm_back(residual, second_scale, second_gain, normed_back)
    residual_grad = upstream + residual_back
    group_grad = ring_gather(residual_grad.astype(jnp.bfloat16), 7)
    attended_grad = jnp.einsum(
        "td,hd->th", group_grad, output_weight, preferred_element_type=jnp.float32
    ).astype(jnp.bfloat16)
    attended_grad = attended_grad.reshape(group_len, pair_heads, frequency_ratio, HEAD_SIZE)
    output_local = jnp.einsum("td,th->dh", group_grad, attended, preferred_element_type=jnp.float32)

    def backward_block(carry, pieces):
        key_acc, value_acc = carry
        start, logsum = pieces
        scores, block_query = block_scores(start)
        probs = jnp.exp(scores - logsum[..., None])
        prob_grad = jnp.einsum(
            "qhgd,khd->hgqk", attended_grad, value_low, preferred_element_type=jnp.float32
        )
        value_acc = value_acc + jnp.einsum(
            "hgqk,qhgd->khd",
            probs.astype(jnp.bfloat16),
            attended_grad,
            preferred_element_type=jnp.float32,
        )
        inner = jnp.sum(probs * prob_grad, -1, keepdims=True)
        score_grad = (probs * (prob_grad - inner)).astype(jnp.bfloat16)
        query_turned = (
            jnp.einsum("hgqk,khd->qhgd", score_grad, key_low, preferred_element_type=jnp.float32)
            * scale
        )
        key_acc = (
            key_acc
            + jnp.einsum(
                "hgqk,qhgd->khd", score_grad, block_query, preferred_element_type=jnp.float32
            )
            * scale
        )
        return ((key_acc, value_acc), query_turned)

    zero_keys = jnp.zeros((group_len, pair_heads, HEAD_SIZE), jnp.float32)
    (key_turned, value_acc), query_blocks = lax.scan(
        backward_block, (zero_keys, zero_keys), (starts, logsum_blocks)
    )
    query_turned = query_blocks.reshape(group_len, query_heads, HEAD_SIZE)
    query_back = (
        rotate_back(query_turned, cosine_table, sine_table)
        .astype(jnp.bfloat16)
        .reshape(group_len, query_heads * HEAD_SIZE)
    )
    key_back = (
        rotate_back(key_turned, cosine_table, sine_table)
        .astype(jnp.bfloat16)
        .reshape(group_len, pair_heads * HEAD_SIZE)
    )
    value_back = value_acc.astype(jnp.bfloat16).reshape(group_len, pair_heads * HEAD_SIZE)
    query_local = jnp.einsum(
        "td,th->dh", group_rows, query_back, preferred_element_type=jnp.float32
    )
    key_local = jnp.einsum("td,th->dh", group_rows, key_back, preferred_element_type=jnp.float32)
    value_local = jnp.einsum(
        "td,th->dh", group_rows, value_back, preferred_element_type=jnp.float32
    )
    normed_part = jnp.einsum(
        "th,dh->td", query_back, query_weight, preferred_element_type=jnp.float32
    )
    normed_part = normed_part + jnp.einsum(
        "th,dh->td", key_back, key_matrix, preferred_element_type=jnp.float32
    )
    normed_part = normed_part + jnp.einsum(
        "th,dh->td", value_back, value_matrix, preferred_element_type=jnp.float32
    )
    attention_gain_local = jnp.sum(normed_part * group_tokens * group_scale, 0)
    small = jnp.concatenate(
        [
            router_local,
            attention_gain_local[:, None],
            expert_gain_local[:, None],
            jnp.zeros((width, 126 - experts_all), jnp.float32),
        ],
        1,
    )
    grads = jnp.concatenate([query_local, key_local, value_local, output_local, small], 1)
    grads, normed_grad = grad_sum(grads.astype(jnp.bfloat16), normed_part.astype(jnp.bfloat16), 4)
    input_back, _ = norm_back(inputs, first_scale, first_gain, normed_grad)
    input_gradient = residual_grad + input_back
    grads = grads.astype(jnp.float32)
    query_wide = query_weight.shape[1]
    key_wide = query_wide + key_matrix.shape[1]
    value_wide = key_wide + value_matrix.shape[1]
    output_wide = value_wide + query_wide
    query_gradient = grads[:, :query_wide]
    key_gradient = grads[:, query_wide:key_wide]
    value_gradient = grads[:, key_wide:value_wide]
    output_gradient = grads[:, value_wide:output_wide].T
    router_gradient = grads[:, output_wide : output_wide + experts_all]
    attention_gain_gradient = grads[:, output_wide + experts_all]
    expert_gain_gradient = grads[:, output_wide + experts_all + 1]
    gate_gradient, up_gradient, down_gradient = grad_layout(weight_grads)
    return (
        layer_output,
        input_gradient,
        attention_gain_gradient,
        query_gradient,
        key_gradient,
        value_gradient,
        output_gradient,
        expert_gain_gradient,
        router_gradient,
        gate_gradient,
        up_gradient,
        down_gradient,
    )


def solution(mesh):
    placed = (
        P(("dp", "expert", "tensor"), None),
        P(("dp", "expert")),
        P(("dp", "expert", "tensor"), None),
        P(),
        P(None, "tensor"),
        P(None, "tensor"),
        P(None, "tensor"),
        P("tensor", None),
        P(),
        P(),
        P("expert", None, "tensor"),
        P("expert", None, "tensor"),
        P("expert", "tensor", None),
        P(("dp", "expert", "tensor"), None),
    )
    return jax.shard_map(
        shards,
        mesh=mesh,
        in_specs=placed,
        out_specs=(
            P(("dp", "expert", "tensor"), None),
            P(("dp", "expert", "tensor"), None),
            P(),
            P(None, "tensor"),
            P(None, "tensor"),
            P(None, "tensor"),
            P("tensor", None),
            P(),
            P(),
            P("expert", None, "tensor"),
            P("expert", None, "tensor"),
            P("expert", "tensor", None),
        ),
        check_vma=False,
    )
```

```python
import functools

import jax
import jax.numpy as jnp
from jax import lax
from jax.experimental import pallas as pl
from jax.experimental.pallas import tpu as pltpu
from jax.sharding import PartitionSpec as P


epsilon = 1e-06
highest = lax.Precision.HIGHEST


def normalize(value_rows, gain):
    scale = lax.rsqrt(jnp.mean(value_rows * value_rows, -1, keepdims=True) + epsilon)
    return (value_rows * scale * gain, scale)


def norm_back(value_rows, scale, gain, upstream):
    weighted = upstream * gain
    inner = jnp.mean(weighted * value_rows, -1, keepdims=True)
    result = scale * weighted - value_rows * scale**3 * inner
    gain_part = jnp.sum(upstream * value_rows * scale, 0)
    return (result, gain_part)


MESH = pl.DeviceIdType.MESH

def ring_gather_kernel(src, out, own_sem, ssem, rsem):
    x = lax.axis_index("tensor")
    def xi(d): return (x + d) % 4
    def peer(o): return {"tensor": xi(o)}
    barrier = pltpu.get_barrier_semaphore()
    for o in (1, -1):
        pl.semaphore_signal(barrier, inc=1, device_id=peer(o), device_id_type=MESH)
    pl.semaphore_wait(barrier, 2)
    def copy(n, block, half, to, own):
        rows = pl.ds(64 * half, 64)
        return pltpu.make_async_remote_copy(
            src_ref=src.at[rows] if own else out.at[block, rows], dst_ref=out.at[block, rows],
            send_sem=ssem.at[n], recv_sem=rsem.at[n], device_id=peer(to), device_id_type=MESH)
    right = [copy(0, x, 0, 1, True), copy(1, x, 1, 1, True)]
    left = [copy(2, x, 1, -1, True), copy(3, x, 0, -1, True)]
    for a, b in zip(right, left):
        a.start(); b.start()
    mine = pltpu.make_async_copy(src, out.at[x], own_sem)
    mine.start()
    copy(0, xi(-1), 0, 1, False).wait_recv()
    on_right = copy(4, xi(-1), 0, 1, False)
    on_right.start()
    copy(2, xi(1), 1, -1, False).wait_recv()
    on_left = copy(5, xi(1), 1, -1, False)
    on_left.start()
    copy(1, xi(-1), 1, 1, False).wait_recv()
    copy(3, xi(1), 0, -1, False).wait_recv()
    copy(4, xi(2), 0, 1, False).wait_recv()
    copy(5, xi(2), 1, -1, False).wait_recv()
    mine.wait()
    for cp in right + left + [on_right, on_left]:
        cp.wait_send()


def ring_gather(shard, cid):
    rows, width = shard.shape
    D = pltpu.SemaphoreType.DMA
    return pl.pallas_call(
        ring_gather_kernel,
        out_shape=jax.ShapeDtypeStruct((4, rows, width), shard.dtype),
        in_specs=[pl.BlockSpec(memory_space=pltpu.VMEM)],
        out_specs=pl.BlockSpec(memory_space=pltpu.VMEM),
        scratch_shapes=[D(()), D((6,)), D((6,))],
        compiler_params=pltpu.CompilerParams(collective_id=cid, has_side_effects=True),
        name="ring_gather",
    )(shard).reshape(4 * rows, width)


NT = (((1,), (1,)), ((), ()))
TN = (((0,), (0,)), ((), ()))


def turn(v, cosine, sine):
    lane = lax.broadcasted_iota(jnp.int32, v.shape, 1)
    count = v.shape[1]
    partner = jnp.where(lane % 64 < 32, pltpu.roll(v, count - 32, 1), pltpu.roll(v, 32, 1))
    times = count // 128
    return v * jnp.concatenate([cosine] * times, 1) + partner * jnp.concatenate([sine] * times, 1)


def attend(group, gain, cosine, sine, bias, wq, wk, wv, wo, rows_ref, q_ref, k_ref, v_ref, mixed_ref, logsum_ref, part_ref):
    f32, low = jnp.float32, jnp.bfloat16
    t = group[...].reshape(512, 1536).astype(f32)
    scale = lax.rsqrt(jnp.mean(t * t, -1, keepdims=True) + epsilon)
    rows_ref[...] = (t * scale * gain[...]).astype(low)
    rows = rows_ref[...]
    cos, sin = cosine[...], sine[...]
    q_ref[...] = (turn(jnp.dot(rows, wq[...], preferred_element_type=f32), cos, sin) * 0.125).astype(low)
    k_ref[...] = turn(jnp.dot(rows, wk[...], preferred_element_type=f32), cos, sin).astype(low)
    v_ref[...] = jnp.dot(rows, wv[...], preferred_element_type=f32).astype(low)
    lane = lax.broadcasted_iota(jnp.int32, (512, 128), 1)
    logsum = jnp.zeros((512, 128), f32)
    for h in range(6):
        kv = slice(64 * (h // 3), 64 * (h // 3) + 64)
        s = lax.dot_general(q_ref[:, 64 * h : 64 * h + 64], k_ref[:, kv], NT, preferred_element_type=f32) + bias[...]
        top = jnp.max(s, -1, keepdims=True)
        p = jnp.exp(s - top)
        total = jnp.sum(p, -1, keepdims=True)
        mixed = jnp.dot(p.astype(low), v_ref[:, kv], preferred_element_type=f32) / total
        mixed_ref[:, 64 * h : 64 * h + 64] = mixed.astype(low)
        logsum = jnp.where(lane == h, top + jnp.log(total), logsum)
    logsum_ref[...] = logsum
    part_ref[...] = jnp.dot(mixed_ref[...], wo[...], preferred_element_type=f32).astype(low).reshape(4, 128, 1536)


def weight_loads(gate, up, router, w, sem):
    return (
        [pltpu.make_async_copy(gate.at[n], w.at[:, pl.ds(128 * n, 128)], sem.at[n]) for n in range(5)]
        + [pltpu.make_async_copy(up.at[n], w.at[:, pl.ds(640 + 128 * n, 128)], sem.at[5 + n]) for n in range(5)]
        + [pltpu.make_async_copy(router, w.at[:, pl.ds(1280, 128)], sem.at[10])]
    )


PAIRS = ((0, 0), (1, 0), (3, 0), (0, 1), (0, 3), (2, 0), (0, 2), (1, 1), (1, 3), (3, 1), (3, 3), (2, 1), (2, 3), (1, 2), (3, 2), (2, 2))


class PlaneGather:
    def __init__(self, place, own, peer, sibling, core, send_sem, recv_sem, sib_send, sib_recv, starts):
        self.starts = starts
        self.place, self.own, self.peer, self.sibling, self.core = place, own, peer, sibling, core
        self.send_sem, self.recv_sem, self.sib_send, self.sib_recv = send_sem, recv_sem, sib_send, sib_recv
        self.later = []

    def copy(self, dx, dz, ox, oz, q, nq, n, own):
        quarter = pl.ds(self.starts[q], self.starts[q + nq] - self.starts[q])
        there = self.place(dx, dz, self.core).at[quarter]
        return pltpu.make_async_remote_copy(
            src_ref=self.own.at[quarter] if own else there, dst_ref=there,
            send_sem=self.send_sem.at[n], recv_sem=self.recv_sem.at[(dx - ox) % 4, (dz - oz) % 4, q],
            device_id=self.peer(ox, oz), device_id_type=MESH)

    def send(self, dx, dz, ox, oz, q, nq, own=False):
        make = functools.partial(self.copy, dx, dz, ox, oz, q, nq, len(self.later), own)
        make().start()
        self.later.append(make)

    def recv(self, dx, dz, q, nq):
        self.copy(dx, dz, 0, 0, q, nq, 0, False).wait_recv()

    def sib_copy(self, core, dx, dz, own=False):
        there = self.place(dx, dz, core)
        return pltpu.make_async_remote_copy(
            src_ref=self.own if own else there, dst_ref=there,
            send_sem=self.sib_send.at[dx % 4, dz % 4], recv_sem=self.sib_recv.at[dx % 4, dz % 4],
            device_id=self.sibling, device_id_type=MESH)

    def sib_pass(self, dx, dz, own=False):
        make = functools.partial(self.sib_copy, self.core, dx, dz, own)
        make().start()
        self.later.append(make)

    def start(self, directions):
        for ox, oz in directions:
            self.send(0, 0, ox, oz, 0, 4, own=True)

    def wave1x(self):
        for s in (1, -1):
            self.recv(s, 0, 0, 4)
            if s == -1:
                self.send(s, 0, 1, 0, 1, 2)
            else:
                self.send(s, 0, -1, 0, 0, 1)
                self.send(s, 0, -1, 0, 3, 1)
            for oz in (1, -1):
                self.send(s, 0, 0, oz, 0, 2)
            self.sib_pass(s, 0)

    def wave1z(self):
        for s in (1, -1):
            self.recv(0, s, 0, 4)
            if s == -1:
                self.send(0, s, 0, 1, 1, 2)
            else:
                self.send(0, s, 0, -1, 0, 1)
                self.send(0, s, 0, -1, 3, 1)
            for ox in (1, -1):
                self.send(0, s, ox, 0, 2, 2)
            self.sib_pass(0, s)

    def wave1(self):
        self.wave1x()
        self.wave1z()

    def wave2(self):
        for q, nq in ((1, 2), (0, 1), (3, 1)):
            self.recv(2, 0, q, nq)
        for oz in (1, -1):
            self.send(2, 0, 0, oz, 0, 2)
        for q, nq in ((1, 2), (0, 1), (3, 1)):
            self.recv(0, 2, q, nq)
        for ox in (1, -1):
            self.send(0, 2, ox, 0, 2, 2)
        self.sib_pass(2, 0)
        self.sib_pass(0, 2)
        for dx in (1, -1):
            for s in (1, -1):
                self.recv(dx, s, 0, 2)
                self.send(dx, s, 0, -s, 0 if s == 1 else 1, 1)
                self.recv(s, dx, 2, 2)
                self.send(s, dx, -s, 0, 2 if s == 1 else 3, 1)
        for dx in (1, -1):
            for dz in (1, -1):
                self.sib_pass(dx, dz)

    def wave3(self):
        for s in (1, -1):
            self.recv(2, s, 0, 2)
            self.send(2, s, 0, -s, 0 if s == 1 else 1, 1)
            self.recv(s, 2, 2, 2)
            self.send(s, 2, -s, 0, 2 if s == 1 else 3, 1)
        for d in (1, -1):
            for q in (0, 1):
                self.recv(d, 2, q, 1)
                self.recv(2, d, q + 2, 1)
        for d in (1, -1):
            self.sib_pass(d, 2)
            self.sib_pass(2, d)

    def wave4(self):
        for q in range(4):
            self.recv(2, 2, q, 1)
        self.sib_pass(2, 2)

    def finish(self):
        for make in self.later:
            make().wait_send()


def front_kernel(tokens, u_own, first_gain, second_gain, cosine, sine, bias, wq, wk, wv, wo, gate_hbm, up_hbm, router_hbm, down_hbm,
                 residual, rows_out, acts_out, u_hbm, group, normed, queries, keys, values, mixed, logsum,
                 part, nr1, nb, nr2, rows, w, down, u_buf, act_buf,
                 gsend, grecv, own_sem, nsend, nrecv, send_sem, recv_sem, sib_send, sib_recv,
                 u_send, u_recv, u_sib_send, u_sib_recv, w_sem, down_sem, u_sem, act_sem, out_sem):
    f32, low = jnp.float32, jnp.bfloat16
    wide = 640
    width = 1536
    x = lax.axis_index("tensor"); e = lax.axis_index("expert")
    z = e // 2; c = e % 2
    first = e * 5
    def xi(d): return (x + d) % 4
    def zi(d): return (z + d) % 4
    def peer(ox, oz):
        return {"expert": zi(oz) * 2 + c, "tensor": xi(ox)}
    sib = {"expert": z * 2 + 1 - c}
    def pair(step):
        if isinstance(step, int):
            return PAIRS[step]
        dx = dz = 0
        for n in range(4):
            here = lax.convert_element_type(step // 4 == n, jnp.int32)
            dx = dx + here * sum(PAIRS[4 * n + m][0] * 4**m for m in range(4))
            dz = dz + here * sum(PAIRS[4 * n + m][1] * 4**m for m in range(4))
        for n in range(3):
            more = lax.convert_element_type(step % 4 > n, jnp.int32)
            dx = dx // (1 + 3 * more)
            dz = dz // (1 + 3 * more)
        dx, dz = dx % 4, dz % 4
        return dx, dz
    def u_loads(step):
        dx, dz = pair(step)
        return pltpu.make_async_copy(u_hbm.at[zi(dz), xi(dx)], u_buf.at[step % 2], u_sem.at[step % 2])
    loads = weight_loads(gate_hbm, up_hbm, router_hbm, w, w_sem) + [pltpu.make_async_copy(down_hbm, down, down_sem)]
    for cp in loads: cp.start()
    barrier = pltpu.get_barrier_semaphore()
    near = [peer(1, 0), peer(-1, 0), peer(0, 1), peer(0, -1), sib]
    for p in near:
        pl.semaphore_signal(barrier, inc=1, device_id=p, device_id_type=MESH)
    pl.semaphore_wait(barrier, len(near))
    pend = []
    def go(cps):
        for cp in cps: cp.start()
        pend.extend(cps)
        return cps
    def block_of(ref):
        return lambda dx, dz, core: ref.at[zi(dz), xi(dx), core]
    cots = PlaneGather(block_of(u_hbm), u_own, peer, sib, c, u_send, u_recv, u_sib_send, u_sib_recv, (0, 48, 96, 112, 128))
    norms = PlaneGather(block_of(rows), rows.at[z, x, c], peer, sib, c, send_sem, recv_sem, sib_send, sib_recv, (0, 16, 32, 80, 128))
    def tok(n, block, half, to, own):
        there = group.at[block, pl.ds(64 * half, 64)]
        return pltpu.make_async_remote_copy(
            src_ref=tokens.at[pl.ds(64 * half, 64)] if own else there, dst_ref=there,
            send_sem=gsend.at[n], recv_sem=grecv.at[n], device_id=peer(to, 0), device_id_type=MESH)
    go([tok(0, x, 0, 1, True), tok(2, x, 1, -1, True)])
    go([tok(1, x, 1, 1, True), tok(3, x, 0, -1, True)])
    mine = pltpu.make_async_copy(u_own, u_hbm.at[z, x, c], own_sem)
    mine.start()
    cots.start(((0, 1), (0, -1)))
    group[x] = tokens[...]
    tok(0, xi(-1), 0, 1, False).wait_recv()
    go([tok(4, xi(-1), 0, 1, False)])
    tok(2, xi(1), 1, -1, False).wait_recv()
    go([tok(5, xi(1), 1, -1, False)])
    cots.start(((1, 0), (-1, 0)))
    cots.sib_pass(0, 0, own=True)
    tok(1, xi(-1), 1, 1, False).wait_recv()
    tok(3, xi(1), 0, -1, False).wait_recv()
    tok(4, xi(2), 0, 1, False).wait_recv()
    tok(5, xi(2), 1, -1, False).wait_recv()
    attend(group, first_gain, cosine, sine, bias, wq, wk, wv, wo, normed, queries, keys, values, mixed, logsum, part)
    def nrc(n, src, dst, to):
        return pltpu.make_async_remote_copy(src_ref=src, dst_ref=dst, send_sem=nsend.at[n], recv_sem=nrecv.at[n],
                                            device_id=peer(to, 0), device_id_type=MESH)
    n1 = go([nrc(0, part.at[xi(2), pl.ds(0, 64)], nr1.at[0], 1), nrc(1, part.at[xi(2), pl.ds(64, 64)], nr1.at[1], -1)])
    n2 = go([nrc(2, part.at[xi(1), pl.ds(64, 64)], nr2.at[0, pl.ds(64, 64)], 1),
             nrc(3, part.at[xi(-1), pl.ds(0, 64)], nr2.at[1, pl.ds(0, 64)], -1)])
    cots.wave1()
    mine.wait()
    cots.sib_copy(1 - c, 0, 0).wait_recv()
    u_loads(0).start()
    n1[0].wait_recv()
    nb[0] = (part[xi(1), 0:64].astype(f32) + nr1[0].astype(f32)).astype(low)
    n3 = go([nrc(4, nb.at[0], nr2.at[0, pl.ds(0, 64)], 1)])
    n1[1].wait_recv()
    nb[1] = (part[xi(-1), 64:128].astype(f32) + nr1[1].astype(f32)).astype(low)
    n3 += go([nrc(5, nb.at[1], nr2.at[1, pl.ds(64, 64)], -1)])
    for cp in n2 + n3: cp.wait_recv()
    total = tokens[...].astype(f32) + part[x].astype(f32) + nr2[0].astype(f32) + nr2[1].astype(f32)
    residual[...] = total
    scale = lax.rsqrt(jnp.mean(total * total, -1, keepdims=True) + epsilon)
    rows[z, x, c] = (total * scale * second_gain[...]).astype(low)
    norms.start(((1, 0), (-1, 0), (0, 1), (0, -1)))
    norms.sib_pass(0, 0, own=True)
    for cp in loads: cp.wait()

    def act_store(step):
        dx, dz = pair(step)
        return pltpu.make_async_copy(act_buf.at[step % 2], acts_out.at[zi(dz), xi(dx)].reshape(256, 2048), act_sem.at[step % 2])
    def row_store(step):
        dx, dz = pair(step)
        there = (zi(dz), xi(dx))
        return pltpu.make_async_copy(rows.at[there], rows_out.at[there], out_sem.at[step])
    def compute(step):
        dx, dz = pair(step)
        norms.sib_copy(1 - c, dx, dz).wait_recv()
        u_loads(step).wait()
        @pl.when(step < 15)
        def _():
            nx, nz = pair(step + 1)
            cots.sib_copy(1 - c, nx, nz).wait_recv()
            u_loads(step + 1).start()
        row_store(step).start()
        @pl.when(step >= 2)
        def _(): act_store(step - 2).wait()
        slot = step % 2
        here = act_buf.at[slot]
        pre = jnp.dot(rows[zi(dz), xi(dx)].reshape(256, width), w[...], preferred_element_type=f32)
        raw = lax.dot_general(u_buf[slot, :, :, 0:width].reshape(256, width), down[...], (((1,), (1,)), ((), ())), preferred_element_type=f32)
        lane = lax.broadcasted_iota(jnp.int32, (256, 128), 1)
        routes = u_buf[slot, :, :, width:].reshape(256, 128).astype(f32).astype(jnp.int32)
        named = lane == routes[:, 0:1]
        for n in range(1, 8):
            named = named | (lane == routes[:, n : n + 1])
        logits = jnp.where(named, pre[:, 2 * wide :], -1e30)
        raised = jnp.exp(logits - jnp.max(logits, -1, keepdims=True))
        gates = raised / jnp.sum(raised, -1, keepdims=True)
        weighted = jnp.zeros((256, 128), f32)
        for n in range(5):
            cols = slice(128 * n, 128 * (n + 1))
            gate = jnp.sum(jnp.where(lane == first + n, gates, 0.0), -1, keepdims=True)
            gate_pre = pre[:, cols]
            up_pre = pre[:, wide + 128 * n : wide + 128 * (n + 1)]
            sig = jax.nn.sigmoid(gate_pre)
            silu = gate_pre * sig
            active = silu * up_pre
            back = raw[:, cols]
            share = gate * jnp.sum(active * back, -1, keepdims=True)
            high = share.astype(low).astype(f32)
            weighted = weighted + jnp.where(lane == first + n, high, 0.0)
            weighted = weighted + jnp.where(lane == first + n + 64, share - high, 0.0)
            back = gate * back
            here[:, cols] = (gate * active).astype(low)
            here[:, wide + 128 * n : wide + 128 * (n + 1)] = (
                back * up_pre * (sig * (1.0 + gate_pre * (1.0 - sig)))
            ).astype(low)
            here[:, 2 * wide + 128 * n : 2 * wide + 128 * (n + 1)] = (back * silu).astype(low)
        here[:, 3 * wide :] = weighted.astype(low)
        act_store(step).start()

    events = ((0, cots.wave2), (1, norms.wave1), (3, cots.wave3), (5, norms.wave2), (7, cots.wave4), (9, norms.wave3), (13, norms.wave4))
    def body(step, _):
        for at, wave in events:
            @pl.when(step == at)
            def _():
                wave()
        compute(step)
        return 0
    lax.fori_loop(0, 16, body, 0)
    act_store(14).wait()
    act_store(15).wait()
    for n in range(16): row_store(n).wait()
    for cp in pend: cp.wait_send()
    cots.finish()
    norms.finish()


def front(tokens, u, first_gain, second_gain, cosine, sine, bias, wq, wk, wv, wo, gate, up, router, down, cid):
    bf, f32 = jnp.bfloat16, jnp.float32
    V = pltpu.VMEM
    D = pltpu.SemaphoreType.DMA
    S = jax.ShapeDtypeStruct
    vm = pl.BlockSpec(memory_space=pltpu.VMEM)
    anym = pl.BlockSpec(memory_space=pl.ANY)
    n, width = tokens.shape
    return pl.pallas_call(
        front_kernel,
        out_shape=(S((n, width), f32), S((4, 4, 2, n, width), bf), S((4, 4, 2, n, 2048), bf), S((4, 4, 2, n, 1664), bf),
                   S((4, n, width), bf), S((512, width), bf), S((512, 384), bf), S((512, 128), bf), S((512, 128), bf),
                   S((512, 384), bf), S((512, 128), f32)),
        in_specs=[vm, anym] + [vm] * 9 + [anym] * 4,
        out_specs=(vm, anym, anym, anym) + (vm,) * 7,
        scratch_shapes=[V((4, n, width), bf), V((2, 64, width), bf), V((2, 64, width), bf), V((2, 128, width), bf),
                        V((4, 4, 2, n, width), bf), V((width, 1408), bf), V((640, width), bf),
                        V((2, 2, n, 1664), bf), V((2, 256, 2048), bf),
                        D((6,)), D((6,)), D(()), D((6,)), D((6,)), D((64,)), D((4, 4, 4)), D((4, 4)), D((4, 4)),
                        D((64,)), D((4, 4, 4)), D((4, 4)), D((4, 4)),
                        D((11,)), D(()), D((2,)), D((2,)), D((16,))],
        compiler_params=pltpu.CompilerParams(collective_id=cid, has_side_effects=True, vmem_limit_bytes=60 << 20),
        name="front",
    )(tokens, u, first_gain, second_gain, cosine, sine, bias, wq, wk, wv, wo, gate, up, router, down)


def attend_back(grad, rows, tokens, cosine, sine, bias, q, k, v, mixed, logsum, extras, wq, wk, wv, wo, g_ref, part_ref,
                back, turned_t, q_back, k_back, v_back, k_acc, v_acc):
    f32, low = jnp.float32, jnp.bfloat16
    back[...] = lax.dot_general(grad[...], wo[...], NT, preferred_element_type=f32).astype(low)
    k_t = k[...].astype(f32).T.astype(low)
    logsum_t = logsum[...].T
    bias_t = bias[...].T
    for h in range(6):
        one = slice(64 * h, 64 * h + 64)
        kv = slice(64 * (h // 3), 64 * (h // 3) + 64)
        s = lax.dot_general(k[:, kv], q[:, one], NT, preferred_element_type=f32) + bias_t
        p = jnp.exp(s - logsum_t[h : h + 1, :])
        grad_p = lax.dot_general(v[:, kv], back[:, one], NT, preferred_element_type=f32)
        both = p * grad_p
        inner = jnp.sum(both, 0, keepdims=True)
        grad_s = (both - p * inner).astype(low)
        v_part = jnp.dot(p.astype(low), back[:, one], preferred_element_type=f32)
        k_part = jnp.dot(grad_s, q[:, one], preferred_element_type=f32)
        if h % 3 == 0:
            v_acc[:, kv] = v_part
            k_acc[:, kv] = k_part
        else:
            v_acc[:, kv] += v_part
            k_acc[:, kv] += k_part
        turned_t[one, :] = jnp.dot(k_t[kv, :], grad_s, preferred_element_type=f32)
    cos, sin = cosine[...], -sine[...]
    q_back[...] = turn(turned_t[...].T * 0.125, cos, sin).astype(low)
    k_back[...] = turn(k_acc[...], cos, sin).astype(low)
    v_back[...] = v_acc[...].astype(low)
    g_ref[:, 0:384] = lax.dot_general(rows[...], q_back[...], TN, preferred_element_type=f32).astype(low)
    g_ref[:, 384:512] = lax.dot_general(rows[...], k_back[...], TN, preferred_element_type=f32).astype(low)
    g_ref[:, 512:640] = lax.dot_general(rows[...], v_back[...], TN, preferred_element_type=f32).astype(low)
    g_ref[:, 640:1024] = lax.dot_general(grad[...], mixed[...], TN, preferred_element_type=f32).astype(low)
    part = (
        lax.dot_general(q_back[...], wq[...], NT, preferred_element_type=f32)
        + lax.dot_general(k_back[...], wk[...], NT, preferred_element_type=f32)
        + lax.dot_general(v_back[...], wv[...], NT, preferred_element_type=f32)
    )
    part_ref[...] = part.astype(low)
    t = tokens[...].astype(f32)
    t = t * lax.rsqrt(jnp.mean(t * t, -1, keepdims=True) + epsilon)
    ones = jnp.ones((512, 128), low)
    gain_part = lax.dot_general((part * t).astype(low), ones, TN, preferred_element_type=f32)
    lane = lax.broadcasted_iota(jnp.int32, (1536, 128), 1)
    g_ref[:, 1024:1152] = jnp.where(lane == 40, gain_part, extras[...]).astype(low)


def attention_back(grad, rows, tokens, cosine, sine, bias, q, k, v, mixed, logsum, extras, wq, wk, wv, wo):
    S = jax.ShapeDtypeStruct
    bf = jnp.bfloat16
    V = pltpu.VMEM
    return pl.pallas_call(
        attend_back,
        out_shape=(S((1536, 1152), bf), S((512, 1536), bf)),
        scratch_shapes=[V((512, 384), bf), V((384, 512), jnp.float32), V((512, 384), bf), V((512, 128), bf), V((512, 128), bf),
                        V((512, 128), jnp.float32), V((512, 128), jnp.float32)],
        compiler_params=pltpu.CompilerParams(vmem_limit_bytes=56 << 20),
        name="attention_back",
    )(grad, rows, tokens, cosine, sine, bias, q, k, v, mixed, logsum, extras, wq, wk, wv, wo)


def attention_tables(documents):
    index = jnp.arange(documents.shape[0], dtype=jnp.int32)
    positions = index - jnp.sum((documents[None, :] < documents[:, None]).astype(jnp.int32), 1)
    freq = 10000.0 ** (-(jnp.arange(32, dtype=jnp.float32) * 2.0 / 64))
    angle = positions.astype(jnp.float32)[:, None] * freq[None, :]
    cos, sin = jnp.cos(angle), jnp.sin(angle)
    allowed = (documents[:, None] == documents[None, :]) & (index[None, :] <= index[:, None])
    return (jnp.concatenate([cos] * 4, 1), jnp.concatenate([-sin, sin] * 2, 1), jnp.where(allowed, 0.0, -1e30).astype(jnp.float32))


def finish_kernel(sums, total, gate, up, down, query, key, value, output, router, gains):
    f32 = jnp.float32
    for n in range(5):
        for i, ref in enumerate((gate, up)):
            ref[n] = sums[:, 0, :, pl.ds(640 * i + 128 * n, 128)].astype(f32).reshape(256, 128)
        down[n] = sums[:, 0, :, pl.ds(1280 + 128 * n, 128)].astype(f32).reshape(256, 128).T
    query[...] = total[:, 0:384].astype(f32)
    key[...] = total[:, 384:512].astype(f32)
    value[...] = total[:, 512:640].astype(f32)
    output[...] = total[:, 640:1024].astype(f32).T
    small = total[:, 1024:1152].astype(f32)
    router[...] = small[:, 0:40]
    gains[...] = small.T[40:48, :]


def finish(sums, total):
    S = jax.ShapeDtypeStruct
    f32 = jnp.float32
    return pl.pallas_call(
        finish_kernel,
        grid=(6,),
        out_shape=(S((5, 1536, 128), f32), S((5, 1536, 128), f32), S((5, 128, 1536), f32), S((1536, 384), f32),
                   S((1536, 128), f32), S((1536, 128), f32), S((384, 1536), f32), S((1536, 40), f32), S((8, 1536), f32)),
        in_specs=[pl.BlockSpec((4, 1, 64, 1920), lambda j: (0, j, 0, 0)), pl.BlockSpec((256, 1152), lambda j: (j, 0))],
        out_specs=(pl.BlockSpec((5, 256, 128), lambda j: (0, j, 0)), pl.BlockSpec((5, 256, 128), lambda j: (0, j, 0)),
                   pl.BlockSpec((5, 128, 256), lambda j: (0, 0, j)), pl.BlockSpec((256, 384), lambda j: (j, 0)),
                   pl.BlockSpec((256, 128), lambda j: (j, 0)), pl.BlockSpec((256, 128), lambda j: (j, 0)),
                   pl.BlockSpec((384, 256), lambda j: (0, j)), pl.BlockSpec((256, 40), lambda j: (j, 0)),
                   pl.BlockSpec((8, 256), lambda j: (0, j))),
        compiler_params=pltpu.CompilerParams(vmem_limit_bytes=32 << 20),
        name="finish",
    )(sums, total)


def grad_sum_kernel(g, n_part, g_out, n_out, q, sib, a3a, a3b, b3, a4, b4, a5a, a5b, b5, a6, b6, extra,
                    nr1, nb, nr2, sib_sems, ssem, rsem, gsend, grecv, gsib_send, gsib_recv, esend, erecv, nsend, nrecv):
    f32, low = jnp.float32, jnp.bfloat16
    x = lax.axis_index("tensor"); e = lax.axis_index("expert"); y = lax.axis_index("dp")
    z = e // 2; c = e % 2
    def zi(d): return (z + d) % 4
    def yi(d): return (y + d) % 4
    def xi(d): return (x + d) % 4
    def peer(oz, oy):
        return {"expert": zi(oz) * 2 + c, "dp": yi(oy)}
    def xpeer(o):
        return {"tensor": xi(o)}
    partner = {"expert": z * 2 + 1 - c}
    barrier = pltpu.get_barrier_semaphore()
    near = [peer(1, 0), peer(-1, 0), peer(0, 1), peer(0, -1), partner, xpeer(1), xpeer(2), xpeer(3)]
    for p in near:
        pl.semaphore_signal(barrier, inc=1, device_id=p, device_id_type=MESH)
    pl.semaphore_wait(barrier, len(near))
    A0, A1, B0, B1 = pl.ds(0, 384), pl.ds(384, 256), pl.ds(640, 256), pl.ds(896, 256)
    A, B = pl.ds(0, 640), pl.ds(640, 512)
    sent = []
    def rc(n, src, dst, to):
        cp = pltpu.make_async_remote_copy(src_ref=src, dst_ref=dst, send_sem=ssem.at[n], recv_sem=rsem.at[n],
                                          device_id=to, device_id_type=MESH)
        return cp
    def go(cps):
        for cp in cps: cp.start()
        sent.extend(cps)
        return cps
    def nrc(n, src, dst, to):
        return pltpu.make_async_remote_copy(src_ref=src, dst_ref=dst, send_sem=nsend.at[n], recv_sem=nrecv.at[n],
                                            device_id=to, device_id_type=MESH)
    sibling = go([pltpu.make_async_remote_copy(src_ref=g.at[1 - c], dst_ref=sib, send_sem=sib_sems.at[0], recv_sem=sib_sems.at[1],
                                               device_id=partner, device_id_type=MESH)])
    n1 = go([nrc(0, n_part.at[xi(2), pl.ds(0, 64)], nr1.at[0], xpeer(1)),
             nrc(1, n_part.at[xi(2), pl.ds(64, 64)], nr1.at[1], xpeer(-1))])
    sibling[0].wait_recv()
    def body(n, _):
        i, j = n // 4, n % 4
        q[i, j] = (g[c, i, j].astype(f32) + sib[i, j].astype(f32)).astype(low)
        return 0
    lax.fori_loop(0, 16, body, 0)
    def add(i, j, cols, *terms):
        t = q[i, j, :, cols].astype(f32)
        for s in terms:
            t = t + s.astype(f32)
        q[i, j, :, cols] = t.astype(low)
    c3 = go([rc(0, q.at[zi(2), :, :, A0], a3a, peer(1, 0)),
             rc(1, q.at[zi(2), :, :, A1], a3b, peer(-1, 0)),
             rc(2, q.at[:, yi(2), :, B0], b3.at[0], peer(0, 1)),
             rc(3, q.at[:, yi(2), :, B1], b3.at[1], peer(0, -1))])
    for cp in n1: cp.wait_recv()
    nb[0, 0:64] = (n_part[xi(1), 0:64].astype(f32) + nr1[0].astype(f32)).astype(low)
    nb[0, 64:128] = n_part[xi(1), 64:128]
    nb[1, 0:64] = n_part[xi(-1), 0:64]
    nb[1, 64:128] = (n_part[xi(-1), 64:128].astype(f32) + nr1[1].astype(f32)).astype(low)
    n2 = go([nrc(2, nb.at[0], nr2.at[0], xpeer(1)), nrc(3, nb.at[1], nr2.at[1], xpeer(-1))])
    for cp in c3: cp.wait_recv()
    def body4(n, _):
        add(zi(1), n, A0, a3a[n])
        add(zi(-1), n, A1, a3b[n])
        add(n, yi(1), B0, b3[0, n])
        add(n, yi(-1), B1, b3[1, n])
        return 0
    lax.fori_loop(0, 4, body4, 0)
    c4 = go([rc(4, q.at[zi(1), :, :, A], a4.at[0], peer(1, 0)),
             rc(5, q.at[zi(-1), :, :, A], a4.at[1], peer(-1, 0)),
             rc(6, q.at[:, yi(1), :, B], b4.at[0], peer(0, 1)),
             rc(7, q.at[:, yi(-1), :, B], b4.at[1], peer(0, -1))])
    for cp in c4: cp.wait_recv()
    def body5(n, _):
        add(z, n, A, a4[0, n], a4[1, n])
        add(n, y, B, b4[0, n], b4[1, n])
        return 0
    lax.fori_loop(0, 4, body5, 0)
    c5 = go([rc(8, q.at[z, yi(2), :, A0], a5a, peer(0, 1)),
             rc(9, q.at[z, yi(2), :, A1], a5b, peer(0, -1)),
             rc(10, q.at[zi(2), y, :, B0], b5.at[0], peer(1, 0)),
             rc(11, q.at[zi(2), y, :, B1], b5.at[1], peer(-1, 0))])
    for cp in n2: cp.wait_recv()
    n_out[...] = n_part[x].astype(f32) + nr2[0].astype(f32) + nr2[1].astype(f32)
    for cp in c5: cp.wait_recv()
    add(z, yi(1), A0, a5a[...])
    add(z, yi(-1), A1, a5b[...])
    add(zi(1), y, B0, b5[0])
    add(zi(-1), y, B1, b5[1])
    c6 = go([rc(12, q.at[z, yi(1), :, A], a6.at[0], peer(0, 1)),
             rc(13, q.at[z, yi(-1), :, A], a6.at[1], peer(0, -1)),
             rc(14, q.at[zi(1), y, :, B], b6.at[0], peer(1, 0)),
             rc(15, q.at[zi(-1), y, :, B], b6.at[1], peer(-1, 0))])
    for cp in c6: cp.wait_recv()
    own = g_out.at[c, z, y]
    own[:, A] = (q[z, y, :, A].astype(f32) + a6[0].astype(f32) + a6[1].astype(f32)).astype(low)
    last = q[z, y, :, B].astype(f32) + b6[0].astype(f32) + b6[1].astype(f32)
    own[:, pl.ds(640, 384)] = last[:, 0:384].astype(low)
    extra[0] = last[:, 384:512].astype(low)
    es = go([pltpu.make_async_remote_copy(src_ref=extra.at[0], dst_ref=extra.at[o], send_sem=esend.at[o], recv_sem=erecv.at[o],
                                          device_id=xpeer(o), device_id_type=MESH) for o in (1, 2, 3)])
    for cp in es: cp.wait_recv()
    own[:, pl.ds(1024, 128)] = (extra[0].astype(f32) + extra[1].astype(f32) + extra[2].astype(f32) + extra[3].astype(f32)).astype(low)

    starts = (0, 384, 640, 896, 1152)
    def part(qq, nq): return pl.ds(starts[qq], starts[qq + nq] - starts[qq])
    count = [0]
    def send(dy, dz, oy, oz, qq, nq):
        cp = pltpu.make_async_remote_copy(
            src_ref=g_out.at[c, zi(dz), yi(dy), :, part(qq, nq)], dst_ref=g_out.at[c, zi(dz), yi(dy), :, part(qq, nq)],
            send_sem=gsend.at[count[0]], recv_sem=grecv.at[(dy - oy) % 4, (dz - oz) % 4, qq],
            device_id=peer(oz, oy), device_id_type=MESH)
        count[0] += 1
        go([cp])
    def recv(dy, dz, qq, nq):
        ref = g_out.at[c, zi(dz), yi(dy), :, part(qq, nq)]
        pltpu.make_async_remote_copy(src_ref=ref, dst_ref=ref, send_sem=gsend.at[0], recv_sem=grecv.at[dy % 4, dz % 4, qq],
                                     device_id=peer(1, 0), device_id_type=MESH).wait_recv()
    def sibcopy(cc, dy, dz):
        ref = g_out.at[cc, zi(dz), yi(dy)]
        return pltpu.make_async_remote_copy(src_ref=ref, dst_ref=ref, send_sem=gsib_send.at[dy % 4, dz % 4],
                                            recv_sem=gsib_recv.at[dy % 4, dz % 4], device_id=partner, device_id_type=MESH)
    def sibsend(dy, dz): go([sibcopy(c, dy, dz)])
    for oy, oz in ((1, 0), (-1, 0), (0, 1), (0, -1)):
        send(0, 0, oy, oz, 0, 4)
    sibsend(0, 0)
    for s in (1, -1):
        recv(s, 0, 0, 4)
        if s == -1:
            send(s, 0, 1, 0, 1, 2)
        else:
            send(s, 0, -1, 0, 0, 1); send(s, 0, -1, 0, 3, 1)
        for oz in (1, -1):
            send(s, 0, 0, oz, 0, 2)
        recv(0, s, 0, 4)
        if s == -1:
            send(0, s, 0, 1, 1, 2)
        else:
            send(0, s, 0, -1, 0, 1); send(0, s, 0, -1, 3, 1)
        for oy in (1, -1):
            send(0, s, oy, 0, 2, 2)
        sibsend(s, 0); sibsend(0, s)
    recv(2, 0, 1, 2); recv(2, 0, 0, 1); recv(2, 0, 3, 1)
    for oz in (1, -1):
        send(2, 0, 0, oz, 0, 2)
    recv(0, 2, 1, 2); recv(0, 2, 0, 1); recv(0, 2, 3, 1)
    for oy in (1, -1):
        send(0, 2, oy, 0, 2, 2)
    sibsend(2, 0); sibsend(0, 2)
    for dy in (1, -1, 2):
        for s in (1, -1):
            recv(dy, s, 0, 2)
            send(dy, s, 0, -s, 0 if s == 1 else 1, 1)
            recv(s, dy, 2, 2)
            send(s, dy, -s, 0, 2 if s == 1 else 3, 1)
    for dy in (1, -1):
        for dz in (1, -1):
            sibsend(dy, dz)
    for d in (1, -1, 2):
        recv(d, 2, 0, 1); recv(d, 2, 1, 1)
        recv(2, d, 2, 1); recv(2, d, 3, 1)
    for d in (1, -1, 2):
        sibsend(d, 2)
        if d != 2: sibsend(2, d)
    for dy in range(4):
        for dz in range(4):
            sibcopy(1 - c, dy, dz).wait_recv()
    for cp in sent: cp.wait_send()


def grad_sum(g, n_part, cid):
    bf = jnp.bfloat16
    V = pltpu.VMEM
    D = pltpu.SemaphoreType.DMA
    vm = pl.BlockSpec(memory_space=pltpu.VMEM)
    g = g.reshape(2, 4, 4, 48, 1152)
    n_part = n_part.reshape(4, 128, 1536)
    total, rows = pl.pallas_call(
        grad_sum_kernel,
        out_shape=(jax.ShapeDtypeStruct((2, 4, 4, 48, 1152), bf), jax.ShapeDtypeStruct((128, 1536), jnp.float32)),
        in_specs=[vm, vm], out_specs=(vm, vm),
        scratch_shapes=[V((4, 4, 48, 1152), bf), V((4, 4, 48, 1152), bf),
                        V((4, 48, 384), bf), V((4, 48, 256), bf), V((2, 4, 48, 256), bf),
                        V((2, 4, 48, 640), bf), V((2, 4, 48, 512), bf),
                        V((48, 384), bf), V((48, 256), bf), V((2, 48, 256), bf),
                        V((2, 48, 640), bf), V((2, 48, 512), bf), V((4, 48, 128), bf),
                        V((2, 64, 1536), bf), V((2, 128, 1536), bf), V((2, 128, 1536), bf),
                        D((2,)), D((16,)), D((16,)), D((40,)), D((4, 4, 4)), D((4, 4)), D((4, 4)), D((4,)), D((4,)), D((4,)), D((4,))],
        compiler_params=pltpu.CompilerParams(collective_id=cid, has_side_effects=True, vmem_limit_bytes=40 << 20),
        name="grad_sum",
    )(g, n_part)
    return total.reshape(1536, 1152), rows


def expert_back_kernel(acts_hbm, x_hbm, u_hbm, gate_hbm, up_hbm, router_hbm, down_hbm, out, dw_out, router_out,
                       w_ref, down_ref, acts, stage, q, sib, a3, b3, a4, b4, a5, b5, a6, b6, xu, acc, dwb, ya, yb,
                       w_sem, down_sem, act_sem, load_sem, sib_send, sib_recv, ssem, rsem, ysend, yrecv):
    f32, low = jnp.float32, jnp.bfloat16
    nk = 12
    wide = 640
    x = lax.axis_index("tensor"); e = lax.axis_index("expert"); y = lax.axis_index("dp")
    z = e // 2; c = e % 2
    def zi(d): return (z + d) % 4
    def xi(d): return (x + d) % 4
    def yi(d): return (y + d) % 4
    def peer(oz, ox):
        return {"expert": zi(oz) * 2 + c, "tensor": xi(ox)}
    def ypeer(o):
        return {"dp": yi(o)}
    partner = {"expert": z * 2 + 1 - c}

    def act_load(n):
        return pltpu.make_async_copy(acts_hbm.at[:, :, n], acts.at[:, :, n], act_sem.at[n])
    def x_load(j, k):
        cols = pl.ds(pl.multiple_of(j * 256, 256), 256)
        return [pltpu.make_async_copy(x_hbm.at[:, :, :, :, cols], xu.at[k % 2], load_sem.at[k % 2, 0])]
    def u_load(j, k):
        cols = pl.ds(pl.multiple_of(j * 256, 256), 256)
        return [pltpu.make_async_copy(u_hbm.at[:, :, :, :, cols], xu.at[k % 2], load_sem.at[k % 2, 1])]
    w_loads = weight_loads(gate_hbm, up_hbm, router_hbm, w_ref, w_sem)
    down_load = pltpu.make_async_copy(down_hbm, down_ref, down_sem)
    down_load.start()
    act_load(1 - c).start()
    act_load(c).start()
    for cp in x_load(0, 0): cp.start()
    for cp in w_loads: cp.start()
    barrier = pltpu.get_barrier_semaphore()
    near = [peer(1, 0), peer(-1, 0), peer(0, 1), peer(0, -1), partner, ypeer(1), ypeer(-1)]
    for p in near:
        pl.semaphore_signal(barrier, inc=1, device_id=p, device_id_type=MESH)
    pl.semaphore_wait(barrier, len(near))

    def sibs(k):
        return [pltpu.make_async_remote_copy(
            src_ref=stage.at[k % 2], dst_ref=sib.at[k % 2],
            send_sem=sib_send.at[k], recv_sem=sib_recv.at[k], device_id=partner, device_id_type=MESH)]
    def rc(k, n, src, dst, to):
        return pltpu.make_async_remote_copy(src_ref=src, dst_ref=dst, send_sem=ssem.at[k, n], recv_sem=rsem.at[k, n],
                                            device_id=to, device_id_type=MESH)
    def copies3(k):
        s = k % 4
        return [rc(k, 0, q.at[k % 9, zi(2), :, pl.ds(0, 32)], a3.at[s, 0], peer(1, 0)),
                rc(k, 1, q.at[k % 9, zi(2), :, pl.ds(32, 32)], a3.at[s, 1], peer(-1, 0)),
                rc(k, 2, q.at[k % 9, :, xi(2), pl.ds(64, 32)], b3.at[s, 0], peer(0, 1)),
                rc(k, 3, q.at[k % 9, :, xi(2), pl.ds(96, 32)], b3.at[s, 1], peer(0, -1))]
    def copies4(k):
        s = k % 4
        return [rc(k, 4, q.at[k % 9, zi(1), :, pl.ds(0, 64)], a4.at[s, 0], peer(1, 0)),
                rc(k, 5, q.at[k % 9, zi(-1), :, pl.ds(0, 64)], a4.at[s, 1], peer(-1, 0)),
                rc(k, 6, q.at[k % 9, :, xi(1), pl.ds(64, 64)], b4.at[s, 0], peer(0, 1)),
                rc(k, 7, q.at[k % 9, :, xi(-1), pl.ds(64, 64)], b4.at[s, 1], peer(0, -1))]
    def copies5(k):
        s = k % 4
        return [rc(k, 8, q.at[k % 9, z, xi(2), pl.ds(0, 32)], a5.at[s, 0], peer(0, 1)),
                rc(k, 9, q.at[k % 9, z, xi(2), pl.ds(32, 32)], a5.at[s, 1], peer(0, -1)),
                rc(k, 10, q.at[k % 9, zi(2), x, pl.ds(64, 32)], b5.at[s, 0], peer(1, 0)),
                rc(k, 11, q.at[k % 9, zi(2), x, pl.ds(96, 32)], b5.at[s, 1], peer(-1, 0))]
    def copies6(k):
        s = k % 4
        return [rc(k, 12, q.at[k % 9, z, xi(1), pl.ds(0, 64)], a6.at[s, 0], peer(0, 1)),
                rc(k, 13, q.at[k % 9, z, xi(-1), pl.ds(0, 64)], a6.at[s, 1], peer(0, -1)),
                rc(k, 14, q.at[k % 9, zi(1), x, pl.ds(64, 64)], b6.at[s, 0], peer(1, 0)),
                rc(k, 15, q.at[k % 9, zi(-1), x, pl.ds(64, 64)], b6.at[s, 1], peer(-1, 0))]
    def add(k, i, j, rows, *terms):
        t = q[k % 9, i, j, rows].astype(f32)
        for s in terms:
            t = t + s.astype(f32)
        q[k % 9, i, j, rows] = t.astype(low)

    def compute(k):
        cols = pl.ds(pl.multiple_of((k // 2) * 256, 256), 256)
        def piece(cc, put):
            def rows(lanes): return acts[:, :, cc, :, lanes].reshape(2048, -1)
            @pl.when(k == 0)
            def _(): act_load(cc).wait()
            @pl.when(k % 2 == 0)
            def _():
                put(jnp.dot(rows(slice(0, wide)), down_ref[:, cols], preferred_element_type=f32))
            @pl.when(k % 2 == 1)
            def _():
                put(lax.dot_general(rows(slice(wide, 2048)), w_ref[cols, :], (((1,), (1,)), ((), ())),
                                    preferred_element_type=f32))
        def put_stage(r):
            stage[k % 2] = r.astype(low).reshape(4, 4, 128, 256)
        def put_own(r):
            q[k % 9] = r.astype(low).reshape(4, 4, 128, 256)
        @pl.when(k == 0)
        def _(): down_load.wait()
        @pl.when(k == 1)
        def _():
            for cp in w_loads: cp.wait()
        piece(1 - c, put_stage)
        for cp in sibs(k): cp.start()
        piece(c, put_own)

    def weight_part(k):
        @pl.when(k % 2 == 0)
        def _():
            for cp in x_load(0, k): cp.wait()
            for cp in u_load(k // 2, k + 1): cp.start()
        @pl.when(k % 2 == 1)
        def _():
            for cp in u_load(0, k): cp.wait()
        @pl.when((k + 1 < nk) & (k % 2 == 1))
        def _():
            for cp in x_load(k // 2 + 1, k + 1): cp.start()
        slot = (k // 2) % 3
        def make(lanes):
            return lax.dot_general(xu[k % 2].reshape(4096, 256), acts[:, :, :, :, lanes].reshape(4096, -1),
                                   (((0,), (0,)), ((), ())), preferred_element_type=f32)
        @pl.when(k % 2 == 0)
        def _():
            acc[...] = make(slice(wide, 2048))
            dwb[slot, :, :, 0 : 2 * wide] = acc[:, 0 : 2 * wide].astype(low).reshape(4, 64, 2 * wide)
            router_out[pl.ds(pl.multiple_of((k // 2) * 256, 256), 256), :] = acc[:, 2 * wide :]
        @pl.when(k % 2 == 1)
        def _():
            acc[:, 0:wide] = make(slice(0, wide))
            dwb[slot, :, :, 2 * wide :] = acc[:, 0:wide].astype(low).reshape(4, 64, wide)

    def yrc(j, n, src, dst, to):
        return pltpu.make_async_remote_copy(src_ref=src, dst_ref=dst, send_sem=ysend.at[j, n], recv_sem=yrecv.at[j, n],
                                            device_id=to, device_id_type=MESH)
    def ycopies1(j):
        s = j % 3
        return [yrc(j, 0, dwb.at[s, yi(2), pl.ds(0, 32)], ya.at[j % 4, 0], ypeer(1)),
                yrc(j, 1, dwb.at[s, yi(2), pl.ds(32, 32)], ya.at[j % 4, 1], ypeer(-1))]
    def ycopies2(j):
        s = j % 3
        return [yrc(j, 2, dwb.at[s, yi(1)], yb.at[j % 4, 0], ypeer(1)),
                yrc(j, 3, dwb.at[s, yi(-1)], yb.at[j % 4, 1], ypeer(-1))]
    def ystage1(j):
        for cp in ycopies1(j): cp.start()
    def ystage2(j):
        for cp in ycopies1(j): cp.wait_recv()
        s = j % 3
        for d, r, m in ((1, 0, 0), (-1, 32, 1)):
            dwb[s, yi(d), pl.ds(r, 32)] = (dwb[s, yi(d), pl.ds(r, 32)].astype(f32) + ya[j % 4, m].astype(f32)).astype(low)
        for cp in ycopies2(j): cp.start()
    def ystage3(j):
        for cp in ycopies2(j): cp.wait_recv()
        dw_out[j] = (dwb[j % 3, y].astype(f32) + yb[j % 4, 0].astype(f32) + yb[j % 4, 1].astype(f32)).astype(low)
        for cp in ycopies1(j) + ycopies2(j): cp.wait_send()

    def stage2(k):
        for cp in sibs(k): cp.wait()
        def body(n, _):
            add(k, n // 4, n % 4, pl.ds(0, 128), sib[k % 2, n // 4, n % 4])
            return 0
        lax.fori_loop(0, 16, body, 0)
        for cp in copies3(k): cp.start()
    def stage4(k):
        for cp in copies3(k): cp.wait_recv()
        s = k % 4
        def body(n, _):
            add(k, zi(1), n, pl.ds(0, 32), a3[s, 0, n])
            add(k, zi(-1), n, pl.ds(32, 32), a3[s, 1, n])
            add(k, n, xi(1), pl.ds(64, 32), b3[s, 0, n])
            add(k, n, xi(-1), pl.ds(96, 32), b3[s, 1, n])
            return 0
        lax.fori_loop(0, 4, body, 0)
        for cp in copies4(k): cp.start()
    def stage5(k):
        for cp in copies4(k): cp.wait_recv()
        s = k % 4
        def body(n, _):
            add(k, z, n, pl.ds(0, 64), a4[s, 0, n], a4[s, 1, n])
            add(k, n, x, pl.ds(64, 64), b4[s, 0, n], b4[s, 1, n])
            return 0
        lax.fori_loop(0, 4, body, 0)
        for cp in copies5(k): cp.start()
    def stage6(k):
        for cp in copies5(k): cp.wait_recv()
        s = k % 4
        add(k, z, xi(1), pl.ds(0, 32), a5[s, 0])
        add(k, z, xi(-1), pl.ds(32, 32), a5[s, 1])
        add(k, zi(1), x, pl.ds(64, 32), b5[s, 0])
        add(k, zi(-1), x, pl.ds(96, 32), b5[s, 1])
        for cp in copies6(k): cp.start()
    def stage7(k):
        for cp in copies6(k): cp.wait_recv()
        s = k % 4
        for h, m in ((0, a6), (64, b6)):
            t = q[k % 9, z, x, pl.ds(h, 64)].astype(f32) + m[s, 0].astype(f32) + m[s, 1].astype(f32)
            out[k % 2, pl.ds(h, 64), pl.ds(pl.multiple_of((k // 2) * 256, 256), 256)] = t
        for cp in copies3(k) + copies4(k) + copies5(k) + copies6(k): cp.wait_send()

    def step(i, _):
        for lag, st in ((8, stage7), (7, stage6), (5, stage5), (3, stage4), (1, stage2)):
            k = i - lag
            @pl.when((k >= 0) & (k < nk))
            def _():
                st(k)
        for lag, st in ((5, ystage3), (3, ystage2)):
            k = i - lag
            @pl.when((k >= 0) & (k < nk) & (k % 2 == 0))
            def _():
                st(k // 2)
        @pl.when(i < nk)
        def _():
            compute(i)
            weight_part(i)
            @pl.when(i % 2 == 1)
            def _():
                ystage1(i // 2)
        return 0
    lax.fori_loop(0, nk + 8, step, 0)


def expert_back(acts, x, u, gate, up, router, down, cid):
    bf = jnp.bfloat16
    V = pltpu.VMEM
    nk = 12
    D = pltpu.SemaphoreType.DMA
    vm = pl.BlockSpec(memory_space=pltpu.VMEM)
    anym = pl.BlockSpec(memory_space=pl.ANY)
    return pl.pallas_call(
        expert_back_kernel,
        out_shape=(jax.ShapeDtypeStruct((2, 128, 1536), jnp.float32),
                   jax.ShapeDtypeStruct((6, 64, 1920), bf),
                   jax.ShapeDtypeStruct((1536, 128), jnp.float32)),
        in_specs=[anym] * 7,
        out_specs=(vm, vm, vm),
        scratch_shapes=[V((1536, 1408), bf), V((640, 1536), bf), V((4, 4, 2, 128, 2048), bf), V((2, 4, 4, 128, 256), bf), V((9, 4, 4, 128, 256), bf), V((2, 4, 4, 128, 256), bf),
                        V((4, 2, 4, 32, 256), bf), V((4, 2, 4, 32, 256), bf),
                        V((4, 2, 4, 64, 256), bf), V((4, 2, 4, 64, 256), bf),
                        V((4, 2, 32, 256), bf), V((4, 2, 32, 256), bf),
                        V((4, 2, 64, 256), bf), V((4, 2, 64, 256), bf),
                        V((2, 4, 4, 2, 128, 256), bf), V((256, 1408), jnp.float32), V((3, 4, 64, 1920), bf),
                        V((4, 2, 32, 1920), bf), V((4, 2, 64, 1920), bf),
                        D((11,)), D(()), D((2,)), D((2, 2)), D((nk,)), D((nk,)), D((nk, 16)), D((nk, 16)), D((6, 4)), D((6, 4))],
        compiler_params=pltpu.CompilerParams(collective_id=cid, has_side_effects=True, vmem_limit_bytes=63 << 20),
        name="expert_back",
    )(acts, x, u, gate, up, router, down)


def shards(
    tokens,
    documents,
    expert_routes,
    attention_gain,
    query_weight,
    key_matrix,
    value_matrix,
    output_weight,
    expert_gain,
    router_weight,
    gate_weight,
    up_weight,
    down_weight,
    out_cotangent,
):
    width = tokens.shape[1]
    local_experts = gate_weight.shape[0]
    experts_all = router_weight.shape[1]
    wide = local_experts * gate_weight.shape[2]
    inputs = tokens.astype(jnp.float32)
    first_gain = attention_gain.astype(jnp.float32)
    second_gain = expert_gain.astype(jnp.float32)
    first_scale = lax.rsqrt(jnp.mean(inputs * inputs, -1, keepdims=True) + epsilon)
    tables = attention_tables(documents)
    attention_weights = (query_weight, key_matrix, value_matrix, output_weight)
    router_pad = jnp.pad(router_weight, ((0, 0), (0, 64 - experts_all)))
    expert_weights = (
        gate_weight,
        up_weight,
        jnp.concatenate([router_pad, router_pad], 1),
        down_weight.reshape(wide, width),
    )
    lined_routes = jnp.pad(expert_routes, ((0, 0), (0, 128 - expert_routes.shape[1])))
    (
        residual,
        plane_rows,
        acts,
        plane_upstream,
        group_tokens,
        group_rows,
        queries,
        keys,
        values,
        attended,
        logsum,
    ) = front(
        tokens,
        jnp.concatenate([out_cotangent, lined_routes.astype(jnp.bfloat16)], 1),
        first_gain.reshape(1, width),
        second_gain.reshape(1, width),
        *tables,
        *attention_weights,
        *expert_weights,
        6,
    )
    experts_index = jnp.arange(experts_all, dtype=jnp.int32)
    second_normed, second_scale = normalize(residual, second_gain)
    second_low = second_normed.astype(jnp.bfloat16)
    def dense_gates(rows, routes):
        named = jnp.any(routes[:, :, None] == experts_index[None, None, :], 1)
        logits = jnp.dot(rows, router_weight, preferred_element_type=jnp.float32)
        logits = jnp.where(named, logits, -1e30)
        raised = jnp.exp(logits - jnp.max(logits, -1, keepdims=True))
        return raised / jnp.sum(raised, -1, keepdims=True)

    sums, weight_grads, router_pairs = expert_back(
        acts, plane_rows, plane_upstream, *expert_weights, 2
    )
    mixture, route_rows = sums[0], sums[1]
    layer_output = (residual + mixture).astype(jnp.bfloat16)
    router_pairs = router_pairs[:, :experts_all] + router_pairs[:, 64 : 64 + experts_all]
    weight_grads = lax.all_gather(weight_grads, "dp", axis=0)
    gates = dense_gates(second_low, expert_routes)
    upstream = out_cotangent.astype(jnp.float32)
    shared = gates * jnp.sum(mixture * upstream, -1, keepdims=True)
    router_local = -jnp.einsum(
        "td,te->de",
        second_low.astype(jnp.float32),
        shared,
        precision=highest,
        preferred_element_type=jnp.float32,
    ) + router_pairs
    normed_back = route_rows - jnp.einsum(
        "te,de->td",
        shared,
        router_weight.astype(jnp.float32),
        precision=highest,
        preferred_element_type=jnp.float32,
    )
    residual_back, expert_gain_local = norm_back(residual, second_scale, second_gain, normed_back)
    residual_grad = upstream + residual_back
    group_grad = ring_gather(residual_grad.astype(jnp.bfloat16), 7)
    small = jnp.concatenate(
        [
            router_local,
            jnp.zeros((width, 1), jnp.float32),
            expert_gain_local[:, None],
            jnp.zeros((width, 126 - experts_all), jnp.float32),
        ],
        1,
    )
    grads, normed_part = attention_back(
        group_grad,
        group_rows,
        group_tokens.reshape(-1, width),
        *tables,
        queries,
        keys,
        values,
        attended,
        logsum,
        small,
        *attention_weights,
    )
    grads, normed_grad = grad_sum(grads, normed_part, 4)
    input_back, _ = norm_back(inputs, first_scale, first_gain, normed_grad)
    input_gradient = residual_grad + input_back
    (
        gate_gradient,
        up_gradient,
        down_gradient,
        query_gradient,
        key_gradient,
        value_gradient,
        output_gradient,
        router_gradient,
        gains,
    ) = finish(weight_grads, grads)
    attention_gain_gradient = gains[0]
    expert_gain_gradient = gains[1]
    return (
        layer_output,
        input_gradient,
        attention_gain_gradient,
        query_gradient,
        key_gradient,
        value_gradient,
        output_gradient,
        expert_gain_gradient,
        router_gradient,
        gate_gradient,
        up_gradient,
        down_gradient,
    )


def solution(mesh):
    placed = (
        P(("dp", "expert", "tensor"), None),
        P(("dp", "expert")),
        P(("dp", "expert", "tensor"), None),
        P(),
        P(None, "tensor"),
        P(None, "tensor"),
        P(None, "tensor"),
        P("tensor", None),
        P(),
        P(),
        P("expert", None, "tensor"),
        P("expert", None, "tensor"),
        P("expert", "tensor", None),
        P(("dp", "expert", "tensor"), None),
    )
    return jax.shard_map(
        shards,
        mesh=mesh,
        in_specs=placed,
        out_specs=(
            P(("dp", "expert", "tensor"), None),
            P(("dp", "expert", "tensor"), None),
            P(),
            P(None, "tensor"),
            P(None, "tensor"),
            P(None, "tensor"),
            P("tensor", None),
            P(),
            P(),
            P("expert", None, "tensor"),
            P("expert", None, "tensor"),
            P("expert", "tensor", None),
        ),
        check_vma=False,
    )
```

```python
import functools

import jax
import jax.numpy as jnp
from jax import lax
from jax.experimental import pallas as pl
from jax.experimental.pallas import tpu as pltpu
from jax.sharding import PartitionSpec as P


epsilon = 1e-06
highest = lax.Precision.HIGHEST


def normalize(value_rows, gain):
    scale = lax.rsqrt(jnp.mean(value_rows * value_rows, -1, keepdims=True) + epsilon)
    return (value_rows * scale * gain, scale)


def norm_back(value_rows, scale, gain, upstream):
    weighted = upstream * gain
    inner = jnp.mean(weighted * value_rows, -1, keepdims=True)
    result = scale * weighted - value_rows * scale**3 * inner
    gain_part = jnp.sum(upstream * value_rows * scale, 0)
    return (result, gain_part)


MESH = pl.DeviceIdType.MESH

NT = (((1,), (1,)), ((), ()))
TN = (((0,), (0,)), ((), ()))


def turn(v, cosine, sine):
    lane = lax.broadcasted_iota(jnp.int32, v.shape, 1)
    count = v.shape[1]
    partner = jnp.where(lane % 64 < 32, pltpu.roll(v, count - 32, 1), pltpu.roll(v, 32, 1))
    times = count // 128
    return v * jnp.concatenate([cosine] * times, 1) + partner * jnp.concatenate([sine] * times, 1)


def attend(group, gain, cosine, sine, bias, wq, wk, wv, wo, rows_ref, q_ref, k_ref, v_ref, mixed_ref, logsum_ref, part_ref):
    f32, low = jnp.float32, jnp.bfloat16
    t = group[...].reshape(512, 1536).astype(f32)
    scale = lax.rsqrt(jnp.mean(t * t, -1, keepdims=True) + epsilon)
    rows_ref[...] = (t * scale * gain[...]).astype(low)
    rows = rows_ref[...]
    cos, sin = cosine[...], sine[...]
    q_ref[...] = (turn(jnp.dot(rows, wq[...], preferred_element_type=f32), cos, sin) * 0.125).astype(low)
    k_ref[...] = turn(jnp.dot(rows, wk[...], preferred_element_type=f32), cos, sin).astype(low)
    v_ref[...] = jnp.dot(rows, wv[...], preferred_element_type=f32).astype(low)
    lane = lax.broadcasted_iota(jnp.int32, (512, 128), 1)
    logsum = jnp.zeros((512, 128), f32)
    for h in range(6):
        kv = slice(64 * (h // 3), 64 * (h // 3) + 64)
        s = lax.dot_general(q_ref[:, 64 * h : 64 * h + 64], k_ref[:, kv], NT, preferred_element_type=f32) + bias[...]
        top = jnp.max(s, -1, keepdims=True)
        p = jnp.exp(s - top)
        total = jnp.sum(p, -1, keepdims=True)
        mixed = jnp.dot(p.astype(low), v_ref[:, kv], preferred_element_type=f32) / total
        mixed_ref[:, 64 * h : 64 * h + 64] = mixed.astype(low)
        logsum = jnp.where(lane == h, top + jnp.log(total), logsum)
    logsum_ref[...] = logsum
    part_ref[...] = jnp.dot(mixed_ref[...], wo[...], preferred_element_type=f32).astype(low).reshape(4, 128, 1536)


def weight_loads(gate, up, router, w, sem):
    return (
        [pltpu.make_async_copy(gate.at[n], w.at[:, pl.ds(128 * n, 128)], sem.at[n]) for n in range(5)]
        + [pltpu.make_async_copy(up.at[n], w.at[:, pl.ds(640 + 128 * n, 128)], sem.at[5 + n]) for n in range(5)]
        + [pltpu.make_async_copy(router, w.at[:, pl.ds(1280, 128)], sem.at[10])]
    )


PAIRS = ((0, 0), (1, 0), (3, 0), (0, 1), (0, 3), (2, 0), (0, 2), (1, 1), (1, 3), (3, 1), (3, 3), (2, 1), (2, 3), (1, 2), (3, 2), (2, 2))


class PlaneGather:
    def __init__(self, place, own, peer, sibling, core, send_sem, recv_sem, sib_send, sib_recv, starts, by_columns=False):
        self.starts, self.by_columns = starts, by_columns
        self.place, self.own, self.peer, self.sibling, self.core = place, own, peer, sibling, core
        self.send_sem, self.recv_sem, self.sib_send, self.sib_recv = send_sem, recv_sem, sib_send, sib_recv
        self.later = []

    def copy(self, dx, dz, ox, oz, q, nq, n, own):
        quarter = pl.ds(self.starts[q], self.starts[q + nq] - self.starts[q])
        quarter = (slice(None), quarter) if self.by_columns else quarter
        there = self.place(dx, dz, self.core).at[quarter]
        return pltpu.make_async_remote_copy(
            src_ref=self.own.at[quarter] if own and self.own is not None else there, dst_ref=there,
            send_sem=self.send_sem.at[n], recv_sem=self.recv_sem.at[(dx - ox) % 4, (dz - oz) % 4, q],
            device_id=self.peer(ox, oz), device_id_type=MESH)

    def send(self, dx, dz, ox, oz, q, nq, own=False):
        if self.starts[q] == self.starts[q + nq]:
            return
        make = functools.partial(self.copy, dx, dz, ox, oz, q, nq, len(self.later), own)
        make().start()
        self.later.append(make)

    def recv(self, dx, dz, q, nq):
        if self.starts[q] == self.starts[q + nq]:
            return
        self.copy(dx, dz, 0, 0, q, nq, 0, False).wait_recv()

    def sib_copy(self, core, dx, dz, own=False):
        there = self.place(dx, dz, core)
        return pltpu.make_async_remote_copy(
            src_ref=self.own if own else there, dst_ref=there,
            send_sem=self.sib_send.at[dx % 4, dz % 4], recv_sem=self.sib_recv.at[dx % 4, dz % 4],
            device_id=self.sibling, device_id_type=MESH)

    def sib_pass(self, dx, dz, own=False):
        make = functools.partial(self.sib_copy, self.core, dx, dz, own)
        make().start()
        self.later.append(make)

    def start(self, directions):
        for ox, oz in directions:
            self.send(0, 0, ox, oz, 0, 4, own=True)

    def wave1x(self):
        for s in (1, -1):
            self.recv(s, 0, 0, 4)
            if s == -1:
                self.send(s, 0, 1, 0, 1, 2)
            else:
                self.send(s, 0, -1, 0, 0, 1)
                self.send(s, 0, -1, 0, 3, 1)
            for oz in (1, -1):
                self.send(s, 0, 0, oz, 0, 2)
            self.sib_pass(s, 0)

    def wave1z(self):
        for s in (1, -1):
            self.recv(0, s, 0, 4)
            if s == -1:
                self.send(0, s, 0, 1, 1, 2)
            else:
                self.send(0, s, 0, -1, 0, 1)
                self.send(0, s, 0, -1, 3, 1)
            for ox in (1, -1):
                self.send(0, s, ox, 0, 2, 2)
            self.sib_pass(0, s)

    def wave1(self):
        self.wave1x()
        self.wave1z()

    def wave2(self):
        for q, nq in ((1, 2), (0, 1), (3, 1)):
            self.recv(2, 0, q, nq)
        for oz in (1, -1):
            self.send(2, 0, 0, oz, 0, 2)
        for q, nq in ((1, 2), (0, 1), (3, 1)):
            self.recv(0, 2, q, nq)
        for ox in (1, -1):
            self.send(0, 2, ox, 0, 2, 2)
        self.sib_pass(2, 0)
        self.sib_pass(0, 2)
        for dx in (1, -1):
            for s in (1, -1):
                self.recv(dx, s, 0, 2)
                self.send(dx, s, 0, -s, 0 if s == 1 else 1, 1)
                self.recv(s, dx, 2, 2)
                self.send(s, dx, -s, 0, 2 if s == 1 else 3, 1)
        for dx in (1, -1):
            for dz in (1, -1):
                self.sib_pass(dx, dz)

    def wave3(self):
        for s in (1, -1):
            self.recv(2, s, 0, 2)
            self.send(2, s, 0, -s, 0 if s == 1 else 1, 1)
            self.recv(s, 2, 2, 2)
            self.send(s, 2, -s, 0, 2 if s == 1 else 3, 1)
        for d in (1, -1):
            for q in (0, 1):
                self.recv(d, 2, q, 1)
                self.recv(2, d, q + 2, 1)
        for d in (1, -1):
            self.sib_pass(d, 2)
            self.sib_pass(2, d)

    def wave4(self):
        for q in range(4):
            self.recv(2, 2, q, 1)
        self.sib_pass(2, 2)

    def finish(self):
        for make in self.later:
            make().wait_send()


def front_kernel(tokens, u_own, first_gain, second_gain, cosine, sine, bias, wq, wk, wv, wo, gate_hbm, up_hbm, router_hbm, down_hbm,
                 residual, rows_out, acts_out, u_hbm, group, normed, queries, keys, values, mixed, logsum,
                 part, nr1, nb, nr2, rows, w, down, u_buf, act_buf,
                 gsend, grecv, own_sem, nsend, nrecv, send_sem, recv_sem, sib_send, sib_recv,
                 u_send, u_recv, u_sib_send, u_sib_recv, w_sem, down_sem, u_sem, act_sem, out_sem):
    f32, low = jnp.float32, jnp.bfloat16
    wide = 640
    width = 1536
    x = lax.axis_index("tensor"); e = lax.axis_index("expert")
    z = e // 2; c = e % 2
    first = e * 5
    def xi(d): return (x + d) % 4
    def zi(d): return (z + d) % 4
    def peer(ox, oz):
        return {"expert": zi(oz) * 2 + c, "tensor": xi(ox)}
    sib = {"expert": z * 2 + 1 - c}
    def pair(step):
        if isinstance(step, int):
            return PAIRS[step]
        dx = dz = 0
        for n in range(4):
            here = lax.convert_element_type(step // 4 == n, jnp.int32)
            dx = dx + here * sum(PAIRS[4 * n + m][0] * 4**m for m in range(4))
            dz = dz + here * sum(PAIRS[4 * n + m][1] * 4**m for m in range(4))
        for n in range(3):
            more = lax.convert_element_type(step % 4 > n, jnp.int32)
            dx = dx // (1 + 3 * more)
            dz = dz // (1 + 3 * more)
        dx, dz = dx % 4, dz % 4
        return dx, dz
    def u_loads(step):
        dx, dz = pair(step)
        return pltpu.make_async_copy(u_hbm.at[zi(dz), xi(dx)], u_buf.at[step % 2], u_sem.at[step % 2])
    loads = weight_loads(gate_hbm, up_hbm, router_hbm, w, w_sem) + [pltpu.make_async_copy(down_hbm, down, down_sem)]
    for cp in loads: cp.start()
    barrier = pltpu.get_barrier_semaphore()
    near = [peer(1, 0), peer(-1, 0), peer(0, 1), peer(0, -1), sib]
    for p in near:
        pl.semaphore_signal(barrier, inc=1, device_id=p, device_id_type=MESH)
    pl.semaphore_wait(barrier, len(near))
    pend = []
    def go(cps):
        for cp in cps: cp.start()
        pend.extend(cps)
        return cps
    def block_of(ref):
        return lambda dx, dz, core: ref.at[zi(dz), xi(dx), core]
    cots = PlaneGather(block_of(u_hbm), u_own, peer, sib, c, u_send, u_recv, u_sib_send, u_sib_recv, (0, 48, 96, 112, 128))
    norms = PlaneGather(block_of(rows), rows.at[z, x, c], peer, sib, c, send_sem, recv_sem, sib_send, sib_recv, (0, 16, 32, 80, 128))
    def tok(n, block, half, to, own):
        there = group.at[block, pl.ds(64 * half, 64)]
        return pltpu.make_async_remote_copy(
            src_ref=tokens.at[pl.ds(64 * half, 64)] if own else there, dst_ref=there,
            send_sem=gsend.at[n], recv_sem=grecv.at[n], device_id=peer(to, 0), device_id_type=MESH)
    go([tok(0, x, 0, 1, True), tok(2, x, 1, -1, True)])
    go([tok(1, x, 1, 1, True), tok(3, x, 0, -1, True)])
    mine = pltpu.make_async_copy(u_own, u_hbm.at[z, x, c], own_sem)
    mine.start()
    cots.start(((0, 1), (0, -1)))
    group[x] = tokens[...]
    tok(0, xi(-1), 0, 1, False).wait_recv()
    go([tok(4, xi(-1), 0, 1, False)])
    tok(2, xi(1), 1, -1, False).wait_recv()
    go([tok(5, xi(1), 1, -1, False)])
    cots.start(((1, 0), (-1, 0)))
    cots.sib_pass(0, 0, own=True)
    tok(1, xi(-1), 1, 1, False).wait_recv()
    tok(3, xi(1), 0, -1, False).wait_recv()
    tok(4, xi(2), 0, 1, False).wait_recv()
    tok(5, xi(2), 1, -1, False).wait_recv()
    attend(group, first_gain, cosine, sine, bias, wq, wk, wv, wo, normed, queries, keys, values, mixed, logsum, part)
    def nrc(n, src, dst, to):
        return pltpu.make_async_remote_copy(src_ref=src, dst_ref=dst, send_sem=nsend.at[n], recv_sem=nrecv.at[n],
                                            device_id=peer(to, 0), device_id_type=MESH)
    n1 = go([nrc(0, part.at[xi(2), pl.ds(0, 64)], nr1.at[0], 1), nrc(1, part.at[xi(2), pl.ds(64, 64)], nr1.at[1], -1)])
    n2 = go([nrc(2, part.at[xi(1), pl.ds(64, 64)], nr2.at[0, pl.ds(64, 64)], 1),
             nrc(3, part.at[xi(-1), pl.ds(0, 64)], nr2.at[1, pl.ds(0, 64)], -1)])
    cots.wave1()
    mine.wait()
    cots.sib_copy(1 - c, 0, 0).wait_recv()
    u_loads(0).start()
    n1[0].wait_recv()
    nb[0] = (part[xi(1), 0:64].astype(f32) + nr1[0].astype(f32)).astype(low)
    n3 = go([nrc(4, nb.at[0], nr2.at[0, pl.ds(0, 64)], 1)])
    n1[1].wait_recv()
    nb[1] = (part[xi(-1), 64:128].astype(f32) + nr1[1].astype(f32)).astype(low)
    n3 += go([nrc(5, nb.at[1], nr2.at[1, pl.ds(64, 64)], -1)])
    for cp in n2 + n3: cp.wait_recv()
    total = tokens[...].astype(f32) + part[x].astype(f32) + nr2[0].astype(f32) + nr2[1].astype(f32)
    residual[...] = total
    scale = lax.rsqrt(jnp.mean(total * total, -1, keepdims=True) + epsilon)
    rows[z, x, c] = (total * scale * second_gain[...]).astype(low)
    norms.start(((1, 0), (-1, 0), (0, 1), (0, -1)))
    norms.sib_pass(0, 0, own=True)
    for cp in loads: cp.wait()

    def act_store(step):
        dx, dz = pair(step)
        return pltpu.make_async_copy(act_buf.at[step % 2], acts_out.at[zi(dz), xi(dx)].reshape(256, 2048), act_sem.at[step % 2])
    def row_store(step):
        dx, dz = pair(step)
        there = (zi(dz), xi(dx))
        return pltpu.make_async_copy(rows.at[there], rows_out.at[there], out_sem.at[step])
    def compute(step):
        dx, dz = pair(step)
        norms.sib_copy(1 - c, dx, dz).wait_recv()
        u_loads(step).wait()
        @pl.when(step < 15)
        def _():
            nx, nz = pair(step + 1)
            cots.sib_copy(1 - c, nx, nz).wait_recv()
            u_loads(step + 1).start()
        row_store(step).start()
        @pl.when(step >= 2)
        def _(): act_store(step - 2).wait()
        slot = step % 2
        here = act_buf.at[slot]
        pre = jnp.dot(rows[zi(dz), xi(dx)].reshape(256, width), w[...], preferred_element_type=f32)
        raw = lax.dot_general(u_buf[slot, :, :, 0:width].reshape(256, width), down[...], (((1,), (1,)), ((), ())), preferred_element_type=f32)
        lane = lax.broadcasted_iota(jnp.int32, (256, 128), 1)
        routes = u_buf[slot, :, :, width:].reshape(256, 128).astype(f32).astype(jnp.int32)
        named = lane == routes[:, 0:1]
        for n in range(1, 8):
            named = named | (lane == routes[:, n : n + 1])
        logits = jnp.where(named, pre[:, 2 * wide :], -1e30)
        raised = jnp.exp(logits - jnp.max(logits, -1, keepdims=True))
        gates = raised / jnp.sum(raised, -1, keepdims=True)
        weighted = jnp.zeros((256, 128), f32)
        for n in range(5):
            cols = slice(128 * n, 128 * (n + 1))
            gate = jnp.sum(jnp.where(lane == first + n, gates, 0.0), -1, keepdims=True)
            gate_pre = pre[:, cols]
            up_pre = pre[:, wide + 128 * n : wide + 128 * (n + 1)]
            sig = jax.nn.sigmoid(gate_pre)
            silu = gate_pre * sig
            active = silu * up_pre
            back = raw[:, cols]
            share = gate * jnp.sum(active * back, -1, keepdims=True)
            high = share.astype(low).astype(f32)
            weighted = weighted + jnp.where(lane == first + n, high, 0.0)
            weighted = weighted + jnp.where(lane == first + n + 64, share - high, 0.0)
            back = gate * back
            here[:, cols] = (gate * active).astype(low)
            here[:, wide + 128 * n : wide + 128 * (n + 1)] = (
                back * up_pre * (sig * (1.0 + gate_pre * (1.0 - sig)))
            ).astype(low)
            here[:, 2 * wide + 128 * n : 2 * wide + 128 * (n + 1)] = (back * silu).astype(low)
        here[:, 3 * wide :] = weighted.astype(low)
        act_store(step).start()

    events = ((0, cots.wave2), (1, norms.wave1), (3, cots.wave3), (5, norms.wave2), (7, cots.wave4), (9, norms.wave3), (13, norms.wave4))
    def body(step, _):
        for at, wave in events:
            @pl.when(step == at)
            def _():
                wave()
        compute(step)
        return 0
    lax.fori_loop(0, 16, body, 0)
    act_store(14).wait()
    act_store(15).wait()
    for n in range(16): row_store(n).wait()
    for cp in pend: cp.wait_send()
    cots.finish()
    norms.finish()


def front(tokens, u, first_gain, second_gain, cosine, sine, bias, wq, wk, wv, wo, gate, up, router, down, cid):
    bf, f32 = jnp.bfloat16, jnp.float32
    V = pltpu.VMEM
    D = pltpu.SemaphoreType.DMA
    S = jax.ShapeDtypeStruct
    vm = pl.BlockSpec(memory_space=pltpu.VMEM)
    anym = pl.BlockSpec(memory_space=pl.ANY)
    n, width = tokens.shape
    return pl.pallas_call(
        front_kernel,
        out_shape=(S((n, width), f32), S((4, 4, 2, n, width), bf), S((4, 4, 2, n, 2048), bf), S((4, 4, 2, n, 1664), bf),
                   S((4, n, width), bf), S((512, width), bf), S((512, 384), bf), S((512, 128), bf), S((512, 128), bf),
                   S((512, 384), bf), S((512, 128), f32)),
        in_specs=[vm, anym] + [vm] * 9 + [anym] * 4,
        out_specs=(vm, anym, anym, anym) + (vm,) * 7,
        scratch_shapes=[V((4, n, width), bf), V((2, 64, width), bf), V((2, 64, width), bf), V((2, 128, width), bf),
                        V((4, 4, 2, n, width), bf), V((width, 1408), bf), V((640, width), bf),
                        V((2, 2, n, 1664), bf), V((2, 256, 2048), bf),
                        D((6,)), D((6,)), D(()), D((6,)), D((6,)), D((64,)), D((4, 4, 4)), D((4, 4)), D((4, 4)),
                        D((64,)), D((4, 4, 4)), D((4, 4)), D((4, 4)),
                        D((11,)), D(()), D((2,)), D((2,)), D((16,))],
        compiler_params=pltpu.CompilerParams(collective_id=cid, has_side_effects=True, vmem_limit_bytes=60 << 20),
        name="front",
    )(tokens, u, first_gain, second_gain, cosine, sine, bias, wq, wk, wv, wo, gate, up, router, down)


class TorusSum:
    def __init__(self, g, out, scratch, sems, starts, place, with_extra):
        self.with_extra = with_extra
        (self.q, self.sib, self.a3, self.a3b, self.b3, self.b3b, self.a4, self.b4,
         self.a5, self.a5b, self.b5, self.b5b, self.a6, self.b6, self.extra) = scratch
        self.ssem, self.rsem, gsend, grecv, gsib_send, gsib_recv = sems
        self.g, self.out = g, out
        self.z, self.y, self.c, self.zi, self.yi, self.peer, self.xpeer, self.partner = place
        self.parts = [pl.ds(starts[n], starts[n + 1] - starts[n]) for n in range(4)]
        self.A = pl.ds(0, starts[2])
        self.B = pl.ds(starts[2], starts[4] - starts[2])
        self.sent = []
        self.back = PlaneGather(
            lambda dy, dz, core: out.at[core, self.zi(dz), self.yi(dy)], None, lambda oy, oz: self.peer(oz, oy), self.partner, self.c,
            gsend, grecv, gsib_send, gsib_recv, starts, True)

    def rc(self, n, src, dst, to):
        return pltpu.make_async_remote_copy(src_ref=src, dst_ref=dst, send_sem=self.ssem.at[n], recv_sem=self.rsem.at[n],
                                            device_id=to, device_id_type=MESH)

    def go(self, cps):
        for cp in cps:
            cp.start()
        self.sent.extend(cps)
        return cps

    def add(self, i, j, cols, *terms):
        t = self.q[i, j, :, cols].astype(jnp.float32)
        for s in terms:
            t = t + s.astype(jnp.float32)
        self.q[i, j, :, cols] = t.astype(jnp.bfloat16)

    def stage1(self):
        self.c1 = self.go([self.rc(16, self.g.at[1 - self.c], self.sib, self.partner)])

    def stage2(self):
        q, zi, yi, peer = self.q, self.zi, self.yi, self.peer
        A0, A1, B0, B1 = self.parts
        self.c1[0].wait_recv()
        def body(n, _):
            i, j = n // 4, n % 4
            q[i, j] = (self.g[self.c, i, j].astype(jnp.float32) + self.sib[i, j].astype(jnp.float32)).astype(jnp.bfloat16)
            return 0
        lax.fori_loop(0, 16, body, 0)
        self.c3 = self.go([self.rc(0, q.at[zi(2), :, :, A0], self.a3, peer(1, 0)),
                           self.rc(1, q.at[zi(2), :, :, A1], self.a3b, peer(-1, 0)),
                           self.rc(2, q.at[:, yi(2), :, B0], self.b3, peer(0, 1)),
                           self.rc(3, q.at[:, yi(2), :, B1], self.b3b, peer(0, -1))])

    def stage4(self):
        q, zi, yi, peer, A, B = self.q, self.zi, self.yi, self.peer, self.A, self.B
        A0, A1, B0, B1 = self.parts
        for cp in self.c3: cp.wait_recv()
        def body(n, _):
            self.add(zi(1), n, A0, self.a3[n])
            self.add(zi(-1), n, A1, self.a3b[n])
            self.add(n, yi(1), B0, self.b3[n])
            self.add(n, yi(-1), B1, self.b3b[n])
            return 0
        lax.fori_loop(0, 4, body, 0)
        self.c4 = self.go([self.rc(4, q.at[zi(1), :, :, A], self.a4.at[0], peer(1, 0)),
                           self.rc(5, q.at[zi(-1), :, :, A], self.a4.at[1], peer(-1, 0)),
                           self.rc(6, q.at[:, yi(1), :, B], self.b4.at[0], peer(0, 1)),
                           self.rc(7, q.at[:, yi(-1), :, B], self.b4.at[1], peer(0, -1))])

    def stage5(self):
        q, z, y, zi, yi, peer = self.q, self.z, self.y, self.zi, self.yi, self.peer
        A0, A1, B0, B1 = self.parts
        for cp in self.c4: cp.wait_recv()
        def body(n, _):
            self.add(z, n, self.A, self.a4[0, n], self.a4[1, n])
            self.add(n, y, self.B, self.b4[0, n], self.b4[1, n])
            return 0
        lax.fori_loop(0, 4, body, 0)
        self.c5 = self.go([self.rc(8, q.at[z, yi(2), :, A0], self.a5, peer(0, 1)),
                           self.rc(9, q.at[z, yi(2), :, A1], self.a5b, peer(0, -1)),
                           self.rc(10, q.at[zi(2), y, :, B0], self.b5, peer(1, 0)),
                           self.rc(11, q.at[zi(2), y, :, B1], self.b5b, peer(-1, 0))])

    def stage6(self):
        q, z, y, zi, yi, peer, A, B = self.q, self.z, self.y, self.zi, self.yi, self.peer, self.A, self.B
        A0, A1, B0, B1 = self.parts
        for cp in self.c5: cp.wait_recv()
        self.add(z, yi(1), A0, self.a5[...])
        self.add(z, yi(-1), A1, self.a5b[...])
        self.add(zi(1), y, B0, self.b5[...])
        self.add(zi(-1), y, B1, self.b5b[...])
        self.c6 = self.go([self.rc(12, q.at[z, yi(1), :, A], self.a6.at[0], peer(0, 1)),
                           self.rc(13, q.at[z, yi(-1), :, A], self.a6.at[1], peer(0, -1)),
                           self.rc(14, q.at[zi(1), y, :, B], self.b6.at[0], peer(1, 0)),
                           self.rc(15, q.at[zi(-1), y, :, B], self.b6.at[1], peer(-1, 0))])

    def stage7(self):
        f32, low = jnp.float32, jnp.bfloat16
        q, z, y = self.q, self.z, self.y
        for cp in self.c6: cp.wait_recv()
        own = self.out.at[self.c, z, y]
        own[:, self.A] = (q[z, y, :, self.A].astype(f32) + self.a6[0].astype(f32) + self.a6[1].astype(f32)).astype(low)
        last = (q[z, y, :, self.B].astype(f32) + self.b6[0].astype(f32) + self.b6[1].astype(f32)).astype(low)
        wide = last.shape[1] - (128 if self.with_extra else 0)
        own[:, pl.ds(self.B.start, wide)] = last[:, 0:wide]
        if not self.with_extra:
            return
        self.extra[0] = last[:, wide:]
        self.cx = self.go([self.rc(16 + o, self.extra.at[0], self.extra.at[o], self.xpeer(o)) for o in (1, 2, 3)])

    def start_back(self):
        f32 = jnp.float32
        if self.with_extra:
            for cp in self.cx: cp.wait_recv()
            extra = self.extra
            total = extra[0].astype(f32) + extra[1].astype(f32) + extra[2].astype(f32) + extra[3].astype(f32)
            self.out[self.c, self.z, self.y, :, pl.ds(self.B.start + self.B.size - 128, 128)] = total.astype(jnp.bfloat16)
        self.back.start(((1, 0), (-1, 0), (0, 1), (0, -1)))
        self.back.sib_pass(0, 0)

    def finish(self):
        for dy in range(4):
            for dz in range(4):
                self.back.sib_copy(1 - self.c, dy, dz).wait_recv()
        for cp in self.sent: cp.wait_send()
        self.back.finish()


def sum_scratch(starts):
    V, bf = pltpu.VMEM, jnp.bfloat16
    w = [starts[n + 1] - starts[n] for n in range(4)]
    a, b = w[0] + w[1], w[2] + w[3]
    D = pltpu.SemaphoreType.DMA
    return ([V((4, 4, 48, a + b), bf)] * 2 + [V((4, 48, n), bf) for n in w] + [V((2, 4, 48, a), bf), V((2, 4, 48, b), bf)]
            + [V((48, n), bf) for n in w] + [V((2, 48, a), bf), V((2, 48, b), bf), V((4, 48, 128), bf)]
            + [D((20,)), D((20,)), D((64,)), D((4, 4, 4)), D((4, 4)), D((4, 4))])


OUTPUT_PARTS = (0, 128, 256, 384, 512)
INPUT_PARTS = (0, 256, 384, 512, 640)


def attention_back_kernel(branch, rows, group, cosine, sine, bias, q, k, v, mixed, logsum, extras, wq, wk, wv, wo, o_out, i_out, n_out,
                          grad, probs, back, turned_t, q_back, k_back, v_back, k_acc, v_acc, gsend, grecv):
    f32, low = jnp.float32, jnp.bfloat16
    x = lax.axis_index("tensor")
    def xi(d): return (x + d) % 4
    def xpeer(o):
        return {"tensor": xi(o)}
    barrier = pltpu.get_barrier_semaphore()
    for o in (1, -1):
        pl.semaphore_signal(barrier, inc=1, device_id=xpeer(o), device_id_type=MESH)
    pl.semaphore_wait(barrier, 2)
    sent = []
    def go(cps):
        for cp in cps: cp.start()
        sent.extend(cps)
        return cps
    def ring(n, block, part, to, own):
        there = grad.at[block, pl.ds(64 * part, 64)]
        return pltpu.make_async_remote_copy(
            src_ref=branch.at[pl.ds(64 * part, 64)] if own else there, dst_ref=there,
            send_sem=gsend.at[n], recv_sem=grecv.at[n], device_id=xpeer(to), device_id_type=MESH)
    go([ring(0, x, 0, 1, True), ring(2, x, 1, -1, True)])
    go([ring(1, x, 1, 1, True), ring(3, x, 0, -1, True)])
    grad[x] = branch[...]
    k_t = k[...].astype(f32).T.astype(low)
    logsum_t = logsum[...].T
    bias_t = bias[...].T
    def heads(h):
        one = slice(64 * h, 64 * h + 64)
        kv = slice(64 * (h // 3), 64 * (h // 3) + 64)
        s = lax.dot_general(k[:, kv], q[:, one], NT, preferred_element_type=f32) + bias_t
        probs[h] = jnp.exp(s - logsum_t[h : h + 1, :])
    for h in range(2): heads(h)
    ring(0, xi(-1), 0, 1, False).wait_recv()
    go([ring(4, xi(-1), 0, 1, False)])
    ring(2, xi(1), 1, -1, False).wait_recv()
    go([ring(5, xi(1), 1, -1, False)])
    for h in range(2, 6): heads(h)
    ring(1, xi(-1), 1, 1, False).wait_recv()
    ring(3, xi(1), 0, -1, False).wait_recv()
    ring(4, xi(2), 0, 1, False).wait_recv()
    ring(5, xi(2), 1, -1, False).wait_recv()

    all_grad = grad[...].reshape(512, 1536)
    o_out[:, 0:384] = lax.dot_general(all_grad, mixed[...], TN, preferred_element_type=f32).astype(low)
    back[...] = lax.dot_general(all_grad, wo[...], NT, preferred_element_type=f32).astype(low)
    for h in range(6):
        one = slice(64 * h, 64 * h + 64)
        kv = slice(64 * (h // 3), 64 * (h // 3) + 64)
        p = probs[h]
        grad_p = lax.dot_general(v[:, kv], back[:, one], NT, preferred_element_type=f32)
        both = p * grad_p
        inner = jnp.sum(both, 0, keepdims=True)
        grad_s = (both - p * inner).astype(low)
        v_part = jnp.dot(p.astype(low), back[:, one], preferred_element_type=f32)
        k_part = jnp.dot(grad_s, q[:, one], preferred_element_type=f32)
        if h % 3 == 0:
            v_acc[:, kv] = v_part
            k_acc[:, kv] = k_part
        else:
            v_acc[:, kv] += v_part
            k_acc[:, kv] += k_part
        turned_t[one, :] = jnp.dot(k_t[kv, :], grad_s, preferred_element_type=f32)
    cos, sin = cosine[...], -sine[...]
    q_back[...] = turn(turned_t[...].T * 0.125, cos, sin).astype(low)
    k_back[...] = turn(k_acc[...], cos, sin).astype(low)
    v_back[...] = v_acc[...].astype(low)
    part = (
        lax.dot_general(q_back[...], wq[...], NT, preferred_element_type=f32)
        + lax.dot_general(k_back[...], wk[...], NT, preferred_element_type=f32)
        + lax.dot_general(v_back[...], wv[...], NT, preferred_element_type=f32)
    )
    n_out[...] = part.astype(low)
    t = group[...].astype(f32)
    t = t * lax.rsqrt(jnp.mean(t * t, -1, keepdims=True) + epsilon)
    ones = jnp.ones((512, 128), low)
    gain_part = lax.dot_general((part * t).astype(low), ones, TN, preferred_element_type=f32)
    lane = lax.broadcasted_iota(jnp.int32, (1536, 128), 1)
    o_out[:, 384:512] = jnp.where(lane == 40, gain_part, extras[...]).astype(low)
    i_out[:, 0:384] = lax.dot_general(rows[...], q_back[...], TN, preferred_element_type=f32).astype(low)
    i_out[:, 384:512] = lax.dot_general(rows[...], k_back[...], TN, preferred_element_type=f32).astype(low)
    i_out[:, 512:640] = lax.dot_general(rows[...], v_back[...], TN, preferred_element_type=f32).astype(low)
    for cp in sent: cp.wait_send()


def attention_back(branch, rows, group, cosine, sine, bias, q, k, v, mixed, logsum, extras, wq, wk, wv, wo, cid):
    S = jax.ShapeDtypeStruct
    bf, f32 = jnp.bfloat16, jnp.float32
    V = pltpu.VMEM
    D = pltpu.SemaphoreType.DMA
    return pl.pallas_call(
        attention_back_kernel,
        out_shape=(S((1536, 512), bf), S((1536, 640), bf), S((512, 1536), bf)),
        scratch_shapes=[V((4, 128, 1536), bf), V((6, 512, 512), f32), V((512, 384), bf), V((384, 512), f32), V((512, 384), bf),
                        V((512, 128), bf), V((512, 128), bf), V((512, 128), f32), V((512, 128), f32), D((6,)), D((6,))],
        compiler_params=pltpu.CompilerParams(collective_id=cid, has_side_effects=True, vmem_limit_bytes=60 << 20),
        name="attention_back",
    )(branch, rows, group, cosine, sine, bias, q, k, v, mixed, logsum, extras, wq, wk, wv, wo)


def grad_sum_kernel(o_sum, i_sum, n_part, o_out, i_out, n_out, nr1, nb, nr2, nsend, nrecv, *scratch):
    f32, low = jnp.float32, jnp.bfloat16
    x = lax.axis_index("tensor"); e = lax.axis_index("expert"); y = lax.axis_index("dp")
    z = e // 2; c = e % 2
    def zi(d): return (z + d) % 4
    def yi(d): return (y + d) % 4
    def xi(d): return (x + d) % 4
    def peer(oz, oy):
        return {"expert": zi(oz) * 2 + c, "dp": yi(oy)}
    def xpeer(o):
        return {"tensor": xi(o)}
    partner = {"expert": z * 2 + 1 - c}
    barrier = pltpu.get_barrier_semaphore()
    near = [peer(1, 0), peer(-1, 0), peer(0, 1), peer(0, -1), partner, xpeer(1), xpeer(2), xpeer(3)]
    for p in near:
        pl.semaphore_signal(barrier, inc=1, device_id=p, device_id_type=MESH)
    pl.semaphore_wait(barrier, len(near))
    sent = []
    def go(cps):
        for cp in cps: cp.start()
        sent.extend(cps)
        return cps
    place = (z, y, c, zi, yi, peer, xpeer, partner)
    half = len(scratch) // 2
    osum = TorusSum(o_sum, o_out, scratch[:15], scratch[15:half], OUTPUT_PARTS, place, True)
    isum = TorusSum(i_sum, i_out, scratch[half : half + 15], scratch[half + 15 :], INPUT_PARTS, place, False)
    osum.stage1()
    def nrc(n, src, dst, to):
        return pltpu.make_async_remote_copy(src_ref=src, dst_ref=dst, send_sem=nsend.at[n], recv_sem=nrecv.at[n],
                                            device_id=xpeer(to), device_id_type=MESH)
    n1 = go([nrc(0, n_part.at[xi(2), pl.ds(0, 64)], nr1.at[0], 1), nrc(1, n_part.at[xi(2), pl.ds(64, 64)], nr1.at[1], -1)])
    n2 = go([nrc(2, n_part.at[xi(1), pl.ds(64, 64)], nr2.at[0, pl.ds(64, 64)], 1),
             nrc(3, n_part.at[xi(-1), pl.ds(0, 64)], nr2.at[1, pl.ds(0, 64)], -1)])
    isum.stage1()
    osum.stage2()
    isum.stage2()
    for cp in n1: cp.wait_recv()
    nb[0] = (n_part[xi(1), 0:64].astype(f32) + nr1[0].astype(f32)).astype(low)
    nb[1] = (n_part[xi(-1), 64:128].astype(f32) + nr1[1].astype(f32)).astype(low)
    n3 = go([nrc(4, nb.at[0], nr2.at[0, pl.ds(0, 64)], 1), nrc(5, nb.at[1], nr2.at[1, pl.ds(64, 64)], -1)])
    osum.stage4()
    isum.stage4()
    osum.stage5()
    isum.stage5()
    osum.stage6()
    isum.stage6()
    osum.stage7()
    isum.stage7()
    isum.start_back()
    osum.start_back()
    for cp in n2 + n3: cp.wait_recv()
    n_out[...] = n_part[x].astype(f32) + nr2[0].astype(f32) + nr2[1].astype(f32)
    isum.back.wave1()
    osum.back.wave1()
    isum.back.wave2()
    osum.back.wave2()
    isum.back.wave3()
    osum.back.wave3()
    isum.back.wave4()
    osum.back.wave4()
    isum.finish()
    osum.finish()
    for cp in sent: cp.wait_send()


def grad_sum(o_part, i_part, n_part, cid):
    S = jax.ShapeDtypeStruct
    bf, f32 = jnp.bfloat16, jnp.float32
    V = pltpu.VMEM
    D = pltpu.SemaphoreType.DMA
    vm = pl.BlockSpec(memory_space=pltpu.VMEM)
    o_sums, i_sums, row_sums = pl.pallas_call(
        grad_sum_kernel,
        out_shape=(S((2, 4, 4, 48, 512), bf), S((2, 4, 4, 48, 640), bf), S((128, 1536), f32)),
        in_specs=[vm] * 3,
        out_specs=(vm,) * 3,
        scratch_shapes=[V((2, 64, 1536), bf), V((2, 64, 1536), bf), V((2, 128, 1536), bf),
                        D((6,)), D((6,))] + sum_scratch(OUTPUT_PARTS) + sum_scratch(INPUT_PARTS),
        compiler_params=pltpu.CompilerParams(collective_id=cid, has_side_effects=True, vmem_limit_bytes=40 << 20),
        name="grad_sum",
    )(o_part.reshape(2, 4, 4, 48, 512), i_part.reshape(2, 4, 4, 48, 640), n_part.reshape(4, 128, 1536))
    return o_sums.reshape(1536, 512), i_sums.reshape(1536, 640), row_sums


def attention_tables(documents):
    index = jnp.arange(documents.shape[0], dtype=jnp.int32)
    positions = index - jnp.sum((documents[None, :] < documents[:, None]).astype(jnp.int32), 1)
    freq = 10000.0 ** (-(jnp.arange(32, dtype=jnp.float32) * 2.0 / 64))
    angle = positions.astype(jnp.float32)[:, None] * freq[None, :]
    cos, sin = jnp.cos(angle), jnp.sin(angle)
    allowed = (documents[:, None] == documents[None, :]) & (index[None, :] <= index[:, None])
    return (jnp.concatenate([cos] * 4, 1), jnp.concatenate([-sin, sin] * 2, 1), jnp.where(allowed, 0.0, -1e30).astype(jnp.float32))


def finish_kernel(sums, o_sums, i_sums, gate, up, down, query, key, value, output, router, first, second):
    f32 = jnp.float32
    for n in range(5):
        for i, ref in enumerate((gate, up)):
            ref[n] = sums[:, 0, :, pl.ds(640 * i + 128 * n, 128)].astype(f32).reshape(256, 128)
        down[n] = sums[:, 0, :, pl.ds(1280 + 128 * n, 128)].astype(f32).reshape(256, 128).T
    query[...] = i_sums[:, 0:384].astype(f32)
    key[...] = i_sums[:, 384:512].astype(f32)
    value[...] = i_sums[:, 512:640].astype(f32)
    output[...] = o_sums[:, 0:384].astype(f32).T
    small = o_sums[:, 384:512].astype(f32).T
    router[...] = small[0:40, :]
    first[...] = small[40:41, :]
    second[...] = small[41:42, :]


def finish(sums, o_sums, i_sums):
    S = jax.ShapeDtypeStruct
    f32 = jnp.float32
    return pl.pallas_call(
        finish_kernel,
        grid=(6,),
        out_shape=(S((5, 1536, 128), f32), S((5, 1536, 128), f32), S((5, 128, 1536), f32), S((1536, 384), f32),
                   S((1536, 128), f32), S((1536, 128), f32), S((384, 1536), f32), S((40, 1536), f32), S((1, 1536), f32), S((1, 1536), f32)),
        in_specs=[pl.BlockSpec((4, 1, 64, 1920), lambda j: (0, j, 0, 0)), pl.BlockSpec((256, 512), lambda j: (j, 0)), pl.BlockSpec((256, 640), lambda j: (j, 0))],
        out_specs=(pl.BlockSpec((5, 256, 128), lambda j: (0, j, 0)), pl.BlockSpec((5, 256, 128), lambda j: (0, j, 0)),
                   pl.BlockSpec((5, 128, 256), lambda j: (0, 0, j)), pl.BlockSpec((256, 384), lambda j: (j, 0)),
                   pl.BlockSpec((256, 128), lambda j: (j, 0)), pl.BlockSpec((256, 128), lambda j: (j, 0)),
                   pl.BlockSpec((384, 256), lambda j: (0, j)), pl.BlockSpec((40, 256), lambda j: (0, j)),
                   pl.BlockSpec((1, 256), lambda j: (0, j)), pl.BlockSpec((1, 256), lambda j: (0, j))),
        compiler_params=pltpu.CompilerParams(vmem_limit_bytes=32 << 20),
        name="finish",
    )(sums, o_sums, i_sums)


def expert_back_kernel(acts_hbm, x_hbm, u_hbm, gate_hbm, up_hbm, router_hbm, down_hbm, out, dw_out, router_out,
                       w_ref, down_ref, acts, stage, q, sib, a3, b3, a4, b4, a5, b5, a6, b6, xu, acc, dwb, ya, yb,
                       w_sem, down_sem, act_sem, load_sem, sib_send, sib_recv, ssem, rsem, ysend, yrecv):
    f32, low = jnp.float32, jnp.bfloat16
    nk = 12
    wide = 640
    x = lax.axis_index("tensor"); e = lax.axis_index("expert"); y = lax.axis_index("dp")
    z = e // 2; c = e % 2
    def zi(d): return (z + d) % 4
    def xi(d): return (x + d) % 4
    def yi(d): return (y + d) % 4
    def peer(oz, ox):
        return {"expert": zi(oz) * 2 + c, "tensor": xi(ox)}
    def ypeer(o):
        return {"dp": yi(o)}
    partner = {"expert": z * 2 + 1 - c}

    def act_load(n):
        return pltpu.make_async_copy(acts_hbm.at[:, :, n], acts.at[:, :, n], act_sem.at[n])
    def x_load(j, k):
        cols = pl.ds(pl.multiple_of(j * 256, 256), 256)
        return [pltpu.make_async_copy(x_hbm.at[:, :, :, :, cols], xu.at[k % 2], load_sem.at[k % 2, 0])]
    def u_load(j, k):
        cols = pl.ds(pl.multiple_of(j * 256, 256), 256)
        return [pltpu.make_async_copy(u_hbm.at[:, :, :, :, cols], xu.at[k % 2], load_sem.at[k % 2, 1])]
    w_loads = weight_loads(gate_hbm, up_hbm, router_hbm, w_ref, w_sem)
    down_load = pltpu.make_async_copy(down_hbm, down_ref, down_sem)
    down_load.start()
    act_load(1 - c).start()
    act_load(c).start()
    for cp in x_load(0, 0): cp.start()
    for cp in w_loads: cp.start()
    barrier = pltpu.get_barrier_semaphore()
    near = [peer(1, 0), peer(-1, 0), peer(0, 1), peer(0, -1), partner, ypeer(1), ypeer(-1)]
    for p in near:
        pl.semaphore_signal(barrier, inc=1, device_id=p, device_id_type=MESH)
    pl.semaphore_wait(barrier, len(near))

    def sibs(k):
        return [pltpu.make_async_remote_copy(
            src_ref=stage.at[k % 2], dst_ref=sib.at[k % 2],
            send_sem=sib_send.at[k], recv_sem=sib_recv.at[k], device_id=partner, device_id_type=MESH)]
    def rc(k, n, src, dst, to):
        return pltpu.make_async_remote_copy(src_ref=src, dst_ref=dst, send_sem=ssem.at[k, n], recv_sem=rsem.at[k, n],
                                            device_id=to, device_id_type=MESH)
    def copies3(k):
        s = k % 4
        return [rc(k, 0, q.at[k % 9, zi(2), :, pl.ds(0, 32)], a3.at[s, 0], peer(1, 0)),
                rc(k, 1, q.at[k % 9, zi(2), :, pl.ds(32, 32)], a3.at[s, 1], peer(-1, 0)),
                rc(k, 2, q.at[k % 9, :, xi(2), pl.ds(64, 32)], b3.at[s, 0], peer(0, 1)),
                rc(k, 3, q.at[k % 9, :, xi(2), pl.ds(96, 32)], b3.at[s, 1], peer(0, -1))]
    def copies4(k):
        s = k % 4
        return [rc(k, 4, q.at[k % 9, zi(1), :, pl.ds(0, 64)], a4.at[s, 0], peer(1, 0)),
                rc(k, 5, q.at[k % 9, zi(-1), :, pl.ds(0, 64)], a4.at[s, 1], peer(-1, 0)),
                rc(k, 6, q.at[k % 9, :, xi(1), pl.ds(64, 64)], b4.at[s, 0], peer(0, 1)),
                rc(k, 7, q.at[k % 9, :, xi(-1), pl.ds(64, 64)], b4.at[s, 1], peer(0, -1))]
    def copies5(k):
        s = k % 4
        return [rc(k, 8, q.at[k % 9, z, xi(2), pl.ds(0, 32)], a5.at[s, 0], peer(0, 1)),
                rc(k, 9, q.at[k % 9, z, xi(2), pl.ds(32, 32)], a5.at[s, 1], peer(0, -1)),
                rc(k, 10, q.at[k % 9, zi(2), x, pl.ds(64, 32)], b5.at[s, 0], peer(1, 0)),
                rc(k, 11, q.at[k % 9, zi(2), x, pl.ds(96, 32)], b5.at[s, 1], peer(-1, 0))]
    def copies6(k):
        s = k % 4
        return [rc(k, 12, q.at[k % 9, z, xi(1), pl.ds(0, 64)], a6.at[s, 0], peer(0, 1)),
                rc(k, 13, q.at[k % 9, z, xi(-1), pl.ds(0, 64)], a6.at[s, 1], peer(0, -1)),
                rc(k, 14, q.at[k % 9, zi(1), x, pl.ds(64, 64)], b6.at[s, 0], peer(1, 0)),
                rc(k, 15, q.at[k % 9, zi(-1), x, pl.ds(64, 64)], b6.at[s, 1], peer(-1, 0))]
    def add(k, i, j, rows, *terms):
        t = q[k % 9, i, j, rows].astype(f32)
        for s in terms:
            t = t + s.astype(f32)
        q[k % 9, i, j, rows] = t.astype(low)

    def product(k, cc, put):
        cols = pl.ds(pl.multiple_of((k // 2) * 256, 256), 256)
        def rows(lanes): return acts[:, :, cc, :, lanes].reshape(2048, -1)
        @pl.when(k % 2 == 0)
        def _():
            put(jnp.dot(rows(slice(0, wide)), down_ref[:, cols], preferred_element_type=f32))
        @pl.when(k % 2 == 1)
        def _():
            put(lax.dot_general(rows(slice(wide, 2048)), w_ref[cols, :], (((1,), (1,)), ((), ())),
                                preferred_element_type=f32))

    def stage1(k):
        @pl.when(k == 0)
        def _():
            down_load.wait()
            act_load(1 - c).wait()
        @pl.when(k == 1)
        def _():
            for cp in w_loads: cp.wait()
        def put(r):
            stage[k % 2] = r.astype(low).reshape(4, 4, 128, 256)
        product(k, 1 - c, put)
        for cp in sibs(k): cp.start()

    def stage2(k):
        for cp in sibs(k): cp.wait()
        def put(r):
            q[k % 9] = (r.reshape(4, 4, 128, 256) + sib[k % 2].astype(f32)).astype(low)
        product(k, c, put)
        for cp in copies3(k): cp.start()

    def weight_part(k):
        @pl.when(k == 0)
        def _(): act_load(c).wait()
        @pl.when(k % 2 == 0)
        def _():
            for cp in x_load(0, k): cp.wait()
            for cp in u_load(k // 2, k + 1): cp.start()
        @pl.when(k % 2 == 1)
        def _():
            for cp in u_load(0, k): cp.wait()
        @pl.when((k + 1 < nk) & (k % 2 == 1))
        def _():
            for cp in x_load(k // 2 + 1, k + 1): cp.start()
        slot = (k // 2) % 3
        def make(lanes):
            return lax.dot_general(xu[k % 2].reshape(4096, 256), acts[:, :, :, :, lanes].reshape(4096, -1),
                                   (((0,), (0,)), ((), ())), preferred_element_type=f32)
        @pl.when(k % 2 == 0)
        def _():
            acc[...] = make(slice(wide, 2048))
            dwb[slot, :, :, 0 : 2 * wide] = acc[:, 0 : 2 * wide].astype(low).reshape(4, 64, 2 * wide)
            router_out[pl.ds(pl.multiple_of((k // 2) * 256, 256), 256), :] = acc[:, 2 * wide :]
        @pl.when(k % 2 == 1)
        def _():
            acc[:, 0:wide] = make(slice(0, wide))
            dwb[slot, :, :, 2 * wide :] = acc[:, 0:wide].astype(low).reshape(4, 64, wide)

    def yrc(j, n, src, dst, to):
        return pltpu.make_async_remote_copy(src_ref=src, dst_ref=dst, send_sem=ysend.at[j, n], recv_sem=yrecv.at[j, n],
                                            device_id=to, device_id_type=MESH)
    def ycopies1(j):
        s = j % 3
        return [yrc(j, 0, dwb.at[s, yi(2), pl.ds(0, 32)], ya.at[j % 4, 0], ypeer(1)),
                yrc(j, 1, dwb.at[s, yi(2), pl.ds(32, 32)], ya.at[j % 4, 1], ypeer(-1))]
    def ycopies2(j):
        s = j % 3
        return [yrc(j, 2, dwb.at[s, yi(1)], yb.at[j % 4, 0], ypeer(1)),
                yrc(j, 3, dwb.at[s, yi(-1)], yb.at[j % 4, 1], ypeer(-1))]
    def ystage1(j):
        for cp in ycopies1(j): cp.start()
    def ystage2(j):
        for cp in ycopies1(j): cp.wait_recv()
        s = j % 3
        for d, r, m in ((1, 0, 0), (-1, 32, 1)):
            dwb[s, yi(d), pl.ds(r, 32)] = (dwb[s, yi(d), pl.ds(r, 32)].astype(f32) + ya[j % 4, m].astype(f32)).astype(low)
        for cp in ycopies2(j): cp.start()
    def ystage3(j):
        for cp in ycopies2(j): cp.wait_recv()
        dw_out[j] = (dwb[j % 3, y].astype(f32) + yb[j % 4, 0].astype(f32) + yb[j % 4, 1].astype(f32)).astype(low)
        for cp in ycopies1(j) + ycopies2(j): cp.wait_send()

    def stage4(k):
        for cp in copies3(k): cp.wait_recv()
        s = k % 4
        def body(n, _):
            add(k, zi(1), n, pl.ds(0, 32), a3[s, 0, n])
            add(k, zi(-1), n, pl.ds(32, 32), a3[s, 1, n])
            add(k, n, xi(1), pl.ds(64, 32), b3[s, 0, n])
            add(k, n, xi(-1), pl.ds(96, 32), b3[s, 1, n])
            return 0
        lax.fori_loop(0, 4, body, 0)
        for cp in copies4(k): cp.start()
    def stage5(k):
        for cp in copies4(k): cp.wait_recv()
        s = k % 4
        def body(n, _):
            add(k, z, n, pl.ds(0, 64), a4[s, 0, n], a4[s, 1, n])
            add(k, n, x, pl.ds(64, 64), b4[s, 0, n], b4[s, 1, n])
            return 0
        lax.fori_loop(0, 4, body, 0)
        for cp in copies5(k): cp.start()
    def stage6(k):
        for cp in copies5(k): cp.wait_recv()
        s = k % 4
        add(k, z, xi(1), pl.ds(0, 32), a5[s, 0])
        add(k, z, xi(-1), pl.ds(32, 32), a5[s, 1])
        add(k, zi(1), x, pl.ds(64, 32), b5[s, 0])
        add(k, zi(-1), x, pl.ds(96, 32), b5[s, 1])
        for cp in copies6(k): cp.start()
    def stage7(k):
        for cp in copies6(k): cp.wait_recv()
        s = k % 4
        for h, m in ((0, a6), (64, b6)):
            t = q[k % 9, z, x, pl.ds(h, 64)].astype(f32) + m[s, 0].astype(f32) + m[s, 1].astype(f32)
            out[k % 2, pl.ds(h, 64), pl.ds(pl.multiple_of((k // 2) * 256, 256), 256)] = t
        for cp in copies3(k) + copies4(k) + copies5(k) + copies6(k): cp.wait_send()

    def step(i, _):
        for lag, st in ((8, stage7), (7, stage6), (5, stage5), (3, stage4), (1, stage2), (0, stage1)):
            k = i - lag
            @pl.when((k >= 0) & (k < nk))
            def _():
                st(k)
        n = i - 0
        for lag, st in ((5, ystage3), (3, ystage2)):
            k = n - lag
            @pl.when((k >= 0) & (k < nk) & (k % 2 == 0))
            def _():
                st(k // 2)
        @pl.when((n >= 0) & (n < nk))
        def _():
            weight_part(n)
            @pl.when(n % 2 == 1)
            def _():
                ystage1(n // 2)
        return 0
    lax.fori_loop(0, nk + 8, step, 0)


def expert_back(acts, x, u, gate, up, router, down, cid):
    bf = jnp.bfloat16
    V = pltpu.VMEM
    nk = 12
    D = pltpu.SemaphoreType.DMA
    vm = pl.BlockSpec(memory_space=pltpu.VMEM)
    anym = pl.BlockSpec(memory_space=pl.ANY)
    return pl.pallas_call(
        expert_back_kernel,
        out_shape=(jax.ShapeDtypeStruct((2, 128, 1536), jnp.float32),
                   jax.ShapeDtypeStruct((6, 64, 1920), bf),
                   jax.ShapeDtypeStruct((1536, 128), jnp.float32)),
        in_specs=[anym] * 7,
        out_specs=(vm, vm, vm),
        scratch_shapes=[V((1536, 1408), bf), V((640, 1536), bf), V((4, 4, 2, 128, 2048), bf), V((2, 4, 4, 128, 256), bf), V((9, 4, 4, 128, 256), bf), V((2, 4, 4, 128, 256), bf),
                        V((4, 2, 4, 32, 256), bf), V((4, 2, 4, 32, 256), bf),
                        V((4, 2, 4, 64, 256), bf), V((4, 2, 4, 64, 256), bf),
                        V((4, 2, 32, 256), bf), V((4, 2, 32, 256), bf),
                        V((4, 2, 64, 256), bf), V((4, 2, 64, 256), bf),
                        V((2, 4, 4, 2, 128, 256), bf), V((256, 1408), jnp.float32), V((3, 4, 64, 1920), bf),
                        V((4, 2, 32, 1920), bf), V((4, 2, 64, 1920), bf),
                        D((11,)), D(()), D((2,)), D((2, 2)), D((nk,)), D((nk,)), D((nk, 16)), D((nk, 16)), D((6, 4)), D((6, 4))],
        compiler_params=pltpu.CompilerParams(collective_id=cid, has_side_effects=True, vmem_limit_bytes=63 << 20),
        name="expert_back",
    )(acts, x, u, gate, up, router, down)


def shards(
    tokens,
    documents,
    expert_routes,
    attention_gain,
    query_weight,
    key_matrix,
    value_matrix,
    output_weight,
    expert_gain,
    router_weight,
    gate_weight,
    up_weight,
    down_weight,
    out_cotangent,
):
    width = tokens.shape[1]
    local_experts = gate_weight.shape[0]
    experts_all = router_weight.shape[1]
    wide = local_experts * gate_weight.shape[2]
    inputs = tokens.astype(jnp.float32)
    first_gain = attention_gain.astype(jnp.float32)
    second_gain = expert_gain.astype(jnp.float32)
    first_scale = lax.rsqrt(jnp.mean(inputs * inputs, -1, keepdims=True) + epsilon)
    tables = attention_tables(documents)
    attention_weights = (query_weight, key_matrix, value_matrix, output_weight)
    router_pad = jnp.pad(router_weight, ((0, 0), (0, 64 - experts_all)))
    expert_weights = (
        gate_weight,
        up_weight,
        jnp.concatenate([router_pad, router_pad], 1),
        down_weight.reshape(wide, width),
    )
    lined_routes = jnp.pad(expert_routes, ((0, 0), (0, 128 - expert_routes.shape[1])))
    (
        residual,
        plane_rows,
        acts,
        plane_upstream,
        group_tokens,
        group_rows,
        queries,
        keys,
        values,
        attended,
        logsum,
    ) = front(
        tokens,
        jnp.concatenate([out_cotangent, lined_routes.astype(jnp.bfloat16)], 1),
        first_gain.reshape(1, width),
        second_gain.reshape(1, width),
        *tables,
        *attention_weights,
        *expert_weights,
        6,
    )
    experts_index = jnp.arange(experts_all, dtype=jnp.int32)
    second_normed, second_scale = normalize(residual, second_gain)
    second_low = second_normed.astype(jnp.bfloat16)
    def dense_gates(rows, routes):
        named = jnp.any(routes[:, :, None] == experts_index[None, None, :], 1)
        logits = jnp.dot(rows, router_weight, preferred_element_type=jnp.float32)
        logits = jnp.where(named, logits, -1e30)
        raised = jnp.exp(logits - jnp.max(logits, -1, keepdims=True))
        return raised / jnp.sum(raised, -1, keepdims=True)

    sums, weight_grads, router_pairs = expert_back(
        acts, plane_rows, plane_upstream, *expert_weights, 2
    )
    mixture, route_rows = sums[0], sums[1]
    layer_output = (residual + mixture).astype(jnp.bfloat16)
    router_pairs = router_pairs[:, :experts_all] + router_pairs[:, 64 : 64 + experts_all]
    weight_grads = lax.all_gather(weight_grads, "dp", axis=0)
    gates = dense_gates(second_low, expert_routes)
    upstream = out_cotangent.astype(jnp.float32)
    shared = gates * jnp.sum(mixture * upstream, -1, keepdims=True)
    router_local = -jnp.einsum(
        "td,te->de",
        second_low.astype(jnp.float32),
        shared,
        precision=highest,
        preferred_element_type=jnp.float32,
    ) + router_pairs
    normed_back = route_rows - jnp.einsum(
        "te,de->td",
        shared,
        router_weight.astype(jnp.float32),
        precision=highest,
        preferred_element_type=jnp.float32,
    )
    residual_back, expert_gain_local = norm_back(residual, second_scale, second_gain, normed_back)
    residual_grad = upstream + residual_back
    small = jnp.concatenate(
        [
            router_local,
            jnp.zeros((width, 1), jnp.float32),
            expert_gain_local[:, None],
            jnp.zeros((width, 126 - experts_all), jnp.float32),
        ],
        1,
    )
    output_part, input_part, normed_part = attention_back(
        residual_grad.astype(jnp.bfloat16),
        group_rows,
        group_tokens.reshape(-1, width),
        *tables,
        queries,
        keys,
        values,
        attended,
        logsum,
        small,
        *attention_weights,
        7,
    )
    output_sums, input_sums, normed_grad = grad_sum(output_part, input_part, normed_part, 4)
    input_back, _ = norm_back(inputs, first_scale, first_gain, normed_grad)
    input_gradient = residual_grad + input_back
    (
        gate_gradient,
        up_gradient,
        down_gradient,
        query_gradient,
        key_gradient,
        value_gradient,
        output_gradient,
        router_gradient,
        attention_gain_gradient,
        expert_gain_gradient,
    ) = finish(weight_grads, output_sums, input_sums)
    router_gradient = router_gradient.T
    attention_gain_gradient = attention_gain_gradient.reshape(width)
    expert_gain_gradient = expert_gain_gradient.reshape(width)
    return (
        layer_output,
        input_gradient,
        attention_gain_gradient,
        query_gradient,
        key_gradient,
        value_gradient,
        output_gradient,
        expert_gain_gradient,
        router_gradient,
        gate_gradient,
        up_gradient,
        down_gradient,
    )


def solution(mesh):
    placed = (
        P(("dp", "expert", "tensor"), None),
        P(("dp", "expert")),
        P(("dp", "expert", "tensor"), None),
        P(),
        P(None, "tensor"),
        P(None, "tensor"),
        P(None, "tensor"),
        P("tensor", None),
        P(),
        P(),
        P("expert", None, "tensor"),
        P("expert", None, "tensor"),
        P("expert", "tensor", None),
        P(("dp", "expert", "tensor"), None),
    )
    return jax.shard_map(
        shards,
        mesh=mesh,
        in_specs=placed,
        out_specs=(
            P(("dp", "expert", "tensor"), None),
            P(("dp", "expert", "tensor"), None),
            P(),
            P(None, "tensor"),
            P(None, "tensor"),
            P(None, "tensor"),
            P("tensor", None),
            P(),
            P(),
            P("expert", None, "tensor"),
            P("expert", None, "tensor"),
            P("expert", "tensor", None),
        ),
        check_vma=False,
    )
```

```python
import functools

import jax
import jax.numpy as jnp
from jax import lax
from jax.experimental import pallas as pl
from jax.experimental.pallas import tpu as pltpu
from jax.sharding import PartitionSpec as P


epsilon = 1e-06


def norm_back(value_rows, scale, gain, upstream):
    weighted = upstream * gain
    inner = jnp.mean(weighted * value_rows, -1, keepdims=True)
    return scale * weighted - value_rows * scale**3 * inner


MESH = pl.DeviceIdType.MESH

NT = (((1,), (1,)), ((), ()))
TN = (((0,), (0,)), ((), ()))


def turn(v, cosine, sine):
    lane = lax.broadcasted_iota(jnp.int32, v.shape, 1)
    count = v.shape[1]
    partner = jnp.where(lane % 64 < 32, pltpu.roll(v, count - 32, 1), pltpu.roll(v, 32, 1))
    times = count // 128
    return v * jnp.concatenate([cosine] * times, 1) + partner * jnp.concatenate([sine] * times, 1)


def attend(group, gain, cosine, sine, bias, wq, wk, wv, wo, rows_ref, q_ref, k_ref, v_ref, mixed_ref, logsum_ref, part_ref):
    f32, low = jnp.float32, jnp.bfloat16
    t = group[...].reshape(512, 1536).astype(f32)
    scale = lax.rsqrt(jnp.mean(t * t, -1, keepdims=True) + epsilon)
    rows_ref[...] = (t * scale * gain[...]).astype(low)
    rows = rows_ref[...]
    cos, sin = cosine[...], sine[...]
    q_ref[...] = (turn(jnp.dot(rows, wq[...], preferred_element_type=f32), cos, sin) * 0.125).astype(low)
    k_ref[...] = turn(jnp.dot(rows, wk[...], preferred_element_type=f32), cos, sin).astype(low)
    v_ref[...] = jnp.dot(rows, wv[...], preferred_element_type=f32).astype(low)
    lane = lax.broadcasted_iota(jnp.int32, (512, 128), 1)
    logsum = jnp.zeros((512, 128), f32)
    for h in range(6):
        kv = slice(64 * (h // 3), 64 * (h // 3) + 64)
        s = lax.dot_general(q_ref[:, 64 * h : 64 * h + 64], k_ref[:, kv], NT, preferred_element_type=f32) + bias[...]
        top = jnp.max(s, -1, keepdims=True)
        p = jnp.exp(s - top)
        total = jnp.sum(p, -1, keepdims=True)
        mixed = jnp.dot(p.astype(low), v_ref[:, kv], preferred_element_type=f32) / total
        mixed_ref[:, 64 * h : 64 * h + 64] = mixed.astype(low)
        logsum = jnp.where(lane == h, top + jnp.log(total), logsum)
    logsum_ref[...] = logsum
    part_ref[...] = jnp.dot(mixed_ref[...], wo[...], preferred_element_type=f32).astype(low).reshape(4, 128, 1536)


def weight_loads(gate, up, router, w, sem):
    return (
        [pltpu.make_async_copy(gate.at[n], w.at[:, pl.ds(128 * n, 128)], sem.at[n]) for n in range(5)]
        + [pltpu.make_async_copy(up.at[n], w.at[:, pl.ds(640 + 128 * n, 128)], sem.at[5 + n]) for n in range(5)]
        + [pltpu.make_async_copy(router, w.at[:, pl.ds(1280, 128)], sem.at[10])]
    )


PAIRS = ((0, 0), (1, 0), (3, 0), (0, 1), (0, 3), (2, 0), (0, 2), (1, 1), (1, 3), (3, 1), (3, 3), (2, 1), (2, 3), (1, 2), (3, 2), (2, 2))


class PlaneGather:
    def __init__(self, place, own, peer, sibling, core, send_sem, recv_sem, sib_send, sib_recv, starts, by_columns=False):
        self.starts, self.by_columns = starts, by_columns
        self.place, self.own, self.peer, self.sibling, self.core = place, own, peer, sibling, core
        self.send_sem, self.recv_sem, self.sib_send, self.sib_recv = send_sem, recv_sem, sib_send, sib_recv
        self.later = []

    def copy(self, dx, dz, ox, oz, q, nq, n, own):
        quarter = pl.ds(self.starts[q], self.starts[q + nq] - self.starts[q])
        quarter = (slice(None), quarter) if self.by_columns else quarter
        there = self.place(dx, dz, self.core).at[quarter]
        return pltpu.make_async_remote_copy(
            src_ref=self.own.at[quarter] if own and self.own is not None else there, dst_ref=there,
            send_sem=self.send_sem.at[n], recv_sem=self.recv_sem.at[(dx - ox) % 4, (dz - oz) % 4, q],
            device_id=self.peer(ox, oz), device_id_type=MESH)

    def send(self, dx, dz, ox, oz, q, nq, own=False):
        if self.starts[q] == self.starts[q + nq]:
            return
        make = functools.partial(self.copy, dx, dz, ox, oz, q, nq, len(self.later), own)
        make().start()
        self.later.append(make)

    def recv(self, dx, dz, q, nq):
        if self.starts[q] == self.starts[q + nq]:
            return
        self.copy(dx, dz, 0, 0, q, nq, 0, False).wait_recv()

    def sib_copy(self, core, dx, dz, own=False):
        there = self.place(dx, dz, core)
        return pltpu.make_async_remote_copy(
            src_ref=self.own if own else there, dst_ref=there,
            send_sem=self.sib_send.at[dx % 4, dz % 4], recv_sem=self.sib_recv.at[dx % 4, dz % 4],
            device_id=self.sibling, device_id_type=MESH)

    def sib_pass(self, dx, dz, own=False):
        make = functools.partial(self.sib_copy, self.core, dx, dz, own)
        make().start()
        self.later.append(make)

    def start(self, directions):
        for ox, oz in directions:
            self.send(0, 0, ox, oz, 0, 4, own=True)

    def wave1x(self):
        for s in (1, -1):
            self.recv(s, 0, 0, 4)
            if s == -1:
                self.send(s, 0, 1, 0, 1, 2)
            else:
                self.send(s, 0, -1, 0, 0, 1)
                self.send(s, 0, -1, 0, 3, 1)
            for oz in (1, -1):
                self.send(s, 0, 0, oz, 0, 2)
            self.sib_pass(s, 0)

    def wave1z(self):
        for s in (1, -1):
            self.recv(0, s, 0, 4)
            if s == -1:
                self.send(0, s, 0, 1, 1, 2)
            else:
                self.send(0, s, 0, -1, 0, 1)
                self.send(0, s, 0, -1, 3, 1)
            for ox in (1, -1):
                self.send(0, s, ox, 0, 2, 2)
            self.sib_pass(0, s)

    def wave1(self):
        self.wave1x()
        self.wave1z()

    def wave2(self):
        for q, nq in ((1, 2), (0, 1), (3, 1)):
            self.recv(2, 0, q, nq)
        for oz in (1, -1):
            self.send(2, 0, 0, oz, 0, 2)
        for q, nq in ((1, 2), (0, 1), (3, 1)):
            self.recv(0, 2, q, nq)
        for ox in (1, -1):
            self.send(0, 2, ox, 0, 2, 2)
        self.sib_pass(2, 0)
        self.sib_pass(0, 2)
        for dx in (1, -1):
            for s in (1, -1):
                self.recv(dx, s, 0, 2)
                self.send(dx, s, 0, -s, 0 if s == 1 else 1, 1)
                self.recv(s, dx, 2, 2)
                self.send(s, dx, -s, 0, 2 if s == 1 else 3, 1)
        for dx in (1, -1):
            for dz in (1, -1):
                self.sib_pass(dx, dz)

    def wave3(self):
        for s in (1, -1):
            self.recv(2, s, 0, 2)
            self.send(2, s, 0, -s, 0 if s == 1 else 1, 1)
            self.recv(s, 2, 2, 2)
            self.send(s, 2, -s, 0, 2 if s == 1 else 3, 1)
        for d in (1, -1):
            for q in (0, 1):
                self.recv(d, 2, q, 1)
                self.recv(2, d, q + 2, 1)
        for d in (1, -1):
            self.sib_pass(d, 2)
            self.sib_pass(2, d)

    def wave4(self):
        for q in range(4):
            self.recv(2, 2, q, 1)
        self.sib_pass(2, 2)

    def finish(self):
        for make in self.later:
            make().wait_send()


def front_kernel(tokens, u_own, first_gain, second_gain, cosine, sine, bias, wq, wk, wv, wo, gate_hbm, up_hbm, router_hbm, down_hbm,
                 residual, rows_out, acts_out, u_hbm, group, normed, queries, keys, values, mixed, logsum,
                 part, nr1, nb, nr2, rows, w, down, u_buf, act_buf,
                 gsend, grecv, own_sem, nsend, nrecv, send_sem, recv_sem, sib_send, sib_recv,
                 u_send, u_recv, u_sib_send, u_sib_recv, w_sem, down_sem, u_sem, act_sem, out_sem):
    f32, low = jnp.float32, jnp.bfloat16
    wide = 640
    width = 1536
    x = lax.axis_index("tensor"); e = lax.axis_index("expert")
    z = e // 2; c = e % 2
    first = e * 5
    def xi(d): return (x + d) % 4
    def zi(d): return (z + d) % 4
    def peer(ox, oz):
        return {"expert": zi(oz) * 2 + c, "tensor": xi(ox)}
    sib = {"expert": z * 2 + 1 - c}
    def pair(step):
        if isinstance(step, int):
            return PAIRS[step]
        dx = dz = 0
        for n in range(4):
            here = lax.convert_element_type(step // 4 == n, jnp.int32)
            dx = dx + here * sum(PAIRS[4 * n + m][0] * 4**m for m in range(4))
            dz = dz + here * sum(PAIRS[4 * n + m][1] * 4**m for m in range(4))
        for n in range(3):
            more = lax.convert_element_type(step % 4 > n, jnp.int32)
            dx = dx // (1 + 3 * more)
            dz = dz // (1 + 3 * more)
        dx, dz = dx % 4, dz % 4
        return dx, dz
    def u_loads(step):
        dx, dz = pair(step)
        return pltpu.make_async_copy(u_hbm.at[zi(dz), xi(dx)], u_buf.at[step % 2], u_sem.at[step % 2])
    loads = weight_loads(gate_hbm, up_hbm, router_hbm, w, w_sem) + [pltpu.make_async_copy(down_hbm, down, down_sem)]
    for cp in loads: cp.start()
    barrier = pltpu.get_barrier_semaphore()
    near = [peer(1, 0), peer(-1, 0), peer(0, 1), peer(0, -1), sib]
    for p in near:
        pl.semaphore_signal(barrier, inc=1, device_id=p, device_id_type=MESH)
    pl.semaphore_wait(barrier, len(near))
    pend = []
    def go(cps):
        for cp in cps: cp.start()
        pend.extend(cps)
        return cps
    def block_of(ref):
        return lambda dx, dz, core: ref.at[zi(dz), xi(dx), core]
    cots = PlaneGather(block_of(u_hbm), u_own, peer, sib, c, u_send, u_recv, u_sib_send, u_sib_recv, (0, 48, 96, 112, 128))
    norms = PlaneGather(block_of(rows), rows.at[z, x, c], peer, sib, c, send_sem, recv_sem, sib_send, sib_recv, (0, 16, 32, 80, 128))
    def tok(n, block, half, to, own):
        there = group.at[block, pl.ds(64 * half, 64)]
        return pltpu.make_async_remote_copy(
            src_ref=tokens.at[pl.ds(64 * half, 64)] if own else there, dst_ref=there,
            send_sem=gsend.at[n], recv_sem=grecv.at[n], device_id=peer(to, 0), device_id_type=MESH)
    go([tok(0, x, 0, 1, True), tok(2, x, 1, -1, True)])
    go([tok(1, x, 1, 1, True), tok(3, x, 0, -1, True)])
    mine = pltpu.make_async_copy(u_own, u_hbm.at[z, x, c], own_sem)
    mine.start()
    cots.start(((0, 1), (0, -1)))
    group[x] = tokens[...]
    tok(0, xi(-1), 0, 1, False).wait_recv()
    go([tok(4, xi(-1), 0, 1, False)])
    tok(2, xi(1), 1, -1, False).wait_recv()
    go([tok(5, xi(1), 1, -1, False)])
    cots.start(((1, 0), (-1, 0)))
    cots.sib_pass(0, 0, own=True)
    tok(1, xi(-1), 1, 1, False).wait_recv()
    tok(3, xi(1), 0, -1, False).wait_recv()
    tok(4, xi(2), 0, 1, False).wait_recv()
    tok(5, xi(2), 1, -1, False).wait_recv()
    attend(group, first_gain, cosine, sine, bias, wq, wk, wv, wo, normed, queries, keys, values, mixed, logsum, part)
    def nrc(n, src, dst, to):
        return pltpu.make_async_remote_copy(src_ref=src, dst_ref=dst, send_sem=nsend.at[n], recv_sem=nrecv.at[n],
                                            device_id=peer(to, 0), device_id_type=MESH)
    n1 = go([nrc(0, part.at[xi(2), pl.ds(0, 64)], nr1.at[0], 1), nrc(1, part.at[xi(2), pl.ds(64, 64)], nr1.at[1], -1)])
    n2 = go([nrc(2, part.at[xi(1), pl.ds(64, 64)], nr2.at[0, pl.ds(64, 64)], 1),
             nrc(3, part.at[xi(-1), pl.ds(0, 64)], nr2.at[1, pl.ds(0, 64)], -1)])
    cots.wave1()
    mine.wait()
    cots.sib_copy(1 - c, 0, 0).wait_recv()
    u_loads(0).start()
    n1[0].wait_recv()
    nb[0] = (part[xi(1), 0:64].astype(f32) + nr1[0].astype(f32)).astype(low)
    n3 = go([nrc(4, nb.at[0], nr2.at[0, pl.ds(0, 64)], 1)])
    n1[1].wait_recv()
    nb[1] = (part[xi(-1), 64:128].astype(f32) + nr1[1].astype(f32)).astype(low)
    n3 += go([nrc(5, nb.at[1], nr2.at[1, pl.ds(64, 64)], -1)])
    for cp in n2 + n3: cp.wait_recv()
    total = tokens[...].astype(f32) + part[x].astype(f32) + nr2[0].astype(f32) + nr2[1].astype(f32)
    residual[...] = total
    scale = lax.rsqrt(jnp.mean(total * total, -1, keepdims=True) + epsilon)
    rows[z, x, c] = (total * scale * second_gain[...]).astype(low)
    norms.start(((1, 0), (-1, 0), (0, 1), (0, -1)))
    norms.sib_pass(0, 0, own=True)
    for cp in loads: cp.wait()

    def act_store(step):
        dx, dz = pair(step)
        return pltpu.make_async_copy(act_buf.at[step % 2], acts_out.at[zi(dz), xi(dx)].reshape(256, 2048), act_sem.at[step % 2])
    def row_store(step):
        dx, dz = pair(step)
        there = (zi(dz), xi(dx))
        return pltpu.make_async_copy(rows.at[there], rows_out.at[there], out_sem.at[step])
    def compute(step):
        dx, dz = pair(step)
        norms.sib_copy(1 - c, dx, dz).wait_recv()
        u_loads(step).wait()
        @pl.when(step < 15)
        def _():
            nx, nz = pair(step + 1)
            cots.sib_copy(1 - c, nx, nz).wait_recv()
            u_loads(step + 1).start()
        row_store(step).start()
        @pl.when(step >= 2)
        def _(): act_store(step - 2).wait()
        slot = step % 2
        here = act_buf.at[slot]
        pre = jnp.dot(rows[zi(dz), xi(dx)].reshape(256, width), w[...], preferred_element_type=f32)
        raw = lax.dot_general(u_buf[slot, :, :, 0:width].reshape(256, width), down[...], (((1,), (1,)), ((), ())), preferred_element_type=f32)
        lane = lax.broadcasted_iota(jnp.int32, (256, 128), 1)
        routes = u_buf[slot, :, :, width:].reshape(256, 128).astype(f32).astype(jnp.int32)
        named = lane == routes[:, 0:1]
        for n in range(1, 8):
            named = named | (lane == routes[:, n : n + 1])
        logits = jnp.where(named, pre[:, 2 * wide :], -1e30)
        raised = jnp.exp(logits - jnp.max(logits, -1, keepdims=True))
        gates = raised / jnp.sum(raised, -1, keepdims=True)
        weighted = jnp.zeros((256, 128), f32)
        for n in range(5):
            cols = slice(128 * n, 128 * (n + 1))
            gate = jnp.sum(jnp.where(lane == first + n, gates, 0.0), -1, keepdims=True)
            gate_pre = pre[:, cols]
            up_pre = pre[:, wide + 128 * n : wide + 128 * (n + 1)]
            sig = jax.nn.sigmoid(gate_pre)
            silu = gate_pre * sig
            active = silu * up_pre
            back = raw[:, cols]
            share = gate * jnp.sum(active * back, -1, keepdims=True)
            high = share.astype(low).astype(f32)
            weighted = weighted + jnp.where(lane == first + n, high, 0.0)
            weighted = weighted + jnp.where(lane == first + n + 64, share - high, 0.0)
            back = gate * back
            here[:, cols] = (gate * active).astype(low)
            here[:, wide + 128 * n : wide + 128 * (n + 1)] = (
                back * up_pre * (sig * (1.0 + gate_pre * (1.0 - sig)))
            ).astype(low)
            here[:, 2 * wide + 128 * n : 2 * wide + 128 * (n + 1)] = (back * silu).astype(low)
        here[:, 3 * wide :] = weighted.astype(low)
        act_store(step).start()

    events = ((0, cots.wave2), (1, norms.wave1), (3, cots.wave3), (5, norms.wave2), (7, cots.wave4), (9, norms.wave3), (13, norms.wave4))
    def body(step, _):
        for at, wave in events:
            @pl.when(step == at)
            def _():
                wave()
        compute(step)
        return 0
    lax.fori_loop(0, 16, body, 0)
    act_store(14).wait()
    act_store(15).wait()
    for n in range(16): row_store(n).wait()
    for cp in pend: cp.wait_send()
    cots.finish()
    norms.finish()


def front(tokens, u, first_gain, second_gain, cosine, sine, bias, wq, wk, wv, wo, gate, up, router, down, cid):
    bf, f32 = jnp.bfloat16, jnp.float32
    V = pltpu.VMEM
    D = pltpu.SemaphoreType.DMA
    S = jax.ShapeDtypeStruct
    vm = pl.BlockSpec(memory_space=pltpu.VMEM)
    anym = pl.BlockSpec(memory_space=pl.ANY)
    n, width = tokens.shape
    return pl.pallas_call(
        front_kernel,
        out_shape=(S((n, width), f32), S((4, 4, 2, n, width), bf), S((4, 4, 2, n, 2048), bf), S((4, 4, 2, n, 1664), bf),
                   S((4, n, width), bf), S((512, width), bf), S((512, 384), bf), S((512, 128), bf), S((512, 128), bf),
                   S((512, 384), bf), S((512, 128), f32)),
        in_specs=[vm, anym] + [vm] * 9 + [anym] * 4,
        out_specs=(vm, anym, anym, anym) + (vm,) * 7,
        scratch_shapes=[V((4, n, width), bf), V((2, 64, width), bf), V((2, 64, width), bf), V((2, 128, width), bf),
                        V((4, 4, 2, n, width), bf), V((width, 1408), bf), V((640, width), bf),
                        V((2, 2, n, 1664), bf), V((2, 256, 2048), bf),
                        D((6,)), D((6,)), D(()), D((6,)), D((6,)), D((64,)), D((4, 4, 4)), D((4, 4)), D((4, 4)),
                        D((64,)), D((4, 4, 4)), D((4, 4)), D((4, 4)),
                        D((11,)), D(()), D((2,)), D((2,)), D((16,))],
        compiler_params=pltpu.CompilerParams(collective_id=cid, has_side_effects=True, vmem_limit_bytes=60 << 20),
        name="front",
    )(tokens, u, first_gain, second_gain, cosine, sine, bias, wq, wk, wv, wo, gate, up, router, down)


class TorusSum:
    def __init__(self, g, out, scratch, sems, starts, place, with_extra):
        self.with_extra = with_extra
        (self.q, self.sib, self.a3, self.a3b, self.b3, self.b3b, self.a4, self.b4,
         self.a5, self.a5b, self.b5, self.b5b, self.a6, self.b6, self.extra) = scratch
        self.ssem, self.rsem, gsend, grecv, gsib_send, gsib_recv = sems
        self.g, self.out = g, out
        self.z, self.y, self.c, self.zi, self.yi, self.peer, self.xpeer, self.partner = place
        self.parts = [pl.ds(starts[n], starts[n + 1] - starts[n]) for n in range(4)]
        self.A = pl.ds(0, starts[2])
        self.B = pl.ds(starts[2], starts[4] - starts[2])
        self.sent = []
        self.back = PlaneGather(
            lambda dy, dz, core: out.at[core, self.zi(dz), self.yi(dy)], None, lambda oy, oz: self.peer(oz, oy), self.partner, self.c,
            gsend, grecv, gsib_send, gsib_recv, starts, True)

    def rc(self, n, src, dst, to):
        return pltpu.make_async_remote_copy(src_ref=src, dst_ref=dst, send_sem=self.ssem.at[n], recv_sem=self.rsem.at[n],
                                            device_id=to, device_id_type=MESH)

    def go(self, cps):
        for cp in cps:
            cp.start()
        self.sent.extend(cps)
        return cps

    def add(self, i, j, cols, *terms):
        t = self.q[i, j, :, cols].astype(jnp.float32)
        for s in terms:
            t = t + s.astype(jnp.float32)
        self.q[i, j, :, cols] = t.astype(jnp.bfloat16)

    def stage1(self):
        self.c1 = self.go([self.rc(16, self.g.at[1 - self.c], self.sib, self.partner)])

    def stage2(self):
        q, zi, yi, peer = self.q, self.zi, self.yi, self.peer
        A0, A1, B0, B1 = self.parts
        self.c1[0].wait_recv()
        def body(n, _):
            i, j = n // 4, n % 4
            q[i, j] = (self.g[self.c, i, j].astype(jnp.float32) + self.sib[i, j].astype(jnp.float32)).astype(jnp.bfloat16)
            return 0
        lax.fori_loop(0, 16, body, 0)
        self.c3 = self.go([self.rc(0, q.at[zi(2), :, :, A0], self.a3, peer(1, 0)),
                           self.rc(1, q.at[zi(2), :, :, A1], self.a3b, peer(-1, 0)),
                           self.rc(2, q.at[:, yi(2), :, B0], self.b3, peer(0, 1)),
                           self.rc(3, q.at[:, yi(2), :, B1], self.b3b, peer(0, -1))])

    def stage4(self):
        q, zi, yi, peer, A, B = self.q, self.zi, self.yi, self.peer, self.A, self.B
        A0, A1, B0, B1 = self.parts
        for cp in self.c3: cp.wait_recv()
        def body(n, _):
            self.add(zi(1), n, A0, self.a3[n])
            self.add(zi(-1), n, A1, self.a3b[n])
            self.add(n, yi(1), B0, self.b3[n])
            self.add(n, yi(-1), B1, self.b3b[n])
            return 0
        lax.fori_loop(0, 4, body, 0)
        self.c4 = self.go([self.rc(4, q.at[zi(1), :, :, A], self.a4.at[0], peer(1, 0)),
                           self.rc(5, q.at[zi(-1), :, :, A], self.a4.at[1], peer(-1, 0)),
                           self.rc(6, q.at[:, yi(1), :, B], self.b4.at[0], peer(0, 1)),
                           self.rc(7, q.at[:, yi(-1), :, B], self.b4.at[1], peer(0, -1))])

    def stage5(self):
        q, z, y, zi, yi, peer = self.q, self.z, self.y, self.zi, self.yi, self.peer
        A0, A1, B0, B1 = self.parts
        for cp in self.c4: cp.wait_recv()
        def body(n, _):
            self.add(z, n, self.A, self.a4[0, n], self.a4[1, n])
            self.add(n, y, self.B, self.b4[0, n], self.b4[1, n])
            return 0
        lax.fori_loop(0, 4, body, 0)
        self.c5 = self.go([self.rc(8, q.at[z, yi(2), :, A0], self.a5, peer(0, 1)),
                           self.rc(9, q.at[z, yi(2), :, A1], self.a5b, peer(0, -1)),
                           self.rc(10, q.at[zi(2), y, :, B0], self.b5, peer(1, 0)),
                           self.rc(11, q.at[zi(2), y, :, B1], self.b5b, peer(-1, 0))])

    def stage6(self):
        q, z, y, zi, yi, peer, A, B = self.q, self.z, self.y, self.zi, self.yi, self.peer, self.A, self.B
        A0, A1, B0, B1 = self.parts
        for cp in self.c5: cp.wait_recv()
        self.add(z, yi(1), A0, self.a5[...])
        self.add(z, yi(-1), A1, self.a5b[...])
        self.add(zi(1), y, B0, self.b5[...])
        self.add(zi(-1), y, B1, self.b5b[...])
        self.c6 = self.go([self.rc(12, q.at[z, yi(1), :, A], self.a6.at[0], peer(0, 1)),
                           self.rc(13, q.at[z, yi(-1), :, A], self.a6.at[1], peer(0, -1)),
                           self.rc(14, q.at[zi(1), y, :, B], self.b6.at[0], peer(1, 0)),
                           self.rc(15, q.at[zi(-1), y, :, B], self.b6.at[1], peer(-1, 0))])

    def stage7(self):
        f32, low = jnp.float32, jnp.bfloat16
        q, z, y = self.q, self.z, self.y
        for cp in self.c6: cp.wait_recv()
        own = self.out.at[self.c, z, y]
        own[:, self.A] = (q[z, y, :, self.A].astype(f32) + self.a6[0].astype(f32) + self.a6[1].astype(f32)).astype(low)
        last = (q[z, y, :, self.B].astype(f32) + self.b6[0].astype(f32) + self.b6[1].astype(f32)).astype(low)
        wide = last.shape[1] - (128 if self.with_extra else 0)
        own[:, pl.ds(self.B.start, wide)] = last[:, 0:wide]
        if not self.with_extra:
            return
        self.extra[0] = last[:, wide:]
        self.cx = self.go([self.rc(16 + o, self.extra.at[0], self.extra.at[o], self.xpeer(o)) for o in (1, 2, 3)])

    def start_back(self):
        f32 = jnp.float32
        if self.with_extra:
            for cp in self.cx: cp.wait_recv()
            extra = self.extra
            total = extra[0].astype(f32) + extra[1].astype(f32) + extra[2].astype(f32) + extra[3].astype(f32)
            self.out[self.c, self.z, self.y, :, pl.ds(self.B.start + self.B.size - 128, 128)] = total.astype(jnp.bfloat16)
        self.back.start(((1, 0), (-1, 0), (0, 1), (0, -1)))
        self.back.sib_pass(0, 0)

    def finish(self):
        for dy in range(4):
            for dz in range(4):
                self.back.sib_copy(1 - self.c, dy, dz).wait_recv()
        for cp in self.sent: cp.wait_send()
        self.back.finish()


def sum_scratch(starts):
    V, bf = pltpu.VMEM, jnp.bfloat16
    w = [starts[n + 1] - starts[n] for n in range(4)]
    a, b = w[0] + w[1], w[2] + w[3]
    D = pltpu.SemaphoreType.DMA
    return ([V((4, 4, 48, a + b), bf)] * 2 + [V((4, 48, n), bf) for n in w] + [V((2, 4, 48, a), bf), V((2, 4, 48, b), bf)]
            + [V((48, n), bf) for n in w] + [V((2, 48, a), bf), V((2, 48, b), bf), V((4, 48, 128), bf)]
            + [D((20,)), D((20,)), D((64,)), D((4, 4, 4)), D((4, 4)), D((4, 4))])


OUTPUT_PARTS = (0, 128, 256, 384, 512)
INPUT_PARTS = (0, 256, 384, 512, 640)


BACK_INPUTS = (
    ((2, 128, 1536), "float32"), ((128, 1536), "float32"), ((128, 1536), "bfloat16"), ((128, 8), "int32"), ((1, 1536), "float32"),
    ((1536, 128), "bfloat16"), ((1536, 128), "float32"), ((512, 1536), "bfloat16"), ((512, 1536), "bfloat16"), ((512, 128), "float32"),
    ((512, 128), "float32"), ((512, 512), "float32"), ((512, 384), "bfloat16"), ((512, 128), "bfloat16"), ((512, 128), "bfloat16"),
    ((512, 384), "bfloat16"), ((512, 128), "float32"), ((1536, 384), "bfloat16"), ((1536, 128), "bfloat16"), ((1536, 128), "bfloat16"),
    ((384, 1536), "bfloat16"),
)


def attention_back_kernel(*refs):
    count = len(BACK_INPUTS)
    given, (residual_grad, o_out, i_out, n_out) = refs[:count], refs[count : count + 4]
    held = refs[count + 4 : 2 * count + 4]
    (sums, residual, cotangent, routes, second_gain, router, router_pairs, rows, group, cosine, sine, bias, q, k, v, mixed, logsum,
     wq, wk, wv, wo) = held
    (branch, grad, probs, back, turned_t, q_back, k_back, v_back, k_acc, v_acc, gsend, grecv, load_sem) = refs[2 * count + 4 :]
    loads = [pltpu.make_async_copy(a, b, load_sem.at[n]) for n, (a, b) in enumerate(zip(given, held))]
    for cp in loads: cp.start()
    f32, low = jnp.float32, jnp.bfloat16
    x = lax.axis_index("tensor")
    def xi(d): return (x + d) % 4
    def xpeer(o):
        return {"tensor": xi(o)}
    barrier = pltpu.get_barrier_semaphore()
    for o in (1, -1):
        pl.semaphore_signal(barrier, inc=1, device_id=xpeer(o), device_id_type=MESH)
    pl.semaphore_wait(barrier, 2)
    sent = []
    def go(cps):
        for cp in cps: cp.start()
        sent.extend(cps)
        return cps
    for cp in loads[:6]: cp.wait()
    res = residual[...]
    scale = lax.rsqrt(jnp.mean(res * res, -1, keepdims=True) + epsilon)
    normed = (res * scale * second_gain[...]).astype(low)
    lane = lax.broadcasted_iota(jnp.int32, (128, 128), 1)
    named = lane == routes[:, 0:1]
    for n in range(1, 8):
        named = named | (lane == routes[:, n : n + 1])
    logits = jnp.where(named, jnp.dot(normed, router[...], preferred_element_type=f32), -1e30)
    raised = jnp.exp(logits - jnp.max(logits, -1, keepdims=True))
    gates = raised / jnp.sum(raised, -1, keepdims=True)
    upstream = cotangent[...].astype(f32)
    shared = gates * jnp.sum(sums[0] * upstream, -1, keepdims=True)
    high = shared.astype(low).astype(f32)
    shared = jnp.where(lane < 64, high, pltpu.roll(shared - high, 64, 1)).astype(low)
    normed_back = sums[1] - lax.dot_general(shared, router[...], NT, preferred_element_type=f32)
    weighted = normed_back * second_gain[...]
    inner = jnp.mean(weighted * res, -1, keepdims=True)
    total = upstream + scale * weighted - res * scale**3 * inner
    residual_grad[...] = total
    branch[...] = total.astype(low)
    def ring(n, block, part, to, own):
        there = grad.at[block, pl.ds(64 * part, 64)]
        return pltpu.make_async_remote_copy(
            src_ref=branch.at[pl.ds(64 * part, 64)] if own else there, dst_ref=there,
            send_sem=gsend.at[n], recv_sem=grecv.at[n], device_id=xpeer(to), device_id_type=MESH)
    go([ring(0, x, 0, 1, True), ring(2, x, 1, -1, True)])
    go([ring(1, x, 1, 1, True), ring(3, x, 0, -1, True)])
    grad[x] = branch[...]
    for cp in loads[6:]: cp.wait()
    k_t = k[...].astype(f32).T.astype(low)
    logsum_t = logsum[...].T
    bias_t = bias[...].T
    def heads(h):
        one = slice(64 * h, 64 * h + 64)
        kv = slice(64 * (h // 3), 64 * (h // 3) + 64)
        s = lax.dot_general(k[:, kv], q[:, one], NT, preferred_element_type=f32) + bias_t
        probs[h] = jnp.exp(s - logsum_t[h : h + 1, :])
    for h in range(2): heads(h)
    ones = jnp.ones((128, 128), low)
    gain_two = lax.dot_general((normed_back * res * scale).astype(low), ones, TN, preferred_element_type=f32)
    extras = router_pairs[...] - lax.dot_general(normed, shared, TN, preferred_element_type=f32)
    extras = extras + pltpu.roll(extras, 64, 1)
    ring(0, xi(-1), 0, 1, False).wait_recv()
    go([ring(4, xi(-1), 0, 1, False)])
    ring(2, xi(1), 1, -1, False).wait_recv()
    go([ring(5, xi(1), 1, -1, False)])
    for h in range(2, 6): heads(h)
    ring(1, xi(-1), 1, 1, False).wait_recv()
    ring(3, xi(1), 0, -1, False).wait_recv()
    ring(4, xi(2), 0, 1, False).wait_recv()
    ring(5, xi(2), 1, -1, False).wait_recv()

    all_grad = grad[...].reshape(512, 1536)
    o_out[:, 0:384] = lax.dot_general(all_grad, mixed[...], TN, preferred_element_type=f32).astype(low)
    back[...] = lax.dot_general(all_grad, wo[...], NT, preferred_element_type=f32).astype(low)
    for h in range(6):
        one = slice(64 * h, 64 * h + 64)
        kv = slice(64 * (h // 3), 64 * (h // 3) + 64)
        p = probs[h]
        grad_p = lax.dot_general(v[:, kv], back[:, one], NT, preferred_element_type=f32)
        both = p * grad_p
        inner = jnp.sum(both, 0, keepdims=True)
        grad_s = (both - p * inner).astype(low)
        v_part = jnp.dot(p.astype(low), back[:, one], preferred_element_type=f32)
        k_part = jnp.dot(grad_s, q[:, one], preferred_element_type=f32)
        if h % 3 == 0:
            v_acc[:, kv] = v_part
            k_acc[:, kv] = k_part
        else:
            v_acc[:, kv] += v_part
            k_acc[:, kv] += k_part
        turned_t[one, :] = jnp.dot(k_t[kv, :], grad_s, preferred_element_type=f32)
    cos, sin = cosine[...], -sine[...]
    q_back[...] = turn(turned_t[...].T * 0.125, cos, sin).astype(low)
    k_back[...] = turn(k_acc[...], cos, sin).astype(low)
    v_back[...] = v_acc[...].astype(low)
    part = (
        lax.dot_general(q_back[...], wq[...], NT, preferred_element_type=f32)
        + lax.dot_general(k_back[...], wk[...], NT, preferred_element_type=f32)
        + lax.dot_general(v_back[...], wv[...], NT, preferred_element_type=f32)
    )
    n_out[...] = part.astype(low)
    t = group[...].astype(f32)
    t = t * lax.rsqrt(jnp.mean(t * t, -1, keepdims=True) + epsilon)
    ones = jnp.ones((512, 128), low)
    gain_part = lax.dot_general((part * t).astype(low), ones, TN, preferred_element_type=f32)
    lane = lax.broadcasted_iota(jnp.int32, (1536, 128), 1)
    o_out[:, 384:512] = jnp.where(lane == 40, gain_part, jnp.where(lane == 41, gain_two, extras)).astype(low)
    i_out[:, 0:384] = lax.dot_general(rows[...], q_back[...], TN, preferred_element_type=f32).astype(low)
    i_out[:, 384:512] = lax.dot_general(rows[...], k_back[...], TN, preferred_element_type=f32).astype(low)
    i_out[:, 512:640] = lax.dot_general(rows[...], v_back[...], TN, preferred_element_type=f32).astype(low)
    for cp in sent: cp.wait_send()


def attention_back(*operands, cid):
    S = jax.ShapeDtypeStruct
    bf, f32 = jnp.bfloat16, jnp.float32
    V = pltpu.VMEM
    D = pltpu.SemaphoreType.DMA
    return pl.pallas_call(
        attention_back_kernel,
        out_shape=(S((128, 1536), f32), S((1536, 512), bf), S((1536, 640), bf), S((512, 1536), bf)),
        in_specs=[pl.BlockSpec(memory_space=pl.ANY)] * len(BACK_INPUTS),
        out_specs=(pl.BlockSpec(memory_space=pltpu.VMEM),) * 4,
        scratch_shapes=[V(shape, jnp.dtype(kind)) for shape, kind in BACK_INPUTS]
        + [V((128, 1536), bf), V((4, 128, 1536), bf), V((6, 512, 512), f32), V((512, 384), bf), V((384, 512), f32),
           V((512, 384), bf), V((512, 128), bf), V((512, 128), bf), V((512, 128), f32), V((512, 128), f32), D((6,)), D((6,)),
           D((len(BACK_INPUTS),))],
        compiler_params=pltpu.CompilerParams(collective_id=cid, has_side_effects=True, vmem_limit_bytes=60 << 20),
        name="attention_back",
    )(*operands)


def grad_sum_kernel(o_sum, i_sum, n_part, o_out, i_out, n_out, nr1, nb, nr2, nsend, nrecv, *scratch):
    f32, low = jnp.float32, jnp.bfloat16
    x = lax.axis_index("tensor"); e = lax.axis_index("expert"); y = lax.axis_index("dp")
    z = e // 2; c = e % 2
    def zi(d): return (z + d) % 4
    def yi(d): return (y + d) % 4
    def xi(d): return (x + d) % 4
    def peer(oz, oy):
        return {"expert": zi(oz) * 2 + c, "dp": yi(oy)}
    def xpeer(o):
        return {"tensor": xi(o)}
    partner = {"expert": z * 2 + 1 - c}
    barrier = pltpu.get_barrier_semaphore()
    near = [peer(1, 0), peer(-1, 0), peer(0, 1), peer(0, -1), partner, xpeer(1), xpeer(2), xpeer(3)]
    for p in near:
        pl.semaphore_signal(barrier, inc=1, device_id=p, device_id_type=MESH)
    pl.semaphore_wait(barrier, len(near))
    sent = []
    def go(cps):
        for cp in cps: cp.start()
        sent.extend(cps)
        return cps
    place = (z, y, c, zi, yi, peer, xpeer, partner)
    half = len(scratch) // 2
    osum = TorusSum(o_sum, o_out, scratch[:15], scratch[15:half], OUTPUT_PARTS, place, True)
    isum = TorusSum(i_sum, i_out, scratch[half : half + 15], scratch[half + 15 :], INPUT_PARTS, place, False)
    osum.stage1()
    def nrc(n, src, dst, to):
        return pltpu.make_async_remote_copy(src_ref=src, dst_ref=dst, send_sem=nsend.at[n], recv_sem=nrecv.at[n],
                                            device_id=xpeer(to), device_id_type=MESH)
    n1 = go([nrc(0, n_part.at[xi(2), pl.ds(0, 64)], nr1.at[0], 1), nrc(1, n_part.at[xi(2), pl.ds(64, 64)], nr1.at[1], -1)])
    n2 = go([nrc(2, n_part.at[xi(1), pl.ds(64, 64)], nr2.at[0, pl.ds(64, 64)], 1),
             nrc(3, n_part.at[xi(-1), pl.ds(0, 64)], nr2.at[1, pl.ds(0, 64)], -1)])
    isum.stage1()
    osum.stage2()
    isum.stage2()
    for cp in n1: cp.wait_recv()
    nb[0] = (n_part[xi(1), 0:64].astype(f32) + nr1[0].astype(f32)).astype(low)
    nb[1] = (n_part[xi(-1), 64:128].astype(f32) + nr1[1].astype(f32)).astype(low)
    n3 = go([nrc(4, nb.at[0], nr2.at[0, pl.ds(0, 64)], 1), nrc(5, nb.at[1], nr2.at[1, pl.ds(64, 64)], -1)])
    osum.stage4()
    isum.stage4()
    osum.stage5()
    isum.stage5()
    osum.stage6()
    isum.stage6()
    osum.stage7()
    isum.stage7()
    isum.start_back()
    osum.start_back()
    for cp in n2 + n3: cp.wait_recv()
    n_out[...] = n_part[x].astype(f32) + nr2[0].astype(f32) + nr2[1].astype(f32)
    isum.back.wave1()
    osum.back.wave1()
    isum.back.wave2()
    osum.back.wave2()
    isum.back.wave3()
    osum.back.wave3()
    isum.back.wave4()
    osum.back.wave4()
    isum.finish()
    osum.finish()
    for cp in sent: cp.wait_send()


def grad_sum(o_part, i_part, n_part, cid):
    S = jax.ShapeDtypeStruct
    bf, f32 = jnp.bfloat16, jnp.float32
    V = pltpu.VMEM
    D = pltpu.SemaphoreType.DMA
    vm = pl.BlockSpec(memory_space=pltpu.VMEM)
    o_sums, i_sums, row_sums = pl.pallas_call(
        grad_sum_kernel,
        out_shape=(S((2, 4, 4, 48, 512), bf), S((2, 4, 4, 48, 640), bf), S((128, 1536), f32)),
        in_specs=[vm] * 3,
        out_specs=(vm,) * 3,
        scratch_shapes=[V((2, 64, 1536), bf), V((2, 64, 1536), bf), V((2, 128, 1536), bf),
                        D((6,)), D((6,))] + sum_scratch(OUTPUT_PARTS) + sum_scratch(INPUT_PARTS),
        compiler_params=pltpu.CompilerParams(collective_id=cid, has_side_effects=True, vmem_limit_bytes=28 << 20),
        name="grad_sum",
    )(o_part.reshape(2, 4, 4, 48, 512), i_part.reshape(2, 4, 4, 48, 640), n_part.reshape(4, 128, 1536))
    return o_sums.reshape(1536, 512), i_sums.reshape(1536, 640), row_sums


def attention_tables(documents):
    index = jnp.arange(documents.shape[0], dtype=jnp.int32)
    positions = index - jnp.sum((documents[None, :] < documents[:, None]).astype(jnp.int32), 1)
    freq = 10000.0 ** (-(jnp.arange(32, dtype=jnp.float32) * 2.0 / 64))
    angle = positions.astype(jnp.float32)[:, None] * freq[None, :]
    cos, sin = jnp.cos(angle), jnp.sin(angle)
    allowed = (documents[:, None] == documents[None, :]) & (index[None, :] <= index[:, None])
    return (jnp.concatenate([cos] * 4, 1), jnp.concatenate([-sin, sin] * 2, 1), jnp.where(allowed, 0.0, -1e30).astype(jnp.float32))


def finish_kernel(sums, o_sums, i_sums, gate, up, down, query, key, value, output, router, first, second):
    f32 = jnp.float32
    for n in range(5):
        for i, ref in enumerate((gate, up)):
            ref[n] = sums[:, 0, :, pl.ds(640 * i + 128 * n, 128)].astype(f32).reshape(256, 128)
        down[n] = sums[:, 0, :, pl.ds(1280 + 128 * n, 128)].astype(f32).reshape(256, 128).T
    query[...] = i_sums[:, 0:384].astype(f32)
    key[...] = i_sums[:, 384:512].astype(f32)
    value[...] = i_sums[:, 512:640].astype(f32)
    output[...] = o_sums[:, 0:384].astype(f32).T
    small = o_sums[:, 384:512].astype(f32).T
    router[...] = small[0:40, :]
    first[...] = small[40:41, :]
    second[...] = small[41:42, :]


def finish(sums, o_sums, i_sums):
    S = jax.ShapeDtypeStruct
    f32 = jnp.float32
    return pl.pallas_call(
        finish_kernel,
        grid=(6,),
        out_shape=(S((5, 1536, 128), f32), S((5, 1536, 128), f32), S((5, 128, 1536), f32), S((1536, 384), f32),
                   S((1536, 128), f32), S((1536, 128), f32), S((384, 1536), f32), S((40, 1536), f32), S((1, 1536), f32), S((1, 1536), f32)),
        in_specs=[pl.BlockSpec((4, 1, 64, 1920), lambda j: (0, j, 0, 0)), pl.BlockSpec((256, 512), lambda j: (j, 0)), pl.BlockSpec((256, 640), lambda j: (j, 0))],
        out_specs=(pl.BlockSpec((5, 256, 128), lambda j: (0, j, 0)), pl.BlockSpec((5, 256, 128), lambda j: (0, j, 0)),
                   pl.BlockSpec((5, 128, 256), lambda j: (0, 0, j)), pl.BlockSpec((256, 384), lambda j: (j, 0)),
                   pl.BlockSpec((256, 128), lambda j: (j, 0)), pl.BlockSpec((256, 128), lambda j: (j, 0)),
                   pl.BlockSpec((384, 256), lambda j: (0, j)), pl.BlockSpec((40, 256), lambda j: (0, j)),
                   pl.BlockSpec((1, 256), lambda j: (0, j)), pl.BlockSpec((1, 256), lambda j: (0, j))),
        compiler_params=pltpu.CompilerParams(vmem_limit_bytes=32 << 20),
        name="finish",
    )(sums, o_sums, i_sums)


def expert_back_kernel(acts_hbm, x_hbm, u_hbm, gate_hbm, up_hbm, router_hbm, down_hbm, out, dw_out, router_out,
                       w_ref, down_ref, acts, stage, q, sib, a3, b3, a4, b4, a5, b5, a6, b6, xu, acc, dwb, ya, yb,
                       w_sem, down_sem, act_sem, load_sem, sib_send, sib_recv, ssem, rsem, ysend, yrecv):
    f32, low = jnp.float32, jnp.bfloat16
    nk = 12
    wide = 640
    x = lax.axis_index("tensor"); e = lax.axis_index("expert"); y = lax.axis_index("dp")
    z = e // 2; c = e % 2
    def zi(d): return (z + d) % 4
    def xi(d): return (x + d) % 4
    def yi(d): return (y + d) % 4
    def peer(oz, ox):
        return {"expert": zi(oz) * 2 + c, "tensor": xi(ox)}
    def ypeer(o):
        return {"dp": yi(o)}
    partner = {"expert": z * 2 + 1 - c}

    def act_load(n):
        return pltpu.make_async_copy(acts_hbm.at[:, :, n], acts.at[:, :, n], act_sem.at[n])
    def x_load(j, k):
        cols = pl.ds(pl.multiple_of(j * 256, 256), 256)
        return [pltpu.make_async_copy(x_hbm.at[:, :, :, :, cols], xu.at[k % 2], load_sem.at[k % 2, 0])]
    def u_load(j, k):
        cols = pl.ds(pl.multiple_of(j * 256, 256), 256)
        return [pltpu.make_async_copy(u_hbm.at[:, :, :, :, cols], xu.at[k % 2], load_sem.at[k % 2, 1])]
    w_loads = weight_loads(gate_hbm, up_hbm, router_hbm, w_ref, w_sem)
    down_load = pltpu.make_async_copy(down_hbm, down_ref, down_sem)
    down_load.start()
    act_load(1 - c).start()
    act_load(c).start()
    for cp in x_load(0, 0): cp.start()
    for cp in w_loads: cp.start()
    barrier = pltpu.get_barrier_semaphore()
    near = [peer(1, 0), peer(-1, 0), peer(0, 1), peer(0, -1), partner, ypeer(1), ypeer(-1)]
    for p in near:
        pl.semaphore_signal(barrier, inc=1, device_id=p, device_id_type=MESH)
    pl.semaphore_wait(barrier, len(near))

    def sibs(k):
        return [pltpu.make_async_remote_copy(
            src_ref=stage.at[k % 2], dst_ref=sib.at[k % 2],
            send_sem=sib_send.at[k], recv_sem=sib_recv.at[k], device_id=partner, device_id_type=MESH)]
    def rc(k, n, src, dst, to):
        return pltpu.make_async_remote_copy(src_ref=src, dst_ref=dst, send_sem=ssem.at[k, n], recv_sem=rsem.at[k, n],
                                            device_id=to, device_id_type=MESH)
    def copies3(k):
        s = k % 4
        return [rc(k, 0, q.at[k % 9, zi(2), :, pl.ds(0, 32)], a3.at[s, 0], peer(1, 0)),
                rc(k, 1, q.at[k % 9, zi(2), :, pl.ds(32, 32)], a3.at[s, 1], peer(-1, 0)),
                rc(k, 2, q.at[k % 9, :, xi(2), pl.ds(64, 32)], b3.at[s, 0], peer(0, 1)),
                rc(k, 3, q.at[k % 9, :, xi(2), pl.ds(96, 32)], b3.at[s, 1], peer(0, -1))]
    def copies4(k):
        s = k % 4
        return [rc(k, 4, q.at[k % 9, zi(1), :, pl.ds(0, 64)], a4.at[s, 0], peer(1, 0)),
                rc(k, 5, q.at[k % 9, zi(-1), :, pl.ds(0, 64)], a4.at[s, 1], peer(-1, 0)),
                rc(k, 6, q.at[k % 9, :, xi(1), pl.ds(64, 64)], b4.at[s, 0], peer(0, 1)),
                rc(k, 7, q.at[k % 9, :, xi(-1), pl.ds(64, 64)], b4.at[s, 1], peer(0, -1))]
    def copies5(k):
        s = k % 4
        return [rc(k, 8, q.at[k % 9, z, xi(2), pl.ds(0, 32)], a5.at[s, 0], peer(0, 1)),
                rc(k, 9, q.at[k % 9, z, xi(2), pl.ds(32, 32)], a5.at[s, 1], peer(0, -1)),
                rc(k, 10, q.at[k % 9, zi(2), x, pl.ds(64, 32)], b5.at[s, 0], peer(1, 0)),
                rc(k, 11, q.at[k % 9, zi(2), x, pl.ds(96, 32)], b5.at[s, 1], peer(-1, 0))]
    def copies6(k):
        s = k % 4
        return [rc(k, 12, q.at[k % 9, z, xi(1), pl.ds(0, 64)], a6.at[s, 0], peer(0, 1)),
                rc(k, 13, q.at[k % 9, z, xi(-1), pl.ds(0, 64)], a6.at[s, 1], peer(0, -1)),
                rc(k, 14, q.at[k % 9, zi(1), x, pl.ds(64, 64)], b6.at[s, 0], peer(1, 0)),
                rc(k, 15, q.at[k % 9, zi(-1), x, pl.ds(64, 64)], b6.at[s, 1], peer(-1, 0))]
    def add(k, i, j, rows, *terms):
        t = q[k % 9, i, j, rows].astype(f32)
        for s in terms:
            t = t + s.astype(f32)
        q[k % 9, i, j, rows] = t.astype(low)

    def product(k, cc, put):
        cols = pl.ds(pl.multiple_of((k // 2) * 256, 256), 256)
        def rows(lanes): return acts[:, :, cc, :, lanes].reshape(2048, -1)
        @pl.when(k % 2 == 0)
        def _():
            put(jnp.dot(rows(slice(0, wide)), down_ref[:, cols], preferred_element_type=f32))
        @pl.when(k % 2 == 1)
        def _():
            put(lax.dot_general(rows(slice(wide, 2048)), w_ref[cols, :], (((1,), (1,)), ((), ())),
                                preferred_element_type=f32))

    def stage1(k):
        @pl.when(k == 0)
        def _():
            down_load.wait()
            act_load(1 - c).wait()
        @pl.when(k == 1)
        def _():
            for cp in w_loads: cp.wait()
        def put(r):
            stage[k % 2] = r.astype(low).reshape(4, 4, 128, 256)
        product(k, 1 - c, put)
        for cp in sibs(k): cp.start()

    def stage2(k):
        for cp in sibs(k): cp.wait()
        def put(r):
            q[k % 9] = (r.reshape(4, 4, 128, 256) + sib[k % 2].astype(f32)).astype(low)
        product(k, c, put)
        for cp in copies3(k): cp.start()

    def weight_part(k):
        @pl.when(k == 0)
        def _(): act_load(c).wait()
        @pl.when(k % 2 == 0)
        def _():
            for cp in x_load(0, k): cp.wait()
            for cp in u_load(k // 2, k + 1): cp.start()
        @pl.when(k % 2 == 1)
        def _():
            for cp in u_load(0, k): cp.wait()
        @pl.when((k + 1 < nk) & (k % 2 == 1))
        def _():
            for cp in x_load(k // 2 + 1, k + 1): cp.start()
        slot = (k // 2) % 3
        def make(lanes):
            return lax.dot_general(xu[k % 2].reshape(4096, 256), acts[:, :, :, :, lanes].reshape(4096, -1),
                                   (((0,), (0,)), ((), ())), preferred_element_type=f32)
        @pl.when(k % 2 == 0)
        def _():
            acc[...] = make(slice(wide, 2048))
            dwb[slot, :, :, 0 : 2 * wide] = acc[:, 0 : 2 * wide].astype(low).reshape(4, 64, 2 * wide)
            router_out[pl.ds(pl.multiple_of((k // 2) * 256, 256), 256), :] = acc[:, 2 * wide :]
        @pl.when(k % 2 == 1)
        def _():
            acc[:, 0:wide] = make(slice(0, wide))
            dwb[slot, :, :, 2 * wide :] = acc[:, 0:wide].astype(low).reshape(4, 64, wide)

    def yrc(j, n, src, dst, to):
        return pltpu.make_async_remote_copy(src_ref=src, dst_ref=dst, send_sem=ysend.at[j, n], recv_sem=yrecv.at[j, n],
                                            device_id=to, device_id_type=MESH)
    def ycopies1(j):
        s = j % 3
        return [yrc(j, 0, dwb.at[s, yi(2), pl.ds(0, 32)], ya.at[j % 4, 0], ypeer(1)),
                yrc(j, 1, dwb.at[s, yi(2), pl.ds(32, 32)], ya.at[j % 4, 1], ypeer(-1))]
    def ycopies2(j):
        s = j % 3
        return [yrc(j, 2, dwb.at[s, yi(1)], yb.at[j % 4, 0], ypeer(1)),
                yrc(j, 3, dwb.at[s, yi(-1)], yb.at[j % 4, 1], ypeer(-1))]
    def ystage1(j):
        for cp in ycopies1(j): cp.start()
    def ystage2(j):
        for cp in ycopies1(j): cp.wait_recv()
        s = j % 3
        for d, r, m in ((1, 0, 0), (-1, 32, 1)):
            dwb[s, yi(d), pl.ds(r, 32)] = (dwb[s, yi(d), pl.ds(r, 32)].astype(f32) + ya[j % 4, m].astype(f32)).astype(low)
        for cp in ycopies2(j): cp.start()
    def ystage3(j):
        for cp in ycopies2(j): cp.wait_recv()
        dw_out[j] = (dwb[j % 3, y].astype(f32) + yb[j % 4, 0].astype(f32) + yb[j % 4, 1].astype(f32)).astype(low)
        for cp in ycopies1(j) + ycopies2(j): cp.wait_send()

    def stage4(k):
        for cp in copies3(k): cp.wait_recv()
        s = k % 4
        def body(n, _):
            add(k, zi(1), n, pl.ds(0, 32), a3[s, 0, n])
            add(k, zi(-1), n, pl.ds(32, 32), a3[s, 1, n])
            add(k, n, xi(1), pl.ds(64, 32), b3[s, 0, n])
            add(k, n, xi(-1), pl.ds(96, 32), b3[s, 1, n])
            return 0
        lax.fori_loop(0, 4, body, 0)
        for cp in copies4(k): cp.start()
    def stage5(k):
        for cp in copies4(k): cp.wait_recv()
        s = k % 4
        def body(n, _):
            add(k, z, n, pl.ds(0, 64), a4[s, 0, n], a4[s, 1, n])
            add(k, n, x, pl.ds(64, 64), b4[s, 0, n], b4[s, 1, n])
            return 0
        lax.fori_loop(0, 4, body, 0)
        for cp in copies5(k): cp.start()
    def stage6(k):
        for cp in copies5(k): cp.wait_recv()
        s = k % 4
        add(k, z, xi(1), pl.ds(0, 32), a5[s, 0])
        add(k, z, xi(-1), pl.ds(32, 32), a5[s, 1])
        add(k, zi(1), x, pl.ds(64, 32), b5[s, 0])
        add(k, zi(-1), x, pl.ds(96, 32), b5[s, 1])
        for cp in copies6(k): cp.start()
    def stage7(k):
        for cp in copies6(k): cp.wait_recv()
        s = k % 4
        for h, m in ((0, a6), (64, b6)):
            t = q[k % 9, z, x, pl.ds(h, 64)].astype(f32) + m[s, 0].astype(f32) + m[s, 1].astype(f32)
            out[k % 2, pl.ds(h, 64), pl.ds(pl.multiple_of((k // 2) * 256, 256), 256)] = t
        for cp in copies3(k) + copies4(k) + copies5(k) + copies6(k): cp.wait_send()

    def step(i, _):
        for lag, st in ((7, stage7), (6, stage6), (5, stage5), (3, stage4), (1, stage2), (0, stage1)):
            k = i - lag
            @pl.when((k >= 0) & (k < nk))
            def _():
                st(k)
        n = i - 0
        for lag, st in ((5, ystage3), (3, ystage2)):
            k = n - lag
            @pl.when((k >= 0) & (k < nk) & (k % 2 == 0))
            def _():
                st(k // 2)
        @pl.when((n >= 0) & (n < nk))
        def _():
            weight_part(n)
            @pl.when(n % 2 == 1)
            def _():
                ystage1(n // 2)
        return 0
    lax.fori_loop(0, nk + 7, step, 0)


def expert_back(acts, x, u, gate, up, router, down, cid):
    bf = jnp.bfloat16
    V = pltpu.VMEM
    nk = 12
    D = pltpu.SemaphoreType.DMA
    vm = pl.BlockSpec(memory_space=pltpu.VMEM)
    anym = pl.BlockSpec(memory_space=pl.ANY)
    return pl.pallas_call(
        expert_back_kernel,
        out_shape=(jax.ShapeDtypeStruct((2, 128, 1536), jnp.float32),
                   jax.ShapeDtypeStruct((6, 64, 1920), bf),
                   jax.ShapeDtypeStruct((1536, 128), jnp.float32)),
        in_specs=[anym] * 7,
        out_specs=(vm, vm, vm),
        scratch_shapes=[V((1536, 1408), bf), V((640, 1536), bf), V((4, 4, 2, 128, 2048), bf), V((2, 4, 4, 128, 256), bf), V((9, 4, 4, 128, 256), bf), V((2, 4, 4, 128, 256), bf),
                        V((4, 2, 4, 32, 256), bf), V((4, 2, 4, 32, 256), bf),
                        V((4, 2, 4, 64, 256), bf), V((4, 2, 4, 64, 256), bf),
                        V((4, 2, 32, 256), bf), V((4, 2, 32, 256), bf),
                        V((4, 2, 64, 256), bf), V((4, 2, 64, 256), bf),
                        V((2, 4, 4, 2, 128, 256), bf), V((256, 1408), jnp.float32), V((3, 4, 64, 1920), bf),
                        V((4, 2, 32, 1920), bf), V((4, 2, 64, 1920), bf),
                        D((11,)), D(()), D((2,)), D((2, 2)), D((nk,)), D((nk,)), D((nk, 16)), D((nk, 16)), D((6, 4)), D((6, 4))],
        compiler_params=pltpu.CompilerParams(collective_id=cid, has_side_effects=True, vmem_limit_bytes=63 << 20),
        name="expert_back",
    )(acts, x, u, gate, up, router, down)


def shards(
    tokens,
    documents,
    expert_routes,
    attention_gain,
    query_weight,
    key_matrix,
    value_matrix,
    output_weight,
    expert_gain,
    router_weight,
    gate_weight,
    up_weight,
    down_weight,
    out_cotangent,
):
    width = tokens.shape[1]
    local_experts = gate_weight.shape[0]
    experts_all = router_weight.shape[1]
    wide = local_experts * gate_weight.shape[2]
    inputs = tokens.astype(jnp.float32)
    first_gain = attention_gain.astype(jnp.float32)
    second_gain = expert_gain.astype(jnp.float32)
    first_scale = lax.rsqrt(jnp.mean(inputs * inputs, -1, keepdims=True) + epsilon)
    tables = attention_tables(documents)
    attention_weights = (query_weight, key_matrix, value_matrix, output_weight)
    router_pad = jnp.pad(router_weight, ((0, 0), (0, 64 - experts_all)))
    expert_weights = (
        gate_weight,
        up_weight,
        jnp.concatenate([router_pad, router_pad], 1),
        down_weight.reshape(wide, width),
    )
    lined_routes = jnp.pad(expert_routes, ((0, 0), (0, 128 - expert_routes.shape[1])))
    (
        residual,
        plane_rows,
        acts,
        plane_upstream,
        group_tokens,
        group_rows,
        queries,
        keys,
        values,
        attended,
        logsum,
    ) = front(
        tokens,
        jnp.concatenate([out_cotangent, lined_routes.astype(jnp.bfloat16)], 1),
        first_gain.reshape(1, width),
        second_gain.reshape(1, width),
        *tables,
        *attention_weights,
        *expert_weights,
        6,
    )
    sums, weight_grads, router_pairs = expert_back(
        acts, plane_rows, plane_upstream, *expert_weights, 2
    )
    layer_output = (residual + sums[0]).astype(jnp.bfloat16)
    weight_grads = lax.all_gather(weight_grads, "dp", axis=0)
    residual_grad, output_part, input_part, normed_part = attention_back(
        sums,
        residual,
        out_cotangent,
        expert_routes,
        second_gain.reshape(1, width),
        expert_weights[2],
        router_pairs,
        group_rows,
        group_tokens.reshape(-1, width),
        *tables,
        queries,
        keys,
        values,
        attended,
        logsum,
        *attention_weights,
        cid=7,
    )
    output_sums, input_sums, normed_grad = grad_sum(output_part, input_part, normed_part, 4)
    input_gradient = residual_grad + norm_back(inputs, first_scale, first_gain, normed_grad)
    (
        gate_gradient,
        up_gradient,
        down_gradient,
        query_gradient,
        key_gradient,
        value_gradient,
        output_gradient,
        router_gradient,
        attention_gain_gradient,
        expert_gain_gradient,
    ) = finish(weight_grads, output_sums, input_sums)
    router_gradient = router_gradient.T
    attention_gain_gradient = attention_gain_gradient.reshape(width)
    expert_gain_gradient = expert_gain_gradient.reshape(width)
    return (
        layer_output,
        input_gradient,
        attention_gain_gradient,
        query_gradient,
        key_gradient,
        value_gradient,
        output_gradient,
        expert_gain_gradient,
        router_gradient,
        gate_gradient,
        up_gradient,
        down_gradient,
    )


def solution(mesh):
    placed = (
        P(("dp", "expert", "tensor"), None),
        P(("dp", "expert")),
        P(("dp", "expert", "tensor"), None),
        P(),
        P(None, "tensor"),
        P(None, "tensor"),
        P(None, "tensor"),
        P("tensor", None),
        P(),
        P(),
        P("expert", None, "tensor"),
        P("expert", None, "tensor"),
        P("expert", "tensor", None),
        P(("dp", "expert", "tensor"), None),
    )
    return jax.shard_map(
        shards,
        mesh=mesh,
        in_specs=placed,
        out_specs=(
            P(("dp", "expert", "tensor"), None),
            P(("dp", "expert", "tensor"), None),
            P(),
            P(None, "tensor"),
            P(None, "tensor"),
            P(None, "tensor"),
            P("tensor", None),
            P(),
            P(),
            P("expert", None, "tensor"),
            P("expert", None, "tensor"),
            P("expert", "tensor", None),
        ),
        check_vma=False,
    )
```

```python
import functools

import jax
import jax.numpy as jnp
from jax import lax
from jax.experimental import pallas as pl
from jax.experimental.pallas import tpu as pltpu
from jax.sharding import PartitionSpec as P


epsilon = 1e-06


def norm_back(value_rows, scale, gain, upstream):
    weighted = upstream * gain
    inner = jnp.mean(weighted * value_rows, -1, keepdims=True)
    return scale * weighted - value_rows * scale**3 * inner


MESH = pl.DeviceIdType.MESH

NT = (((1,), (1,)), ((), ()))
TN = (((0,), (0,)), ((), ()))


def turn(v, cosine, sine):
    lane = lax.broadcasted_iota(jnp.int32, v.shape, 1)
    count = v.shape[1]
    partner = jnp.where(lane % 64 < 32, pltpu.roll(v, count - 32, 1), pltpu.roll(v, 32, 1))
    times = count // 128
    return v * jnp.concatenate([cosine] * times, 1) + partner * jnp.concatenate([sine] * times, 1)


def attend(group, gain, cosine, sine, bias, wq, wk, wv, wo, rows_ref, q_ref, k_ref, v_ref, mixed_ref, logsum_ref, part_ref):
    f32, low = jnp.float32, jnp.bfloat16
    t = group[...].reshape(512, 1536).astype(f32)
    scale = lax.rsqrt(jnp.mean(t * t, -1, keepdims=True) + epsilon)
    rows_ref[...] = (t * scale * gain[...]).astype(low)
    rows = rows_ref[...]
    cos, sin = cosine[...], sine[...]
    q_ref[...] = (turn(jnp.dot(rows, wq[...], preferred_element_type=f32), cos, sin) * 0.125).astype(low)
    k_ref[...] = turn(jnp.dot(rows, wk[...], preferred_element_type=f32), cos, sin).astype(low)
    v_ref[...] = jnp.dot(rows, wv[...], preferred_element_type=f32).astype(low)
    lane = lax.broadcasted_iota(jnp.int32, (512, 128), 1)
    logsum = jnp.zeros((512, 128), f32)
    for h in range(6):
        kv = slice(64 * (h // 3), 64 * (h // 3) + 64)
        s = lax.dot_general(q_ref[:, 64 * h : 64 * h + 64], k_ref[:, kv], NT, preferred_element_type=f32) + bias[...]
        top = jnp.max(s, -1, keepdims=True)
        p = jnp.exp(s - top)
        total = jnp.sum(p, -1, keepdims=True)
        mixed = jnp.dot(p.astype(low), v_ref[:, kv], preferred_element_type=f32) / total
        mixed_ref[:, 64 * h : 64 * h + 64] = mixed.astype(low)
        logsum = jnp.where(lane == h, top + jnp.log(total), logsum)
    logsum_ref[...] = logsum
    part_ref[...] = jnp.dot(mixed_ref[...], wo[...], preferred_element_type=f32).astype(low).reshape(4, 128, 1536)


def weight_loads(gate, up, router, w, sem):
    return (
        [pltpu.make_async_copy(gate.at[n], w.at[:, pl.ds(128 * n, 128)], sem.at[n]) for n in range(5)]
        + [pltpu.make_async_copy(up.at[n], w.at[:, pl.ds(640 + 128 * n, 128)], sem.at[5 + n]) for n in range(5)]
        + [pltpu.make_async_copy(router, w.at[:, pl.ds(1280, 128)], sem.at[10])]
    )


PAIRS = ((0, 0), (1, 0), (3, 0), (0, 1), (0, 3), (2, 0), (0, 2), (1, 1), (1, 3), (3, 1), (3, 3), (2, 1), (2, 3), (1, 2), (3, 2), (2, 2))


class PlaneGather:
    def __init__(self, place, own, peer, sibling, core, send_sem, recv_sem, sib_send, sib_recv, starts, by_columns=False):
        self.starts, self.by_columns = starts, by_columns
        self.place, self.own, self.peer, self.sibling, self.core = place, own, peer, sibling, core
        self.send_sem, self.recv_sem, self.sib_send, self.sib_recv = send_sem, recv_sem, sib_send, sib_recv
        self.later = []

    def copy(self, dx, dz, ox, oz, q, nq, n, own):
        quarter = pl.ds(self.starts[q], self.starts[q + nq] - self.starts[q])
        quarter = (slice(None), quarter) if self.by_columns else quarter
        there = self.place(dx, dz, self.core).at[quarter]
        return pltpu.make_async_remote_copy(
            src_ref=self.own.at[quarter] if own and self.own is not None else there, dst_ref=there,
            send_sem=self.send_sem.at[n], recv_sem=self.recv_sem.at[(dx - ox) % 4, (dz - oz) % 4, q],
            device_id=self.peer(ox, oz), device_id_type=MESH)

    def send(self, dx, dz, ox, oz, q, nq, own=False):
        if self.starts[q] == self.starts[q + nq]:
            return
        make = functools.partial(self.copy, dx, dz, ox, oz, q, nq, len(self.later), own)
        make().start()
        self.later.append(make)

    def recv(self, dx, dz, q, nq):
        if self.starts[q] == self.starts[q + nq]:
            return
        self.copy(dx, dz, 0, 0, q, nq, 0, False).wait_recv()

    def sib_copy(self, core, dx, dz, own=False):
        there = self.place(dx, dz, core)
        return pltpu.make_async_remote_copy(
            src_ref=self.own if own else there, dst_ref=there,
            send_sem=self.sib_send.at[dx % 4, dz % 4], recv_sem=self.sib_recv.at[dx % 4, dz % 4],
            device_id=self.sibling, device_id_type=MESH)

    def sib_pass(self, dx, dz, own=False):
        make = functools.partial(self.sib_copy, self.core, dx, dz, own)
        make().start()
        self.later.append(make)

    def start(self, directions):
        for ox, oz in directions:
            self.send(0, 0, ox, oz, 0, 4, own=True)

    def wave1x(self):
        for s in (1, -1):
            self.recv(s, 0, 0, 4)
            if s == -1:
                self.send(s, 0, 1, 0, 1, 2)
            else:
                self.send(s, 0, -1, 0, 0, 1)
                self.send(s, 0, -1, 0, 3, 1)
            for oz in (1, -1):
                self.send(s, 0, 0, oz, 0, 2)
            self.sib_pass(s, 0)

    def wave1z(self):
        for s in (1, -1):
            self.recv(0, s, 0, 4)
            if s == -1:
                self.send(0, s, 0, 1, 1, 2)
            else:
                self.send(0, s, 0, -1, 0, 1)
                self.send(0, s, 0, -1, 3, 1)
            for ox in (1, -1):
                self.send(0, s, ox, 0, 2, 2)
            self.sib_pass(0, s)

    def wave1(self):
        self.wave1x()
        self.wave1z()

    def wave2(self):
        for q, nq in ((1, 2), (0, 1), (3, 1)):
            self.recv(2, 0, q, nq)
        for oz in (1, -1):
            self.send(2, 0, 0, oz, 0, 2)
        for q, nq in ((1, 2), (0, 1), (3, 1)):
            self.recv(0, 2, q, nq)
        for ox in (1, -1):
            self.send(0, 2, ox, 0, 2, 2)
        self.sib_pass(2, 0)
        self.sib_pass(0, 2)
        for dx in (1, -1):
            for s in (1, -1):
                self.recv(dx, s, 0, 2)
                self.send(dx, s, 0, -s, 0 if s == 1 else 1, 1)
                self.recv(s, dx, 2, 2)
                self.send(s, dx, -s, 0, 2 if s == 1 else 3, 1)
        for dx in (1, -1):
            for dz in (1, -1):
                self.sib_pass(dx, dz)

    def wave3(self):
        for s in (1, -1):
            self.recv(2, s, 0, 2)
            self.send(2, s, 0, -s, 0 if s == 1 else 1, 1)
            self.recv(s, 2, 2, 2)
            self.send(s, 2, -s, 0, 2 if s == 1 else 3, 1)
        for d in (1, -1):
            for q in (0, 1):
                self.recv(d, 2, q, 1)
                self.recv(2, d, q + 2, 1)
        for d in (1, -1):
            self.sib_pass(d, 2)
            self.sib_pass(2, d)

    def wave4(self):
        for q in range(4):
            self.recv(2, 2, q, 1)
        self.sib_pass(2, 2)

    def finish(self):
        for make in self.later:
            make().wait_send()


def front_kernel(tokens, u_own, first_gain, second_gain, cosine, sine, bias, wq, wk, wv, wo, gate_hbm, up_hbm, router_hbm, down_hbm,
                 residual, rows_out, acts_out, u_hbm, group, normed, queries, keys, values, mixed, logsum,
                 part, nr1, nb, nr2, rows, w, down, u_buf, act_buf,
                 gsend, grecv, own_sem, nsend, nrecv, send_sem, recv_sem, sib_send, sib_recv,
                 u_send, u_recv, u_sib_send, u_sib_recv, w_sem, down_sem, u_sem, act_sem, out_sem):
    f32, low = jnp.float32, jnp.bfloat16
    wide = 640
    width = 1536
    x = lax.axis_index("tensor"); e = lax.axis_index("expert")
    z = e // 2; c = e % 2
    first = e * 5
    def xi(d): return (x + d) % 4
    def zi(d): return (z + d) % 4
    def peer(ox, oz):
        return {"expert": zi(oz) * 2 + c, "tensor": xi(ox)}
    sib = {"expert": z * 2 + 1 - c}
    def pair(step):
        if isinstance(step, int):
            return PAIRS[step]
        dx = dz = 0
        for n in range(4):
            here = lax.convert_element_type(step // 4 == n, jnp.int32)
            dx = dx + here * sum(PAIRS[4 * n + m][0] * 4**m for m in range(4))
            dz = dz + here * sum(PAIRS[4 * n + m][1] * 4**m for m in range(4))
        for n in range(3):
            more = lax.convert_element_type(step % 4 > n, jnp.int32)
            dx = dx // (1 + 3 * more)
            dz = dz // (1 + 3 * more)
        dx, dz = dx % 4, dz % 4
        return dx, dz
    def u_loads(step):
        dx, dz = pair(step)
        return pltpu.make_async_copy(u_hbm.at[zi(dz), xi(dx)], u_buf.at[step % 2], u_sem.at[step % 2])
    loads = weight_loads(gate_hbm, up_hbm, router_hbm, w, w_sem) + [pltpu.make_async_copy(down_hbm, down, down_sem)]
    for cp in loads: cp.start()
    barrier = pltpu.get_barrier_semaphore()
    near = [peer(1, 0), peer(-1, 0), peer(0, 1), peer(0, -1), sib]
    for p in near:
        pl.semaphore_signal(barrier, inc=1, device_id=p, device_id_type=MESH)
    pl.semaphore_wait(barrier, len(near))
    pend = []
    def go(cps):
        for cp in cps: cp.start()
        pend.extend(cps)
        return cps
    def block_of(ref):
        return lambda dx, dz, core: ref.at[zi(dz), xi(dx), core]
    cots = PlaneGather(block_of(u_hbm), u_own, peer, sib, c, u_send, u_recv, u_sib_send, u_sib_recv, (0, 48, 96, 112, 128))
    norms = PlaneGather(block_of(rows), rows.at[z, x, c], peer, sib, c, send_sem, recv_sem, sib_send, sib_recv, (0, 16, 32, 80, 128))
    def tok(n, block, half, to, own):
        there = group.at[block, pl.ds(64 * half, 64)]
        return pltpu.make_async_remote_copy(
            src_ref=tokens.at[pl.ds(64 * half, 64)] if own else there, dst_ref=there,
            send_sem=gsend.at[n], recv_sem=grecv.at[n], device_id=peer(to, 0), device_id_type=MESH)
    go([tok(0, x, 0, 1, True), tok(2, x, 1, -1, True)])
    go([tok(1, x, 1, 1, True), tok(3, x, 0, -1, True)])
    mine = pltpu.make_async_copy(u_own, u_hbm.at[z, x, c], own_sem)
    mine.start()
    cots.start(((0, 1), (0, -1)))
    group[x] = tokens[...]
    tok(0, xi(-1), 0, 1, False).wait_recv()
    go([tok(4, xi(-1), 0, 1, False)])
    tok(2, xi(1), 1, -1, False).wait_recv()
    go([tok(5, xi(1), 1, -1, False)])
    cots.start(((1, 0), (-1, 0)))
    cots.sib_pass(0, 0, own=True)
    tok(1, xi(-1), 1, 1, False).wait_recv()
    tok(3, xi(1), 0, -1, False).wait_recv()
    tok(4, xi(2), 0, 1, False).wait_recv()
    tok(5, xi(2), 1, -1, False).wait_recv()
    attend(group, first_gain, cosine, sine, bias, wq, wk, wv, wo, normed, queries, keys, values, mixed, logsum, part)
    def nrc(n, src, dst, to):
        return pltpu.make_async_remote_copy(src_ref=src, dst_ref=dst, send_sem=nsend.at[n], recv_sem=nrecv.at[n],
                                            device_id=peer(to, 0), device_id_type=MESH)
    n1 = go([nrc(0, part.at[xi(2), pl.ds(0, 64)], nr1.at[0], 1), nrc(1, part.at[xi(2), pl.ds(64, 64)], nr1.at[1], -1)])
    n2 = go([nrc(2, part.at[xi(1), pl.ds(64, 64)], nr2.at[0, pl.ds(64, 64)], 1),
             nrc(3, part.at[xi(-1), pl.ds(0, 64)], nr2.at[1, pl.ds(0, 64)], -1)])
    cots.wave1()
    mine.wait()
    cots.sib_copy(1 - c, 0, 0).wait_recv()
    u_loads(0).start()
    n1[0].wait_recv()
    nb[0] = (part[xi(1), 0:64].astype(f32) + nr1[0].astype(f32)).astype(low)
    n3 = go([nrc(4, nb.at[0], nr2.at[0, pl.ds(0, 64)], 1)])
    n1[1].wait_recv()
    nb[1] = (part[xi(-1), 64:128].astype(f32) + nr1[1].astype(f32)).astype(low)
    n3 += go([nrc(5, nb.at[1], nr2.at[1, pl.ds(64, 64)], -1)])
    for cp in n2 + n3: cp.wait_recv()
    total = tokens[...].astype(f32) + part[x].astype(f32) + nr2[0].astype(f32) + nr2[1].astype(f32)
    residual[...] = total
    scale = lax.rsqrt(jnp.mean(total * total, -1, keepdims=True) + epsilon)
    rows[z, x, c] = (total * scale * second_gain[...]).astype(low)
    norms.start(((1, 0), (-1, 0), (0, 1), (0, -1)))
    norms.sib_pass(0, 0, own=True)
    for cp in loads: cp.wait()

    def act_store(step):
        dx, dz = pair(step)
        return pltpu.make_async_copy(act_buf.at[step % 2], acts_out.at[zi(dz), xi(dx)].reshape(256, 2048), act_sem.at[step % 2])
    def row_store(step):
        dx, dz = pair(step)
        there = (zi(dz), xi(dx))
        return pltpu.make_async_copy(rows.at[there], rows_out.at[there], out_sem.at[step])
    def compute(step):
        dx, dz = pair(step)
        norms.sib_copy(1 - c, dx, dz).wait_recv()
        u_loads(step).wait()
        @pl.when(step < 15)
        def _():
            nx, nz = pair(step + 1)
            cots.sib_copy(1 - c, nx, nz).wait_recv()
            u_loads(step + 1).start()
        row_store(step).start()
        @pl.when(step >= 2)
        def _(): act_store(step - 2).wait()
        slot = step % 2
        here = act_buf.at[slot]
        pre = jnp.dot(rows[zi(dz), xi(dx)].reshape(256, width), w[...], preferred_element_type=f32)
        raw = lax.dot_general(u_buf[slot, :, :, 0:width].reshape(256, width), down[...], (((1,), (1,)), ((), ())), preferred_element_type=f32)
        lane = lax.broadcasted_iota(jnp.int32, (256, 128), 1)
        routes = u_buf[slot, :, :, width:].reshape(256, 128).astype(f32).astype(jnp.int32)
        named = lane == routes[:, 0:1]
        for n in range(1, 8):
            named = named | (lane == routes[:, n : n + 1])
        logits = jnp.where(named, pre[:, 2 * wide :], -1e30)
        raised = jnp.exp(logits - jnp.max(logits, -1, keepdims=True))
        gates = raised / jnp.sum(raised, -1, keepdims=True)
        weighted = jnp.zeros((256, 128), f32)
        for n in range(5):
            cols = slice(128 * n, 128 * (n + 1))
            gate = jnp.sum(jnp.where(lane == first + n, gates, 0.0), -1, keepdims=True)
            gate_pre = pre[:, cols]
            up_pre = pre[:, wide + 128 * n : wide + 128 * (n + 1)]
            sig = jax.nn.sigmoid(gate_pre)
            silu = gate_pre * sig
            active = silu * up_pre
            back = raw[:, cols]
            share = gate * jnp.sum(active * back, -1, keepdims=True)
            high = share.astype(low).astype(f32)
            weighted = weighted + jnp.where(lane == first + n, high, 0.0)
            weighted = weighted + jnp.where(lane == first + n + 64, share - high, 0.0)
            back = gate * back
            here[:, cols] = (gate * active).astype(low)
            here[:, wide + 128 * n : wide + 128 * (n + 1)] = (
                back * up_pre * (sig * (1.0 + gate_pre * (1.0 - sig)))
            ).astype(low)
            here[:, 2 * wide + 128 * n : 2 * wide + 128 * (n + 1)] = (back * silu).astype(low)
        here[:, 3 * wide :] = weighted.astype(low)
        act_store(step).start()

    events = ((0, cots.wave2), (1, norms.wave1), (3, cots.wave3), (5, norms.wave2), (7, cots.wave4), (9, norms.wave3), (13, norms.wave4))
    def body(step, _):
        for at, wave in events:
            @pl.when(step == at)
            def _():
                wave()
        compute(step)
        return 0
    lax.fori_loop(0, 16, body, 0)
    act_store(14).wait()
    act_store(15).wait()
    for n in range(16): row_store(n).wait()
    for cp in pend: cp.wait_send()
    cots.finish()
    norms.finish()


def front(tokens, u, first_gain, second_gain, cosine, sine, bias, wq, wk, wv, wo, gate, up, router, down, cid):
    bf, f32 = jnp.bfloat16, jnp.float32
    V = pltpu.VMEM
    D = pltpu.SemaphoreType.DMA
    S = jax.ShapeDtypeStruct
    vm = pl.BlockSpec(memory_space=pltpu.VMEM)
    anym = pl.BlockSpec(memory_space=pl.ANY)
    n, width = tokens.shape
    return pl.pallas_call(
        front_kernel,
        out_shape=(S((n, width), f32), S((4, 4, 2, n, width), bf), S((4, 4, 2, n, 2048), bf), S((4, 4, 2, n, 1664), bf),
                   S((4, n, width), bf), S((512, width), bf), S((512, 384), bf), S((512, 128), bf), S((512, 128), bf),
                   S((512, 384), bf), S((512, 128), f32)),
        in_specs=[vm, anym] + [vm] * 9 + [anym] * 4,
        out_specs=(vm, anym, anym, anym) + (vm,) * 7,
        scratch_shapes=[V((4, n, width), bf), V((2, 64, width), bf), V((2, 64, width), bf), V((2, 128, width), bf),
                        V((4, 4, 2, n, width), bf), V((width, 1408), bf), V((640, width), bf),
                        V((2, 2, n, 1664), bf), V((2, 256, 2048), bf),
                        D((6,)), D((6,)), D(()), D((6,)), D((6,)), D((64,)), D((4, 4, 4)), D((4, 4)), D((4, 4)),
                        D((64,)), D((4, 4, 4)), D((4, 4)), D((4, 4)),
                        D((11,)), D(()), D((2,)), D((2,)), D((16,))],
        compiler_params=pltpu.CompilerParams(collective_id=cid, has_side_effects=True, vmem_limit_bytes=60 << 20),
        name="front",
    )(tokens, u, first_gain, second_gain, cosine, sine, bias, wq, wk, wv, wo, gate, up, router, down)


class TorusSum:
    def __init__(self, g, out, scratch, sems, starts, place, with_extra):
        self.with_extra = with_extra
        (self.q, self.sib, self.a3, self.a3b, self.b3, self.b3b, self.a4, self.b4,
         self.a5, self.a5b, self.b5, self.b5b, self.a6, self.b6, self.extra) = scratch
        self.ssem, self.rsem, gsend, grecv, gsib_send, gsib_recv = sems
        self.g, self.out = g, out
        self.z, self.y, self.c, self.zi, self.yi, self.peer, self.xpeer, self.partner = place
        self.parts = [pl.ds(starts[n], starts[n + 1] - starts[n]) for n in range(4)]
        self.A = pl.ds(0, starts[2])
        self.B = pl.ds(starts[2], starts[4] - starts[2])
        self.sent = []
        self.back = PlaneGather(
            lambda dy, dz, core: out.at[core, self.zi(dz), self.yi(dy)], None, lambda oy, oz: self.peer(oz, oy), self.partner, self.c,
            gsend, grecv, gsib_send, gsib_recv, starts, True)

    def rc(self, n, src, dst, to):
        return pltpu.make_async_remote_copy(src_ref=src, dst_ref=dst, send_sem=self.ssem.at[n], recv_sem=self.rsem.at[n],
                                            device_id=to, device_id_type=MESH)

    def go(self, cps):
        for cp in cps:
            cp.start()
        self.sent.extend(cps)
        return cps

    def add(self, i, j, cols, *terms):
        t = self.q[i, j, :, cols].astype(jnp.float32)
        for s in terms:
            t = t + s.astype(jnp.float32)
        self.q[i, j, :, cols] = t.astype(jnp.bfloat16)

    def stage1(self):
        self.c1 = self.go([self.rc(16, self.g.at[1 - self.c], self.sib, self.partner)])

    def stage2(self):
        q, zi, yi, peer = self.q, self.zi, self.yi, self.peer
        A0, A1, B0, B1 = self.parts
        self.c1[0].wait_recv()
        def body(n, _):
            i, j = n // 4, n % 4
            q[i, j] = (self.g[self.c, i, j].astype(jnp.float32) + self.sib[i, j].astype(jnp.float32)).astype(jnp.bfloat16)
            return 0
        lax.fori_loop(0, 16, body, 0)
        self.c3 = self.go([self.rc(0, q.at[zi(2), :, :, A0], self.a3, peer(1, 0)),
                           self.rc(1, q.at[zi(2), :, :, A1], self.a3b, peer(-1, 0)),
                           self.rc(2, q.at[:, yi(2), :, B0], self.b3, peer(0, 1)),
                           self.rc(3, q.at[:, yi(2), :, B1], self.b3b, peer(0, -1))])

    def stage4(self):
        q, zi, yi, peer, A, B = self.q, self.zi, self.yi, self.peer, self.A, self.B
        A0, A1, B0, B1 = self.parts
        for cp in self.c3: cp.wait_recv()
        def body(n, _):
            self.add(zi(1), n, A0, self.a3[n])
            self.add(zi(-1), n, A1, self.a3b[n])
            self.add(n, yi(1), B0, self.b3[n])
            self.add(n, yi(-1), B1, self.b3b[n])
            return 0
        lax.fori_loop(0, 4, body, 0)
        self.c4 = self.go([self.rc(4, q.at[zi(1), :, :, A], self.a4.at[0], peer(1, 0)),
                           self.rc(5, q.at[zi(-1), :, :, A], self.a4.at[1], peer(-1, 0)),
                           self.rc(6, q.at[:, yi(1), :, B], self.b4.at[0], peer(0, 1)),
                           self.rc(7, q.at[:, yi(-1), :, B], self.b4.at[1], peer(0, -1))])

    def stage5(self):
        q, z, y, zi, yi, peer = self.q, self.z, self.y, self.zi, self.yi, self.peer
        A0, A1, B0, B1 = self.parts
        for cp in self.c4: cp.wait_recv()
        def body(n, _):
            self.add(z, n, self.A, self.a4[0, n], self.a4[1, n])
            self.add(n, y, self.B, self.b4[0, n], self.b4[1, n])
            return 0
        lax.fori_loop(0, 4, body, 0)
        self.c5 = self.go([self.rc(8, q.at[z, yi(2), :, A0], self.a5, peer(0, 1)),
                           self.rc(9, q.at[z, yi(2), :, A1], self.a5b, peer(0, -1)),
                           self.rc(10, q.at[zi(2), y, :, B0], self.b5, peer(1, 0)),
                           self.rc(11, q.at[zi(2), y, :, B1], self.b5b, peer(-1, 0))])

    def stage6(self):
        q, z, y, zi, yi, peer, A, B = self.q, self.z, self.y, self.zi, self.yi, self.peer, self.A, self.B
        A0, A1, B0, B1 = self.parts
        for cp in self.c5: cp.wait_recv()
        self.add(z, yi(1), A0, self.a5[...])
        self.add(z, yi(-1), A1, self.a5b[...])
        self.add(zi(1), y, B0, self.b5[...])
        self.add(zi(-1), y, B1, self.b5b[...])
        self.c6 = self.go([self.rc(12, q.at[z, yi(1), :, A], self.a6.at[0], peer(0, 1)),
                           self.rc(13, q.at[z, yi(-1), :, A], self.a6.at[1], peer(0, -1)),
                           self.rc(14, q.at[zi(1), y, :, B], self.b6.at[0], peer(1, 0)),
                           self.rc(15, q.at[zi(-1), y, :, B], self.b6.at[1], peer(-1, 0))])

    def stage7(self):
        f32, low = jnp.float32, jnp.bfloat16
        q, z, y = self.q, self.z, self.y
        for cp in self.c6: cp.wait_recv()
        own = self.out.at[self.c, z, y]
        own[:, self.A] = (q[z, y, :, self.A].astype(f32) + self.a6[0].astype(f32) + self.a6[1].astype(f32)).astype(low)
        last = (q[z, y, :, self.B].astype(f32) + self.b6[0].astype(f32) + self.b6[1].astype(f32)).astype(low)
        wide = last.shape[1] - (128 if self.with_extra else 0)
        own[:, pl.ds(self.B.start, wide)] = last[:, 0:wide]
        if not self.with_extra:
            return
        self.extra[0] = last[:, wide:]
        self.cx = self.go([self.rc(16 + o, self.extra.at[0], self.extra.at[o], self.xpeer(o)) for o in (1, 2, 3)])

    def start_back(self):
        f32 = jnp.float32
        if self.with_extra:
            for cp in self.cx: cp.wait_recv()
            extra = self.extra
            total = extra[0].astype(f32) + extra[1].astype(f32) + extra[2].astype(f32) + extra[3].astype(f32)
            self.out[self.c, self.z, self.y, :, pl.ds(self.B.start + self.B.size - 128, 128)] = total.astype(jnp.bfloat16)
        self.back.start(((1, 0), (-1, 0), (0, 1), (0, -1)))
        self.back.sib_pass(0, 0)

    def finish(self):
        for dy in range(4):
            for dz in range(4):
                self.back.sib_copy(1 - self.c, dy, dz).wait_recv()
        for cp in self.sent: cp.wait_send()
        self.back.finish()


def sum_scratch(starts):
    V, bf = pltpu.VMEM, jnp.bfloat16
    w = [starts[n + 1] - starts[n] for n in range(4)]
    a, b = w[0] + w[1], w[2] + w[3]
    D = pltpu.SemaphoreType.DMA
    return ([V((4, 4, 48, a + b), bf)] * 2 + [V((4, 48, n), bf) for n in w] + [V((2, 4, 48, a), bf), V((2, 4, 48, b), bf)]
            + [V((48, n), bf) for n in w] + [V((2, 48, a), bf), V((2, 48, b), bf), V((4, 48, 128), bf)]
            + [D((20,)), D((20,)), D((64,)), D((4, 4, 4)), D((4, 4)), D((4, 4))])


OUTPUT_PARTS = (0, 128, 256, 384, 512)
INPUT_PARTS = (0, 256, 384, 512, 640)


BACK_INPUTS = (
    ((2, 128, 1536), "float32"), ((128, 1536), "float32"), ((128, 1536), "bfloat16"), ((128, 8), "int32"), ((1, 1536), "float32"),
    ((1536, 128), "bfloat16"), ((1536, 128), "float32"), ((512, 1536), "bfloat16"), ((512, 1536), "bfloat16"), ((512, 128), "float32"),
    ((512, 128), "float32"), ((512, 512), "float32"), ((512, 384), "bfloat16"), ((512, 128), "bfloat16"), ((512, 128), "bfloat16"),
    ((512, 384), "bfloat16"), ((512, 128), "float32"), ((1536, 384), "bfloat16"), ((1536, 128), "bfloat16"), ((1536, 128), "bfloat16"),
    ((384, 1536), "bfloat16"),
)


def attention_back_kernel(*refs):
    count = len(BACK_INPUTS)
    given, (residual_grad, o_out, i_out, n_out) = refs[:count], refs[count : count + 4]
    held = refs[count + 4 : 2 * count + 4]
    (sums, residual, cotangent, routes, second_gain, router, router_pairs, rows, group, cosine, sine, bias, q, k, v, mixed, logsum,
     wq, wk, wv, wo) = held
    (branch, grad, probs, back, turned_t, q_back, k_back, v_back, k_acc, v_acc, gsend, grecv, load_sem) = refs[2 * count + 4 :]
    loads = [pltpu.make_async_copy(a, b, load_sem.at[n]) for n, (a, b) in enumerate(zip(given, held))]
    for cp in loads: cp.start()
    f32, low = jnp.float32, jnp.bfloat16
    x = lax.axis_index("tensor")
    def xi(d): return (x + d) % 4
    def xpeer(o):
        return {"tensor": xi(o)}
    barrier = pltpu.get_barrier_semaphore()
    for o in (1, -1):
        pl.semaphore_signal(barrier, inc=1, device_id=xpeer(o), device_id_type=MESH)
    pl.semaphore_wait(barrier, 2)
    sent = []
    def go(cps):
        for cp in cps: cp.start()
        sent.extend(cps)
        return cps
    for cp in loads[:6]: cp.wait()
    res = residual[...]
    scale = lax.rsqrt(jnp.mean(res * res, -1, keepdims=True) + epsilon)
    normed = (res * scale * second_gain[...]).astype(low)
    lane = lax.broadcasted_iota(jnp.int32, (128, 128), 1)
    named = lane == routes[:, 0:1]
    for n in range(1, 8):
        named = named | (lane == routes[:, n : n + 1])
    logits = jnp.where(named, jnp.dot(normed, router[...], preferred_element_type=f32), -1e30)
    raised = jnp.exp(logits - jnp.max(logits, -1, keepdims=True))
    gates = raised / jnp.sum(raised, -1, keepdims=True)
    upstream = cotangent[...].astype(f32)
    shared = gates * jnp.sum(sums[0] * upstream, -1, keepdims=True)
    high = shared.astype(low).astype(f32)
    shared = jnp.where(lane < 64, high, pltpu.roll(shared - high, 64, 1)).astype(low)
    normed_back = sums[1] - lax.dot_general(shared, router[...], NT, preferred_element_type=f32)
    weighted = normed_back * second_gain[...]
    inner = jnp.mean(weighted * res, -1, keepdims=True)
    total = upstream + scale * weighted - res * scale**3 * inner
    residual_grad[...] = total
    branch[...] = total.astype(low)
    def ring(n, block, part, to, own):
        there = grad.at[block, pl.ds(64 * part, 64)]
        return pltpu.make_async_remote_copy(
            src_ref=branch.at[pl.ds(64 * part, 64)] if own else there, dst_ref=there,
            send_sem=gsend.at[n], recv_sem=grecv.at[n], device_id=xpeer(to), device_id_type=MESH)
    go([ring(0, x, 0, 1, True), ring(2, x, 1, -1, True)])
    go([ring(1, x, 1, 1, True), ring(3, x, 0, -1, True)])
    grad[x] = branch[...]
    for cp in loads[6:]: cp.wait()
    k_t = k[...].astype(f32).T.astype(low)
    logsum_t = logsum[...].T
    bias_t = bias[...].T
    def heads(h):
        one = slice(64 * h, 64 * h + 64)
        kv = slice(64 * (h // 3), 64 * (h // 3) + 64)
        s = lax.dot_general(k[:, kv], q[:, one], NT, preferred_element_type=f32) + bias_t
        probs[h] = jnp.exp(s - logsum_t[h : h + 1, :])
    for h in range(2): heads(h)
    ones = jnp.ones((128, 128), low)
    gain_two = lax.dot_general((normed_back * res * scale).astype(low), ones, TN, preferred_element_type=f32)
    extras = router_pairs[...] - lax.dot_general(normed, shared, TN, preferred_element_type=f32)
    extras = extras + pltpu.roll(extras, 64, 1)
    ring(0, xi(-1), 0, 1, False).wait_recv()
    go([ring(4, xi(-1), 0, 1, False)])
    ring(2, xi(1), 1, -1, False).wait_recv()
    go([ring(5, xi(1), 1, -1, False)])
    for h in range(2, 6): heads(h)
    ring(1, xi(-1), 1, 1, False).wait_recv()
    ring(3, xi(1), 0, -1, False).wait_recv()
    ring(4, xi(2), 0, 1, False).wait_recv()
    ring(5, xi(2), 1, -1, False).wait_recv()

    all_grad = grad[...].reshape(512, 1536)
    o_out[:, 0:384] = lax.dot_general(all_grad, mixed[...], TN, preferred_element_type=f32).astype(low)
    back[...] = lax.dot_general(all_grad, wo[...], NT, preferred_element_type=f32).astype(low)
    for h in range(6):
        one = slice(64 * h, 64 * h + 64)
        kv = slice(64 * (h // 3), 64 * (h // 3) + 64)
        p = probs[h]
        grad_p = lax.dot_general(v[:, kv], back[:, one], NT, preferred_element_type=f32)
        both = p * grad_p
        inner = jnp.sum(both, 0, keepdims=True)
        grad_s = (both - p * inner).astype(low)
        v_part = jnp.dot(p.astype(low), back[:, one], preferred_element_type=f32)
        k_part = jnp.dot(grad_s, q[:, one], preferred_element_type=f32)
        if h % 3 == 0:
            v_acc[:, kv] = v_part
            k_acc[:, kv] = k_part
        else:
            v_acc[:, kv] += v_part
            k_acc[:, kv] += k_part
        turned_t[one, :] = jnp.dot(k_t[kv, :], grad_s, preferred_element_type=f32)
    cos, sin = cosine[...], -sine[...]
    q_back[...] = turn(turned_t[...].T * 0.125, cos, sin).astype(low)
    k_back[...] = turn(k_acc[...], cos, sin).astype(low)
    v_back[...] = v_acc[...].astype(low)
    part = (
        lax.dot_general(q_back[...], wq[...], NT, preferred_element_type=f32)
        + lax.dot_general(k_back[...], wk[...], NT, preferred_element_type=f32)
        + lax.dot_general(v_back[...], wv[...], NT, preferred_element_type=f32)
    )
    n_out[...] = part.astype(low)
    t = group[...].astype(f32)
    t = t * lax.rsqrt(jnp.mean(t * t, -1, keepdims=True) + epsilon)
    ones = jnp.ones((512, 128), low)
    gain_part = lax.dot_general((part * t).astype(low), ones, TN, preferred_element_type=f32)
    lane = lax.broadcasted_iota(jnp.int32, (1536, 128), 1)
    o_out[:, 384:512] = jnp.where(lane == 40, gain_part, jnp.where(lane == 41, gain_two, extras)).astype(low)
    i_out[:, 0:384] = lax.dot_general(rows[...], q_back[...], TN, preferred_element_type=f32).astype(low)
    i_out[:, 384:512] = lax.dot_general(rows[...], k_back[...], TN, preferred_element_type=f32).astype(low)
    i_out[:, 512:640] = lax.dot_general(rows[...], v_back[...], TN, preferred_element_type=f32).astype(low)
    for cp in sent: cp.wait_send()


def attention_back(*operands, cid):
    S = jax.ShapeDtypeStruct
    bf, f32 = jnp.bfloat16, jnp.float32
    V = pltpu.VMEM
    D = pltpu.SemaphoreType.DMA
    return pl.pallas_call(
        attention_back_kernel,
        out_shape=(S((128, 1536), f32), S((1536, 512), bf), S((1536, 640), bf), S((512, 1536), bf)),
        in_specs=[pl.BlockSpec(memory_space=pl.ANY)] * len(BACK_INPUTS),
        out_specs=(pl.BlockSpec(memory_space=pltpu.VMEM),) * 4,
        scratch_shapes=[V(shape, jnp.dtype(kind)) for shape, kind in BACK_INPUTS]
        + [V((128, 1536), bf), V((4, 128, 1536), bf), V((6, 512, 512), f32), V((512, 384), bf), V((384, 512), f32),
           V((512, 384), bf), V((512, 128), bf), V((512, 128), bf), V((512, 128), f32), V((512, 128), f32), D((6,)), D((6,)),
           D((len(BACK_INPUTS),))],
        compiler_params=pltpu.CompilerParams(collective_id=cid, has_side_effects=True, vmem_limit_bytes=60 << 20),
        name="attention_back",
    )(*operands)


def grad_sum_kernel(o_sum, i_sum, n_part, o_out, i_out, n_out, nr1, nb, nr2, nsend, nrecv, *scratch):
    f32, low = jnp.float32, jnp.bfloat16
    x = lax.axis_index("tensor"); e = lax.axis_index("expert"); y = lax.axis_index("dp")
    z = e // 2; c = e % 2
    def zi(d): return (z + d) % 4
    def yi(d): return (y + d) % 4
    def xi(d): return (x + d) % 4
    def peer(oz, oy):
        return {"expert": zi(oz) * 2 + c, "dp": yi(oy)}
    def xpeer(o):
        return {"tensor": xi(o)}
    partner = {"expert": z * 2 + 1 - c}
    barrier = pltpu.get_barrier_semaphore()
    near = [peer(1, 0), peer(-1, 0), peer(0, 1), peer(0, -1), partner, xpeer(1), xpeer(2), xpeer(3)]
    for p in near:
        pl.semaphore_signal(barrier, inc=1, device_id=p, device_id_type=MESH)
    pl.semaphore_wait(barrier, len(near))
    sent = []
    def go(cps):
        for cp in cps: cp.start()
        sent.extend(cps)
        return cps
    place = (z, y, c, zi, yi, peer, xpeer, partner)
    half = len(scratch) // 2
    osum = TorusSum(o_sum, o_out, scratch[:15], scratch[15:half], OUTPUT_PARTS, place, True)
    isum = TorusSum(i_sum, i_out, scratch[half : half + 15], scratch[half + 15 :], INPUT_PARTS, place, False)
    osum.stage1()
    def nrc(n, src, dst, to):
        return pltpu.make_async_remote_copy(src_ref=src, dst_ref=dst, send_sem=nsend.at[n], recv_sem=nrecv.at[n],
                                            device_id=xpeer(to), device_id_type=MESH)
    n1 = go([nrc(0, n_part.at[xi(2), pl.ds(0, 64)], nr1.at[0], 1), nrc(1, n_part.at[xi(2), pl.ds(64, 64)], nr1.at[1], -1)])
    n2 = go([nrc(2, n_part.at[xi(1), pl.ds(64, 64)], nr2.at[0, pl.ds(64, 64)], 1),
             nrc(3, n_part.at[xi(-1), pl.ds(0, 64)], nr2.at[1, pl.ds(0, 64)], -1)])
    isum.stage1()
    osum.stage2()
    isum.stage2()
    for cp in n1: cp.wait_recv()
    nb[0] = (n_part[xi(1), 0:64].astype(f32) + nr1[0].astype(f32)).astype(low)
    nb[1] = (n_part[xi(-1), 64:128].astype(f32) + nr1[1].astype(f32)).astype(low)
    n3 = go([nrc(4, nb.at[0], nr2.at[0, pl.ds(0, 64)], 1), nrc(5, nb.at[1], nr2.at[1, pl.ds(64, 64)], -1)])
    osum.stage4()
    isum.stage4()
    osum.stage5()
    isum.stage5()
    osum.stage6()
    isum.stage6()
    osum.stage7()
    isum.stage7()
    isum.start_back()
    osum.start_back()
    for cp in n2 + n3: cp.wait_recv()
    n_out[...] = n_part[x].astype(f32) + nr2[0].astype(f32) + nr2[1].astype(f32)
    isum.back.wave1()
    osum.back.wave1()
    isum.back.wave2()
    osum.back.wave2()
    isum.back.wave3()
    osum.back.wave3()
    isum.back.wave4()
    osum.back.wave4()
    isum.finish()
    osum.finish()
    for cp in sent: cp.wait_send()


def grad_sum(o_part, i_part, n_part, cid):
    S = jax.ShapeDtypeStruct
    bf, f32 = jnp.bfloat16, jnp.float32
    V = pltpu.VMEM
    D = pltpu.SemaphoreType.DMA
    vm = pl.BlockSpec(memory_space=pltpu.VMEM)
    o_sums, i_sums, row_sums = pl.pallas_call(
        grad_sum_kernel,
        out_shape=(S((2, 4, 4, 48, 512), bf), S((2, 4, 4, 48, 640), bf), S((128, 1536), f32)),
        in_specs=[vm] * 3,
        out_specs=(vm,) * 3,
        scratch_shapes=[V((2, 64, 1536), bf), V((2, 64, 1536), bf), V((2, 128, 1536), bf),
                        D((6,)), D((6,))] + sum_scratch(OUTPUT_PARTS) + sum_scratch(INPUT_PARTS),
        compiler_params=pltpu.CompilerParams(collective_id=cid, has_side_effects=True, vmem_limit_bytes=28 << 20),
        name="grad_sum",
    )(o_part.reshape(2, 4, 4, 48, 512), i_part.reshape(2, 4, 4, 48, 640), n_part.reshape(4, 128, 1536))
    return o_sums.reshape(1536, 512), i_sums.reshape(1536, 640), row_sums


def attention_tables(documents):
    index = jnp.arange(documents.shape[0], dtype=jnp.int32)
    positions = index - jnp.sum((documents[None, :] < documents[:, None]).astype(jnp.int32), 1)
    freq = 10000.0 ** (-(jnp.arange(32, dtype=jnp.float32) * 2.0 / 64))
    angle = positions.astype(jnp.float32)[:, None] * freq[None, :]
    cos, sin = jnp.cos(angle), jnp.sin(angle)
    allowed = (documents[:, None] == documents[None, :]) & (index[None, :] <= index[:, None])
    return (jnp.concatenate([cos] * 4, 1), jnp.concatenate([-sin, sin] * 2, 1), jnp.where(allowed, 0.0, -1e30).astype(jnp.float32))


def finish_kernel(sums, o_sums, i_sums, gate, up, down, query, key, value, output, router, first, second):
    f32 = jnp.float32
    for n in range(5):
        for i, ref in enumerate((gate, up)):
            ref[n] = sums[:, 0, :, pl.ds(640 * i + 128 * n, 128)].astype(f32).reshape(256, 128)
        down[n] = sums[:, 0, :, pl.ds(1280 + 128 * n, 128)].astype(f32).reshape(256, 128).T
    query[...] = i_sums[:, 0:384].astype(f32)
    key[...] = i_sums[:, 384:512].astype(f32)
    value[...] = i_sums[:, 512:640].astype(f32)
    output[...] = o_sums[:, 0:384].astype(f32).T
    small = o_sums[:, 384:512].astype(f32).T
    router[...] = small[0:40, :]
    first[...] = small[40:41, :]
    second[...] = small[41:42, :]


def finish(sums, o_sums, i_sums):
    S = jax.ShapeDtypeStruct
    f32 = jnp.float32
    return pl.pallas_call(
        finish_kernel,
        grid=(6,),
        out_shape=(S((5, 1536, 128), f32), S((5, 1536, 128), f32), S((5, 128, 1536), f32), S((1536, 384), f32),
                   S((1536, 128), f32), S((1536, 128), f32), S((384, 1536), f32), S((40, 1536), f32), S((1, 1536), f32), S((1, 1536), f32)),
        in_specs=[pl.BlockSpec((4, 1, 64, 1920), lambda j: (0, j, 0, 0)), pl.BlockSpec((256, 512), lambda j: (j, 0)), pl.BlockSpec((256, 640), lambda j: (j, 0))],
        out_specs=(pl.BlockSpec((5, 256, 128), lambda j: (0, j, 0)), pl.BlockSpec((5, 256, 128), lambda j: (0, j, 0)),
                   pl.BlockSpec((5, 128, 256), lambda j: (0, 0, j)), pl.BlockSpec((256, 384), lambda j: (j, 0)),
                   pl.BlockSpec((256, 128), lambda j: (j, 0)), pl.BlockSpec((256, 128), lambda j: (j, 0)),
                   pl.BlockSpec((384, 256), lambda j: (0, j)), pl.BlockSpec((40, 256), lambda j: (0, j)),
                   pl.BlockSpec((1, 256), lambda j: (0, j)), pl.BlockSpec((1, 256), lambda j: (0, j))),
        compiler_params=pltpu.CompilerParams(vmem_limit_bytes=32 << 20),
        name="finish",
    )(sums, o_sums, i_sums)


def expert_back_kernel(acts_hbm, x_hbm, u_hbm, gate_hbm, up_hbm, router_hbm, down_hbm, out, dw_out, router_out,
                       w_ref, down_ref, acts, stage, q, sib, a3, b3, a4, b4, a5, b5, a6, b6, xu, acc, dwb, ya, yb,
                       w_sem, down_sem, act_sem, load_sem, sib_send, sib_recv, ssem, rsem, ysend, yrecv):
    f32, low = jnp.float32, jnp.bfloat16
    nk = 12
    wide = 640
    x = lax.axis_index("tensor"); e = lax.axis_index("expert"); y = lax.axis_index("dp")
    z = e // 2; c = e % 2
    def zi(d): return (z + d) % 4
    def xi(d): return (x + d) % 4
    def yi(d): return (y + d) % 4
    def peer(oz, ox):
        return {"expert": zi(oz) * 2 + c, "tensor": xi(ox)}
    def ypeer(o):
        return {"dp": yi(o)}
    partner = {"expert": z * 2 + 1 - c}

    def act_load(n):
        return pltpu.make_async_copy(acts_hbm.at[:, :, n], acts.at[:, :, n], act_sem.at[n])
    def x_load(j, k):
        cols = pl.ds(pl.multiple_of(j * 256, 256), 256)
        return [pltpu.make_async_copy(x_hbm.at[:, :, :, :, cols], xu.at[k % 2], load_sem.at[k % 2, 0])]
    def u_load(j, k):
        cols = pl.ds(pl.multiple_of(j * 256, 256), 256)
        return [pltpu.make_async_copy(u_hbm.at[:, :, :, :, cols], xu.at[k % 2], load_sem.at[k % 2, 1])]
    w_loads = weight_loads(gate_hbm, up_hbm, router_hbm, w_ref, w_sem)
    down_load = pltpu.make_async_copy(down_hbm, down_ref, down_sem)
    down_load.start()
    act_load(1 - c).start()
    act_load(c).start()
    for cp in x_load(0, 0): cp.start()
    for cp in w_loads: cp.start()
    barrier = pltpu.get_barrier_semaphore()
    near = [peer(1, 0), peer(-1, 0), peer(0, 1), peer(0, -1), partner, ypeer(1), ypeer(-1)]
    for p in near:
        pl.semaphore_signal(barrier, inc=1, device_id=p, device_id_type=MESH)
    pl.semaphore_wait(barrier, len(near))

    def sibs(k):
        return [pltpu.make_async_remote_copy(
            src_ref=stage.at[k % 2], dst_ref=sib.at[k % 2],
            send_sem=sib_send.at[k], recv_sem=sib_recv.at[k], device_id=partner, device_id_type=MESH)]
    def rc(k, n, src, dst, to):
        return pltpu.make_async_remote_copy(src_ref=src, dst_ref=dst, send_sem=ssem.at[k, n], recv_sem=rsem.at[k, n],
                                            device_id=to, device_id_type=MESH)
    def copies3(k):
        s = k % 4
        return [rc(k, 0, q.at[k % 9, zi(2), :, pl.ds(0, 32)], a3.at[s, 0], peer(1, 0)),
                rc(k, 1, q.at[k % 9, zi(2), :, pl.ds(32, 32)], a3.at[s, 1], peer(-1, 0)),
                rc(k, 2, q.at[k % 9, :, xi(2), pl.ds(64, 32)], b3.at[s, 0], peer(0, 1)),
                rc(k, 3, q.at[k % 9, :, xi(2), pl.ds(96, 32)], b3.at[s, 1], peer(0, -1))]
    def copies4(k):
        s = k % 4
        return [rc(k, 4, q.at[k % 9, zi(1), :, pl.ds(0, 64)], a4.at[s, 0], peer(1, 0)),
                rc(k, 5, q.at[k % 9, zi(-1), :, pl.ds(0, 64)], a4.at[s, 1], peer(-1, 0)),
                rc(k, 6, q.at[k % 9, :, xi(1), pl.ds(64, 64)], b4.at[s, 0], peer(0, 1)),
                rc(k, 7, q.at[k % 9, :, xi(-1), pl.ds(64, 64)], b4.at[s, 1], peer(0, -1))]
    def copies5(k):
        s = k % 4
        return [rc(k, 8, q.at[k % 9, z, xi(2), pl.ds(0, 32)], a5.at[s, 0], peer(0, 1)),
                rc(k, 9, q.at[k % 9, z, xi(2), pl.ds(32, 32)], a5.at[s, 1], peer(0, -1)),
                rc(k, 10, q.at[k % 9, zi(2), x, pl.ds(64, 32)], b5.at[s, 0], peer(1, 0)),
                rc(k, 11, q.at[k % 9, zi(2), x, pl.ds(96, 32)], b5.at[s, 1], peer(-1, 0))]
    def copies6(k):
        s = k % 4
        return [rc(k, 12, q.at[k % 9, z, xi(1), pl.ds(0, 64)], a6.at[s, 0], peer(0, 1)),
                rc(k, 13, q.at[k % 9, z, xi(-1), pl.ds(0, 64)], a6.at[s, 1], peer(0, -1)),
                rc(k, 14, q.at[k % 9, zi(1), x, pl.ds(64, 64)], b6.at[s, 0], peer(1, 0)),
                rc(k, 15, q.at[k % 9, zi(-1), x, pl.ds(64, 64)], b6.at[s, 1], peer(-1, 0))]
    def add(k, i, j, rows, *terms):
        t = q[k % 9, i, j, rows].astype(f32)
        for s in terms:
            t = t + s.astype(f32)
        q[k % 9, i, j, rows] = t.astype(low)

    def product(k, cc, put):
        cols = pl.ds(pl.multiple_of((k // 2) * 256, 256), 256)
        def rows(lanes): return acts[:, :, cc, :, lanes].reshape(2048, -1)
        @pl.when(k % 2 == 0)
        def _():
            put(jnp.dot(rows(slice(0, wide)), down_ref[:, cols], preferred_element_type=f32))
        @pl.when(k % 2 == 1)
        def _():
            put(lax.dot_general(rows(slice(wide, 2048)), w_ref[cols, :], (((1,), (1,)), ((), ())),
                                preferred_element_type=f32))

    def stage1(k):
        @pl.when(k == 0)
        def _():
            down_load.wait()
            act_load(1 - c).wait()
        @pl.when(k == 1)
        def _():
            for cp in w_loads: cp.wait()
        def put(r):
            stage[k % 2] = r.astype(low).reshape(4, 4, 128, 256)
        product(k, 1 - c, put)
        for cp in sibs(k): cp.start()

    def stage2(k):
        @pl.when(k == 0)
        def _(): act_load(c).wait()
        for cp in sibs(k): cp.wait()
        def put(r):
            q[k % 9] = (r.reshape(4, 4, 128, 256) + sib[k % 2].astype(f32)).astype(low)
        product(k, c, put)
        for cp in copies3(k): cp.start()

    def weight_part(k):
        @pl.when(k % 2 == 0)
        def _():
            for cp in x_load(0, k): cp.wait()
            for cp in u_load(k // 2, k + 1): cp.start()
        @pl.when(k % 2 == 1)
        def _():
            for cp in u_load(0, k): cp.wait()
        @pl.when((k + 1 < nk) & (k % 2 == 1))
        def _():
            for cp in x_load(k // 2 + 1, k + 1): cp.start()
        slot = (k // 2) % 3
        def make(lanes):
            return lax.dot_general(xu[k % 2].reshape(4096, 256), acts[:, :, :, :, lanes].reshape(4096, -1),
                                   (((0,), (0,)), ((), ())), preferred_element_type=f32)
        @pl.when(k % 2 == 0)
        def _():
            acc[...] = make(slice(wide, 2048))
            dwb[slot, :, :, 0 : 2 * wide] = acc[:, 0 : 2 * wide].astype(low).reshape(4, 64, 2 * wide)
            router_out[pl.ds(pl.multiple_of((k // 2) * 256, 256), 256), :] = acc[:, 2 * wide :]
        @pl.when(k % 2 == 1)
        def _():
            acc[:, 0:wide] = make(slice(0, wide))
            dwb[slot, :, :, 2 * wide :] = acc[:, 0:wide].astype(low).reshape(4, 64, wide)

    def yrc(j, n, src, dst, to):
        return pltpu.make_async_remote_copy(src_ref=src, dst_ref=dst, send_sem=ysend.at[j, n], recv_sem=yrecv.at[j, n],
                                            device_id=to, device_id_type=MESH)
    def ycopies1(j):
        s = j % 3
        return [yrc(j, 0, dwb.at[s, yi(2), pl.ds(0, 32)], ya.at[j % 4, 0], ypeer(1)),
                yrc(j, 1, dwb.at[s, yi(2), pl.ds(32, 32)], ya.at[j % 4, 1], ypeer(-1))]
    def ycopies2(j):
        s = j % 3
        return [yrc(j, 2, dwb.at[s, yi(1)], yb.at[j % 4, 0], ypeer(1)),
                yrc(j, 3, dwb.at[s, yi(-1)], yb.at[j % 4, 1], ypeer(-1))]
    def ystage1(j):
        for cp in ycopies1(j): cp.start()
    def ystage2(j):
        for cp in ycopies1(j): cp.wait_recv()
        s = j % 3
        for d, r, m in ((1, 0, 0), (-1, 32, 1)):
            dwb[s, yi(d), pl.ds(r, 32)] = (dwb[s, yi(d), pl.ds(r, 32)].astype(f32) + ya[j % 4, m].astype(f32)).astype(low)
        for cp in ycopies2(j): cp.start()
    def ystage3(j):
        for cp in ycopies2(j): cp.wait_recv()
        dw_out[j] = (dwb[j % 3, y].astype(f32) + yb[j % 4, 0].astype(f32) + yb[j % 4, 1].astype(f32)).astype(low)
        for cp in ycopies1(j) + ycopies2(j): cp.wait_send()

    def stage4(k):
        for cp in copies3(k): cp.wait_recv()
        s = k % 4
        def body(n, _):
            add(k, zi(1), n, pl.ds(0, 32), a3[s, 0, n])
            add(k, zi(-1), n, pl.ds(32, 32), a3[s, 1, n])
            add(k, n, xi(1), pl.ds(64, 32), b3[s, 0, n])
            add(k, n, xi(-1), pl.ds(96, 32), b3[s, 1, n])
            return 0
        lax.fori_loop(0, 4, body, 0)
        for cp in copies4(k): cp.start()
    def stage5(k):
        for cp in copies4(k): cp.wait_recv()
        s = k % 4
        def body(n, _):
            add(k, z, n, pl.ds(0, 64), a4[s, 0, n], a4[s, 1, n])
            add(k, n, x, pl.ds(64, 64), b4[s, 0, n], b4[s, 1, n])
            return 0
        lax.fori_loop(0, 4, body, 0)
        for cp in copies5(k): cp.start()
    def stage6(k):
        for cp in copies5(k): cp.wait_recv()
        s = k % 4
        add(k, z, xi(1), pl.ds(0, 32), a5[s, 0])
        add(k, z, xi(-1), pl.ds(32, 32), a5[s, 1])
        add(k, zi(1), x, pl.ds(64, 32), b5[s, 0])
        add(k, zi(-1), x, pl.ds(96, 32), b5[s, 1])
        for cp in copies6(k): cp.start()
    def stage7(k):
        for cp in copies6(k): cp.wait_recv()
        s = k % 4
        for h, m in ((0, a6), (64, b6)):
            t = q[k % 9, z, x, pl.ds(h, 64)].astype(f32) + m[s, 0].astype(f32) + m[s, 1].astype(f32)
            out[k % 2, pl.ds(h, 64), pl.ds(pl.multiple_of((k // 2) * 256, 256), 256)] = t
        for cp in copies3(k) + copies4(k) + copies5(k) + copies6(k): cp.wait_send()

    def step(i, _):
        for lag, st in ((7, stage7), (6, stage6), (5, stage5), (3, stage4), (1, stage2), (0, stage1)):
            k = i - lag
            @pl.when((k >= 0) & (k < nk))
            def _():
                st(k)
        n = i - 1
        for lag, st in ((5, ystage3), (3, ystage2)):
            k = n - lag
            @pl.when((k >= 0) & (k < nk) & (k % 2 == 0))
            def _():
                st(k // 2)
        @pl.when((n >= 0) & (n < nk))
        def _():
            weight_part(n)
            @pl.when(n % 2 == 1)
            def _():
                ystage1(n // 2)
        return 0
    lax.fori_loop(0, nk + 7, step, 0)


def expert_back(acts, x, u, gate, up, router, down, cid):
    bf = jnp.bfloat16
    V = pltpu.VMEM
    nk = 12
    D = pltpu.SemaphoreType.DMA
    vm = pl.BlockSpec(memory_space=pltpu.VMEM)
    anym = pl.BlockSpec(memory_space=pl.ANY)
    return pl.pallas_call(
        expert_back_kernel,
        out_shape=(jax.ShapeDtypeStruct((2, 128, 1536), jnp.float32),
                   jax.ShapeDtypeStruct((6, 64, 1920), bf),
                   jax.ShapeDtypeStruct((1536, 128), jnp.float32)),
        in_specs=[anym] * 7,
        out_specs=(vm, vm, vm),
        scratch_shapes=[V((1536, 1408), bf), V((640, 1536), bf), V((4, 4, 2, 128, 2048), bf), V((2, 4, 4, 128, 256), bf), V((9, 4, 4, 128, 256), bf), V((2, 4, 4, 128, 256), bf),
                        V((4, 2, 4, 32, 256), bf), V((4, 2, 4, 32, 256), bf),
                        V((4, 2, 4, 64, 256), bf), V((4, 2, 4, 64, 256), bf),
                        V((4, 2, 32, 256), bf), V((4, 2, 32, 256), bf),
                        V((4, 2, 64, 256), bf), V((4, 2, 64, 256), bf),
                        V((2, 4, 4, 2, 128, 256), bf), V((256, 1408), jnp.float32), V((3, 4, 64, 1920), bf),
                        V((4, 2, 32, 1920), bf), V((4, 2, 64, 1920), bf),
                        D((11,)), D(()), D((2,)), D((2, 2)), D((nk,)), D((nk,)), D((nk, 16)), D((nk, 16)), D((6, 4)), D((6, 4))],
        compiler_params=pltpu.CompilerParams(collective_id=cid, has_side_effects=True, vmem_limit_bytes=63 << 20),
        name="expert_back",
    )(acts, x, u, gate, up, router, down)


def shards(
    tokens,
    documents,
    expert_routes,
    attention_gain,
    query_weight,
    key_matrix,
    value_matrix,
    output_weight,
    expert_gain,
    router_weight,
    gate_weight,
    up_weight,
    down_weight,
    out_cotangent,
):
    width = tokens.shape[1]
    local_experts = gate_weight.shape[0]
    experts_all = router_weight.shape[1]
    wide = local_experts * gate_weight.shape[2]
    inputs = tokens.astype(jnp.float32)
    first_gain = attention_gain.astype(jnp.float32)
    second_gain = expert_gain.astype(jnp.float32)
    first_scale = lax.rsqrt(jnp.mean(inputs * inputs, -1, keepdims=True) + epsilon)
    tables = attention_tables(documents)
    attention_weights = (query_weight, key_matrix, value_matrix, output_weight)
    router_pad = jnp.pad(router_weight, ((0, 0), (0, 64 - experts_all)))
    expert_weights = (
        gate_weight,
        up_weight,
        jnp.concatenate([router_pad, router_pad], 1),
        down_weight.reshape(wide, width),
    )
    lined_routes = jnp.pad(expert_routes, ((0, 0), (0, 128 - expert_routes.shape[1])))
    (
        residual,
        plane_rows,
        acts,
        plane_upstream,
        group_tokens,
        group_rows,
        queries,
        keys,
        values,
        attended,
        logsum,
    ) = front(
        tokens,
        jnp.concatenate([out_cotangent, lined_routes.astype(jnp.bfloat16)], 1),
        first_gain.reshape(1, width),
        second_gain.reshape(1, width),
        *tables,
        *attention_weights,
        *expert_weights,
        6,
    )
    sums, weight_grads, router_pairs = expert_back(
        acts, plane_rows, plane_upstream, *expert_weights, 2
    )
    layer_output = (residual + sums[0]).astype(jnp.bfloat16)
    weight_grads = lax.all_gather(weight_grads, "dp", axis=0)
    residual_grad, output_part, input_part, normed_part = attention_back(
        sums,
        residual,
        out_cotangent,
        expert_routes,
        second_gain.reshape(1, width),
        expert_weights[2],
        router_pairs,
        group_rows,
        group_tokens.reshape(-1, width),
        *tables,
        queries,
        keys,
        values,
        attended,
        logsum,
        *attention_weights,
        cid=7,
    )
    output_sums, input_sums, normed_grad = grad_sum(output_part, input_part, normed_part, 4)
    input_gradient = residual_grad + norm_back(inputs, first_scale, first_gain, normed_grad)
    (
        gate_gradient,
        up_gradient,
        down_gradient,
        query_gradient,
        key_gradient,
        value_gradient,
        output_gradient,
        router_gradient,
        attention_gain_gradient,
        expert_gain_gradient,
    ) = finish(weight_grads, output_sums, input_sums)
    router_gradient = router_gradient.T
    attention_gain_gradient = attention_gain_gradient.reshape(width)
    expert_gain_gradient = expert_gain_gradient.reshape(width)
    return (
        layer_output,
        input_gradient,
        attention_gain_gradient,
        query_gradient,
        key_gradient,
        value_gradient,
        output_gradient,
        expert_gain_gradient,
        router_gradient,
        gate_gradient,
        up_gradient,
        down_gradient,
    )


def solution(mesh):
    placed = (
        P(("dp", "expert", "tensor"), None),
        P(("dp", "expert")),
        P(("dp", "expert", "tensor"), None),
        P(),
        P(None, "tensor"),
        P(None, "tensor"),
        P(None, "tensor"),
        P("tensor", None),
        P(),
        P(),
        P("expert", None, "tensor"),
        P("expert", None, "tensor"),
        P("expert", "tensor", None),
        P(("dp", "expert", "tensor"), None),
    )
    return jax.shard_map(
        shards,
        mesh=mesh,
        in_specs=placed,
        out_specs=(
            P(("dp", "expert", "tensor"), None),
            P(("dp", "expert", "tensor"), None),
            P(),
            P(None, "tensor"),
            P(None, "tensor"),
            P(None, "tensor"),
            P("tensor", None),
            P(),
            P(),
            P("expert", None, "tensor"),
            P("expert", None, "tensor"),
            P("expert", "tensor", None),
        ),
        check_vma=False,
    )
```
